32 devices in a mesh: batch: 2 (over x), chan: 16 (over z, y, core).
Axes of the slice: x: 2, y: 2, z: 4, core: 2. Of those that a mesh axis runs over, the one named last changes fastest.
Arguments:
- layer_in: bfloat16 [4, 768, 4096], P('batch', 'chan'), may hold values from -6 to 6
- seq_lengths: int32 [4], P('batch'), may hold values from 256 to 4096, as said below
- ln1_gain: bfloat16 [768], P('chan'), may hold values from 0.5 to 1.5
- first_norm_bias: bfloat16 [768], P('chan'), may hold values from -1.75 to 1.75
- in_weight: bfloat16 [768, 3, 768], P(None, None, 'chan'), may hold values from -0.21875 to 0.21875
- in_bias: bfloat16 [3, 768], P(None, 'chan'), may hold values from -1.75 to 1.75
- short_weight: bfloat16 [3, 3, 768], P(None, None, 'chan'), may hold values from -3.5 to 3.5
- short_bias: bfloat16 [3, 768], P(None, 'chan'), may hold values from -1.75 to 1.75
- filt_in: float32 [33, 64], replicated, may hold values from -1 to 1
- filt_in_bias: float32 [64], replicated, may hold values from -3 to 3
- filt_mid: float32 [64, 64], replicated, may hold values from -0.75 to 0.75
- filt_mid_bias: float32 [64], replicated, may hold values from -3 to 3
- sine_freq: float32 [64], replicated, may hold values from 1 to 8
- filt_out: float32 [64, 768], P(None, 'chan'), may hold values from -0.0625 to 0.0625
- decay_rate: float32 [768], P('chan'), may hold values from 0.5 to 100
- conv_bias: float32 [768], P('chan'), may hold values from -6 to 6
- out_weight: bfloat16 [768, 768], P('chan'), may hold values from -0.21875 to 0.21875
- out_bias: bfloat16 [768], P('chan'), may hold values from -1.75 to 1.75
- ln2_gain: bfloat16 [768], P('chan'), may hold values from 0.5 to 1.5
- second_norm_bias: bfloat16 [768], P('chan'), may hold values from -1.75 to 1.75
- up_weight: bfloat16 [3072, 768], P('chan'), may hold values from -0.21875 to 0.21875
- up_bias: bfloat16 [3072], P('chan'), may hold values from -1.75 to 1.75
- down_weight: bfloat16 [3072, 768], P('chan'), may hold values from -0.109375 to 0.109375
- down_bias: bfloat16 [768], P('chan'), may hold values from -1.75 to 1.75
- cotangent: bfloat16 [4, 768, 4096], P('batch', 'chan'), may hold values from -6 to 6
Outputs:
- layer_out: bfloat16 [4, 768, 4096], P('batch', 'chan')
- grad_layer_in: float32 [4, 768, 4096], P('batch', 'chan')
- grad_ln1_gain: float32 [768], P('chan')
- grad_ln1_bias: float32 [768], P('chan')
- grad_in_weight: float32 [768, 3, 768], P('batch', None, 'chan')
- grad_in_bias: float32 [3, 768], P(None, 'chan')
- grad_short_weight: float32 [3, 3, 768], P(None, None, 'chan')
- grad_short_bias: float32 [3, 768], P(None, 'chan')
- grad_filt_in: float32 [33, 64], replicated
- grad_filt_in_bias: float32 [64], replicated
- grad_filt_mid: float32 [64, 64], replicated
- grad_filt_mid_bias: float32 [64], replicated
- grad_sine_freq: float32 [64], replicated
- grad_filt_out: float32 [64, 768], P(None, 'chan')
- grad_decay_rate: float32 [768], P('chan')
- grad_conv_bias: float32 [768], P('chan')
- grad_out_weight: float32 [768, 768], P('chan', 'batch')
- grad_out_bias: float32 [768], P('chan')
- grad_ln2_gain: float32 [768], P('chan')
- grad_ln2_bias: float32 [768], P('chan')
- grad_up_weight: float32 [3072, 768], P('chan', 'batch')
- grad_up_bias: float32 [3072], P('chan')
- grad_down_weight: float32 [3072, 768], P('chan', 'batch')
- grad_down_bias: float32 [768], P('chan')
The draws below stay inside these ranges and needn't reach their ends.
Inputs may be any that keep to these rules, and one draw needn't show every extreme that they name: `seq_lengths`: among the 2 consecutive rows of one index of batch, at least one has length 4096.
All inputs are finite; a program needn't handle non-finite values.
Results may differ from the reference program's by a relative error of at most 0.0093.
Values may be sent and summed in bfloat16 or wider, within the bound.
No kernel may reach another device: no remote copies, remote signals or barrier semaphores. Data moves between devices by JAX's collectives and lax.ppermute only.
A program may use at most 256 MiB of HBM per device.

```python
import math
import jax
import jax.numpy as jnp
from jax import lax

D = 768
FF = 3072
FORD = 64
EMB = 33
KS = 3
MINLEN = 256
LMAX = 4096
SEQ_DEV = 2
SEQS = 4


def draw_seq_lengths(key, part):
    key = jax.random.fold_in(key, 11)
    first_key, second_key = jax.random.split(key)
    groups = SEQS // SEQ_DEV
    lengths = jax.random.randint(first_key, (groups, SEQ_DEV), MINLEN, LMAX + 1)
    longest = jax.random.randint(second_key, (groups, 1), 0, SEQ_DEV)
    slots = lax.iota(jnp.int32, SEQ_DEV)[None, :]
    lengths = jnp.where(slots == longest, LMAX, lengths)
    return lengths.reshape(SEQS).astype(jnp.int32)


def steps_of(stream_key, shape, cuts, low, high):
    gain = 1.0
    for position, blocks in cuts:
        heights = jax.random.uniform(jax.random.fold_in(jax.random.fold_in(stream_key, 6), position), (blocks,), jnp.float32, low / len(cuts), high / len(cuts))
        gain = gain * jnp.repeat(jnp.exp(heights), shape[position] // blocks).reshape((-1,) + (1,) * (len(shape) - 1 - position))
    return gain


def normal_values(rng, extent, scale, bound, cuts=(), held_as=jnp.bfloat16):
    values = jax.random.normal(rng, extent, jnp.float32) * scale
    if len(cuts) > 0:
        values = steps_of(rng, extent, cuts, -0.22, 0.18) * values
    return jnp.clip(values, min=-bound, max=bound).astype(held_as)


def setup_inputs(seed: int = 0) -> dict:
    seeds = jax.random.split(jax.random.key(seed), 26)
    return {
        "layer_in": normal_values(seeds[0], (SEQS, D, LMAX), 1.0, 6.0, ((0, 2), (1, 16))),
        "seq_lengths": draw_seq_lengths(jax.random.fold_in(seeds[25], 71), 0),
        "ln1_gain": jnp.clip(1.0 + 0.1 * jax.random.normal(seeds[2], (D,), jnp.float32), 0.5, 1.5).astype(jnp.bfloat16),
        "first_norm_bias": normal_values(seeds[3], (D,), 0.3, 1.75, ((0, 16),)),
        "in_weight": normal_values(seeds[4], (D, 3, D), D ** -0.5, 0.21875, ((2, 16),)),
        "in_bias": normal_values(seeds[5], (3, D), 0.3, 1.75, ((1, 16),)),
        "short_weight": normal_values(seeds[6], (KS, 3, D), 0.6, 3.5, ((2, 16),)),
        "short_bias": normal_values(seeds[7], (3, D), 0.3, 1.75, ((1, 16),)),
        "filt_in": normal_values(seeds[8], (EMB, FORD), EMB ** -0.5, 1.0, (), jnp.float32),
        "filt_in_bias": normal_values(seeds[9], (FORD,), 0.5, 3.0, (), jnp.float32),
        "filt_mid": normal_values(seeds[10], (FORD, FORD), FORD ** -0.5, 0.75, (), jnp.float32),
        "filt_mid_bias": normal_values(seeds[11], (FORD,), 0.5, 3.0, (), jnp.float32),
        "sine_freq": jnp.clip(jnp.exp(jax.random.uniform(seeds[12], (FORD,), jnp.float32, math.log(1.0), math.log(8.0))), 1.0, 8.0),
        "filt_out": normal_values(seeds[13], (FORD, D), 0.01, 0.0625, ((1, 16),), jnp.float32),
        "decay_rate": jnp.clip(jnp.exp(math.log(100.0) - 5.2983174 * jax.random.uniform(seeds[14], (D,), jnp.float32) ** steps_of(seeds[14], (D,), ((0, 16),), -0.2, 0.2)), 0.5, 100.0),
        "conv_bias": normal_values(seeds[15], (D,), 1.0, 6.0, ((0, 16),), jnp.float32),
        "out_weight": normal_values(seeds[16], (D, D), D ** -0.5, 0.21875, ((0, 16),)),
        "out_bias": normal_values(seeds[17], (D,), 0.3, 1.75, ((0, 16),)),
        "ln2_gain": jnp.clip(1.0 + 0.1 * jax.random.normal(seeds[18], (D,), jnp.float32), 0.5, 1.5).astype(jnp.bfloat16),
        "second_norm_bias": normal_values(seeds[19], (D,), 0.3, 1.75, ((0, 16),)),
        "up_weight": normal_values(seeds[20], (FF, D), D ** -0.5, 0.21875, ((0, 16),)),
        "up_bias": normal_values(seeds[21], (FF,), 0.3, 1.75, ((0, 16),)),
        "down_weight": normal_values(seeds[22], (FF, D), FF ** -0.5, 0.109375, ((0, 16),)),
        "down_bias": normal_values(seeds[23], (D,), 0.3, 1.75, ((0, 16),)),
        "cotangent": normal_values(seeds[24], (SEQS, D, LMAX), 1.0, 6.0, ((0, 2), (1, 16))),
    }


@jax.custom_vjp
def low(v):
    return lax.optimization_barrier(v.astype(jnp.bfloat16)).astype(jnp.float32)

@jax.custom_vjp
def low_back(v):
    return v

def low_keep(v):
    return (low(v), None)

def low_pass(kept, grad):
    return (grad,)

def back_keep(v):
    return (v, None)

def back_low(kept, grad):
    return (low(grad),)
low.defvjp(low_keep, low_pass)
low_back.defvjp(back_keep, back_low)
epsilon = 1e-05
decay_floor = 0.05
highest = lax.Precision.HIGHEST

def position_table(begin_at, row_count, length):
    places = begin_at + lax.iota(jnp.int32, row_count)
    orders = lax.iota(jnp.int32, (EMB - 1) // 2) + 1
    turn_count = places[:, None] * orders[None, :] % length
    phases = turn_count.astype(jnp.float32) * (2.0 * math.pi / length)
    ramp_pos = places.astype(jnp.float32) / (length - 1)
    return (jnp.concatenate([ramp_pos[:, None], jnp.cos(phases), -jnp.sin(phases)], axis=1), ramp_pos)

def make_filter(pos_table, ramp_pos, w_first, b_first, w_second, b_second, sine_rate, w_last, decay_rates):
    first_hidden = jnp.sin(sine_rate * (jnp.dot(pos_table, w_first, precision=highest) + b_first))
    second_hidden = jnp.sin(sine_rate * (jnp.dot(first_hidden, w_second, precision=highest) + b_second))
    raw_filter = jnp.dot(second_hidden, w_last, precision=highest)
    return raw_filter * (jnp.exp(-ramp_pos[:, None] * decay_rates[None, :]) + decay_floor)

def layer_norm(values, gain_vec, offset):
    center = values - lax.optimization_barrier(jnp.mean(values, axis=-1, keepdims=True))
    spread_sq = lax.optimization_barrier(jnp.mean(center * center, axis=-1, keepdims=True))
    return center * lax.rsqrt(spread_sq + epsilon) * gain_vec + offset

def long_conv(signal, kernel):
    length = signal.shape[1]
    spectrum = jnp.fft.rfft(signal, n=2 * length, axis=1) * jnp.fft.rfft(kernel, n=2 * length, axis=0)[None]
    return jnp.fft.irfft(spectrum, n=2 * length, axis=1)[:, :length]

def forward(layer_in, ln1_gain, first_norm_bias, in_weight, in_bias, short_weight, short_bias, filt_in, filt_in_bias, filt_mid, filt_mid_bias, sine_freq, filt_out, decay_rate, conv_bias, out_weight, out_bias, ln2_gain, second_norm_bias, up_weight, up_bias, down_weight, down_bias, live_mask):
    seq_count = layer_in.shape[0]
    token_rows = jnp.transpose(layer_in, (0, 2, 1)).reshape(-1, D)
    normed = layer_norm(token_rows, ln1_gain, first_norm_bias)
    projected = low_back(jnp.dot(low(normed), in_weight.reshape(D, 3 * D), precision=highest))
    projected = projected.reshape(seq_count, LMAX, 3, D) + in_bias
    padded = jnp.pad(projected, ((0, 0), (KS - 1, 0), (0, 0), (0, 0)))
    shorted = short_bias + jnp.zeros_like(projected)
    for offset in range(KS):
        shorted = shorted + short_weight[offset] * padded[:, KS - 1 - offset:KS - 1 - offset + LMAX]
    pos_table, ramp_pos = position_table(0, LMAX, LMAX)
    kernel = make_filter(pos_table, ramp_pos, filt_in, filt_in_bias, filt_mid, filt_mid_bias, sine_freq, filt_out, decay_rate)
    mixed_in = shorted[:, :, 2] * shorted[:, :, 1]
    convolved = long_conv(mixed_in, kernel) + conv_bias * mixed_in
    gated_out = convolved * shorted[:, :, 0]
    branch = low_back(jnp.dot(low(gated_out.reshape(-1, D)), out_weight, precision=highest)) + out_bias
    residual_stream = token_rows + branch
    second_normed_rows = layer_norm(residual_stream, ln2_gain, second_norm_bias)
    hidden = low_back(jnp.dot(low(second_normed_rows), up_weight.T, precision=highest)) + up_bias
    activated = jax.nn.gelu(hidden, approximate=True)
    mlp_out = low_back(jnp.dot(low(activated), down_weight, precision=highest)) + down_bias
    result_rows = live_mask[:, None] * (residual_stream + mlp_out)
    return jnp.transpose(result_rows.reshape(seq_count, LMAX, D), (0, 2, 1))

def reference(layer_in, seq_lengths, ln1_gain, first_norm_bias, in_weight, in_bias, short_weight, short_bias, filt_in, filt_in_bias, filt_mid, filt_mid_bias, sine_freq, filt_out, decay_rate, conv_bias, out_weight, out_bias, ln2_gain, second_norm_bias, up_weight, up_bias, down_weight, down_bias, cotangent):
    positions = lax.iota(jnp.int32, LMAX)
    live_mask = (positions[None, :] < seq_lengths[:, None]).astype(jnp.float32).reshape(-1)
    floats = tuple((array_in.astype(jnp.float32) for array_in in (layer_in, ln1_gain, first_norm_bias, in_weight, in_bias, short_weight, short_bias, filt_in, filt_in_bias, filt_mid, filt_mid_bias, sine_freq, filt_out, decay_rate, conv_bias, out_weight, out_bias, ln2_gain, second_norm_bias, up_weight, up_bias, down_weight, down_bias)))

    def masked(*params):
        return forward(*params, live_mask)
    result, pullback = jax.vjp(masked, *floats)
    gradients = pullback(cotangent.astype(jnp.float32))
    return (result.astype(jnp.bfloat16), gradients[0], gradients[1], gradients[2], gradients[3], gradients[4], gradients[5], gradients[6], gradients[7], gradients[8], gradients[9], gradients[10], gradients[11], gradients[12], gradients[13], gradients[14], gradients[15], gradients[16], gradients[17], gradients[18], gradients[19], gradients[20], gradients[21], gradients[22])
```

```python
import math

import jax
import jax.numpy as jnp
import numpy as np
from jax import lax
from jax.experimental import pallas as pl
from jax.experimental.pallas import tpu as pltpu
from jax.sharding import PartitionSpec as P

EMB = 33
KS = 3
LMAX = 4096
LANE = 128
COARSE = LMAX // LANE
REPS = tuple(ka + 8 * kb for ka, count in ((0, 5), (1, 8), (2, 8), (3, 8), (4, 4)) for kb in range(count))
PLACE = {k1: i for i, k1 in enumerate(REPS)}
epsilon = 1e-05
decay_floor = 0.05
highest = lax.Precision.HIGHEST
f32 = jnp.float32
bf16 = jnp.bfloat16
vmem_limit = 56 * 1024 * 1024


def unit(turns):
    angle = 2.0 * math.pi * turns
    return math.cos(angle), math.sin(angle)


def scaled(z, c, s):
    re, im = z
    if im is None:
        return re * c, re * s
    return re * c - im * s, re * s + im * c


def plus(a, b):
    return a[0] + b[0], a[1] + b[1]


def minus(a, b):
    return a[0] - b[0], a[1] - b[1]


def dft4(z, sign):
    s0, d0 = plus(z[0], z[2]), minus(z[0], z[2])
    s1, d1 = plus(z[1], z[3]), minus(z[1], z[3])
    turned = (-d1[1], d1[0]) if sign > 0 else (d1[1], -d1[0])
    return [plus(s0, s1), plus(d0, turned), minus(s0, s1), minus(d0, turned)]


def dft8(z, sign):
    even, odd = dft4(z[0::2], sign), dft4(z[1::2], sign)
    c = math.sqrt(0.5)
    o1 = odd[1]
    o3 = odd[3]
    if sign > 0:
        odd1 = ((o1[0] - o1[1]) * c, (o1[0] + o1[1]) * c)
        odd2 = (-odd[2][1], odd[2][0])
        odd3 = ((-o3[0] - o3[1]) * c, (o3[0] - o3[1]) * c)
    else:
        odd1 = ((o1[0] + o1[1]) * c, (o1[1] - o1[0]) * c)
        odd2 = (odd[2][1], -odd[2][0])
        odd3 = ((o3[1] - o3[0]) * c, (-o3[0] - o3[1]) * c)
    turned = [odd[0], odd1, odd2, odd3]
    return [plus(even[i], turned[i]) for i in range(4)] + [minus(even[i], turned[i]) for i in range(4)]


def coarse_forward(xs, put):
    c = math.sqrt(0.5)
    cols = {ka: [None] * 8 for ka in range(5)}
    for b in range(8):
        x0, x1, x2, x3 = xs[b], xs[8 + b], xs[16 + b], xs[24 + b]
        s02, d02, s13, d13 = x0 + x2, x0 - x2, x1 + x3, x1 - x3
        d13c, s13c = d13 * c, s13 * c
        cols[0][b] = s02 + s13
        cols[4][b] = scaled((s02 - s13, None), *unit(-4 * b / 64))
        cols[2][b] = scaled((d02, -d13), *unit(-2 * b / 64))
        cols[1][b] = scaled((x0 + d13c, -s13c - x2), *unit(-b / 64))
        cols[3][b] = scaled((x0 - d13c, x2 - s13c), *unit(-3 * b / 64))
    for ka in (1, 2, 3):
        for kb, z in enumerate(dft8(cols[ka], -1)):
            put(ka + 8 * kb, z)
    for kb, z in enumerate(dft8(cols[4], -1)[:4]):
        put(4 + 8 * kb, z)
    r = cols[0]
    s04, d04, s26, d26 = r[0] + r[4], r[0] - r[4], r[2] + r[6], r[2] - r[6]
    s15, d15, s37, d37 = r[1] + r[5], r[1] - r[5], r[3] + r[7], r[3] - r[7]
    p, q = (d15 - d37) * c, (d15 + d37) * c
    even, odd = s04 + s26, s15 + s37
    put(0, (even + odd, None))
    put(32, (even - odd, None))
    put(16, (s04 - s26, s37 - s15))
    put(8, (d04 + p, -d26 - q))
    put(24, (d04 - p, d26 - q))


def coarse_inverse(get):
    c = math.sqrt(0.5)
    u = {}
    for ka in (1, 2, 3):
        back = dft8([get(ka + 8 * kb) for kb in range(8)], 1)
        u[ka] = [scaled(back[b], *unit(b * ka / 64)) for b in range(8)]
    v0, v32 = get(0)[0], get(32)[0]
    v8, v16, v24 = get(8), get(16), get(24)
    flat = []
    for b in range(8):
        total = v0 + v32 if b % 2 == 0 else v0 - v32
        for kb, v in ((1, v8), (2, v16), (3, v24)):
            co, si = unit(b * kb / 8)
            if abs(co) > 1e-9:
                total = total + v[0] * (2.0 * co)
            if abs(si) > 1e-9:
                total = total - v[1] * (2.0 * si)
        flat.append(total)
    odd = [get(4 + 8 * kb) for kb in range(4)]
    odd = odd + [(z[0], -z[1]) for z in odd[::-1]]
    half = dft8(odd, 1)
    quarter = []
    for b in range(8):
        co, si = unit(4 * b / 64)
        quarter.append(half[b][0] * co - half[b][1] * si)
    out = [None] * COARSE
    for b in range(8):
        u1, u2, u3 = u[1][b], u[2][b], u[3][b]
        s, d = flat[b] + quarter[b], flat[b] - quarter[b]
        dr, sr = (u1[0] - u3[0]) * c, u1[0] + u3[0]
        si_, di = (u1[1] + u3[1]) * c, u1[1] - u3[1]
        out[b] = s + 2.0 * (sr + u2[0])
        out[16 + b] = s - 2.0 * (di + u2[0])
        out[8 + b] = d + 2.0 * (dr - si_ - u2[1])
        out[24 + b] = d + 2.0 * (u2[1] - dr - si_)
    return out


def transform_tables():
    fine = np.arange(LANE)
    angle = 2.0 * math.pi * ((fine[:, None] * fine[None, :]) % LANE) / LANE
    co, si = np.cos(angle), np.sin(angle)
    ahead = np.block([[co, -si], [si, co]])
    back = ahead.T / (2.0 * LMAX)
    reps = np.array(REPS)
    turn = 2.0 * math.pi * ((reps[:, None] * fine[None, :]) % (2 * LMAX)) / (2 * LMAX)
    twist = np.concatenate([np.cos(turn), -np.sin(turn)], axis=1)[:, None, :]

    def pieces(table):
        table = table.astype(np.float32)
        upper = table.astype(jnp.bfloat16)
        lower = (table - upper.astype(np.float32)).astype(jnp.bfloat16)
        return np.stack([upper, lower])

    return pieces(ahead), pieces(back), twist.astype(np.float32)


AHEAD, BACK, TWIST = transform_tables()


def three_pass(values, table_ref):
    upper = values.astype(bf16)
    lower = (values - upper.astype(f32)).astype(bf16)
    t0, t1 = table_ref[0], table_ref[1]
    return (
        jnp.dot(upper, t0, preferred_element_type=f32)
        + jnp.dot(lower, t0, preferred_element_type=f32)
        + jnp.dot(upper, t1, preferred_element_type=f32)
    )


def rows_forward(xs_ref, spec_ref, rows):
    def step(g, carry):
        at = pl.ds(pl.multiple_of(g * 8, 8), 8)
        xs = [xs_ref[n, at, :] for n in range(COARSE)]

        def put(k1, z):
            i = PLACE[k1]
            spec_ref[i, at, 0:LANE] = z[0]
            spec_ref[i, at, LANE : 2 * LANE] = jnp.zeros_like(z[0]) if z[1] is None else z[1]

        coarse_forward(xs, put)
        return carry

    lax.fori_loop(0, rows // 8, step, 0)


def rows_inverse(spec_ref, ys_ref, rows):
    def step(g, carry):
        at = pl.ds(pl.multiple_of(g * 8, 8), 8)

        def get(k1):
            i = PLACE[k1]
            return spec_ref[i, at, 0:LANE], spec_ref[i, at, LANE : 2 * LANE]

        for n, y in enumerate(coarse_inverse(get)):
            ys_ref[n, at, :] = y
        return carry

    lax.fori_loop(0, rows // 8, step, 0)


def fine_forward(spec, twist, ahead_ref):
    re, im = spec[:, :LANE], spec[:, LANE:]
    tr, ti = twist[:, :LANE], twist[:, LANE:]
    return three_pass(jnp.concatenate([re * tr - im * ti, re * ti + im * tr], axis=1), ahead_ref)


def fine_inverse(spec, twist, back_ref):
    v = three_pass(spec, back_ref)
    re, im = v[:, :LANE], v[:, LANE:]
    tr, ti = twist[:, :LANE], twist[:, LANE:]
    return jnp.concatenate([re * tr + im * ti, im * tr - re * ti], axis=1)


def times(a, b):
    ar, ai, br, bi = a[:, :LANE], a[:, LANE:], b[:, :LANE], b[:, LANE:]
    return jnp.concatenate([ar * br - ai * bi, ar * bi + ai * br], axis=1)


def times_conj(a, b):
    ar, ai, br, bi = a[:, :LANE], a[:, LANE:], b[:, :LANE], b[:, LANE:]
    return jnp.concatenate([ar * br + ai * bi, ai * br - ar * bi], axis=1)


def spread(blocks_ref, xs_ref):
    per = blocks_ref.shape[2] // LANE
    for n in range(COARSE):
        r = n % per
        xs_ref[n] = blocks_ref[n // per, :, r * LANE : (r + 1) * LANE].astype(f32)


def filter_spectrum_body(filter_ref, twist_ref, ahead_ref, out_ref, xs_ref):
    rows = filter_ref.shape[0]
    for n in range(COARSE):
        xs_ref[n] = filter_ref[:, n * LANE : (n + 1) * LANE]
    rows_forward(xs_ref, out_ref, rows)

    def step(i, carry):
        out_ref[i] = fine_forward(out_ref[i], twist_ref[i], ahead_ref)
        return carry

    lax.fori_loop(0, len(REPS), step, 0)


def conv_forward_body(seqs, mixed_ref, filt_ref, bias_ref, twist_ref, ahead_ref, back_ref, out_ref, spec_ref, xs_ref, work_ref):
    rows = mixed_ref.shape[1]
    spread(mixed_ref, xs_ref)
    rows_forward(xs_ref, spec_ref, rows)

    def step(i, carry):
        z = fine_forward(spec_ref[i], twist_ref[i], ahead_ref)
        spec_ref[i] = z
        k = filt_ref[i]
        work_ref[i] = fine_inverse(times(z, jnp.concatenate([k] * seqs, axis=0)), twist_ref[i], back_ref)
        return carry

    lax.fori_loop(0, len(REPS), step, 0)
    ys_ref = xs_ref
    rows_inverse(work_ref, ys_ref, rows)
    per = mixed_ref.shape[2] // LANE
    bias = jnp.concatenate([bias_ref[...]] * seqs, axis=0)
    for n in range(COARSE):
        at = (n // per, slice(None), slice((n % per) * LANE, (n % per + 1) * LANE))
        out_ref[at] = (ys_ref[n] + bias * mixed_ref[at].astype(f32)).astype(bf16)


def conv_backward_body(
    seqs, d_ref, mixed_ref, mixed_spec_ref, filt_ref, bias_ref, twist_ref, ahead_ref, back_ref, out_ref, dfilt_ref, dbias_ref, xs_ref, spec_ref, work_ref, ys_ref
):
    rows = d_ref.shape[1]
    chans = rows // seqs
    spread(d_ref, xs_ref)
    rows_forward(xs_ref, spec_ref, rows)

    def step(i, carry):
        z = fine_forward(spec_ref[i], twist_ref[i], ahead_ref)
        k = jnp.concatenate([filt_ref[i]] * seqs, axis=0)
        cross = times_conj(z, mixed_spec_ref[i])
        cross = sum(cross[s * chans : (s + 1) * chans] for s in range(seqs))
        both = jnp.concatenate([times_conj(z, k), cross], axis=0)
        work_ref[i] = fine_inverse(both, twist_ref[i], back_ref)
        return carry

    lax.fori_loop(0, len(REPS), step, 0)
    rows_inverse(work_ref, ys_ref, rows + chans)
    per = d_ref.shape[2] // LANE
    bias = jnp.concatenate([bias_ref[...]] * seqs, axis=0)
    total = jnp.zeros((rows, LANE), f32)
    for n in range(COARSE):
        at = (n // per, slice(None), slice((n % per) * LANE, (n % per + 1) * LANE))
        d = xs_ref[n]
        out_ref[at] = (ys_ref[n, :rows, :] + bias * d).astype(bf16)
        total = total + d * mixed_ref[at].astype(f32)
        dfilt_ref[:, n * LANE : (n + 1) * LANE] = ys_ref[n, rows:, :]
    total = sum(total[s * chans : (s + 1) * chans] for s in range(seqs))
    dbias_ref[...] = jnp.sum(total, axis=1, keepdims=True)


def whole_call(body, out_shape, scratch, *args):
    return pl.pallas_call(
        body,
        out_shape=out_shape,
        in_specs=[pl.BlockSpec(memory_space=pltpu.VMEM)] * len(args),
        out_specs=jax.tree.map(lambda _: pl.BlockSpec(memory_space=pltpu.VMEM), out_shape),
        scratch_shapes=scratch,
        compiler_params=pltpu.CompilerParams(vmem_limit_bytes=vmem_limit),
    )(*args)


def filter_spectrum(filt):
    rows = filt.shape[0]
    return whole_call(
        filter_spectrum_body,
        jax.ShapeDtypeStruct((len(REPS), rows, 2 * LANE), f32),
        [pltpu.VMEM((COARSE, rows, LANE), f32)],
        filt,
        jnp.asarray(TWIST),
        jnp.asarray(AHEAD),
    )


def conv_forward(mixed, filt_spec, bias, seqs):
    blocks, rows, width = mixed.shape
    n = len(REPS)
    return whole_call(
        lambda *refs: conv_forward_body(seqs, *refs),
        (jax.ShapeDtypeStruct(mixed.shape, bf16), jax.ShapeDtypeStruct((n, rows, 2 * LANE), f32)),
        [pltpu.VMEM((COARSE, rows, LANE), f32), pltpu.VMEM((n, rows, 2 * LANE), f32)],
        mixed,
        filt_spec,
        bias,
        jnp.asarray(TWIST),
        jnp.asarray(AHEAD),
        jnp.asarray(BACK),
    )


def conv_backward(d_conv, mixed, mixed_spec, filt_spec, bias, seqs):
    blocks, rows, width = mixed.shape
    chans = rows // seqs
    n = len(REPS)
    return whole_call(
        lambda *refs: conv_backward_body(seqs, *refs),
        (
            jax.ShapeDtypeStruct(mixed.shape, bf16),
            jax.ShapeDtypeStruct((chans, LMAX), f32),
            jax.ShapeDtypeStruct((chans, 1), f32),
        ),
        [
            pltpu.VMEM((COARSE, rows, LANE), f32),
            pltpu.VMEM((n, rows, 2 * LANE), f32),
            pltpu.VMEM((n, rows + chans, 2 * LANE), f32),
            pltpu.VMEM((COARSE, rows + chans, LANE), f32),
        ],
        d_conv,
        mixed,
        mixed_spec,
        filt_spec,
        bias,
        jnp.asarray(TWIST),
        jnp.asarray(AHEAD),
        jnp.asarray(BACK),
    )


def earlier(values, halo, by):
    lane = lax.broadcasted_iota(jnp.int32, values.shape, 1)
    moved = pltpu.roll(values, by, 1)
    for i in range(by):
        moved = jnp.where(lane == i, halo[:, KS - 1 - by + i : KS - by + i], moved)
    return moved


def later(values, halo, by):
    width = values.shape[1]
    lane = lax.broadcasted_iota(jnp.int32, values.shape, 1)
    moved = pltpu.roll(values, width - by, 1)
    for i in range(by):
        moved = jnp.where(lane == width - by + i, halo[:, i : i + 1], moved)
    return moved


def short_forward_body(seqs, proj_ref, halo_ref, prm_ref, short_ref, mixed_ref):
    width = proj_ref.shape[3] // seqs
    mixed = []
    for s in range(seqs):
        part = slice(s * width, (s + 1) * width)
        parts = []
        for i in range(3):
            prm = prm_ref[0, i]
            x = proj_ref[0, i, :, part] + prm[:, 0:1]
            halo = halo_ref[0, i][:, s * (KS - 1) : (s + 1) * (KS - 1)]
            y = prm[:, 1:2] + prm[:, 2:3] * x
            for j in range(1, KS):
                y = y + prm[:, 2 + j : 3 + j] * earlier(x, halo, j)
            short_ref[0, i, :, part] = y
            parts.append(y)
        mixed.append(parts[1] * parts[2])
    mixed_ref[0] = jnp.concatenate(mixed, axis=0).astype(bf16)


def short_forward(proj, halo, prm, seqs):
    devices, _, chans, cols = proj.shape
    block = lambda a: pl.BlockSpec((1,) + a.shape[1:], lambda d: (d,) + (0,) * (len(a.shape) - 1))
    out = (
        jax.ShapeDtypeStruct(proj.shape, f32),
        jax.ShapeDtypeStruct((devices, seqs * chans, cols // seqs), bf16),
    )
    return pl.pallas_call(
        lambda *refs: short_forward_body(seqs, *refs),
        grid=(devices,),
        out_shape=out,
        in_specs=[block(proj), block(halo), block(prm)],
        out_specs=tuple(block(o) for o in out),
        compiler_params=pltpu.CompilerParams(vmem_limit_bytes=vmem_limit),
    )(proj, halo, prm)


def short_backward_body(seqs, d_gated_ref, conv_ref, d_mixed_ref, proj_ref, halo_ref, short_ref, head_ref, prm_ref, out_ref, sums_ref):
    width = proj_ref.shape[3] // seqs
    sums = [[0.0] * (2 + KS) for _ in range(3)]
    for s in range(seqs):
        part = slice(s * width, (s + 1) * width)
        d_mixed = d_mixed_ref[0, :, part]
        d_short = (
            d_gated_ref[0, :, part] * conv_ref[0, :, part],
            d_mixed * short_ref[0, 2, :, part],
            d_mixed * short_ref[0, 1, :, part],
        )
        for i in range(3):
            prm = prm_ref[0, i]
            d = d_short[i]
            x = proj_ref[0, i, :, part] + prm[:, 0:1]
            halo = halo_ref[0, i][:, s * (KS - 1) : (s + 1) * (KS - 1)]
            head = head_ref[0, i][:, s * (KS - 1) : (s + 1) * (KS - 1)]
            back = prm[:, 2:3] * d
            sums[i][1] = sums[i][1] + jnp.sum(d, axis=1, keepdims=True)
            sums[i][2] = sums[i][2] + jnp.sum(d * x, axis=1, keepdims=True)
            for j in range(1, KS):
                back = back + prm[:, 2 + j : 3 + j] * later(d, head, j)
                sums[i][2 + j] = sums[i][2 + j] + jnp.sum(d * earlier(x, halo, j), axis=1, keepdims=True)
            sums[i][0] = sums[i][0] + jnp.sum(back, axis=1, keepdims=True)
            out_ref[0, i, :, part] = back
    for i in range(3):
        lane = lax.broadcasted_iota(jnp.int32, sums_ref.shape[2:], 1)
        total = jnp.zeros(sums_ref.shape[2:], f32)
        for k in range(2 + KS):
            total = jnp.where(lane == k, sums[i][k], total)
        sums_ref[0, i] = total


def short_backward(d_gated, conv, d_mixed, proj, halo, short, head, prm, seqs):
    devices, _, chans, cols = proj.shape
    block = lambda a: pl.BlockSpec((1,) + a.shape[1:], lambda d: (d,) + (0,) * (len(a.shape) - 1))
    args = (d_gated, conv, d_mixed, proj, halo, short, head, prm)
    out = (jax.ShapeDtypeStruct(proj.shape, f32), jax.ShapeDtypeStruct(prm.shape, f32))
    return pl.pallas_call(
        lambda *refs: short_backward_body(seqs, *refs),
        grid=(devices,),
        out_shape=out,
        in_specs=[block(a) for a in args],
        out_specs=tuple(block(o) for o in out),
        compiler_params=pltpu.CompilerParams(vmem_limit_bytes=vmem_limit),
    )(*args)


def position_table():
    places = np.arange(LMAX)
    orders = np.arange(1, (EMB - 1) // 2 + 1)
    turns = 2.0 * math.pi * ((orders[:, None] * places[None, :]) % LMAX) / LMAX
    ramp = places[None, :] / (LMAX - 1)
    return np.concatenate([ramp, np.cos(turns), -np.sin(turns)], axis=0).astype(np.float32)


FEAT = position_table()


def mm(a, b, dims):
    return lax.dot_general(a, b, (dims, ((), ())), precision=highest, preferred_element_type=f32)


NN = ((1,), (0,))
TN = ((0,), (0,))
NT = ((1,), (1,))


def mm16(a, b, dims):
    return lax.dot_general(a, b, (dims, ((), ())), preferred_element_type=f32)


def exchange(values):
    return lax.all_to_all(values, "chan", split_axis=0, concat_axis=0, tiled=True)


def norm_forward(values):
    mean = jnp.mean(values, axis=0, keepdims=True)
    centered = values - mean
    var = jnp.mean(centered * centered, axis=0, keepdims=True)
    inverse = lax.rsqrt(var + epsilon)
    return centered * inverse, inverse


def norm_backward(scaled_grad, normed, inverse):
    return inverse * (
        scaled_grad
        - jnp.mean(scaled_grad, axis=0, keepdims=True)
        - normed * jnp.mean(scaled_grad * normed, axis=0, keepdims=True)
    )


def on_device(
    layer_in,
    seq_lengths,
    ln1_gain,
    first_norm_bias,
    in_weight,
    in_bias,
    short_weight,
    short_bias,
    filt_in,
    filt_in_bias,
    filt_mid,
    filt_mid_bias,
    sine_freq,
    filt_out,
    decay_rate,
    conv_bias,
    out_weight,
    out_bias,
    ln2_gain,
    second_norm_bias,
    up_weight,
    up_bias,
    down_weight,
    down_bias,
    cotangent,
):
    seqs, chans, _ = layer_in.shape
    devices = lax.axis_size("chan")
    groups = lax.axis_size("batch")
    width = LMAX // devices
    dim = chans * devices
    cols = seqs * width
    hid = up_weight.shape[0]
    place = lax.axis_index("chan")

    def to_blocks(values):
        return (
            values.reshape(seqs, chans, devices, width)
            .transpose(2, 0, 1, 3)
            .reshape(devices, seqs * chans, width)
        )

    def from_blocks(blocks):
        return (
            blocks.reshape(devices, seqs, chans, width)
            .transpose(1, 2, 0, 3)
            .reshape(seqs, chans, LMAX)
        )

    def rows_of(blocks):
        return (
            blocks.reshape(devices, seqs, chans, width)
            .transpose(0, 2, 1, 3)
            .reshape(dim, cols)
        )

    def blocks_of(values):
        return (
            values.reshape(devices, chans, seqs, width)
            .transpose(0, 2, 1, 3)
            .reshape(devices, seqs * chans, width)
        )

    x_blocks = exchange(to_blocks(layer_in))
    small = jnp.concatenate(
        [
            in_bias.reshape(-1),
            short_bias.reshape(-1),
            short_weight.reshape(-1),
            ln1_gain,
            first_norm_bias,
            ln2_gain,
            second_norm_bias,
            out_bias,
            down_bias,
            up_bias,
        ]
    )
    small_rows = -(-small.shape[0] // (16 * dim)) * 16
    small = jnp.pad(small, (0, small_rows * dim - small.shape[0])).reshape(small_rows, dim)
    in_rows = in_weight.transpose(1, 2, 0).reshape(3 * chans, dim)
    gathered = lax.all_gather(jnp.concatenate([in_rows, small], axis=0), "chan", axis=0)
    cot_blocks = exchange(to_blocks(cotangent))
    out_all = lax.all_gather(out_weight, "chan", axis=0, tiled=True)
    up_all = lax.all_gather(up_weight, "chan", axis=0, tiled=True)
    down_all = lax.all_gather(down_weight, "chan", axis=0, tiled=True)

    in_all = gathered[:, : 3 * chans].reshape(3 * dim, dim)
    small_all = gathered[:, 3 * chans :].reshape(devices, small_rows * dim).astype(f32)
    by_chan = small_all[:, : 21 * chans].reshape(devices, 21, chans)
    up_bias_all = small_all[:, 21 * chans : 21 * chans + hid].reshape(devices * hid, 1)
    prm = jnp.concatenate(
        [
            by_chan[:, 0:3, None],
            by_chan[:, 3:6, None],
            by_chan[:, 6:15].reshape(devices, KS, 3, chans).transpose(0, 2, 1, 3),
            jnp.zeros((devices, 3, 8 - 2 - KS, chans), f32),
        ],
        axis=2,
    ).transpose(0, 1, 3, 2)
    wide = by_chan[:, 15:21].transpose(1, 0, 2).reshape(6, dim, 1)
    gain1, shift1, gain2, shift2, out_b, down_b = (wide[i] for i in range(6))

    feat = jnp.asarray(FEAT)
    ramp = feat[0:1]
    rate = sine_freq[:, None]
    pre1 = mm(filt_in, feat, TN) + filt_in_bias[:, None]
    h1 = jnp.sin(rate * pre1)
    pre2 = mm(filt_mid, h1, TN) + filt_mid_bias[:, None]
    h2 = jnp.sin(rate * pre2)
    raw = mm(filt_out, h2, TN)
    falling = jnp.exp(-ramp * decay_rate[:, None])
    env = falling + decay_floor
    filt_spec = filter_spectrum(raw * env)
    bias_col = conv_bias[:, None]

    x = rows_of(x_blocks).astype(f32)
    xhat1, rstd1 = norm_forward(x)
    xn1 = (xhat1 * gain1 + shift1).astype(bf16)
    proj = mm16(in_all, xn1, NN).reshape(devices, 3, chans, cols)
    tails = jnp.concatenate(
        [proj[..., (s + 1) * width - (KS - 1) : (s + 1) * width] for s in range(seqs)], axis=-1
    ).reshape(3 * dim, seqs * (KS - 1)).T + prm[..., 0].reshape(1, 3 * dim)
    halo = lax.ppermute(tails, "chan", [(i, i + 1) for i in range(devices - 1)])
    halo = halo.T.reshape(devices, 3, chans, seqs * (KS - 1))
    short, mixed = short_forward(proj, halo, prm, seqs)

    mixed_chan = exchange(mixed)
    conv_chan, mixed_spec = conv_forward(mixed_chan, filt_spec, bias_col, seqs)
    conv = rows_of(exchange(conv_chan)).astype(f32)

    gate_out = short[:, 0].reshape(dim, cols)
    gated = (conv * gate_out).astype(bf16)
    residual = x + mm16(out_all, gated, TN) + out_b
    xhat2, rstd2 = norm_forward(residual)
    xn2 = (xhat2 * gain2 + shift2).astype(bf16)
    hidden = mm16(up_all, xn2, NN) + up_bias_all
    act, gelu_pull = jax.vjp(lambda v: jax.nn.gelu(v, approximate=True), hidden)
    act = act.astype(bf16)
    positions = place * width + lax.iota(jnp.int32, width)
    live = (positions[None, :] < seq_lengths[:, None]).astype(f32).reshape(1, cols)
    result = live * (residual + mm16(down_all, act, TN) + down_b)
    out_blocks = exchange(blocks_of(result.astype(bf16)))
    d_final = live * rows_of(cot_blocks).astype(f32)
    d_mlp = d_final.astype(bf16)
    d_hidden = gelu_pull(mm16(down_all, d_mlp, NN))[0]
    d_hidden_low = d_hidden.astype(bf16)
    g_up_bias = jnp.sum(d_hidden, axis=1)
    g_down = mm16(act, d_mlp, NT)
    g_up = mm16(d_hidden_low, xn2, NT)
    d_xn2 = mm16(up_all, d_hidden_low, TN)
    d_residual = d_final + norm_backward(d_xn2 * gain2, xhat2, rstd2)
    d_branch = d_residual.astype(bf16)
    g_out = mm16(gated, d_branch, NT)
    d_gated = mm16(out_all, d_branch, NN)
    d_conv = exchange(blocks_of((d_gated * gate_out).astype(bf16)))

    def scatter(table):
        rows = table.shape[0] // devices
        table = table.astype(bf16).reshape(devices, rows, groups, dim // groups).transpose(2, 0, 1, 3)
        return lax.psum_scatter(
            table.reshape(groups * devices, rows, dim // groups),
            ("batch", "chan"),
            scatter_dimension=0,
            tiled=True,
        )[0].astype(f32)

    early = scatter(
        jnp.concatenate(
            [
                g_up.reshape(devices, hid, dim),
                g_down.reshape(devices, hid, dim),
                g_out.reshape(devices, chans, dim),
            ],
            axis=1,
        ).reshape(devices * (2 * hid + chans), dim)
    )
    up_grad, down_grad, out_grad = early[:hid], early[hid : 2 * hid], early[2 * hid :]

    d_mixed_chan, d_filter, g_conv_bias = conv_backward(
        d_conv, mixed_chan, mixed_spec, filt_spec, bias_col, seqs
    )
    d_mixed = rows_of(exchange(d_mixed_chan)).astype(f32)

    q = d_filter * env
    g_filt_out = mm(h2, q, NT)
    g_decay = -jnp.sum(d_filter * raw * falling * ramp, axis=1)
    u2 = mm(filt_out, q, NN) * jnp.cos(rate * pre2)
    fu2 = rate * u2
    u1 = mm(filt_mid, fu2, NN) * jnp.cos(rate * pre1)
    fu1 = rate * u1
    filt_grads = jnp.concatenate(
        [
            mm(feat, fu1, NT).reshape(-1),
            jnp.sum(fu1, axis=1),
            mm(h1, fu2, NT).reshape(-1),
            jnp.sum(fu2, axis=1),
            jnp.sum(u2 * pre2 + u1 * pre1, axis=1),
        ]
    )

    def split(values):
        return values.reshape(devices, chans, cols)

    starts = [slice(s * width, s * width + KS - 1) for s in range(seqs)]
    pick = lambda v: jnp.concatenate([v[..., at] for at in starts], axis=-1)
    hd = pick(split(d_mixed))
    hs = pick(short)
    heads = jnp.stack([pick(split(d_gated)) * pick(split(conv)), hd * hs[:, 2], hd * hs[:, 1]], axis=1)
    heads = heads.reshape(3 * dim, seqs * (KS - 1)).T
    head = lax.ppermute(heads, "chan", [(i + 1, i) for i in range(devices - 1)])
    head = head.T.reshape(devices, 3, chans, seqs * (KS - 1))
    d_proj, sums = short_backward(
        split(d_gated), split(conv), split(d_mixed), proj, halo, short, head, prm, seqs
    )
    d_proj_low = d_proj.reshape(3 * dim, cols).astype(bf16)
    d_xn1 = mm16(in_all, d_proj_low, TN)
    in_grad = scatter(mm16(d_proj_low, xn1, NT))
    grad_in = d_residual + norm_backward(d_xn1 * gain1, xhat1, rstd1)
    grad_blocks = exchange(blocks_of(grad_in.astype(bf16)))

    tokens = jnp.concatenate(
        [
            sums[..., : 2 + KS].transpose(0, 3, 1, 2).reshape(devices, 3 * (2 + KS) * chans),
            jnp.sum(d_xn1 * xhat1, axis=1).reshape(devices, chans),
            jnp.sum(d_xn1, axis=1).reshape(devices, chans),
            jnp.sum(d_residual, axis=1).reshape(devices, chans),
            jnp.sum(d_xn2 * xhat2, axis=1).reshape(devices, chans),
            jnp.sum(d_xn2, axis=1).reshape(devices, chans),
            jnp.sum(d_final, axis=1).reshape(devices, chans),
            g_up_bias.reshape(devices, hid),
            jnp.broadcast_to(filt_grads[None], (devices, filt_grads.shape[0])),
        ],
        axis=1,
    )
    count = tokens.shape[1]
    tokens = jnp.pad(tokens, ((0, 0), (0, -count % 1024))).reshape(devices, -1, LANE)
    totals = jnp.sum(exchange(tokens), axis=0).reshape(-1)[:count]
    own = jnp.concatenate([totals, g_conv_bias[:, 0], g_decay, g_filt_out.reshape(-1)])
    own = lax.psum(own, "batch")
    cut = [0]

    def take(*shape):
        n = math.prod(shape)
        part = own[cut[0] : cut[0] + n].reshape(shape)
        cut[0] += n
        return part

    g_in_bias = take(3, chans)
    g_short_bias = take(3, chans)
    g_short_weight = take(KS, 3, chans)
    g_gain1, g_shift1, g_out_b, g_gain2, g_shift2, g_down_b = (take(chans) for _ in range(6))
    g_up_b = take(hid)
    ford = filt_mid.shape[0]
    g_filt_in, g_filt_in_bias = take(EMB, ford), take(ford)
    g_filt_mid, g_filt_mid_bias, g_sine = take(ford, ford), take(ford), take(ford)
    g_conv_b, g_decay_rate, g_filt_last = take(chans), take(chans), take(ford, chans)

    return (
        from_blocks(out_blocks),
        from_blocks(grad_blocks).astype(f32),
        g_gain1,
        g_shift1,
        in_grad.reshape(3, chans, dim // groups).transpose(2, 0, 1),
        g_in_bias,
        g_short_weight,
        g_short_bias,
        g_filt_in,
        g_filt_in_bias,
        g_filt_mid,
        g_filt_mid_bias,
        g_sine,
        g_filt_last,
        g_decay_rate,
        g_conv_b,
        out_grad,
        g_out_b,
        g_gain2,
        g_shift2,
        up_grad,
        g_up_b,
        down_grad,
        g_down_b,
    )


def solution(mesh):
    token = P("batch", "chan", None)
    chan = P("chan")
    rows = P("chan", None)
    two = P(None, "chan")
    three = P(None, None, "chan")
    in_specs = (
        token, P("batch"), chan, chan, three, two, three, two, P(), P(), P(), P(), P(), two, chan, chan,
        rows, chan, chan, chan, rows, chan, rows, chan, token,
    )
    table = P("chan", "batch")
    out_specs = (
        token, token, chan, chan, P("batch", None, "chan"), two, three, two, P(), P(), P(), P(), P(), two,
        chan, chan, table, chan, chan, chan, table, chan, table, chan,
    )
    return jax.shard_map(
        on_device, mesh=mesh, in_specs=in_specs, out_specs=out_specs, check_vma=False
    )
```

```python
import math

import jax
import jax.numpy as jnp
import numpy as np
from jax import lax
from jax.experimental import pallas as pl
from jax.experimental.pallas import tpu as pltpu
from jax.sharding import PartitionSpec as P

EMB = 33
KS = 3
LMAX = 4096
LANE = 128
COARSE = LMAX // LANE
REPS = tuple(ka + 8 * kb for ka, count in ((0, 5), (1, 8), (2, 8), (3, 8), (4, 4)) for kb in range(count))
PLACE = {k1: i for i, k1 in enumerate(REPS)}
epsilon = 1e-05
decay_floor = 0.05
highest = lax.Precision.HIGHEST
f32 = jnp.float32
bf16 = jnp.bfloat16
vmem_limit = 56 * 1024 * 1024
HEAD_ROWS = 16
SUM_ROWS = 16
BATCH = 3
PRM = 32


def unit(turns):
    angle = 2.0 * math.pi * turns
    return math.cos(angle), math.sin(angle)


def scaled(z, c, s):
    re, im = z
    if im is None:
        return re * c, re * s
    return re * c - im * s, re * s + im * c


def plus(a, b):
    return a[0] + b[0], a[1] + b[1]


def minus(a, b):
    return a[0] - b[0], a[1] - b[1]


def dft4(z, sign):
    s0, d0 = plus(z[0], z[2]), minus(z[0], z[2])
    s1, d1 = plus(z[1], z[3]), minus(z[1], z[3])
    turned = (-d1[1], d1[0]) if sign > 0 else (d1[1], -d1[0])
    return [plus(s0, s1), plus(d0, turned), minus(s0, s1), minus(d0, turned)]


def dft8(z, sign):
    even, odd = dft4(z[0::2], sign), dft4(z[1::2], sign)
    c = math.sqrt(0.5)
    o1 = odd[1]
    o3 = odd[3]
    if sign > 0:
        odd1 = ((o1[0] - o1[1]) * c, (o1[0] + o1[1]) * c)
        odd2 = (-odd[2][1], odd[2][0])
        odd3 = ((-o3[0] - o3[1]) * c, (o3[0] - o3[1]) * c)
    else:
        odd1 = ((o1[0] + o1[1]) * c, (o1[1] - o1[0]) * c)
        odd2 = (odd[2][1], -odd[2][0])
        odd3 = ((o3[1] - o3[0]) * c, (-o3[0] - o3[1]) * c)
    turned = [odd[0], odd1, odd2, odd3]
    return [plus(even[i], turned[i]) for i in range(4)] + [minus(even[i], turned[i]) for i in range(4)]


def coarse_forward(xs, put):
    c = math.sqrt(0.5)
    cols = {ka: [None] * 8 for ka in range(5)}
    for b in range(8):
        x0, x1, x2, x3 = xs[b], xs[8 + b], xs[16 + b], xs[24 + b]
        s02, d02, s13, d13 = x0 + x2, x0 - x2, x1 + x3, x1 - x3
        d13c, s13c = d13 * c, s13 * c
        cols[0][b] = s02 + s13
        cols[4][b] = scaled((s02 - s13, None), *unit(-4 * b / 64))
        cols[2][b] = scaled((d02, -d13), *unit(-2 * b / 64))
        cols[1][b] = scaled((x0 + d13c, -s13c - x2), *unit(-b / 64))
        cols[3][b] = scaled((x0 - d13c, x2 - s13c), *unit(-3 * b / 64))
    for ka in (1, 2, 3):
        for kb, z in enumerate(dft8(cols[ka], -1)):
            put(ka + 8 * kb, z)
    for kb, z in enumerate(dft8(cols[4], -1)[:4]):
        put(4 + 8 * kb, z)
    r = cols[0]
    s04, d04, s26, d26 = r[0] + r[4], r[0] - r[4], r[2] + r[6], r[2] - r[6]
    s15, d15, s37, d37 = r[1] + r[5], r[1] - r[5], r[3] + r[7], r[3] - r[7]
    p, q = (d15 - d37) * c, (d15 + d37) * c
    even, odd = s04 + s26, s15 + s37
    put(0, (even + odd, None))
    put(32, (even - odd, None))
    put(16, (s04 - s26, s37 - s15))
    put(8, (d04 + p, -d26 - q))
    put(24, (d04 - p, d26 - q))


def coarse_inverse(get):
    c = math.sqrt(0.5)
    u = {}
    for ka in (1, 2, 3):
        back = dft8([get(ka + 8 * kb) for kb in range(8)], 1)
        u[ka] = [scaled(back[b], *unit(b * ka / 64)) for b in range(8)]
    v0, v32 = get(0)[0], get(32)[0]
    v8, v16, v24 = get(8), get(16), get(24)
    flat = []
    for b in range(8):
        total = v0 + v32 if b % 2 == 0 else v0 - v32
        for kb, v in ((1, v8), (2, v16), (3, v24)):
            co, si = unit(b * kb / 8)
            if abs(co) > 1e-9:
                total = total + v[0] * (2.0 * co)
            if abs(si) > 1e-9:
                total = total - v[1] * (2.0 * si)
        flat.append(total)
    odd = [get(4 + 8 * kb) for kb in range(4)]
    odd = odd + [(z[0], -z[1]) for z in odd[::-1]]
    half = dft8(odd, 1)
    quarter = []
    for b in range(8):
        co, si = unit(4 * b / 64)
        quarter.append(half[b][0] * co - half[b][1] * si)
    out = [None] * COARSE
    for b in range(8):
        u1, u2, u3 = u[1][b], u[2][b], u[3][b]
        s, d = flat[b] + quarter[b], flat[b] - quarter[b]
        dr, sr = (u1[0] - u3[0]) * c, u1[0] + u3[0]
        si_, di = (u1[1] + u3[1]) * c, u1[1] - u3[1]
        out[b] = s + 2.0 * (sr + u2[0])
        out[16 + b] = s - 2.0 * (di + u2[0])
        out[8 + b] = d + 2.0 * (dr - si_ - u2[1])
        out[24 + b] = d + 2.0 * (u2[1] - dr - si_)
    return out


def transform_tables():
    fine = np.arange(LANE)
    angle = 2.0 * math.pi * ((fine[:, None] * fine[None, :]) % LANE) / LANE
    co, si = np.cos(angle), np.sin(angle)
    ahead = np.block([[co, -si], [si, co]])
    back = ahead.T / (2.0 * LMAX)
    reps = np.array(REPS)
    turn = 2.0 * math.pi * ((reps[:, None] * fine[None, :]) % (2 * LMAX)) / (2 * LMAX)
    twist = np.concatenate([np.cos(turn), -np.sin(turn)], axis=1)[:, None, :]

    def pieces(table):
        table = table.astype(np.float32)
        upper = table.astype(jnp.bfloat16)
        lower = (table - upper.astype(np.float32)).astype(jnp.bfloat16)
        return np.stack([upper, lower])

    return pieces(ahead), pieces(back), twist.astype(np.float32)


AHEAD, BACK, TWIST = transform_tables()


def three_pass(values, table_ref):
    upper = values.astype(bf16)
    lower = (values - upper.astype(f32)).astype(bf16)
    t0, t1 = table_ref[0], table_ref[1]
    return (
        jnp.dot(upper, t0, preferred_element_type=f32)
        + jnp.dot(lower, t0, preferred_element_type=f32)
        + jnp.dot(upper, t1, preferred_element_type=f32)
    )


def rows_forward(xs_ref, spec_ref, rows):
    def step(g, carry):
        at = pl.ds(pl.multiple_of(g * 8, 8), 8)
        xs = [xs_ref[n, at, :] for n in range(COARSE)]

        def put(k1, z):
            i = PLACE[k1]
            spec_ref[i, at, 0:LANE] = z[0]
            spec_ref[i, at, LANE : 2 * LANE] = jnp.zeros_like(z[0]) if z[1] is None else z[1]

        coarse_forward(xs, put)
        return carry

    lax.fori_loop(0, rows // 8, step, 0)


def rows_inverse(spec_ref, ys_ref, rows):
    def step(g, carry):
        at = pl.ds(pl.multiple_of(g * 8, 8), 8)

        def get(k1):
            i = PLACE[k1]
            return spec_ref[i, at, 0:LANE], spec_ref[i, at, LANE : 2 * LANE]

        for n, y in enumerate(coarse_inverse(get)):
            ys_ref[n, at, :] = y
        return carry

    lax.fori_loop(0, rows // 8, step, 0)


def fine_forward(spec, twist, ahead_ref):
    re, im = spec[:, :LANE], spec[:, LANE:]
    tr, ti = twist[:, :LANE], twist[:, LANE:]
    return three_pass(jnp.concatenate([re * tr - im * ti, re * ti + im * tr], axis=1), ahead_ref)


def fine_inverse(spec, twist, back_ref):
    v = three_pass(spec, back_ref)
    re, im = v[:, :LANE], v[:, LANE:]
    tr, ti = twist[:, :LANE], twist[:, LANE:]
    return jnp.concatenate([re * tr + im * ti, im * tr - re * ti], axis=1)


def times(a, b):
    ar, ai, br, bi = a[:, :LANE], a[:, LANE:], b[:, :LANE], b[:, LANE:]
    return jnp.concatenate([ar * br - ai * bi, ar * bi + ai * br], axis=1)


def times_conj(a, b):
    ar, ai, br, bi = a[:, :LANE], a[:, LANE:], b[:, :LANE], b[:, LANE:]
    return jnp.concatenate([ar * br + ai * bi, ai * br - ar * bi], axis=1)


def together(values):
    return values.reshape(values.shape[0] * values.shape[1], values.shape[2])


def apart(values):
    return values.reshape(BATCH, values.shape[0] // BATCH, values.shape[1])


def twists(twist_ref, at, rows):
    return together(jnp.broadcast_to(twist_ref[at], (BATCH, rows, 2 * LANE)))


def spread(blocks_ref, xs_ref):
    per = blocks_ref.shape[2] // LANE
    for n in range(COARSE):
        r = n % per
        xs_ref[n] = blocks_ref[n // per, :, r * LANE : (r + 1) * LANE].astype(f32)


def filter_spectrum_body(filter_ref, twist_ref, ahead_ref, out_ref, xs_ref):
    rows = filter_ref.shape[0]
    for n in range(COARSE):
        xs_ref[n] = filter_ref[:, n * LANE : (n + 1) * LANE]
    rows_forward(xs_ref, out_ref, rows)

    def step(i, carry):
        at = pl.ds(i * BATCH, BATCH)
        out_ref[at] = apart(fine_forward(together(out_ref[at]), twists(twist_ref, at, rows), ahead_ref))
        return carry

    lax.fori_loop(0, len(REPS) // BATCH, step, 0)


def conv_forward_body(seqs, mixed_ref, filt_ref, bias_ref, twist_ref, ahead_ref, back_ref, out_ref, spec_ref, xs_ref, work_ref):
    rows = mixed_ref.shape[1]
    spread(mixed_ref, xs_ref)
    rows_forward(xs_ref, spec_ref, rows)

    def step(i, carry):
        at = pl.ds(i * BATCH, BATCH)
        twist = twists(twist_ref, at, rows)
        z = fine_forward(together(spec_ref[at]), twist, ahead_ref)
        spec_ref[at] = apart(z)
        k = together(jnp.concatenate([filt_ref[at]] * seqs, axis=1))
        work_ref[at] = apart(fine_inverse(times(z, k), twist, back_ref))
        return carry

    lax.fori_loop(0, len(REPS) // BATCH, step, 0)
    ys_ref = xs_ref
    rows_inverse(work_ref, ys_ref, rows)
    per = mixed_ref.shape[2] // LANE
    bias = jnp.concatenate([bias_ref[...]] * seqs, axis=0)
    for n in range(COARSE):
        at = (n // per, slice(None), slice((n % per) * LANE, (n % per + 1) * LANE))
        out_ref[at] = (ys_ref[n] + bias * mixed_ref[at].astype(f32)).astype(bf16)


def heads_out(out_ref, block, y):
    rows, width = y.shape[0], out_ref.shape[2]
    square = jnp.concatenate([y, jnp.zeros((LANE - rows, LANE), f32)], axis=0) if rows < LANE else y
    head = square.T[:HEAD_ROWS]
    if width > LANE:
        head = jnp.concatenate([head, jnp.zeros((HEAD_ROWS, width - LANE), f32)], axis=1)
    out_ref[block, rows:, :] = head.astype(bf16)


def conv_backward_body(
    seqs, d_ref, mixed_ref, mixed_spec_ref, filt_ref, bias_ref, twist_ref, ahead_ref, back_ref, out_ref, dfilt_ref, dbias_ref, xs_ref, spec_ref, work_ref, ys_ref
):
    rows = d_ref.shape[1]
    chans = rows // seqs
    spread(d_ref, xs_ref)
    rows_forward(xs_ref, spec_ref, rows)

    def step(i, carry):
        at = pl.ds(i * BATCH, BATCH)
        z = fine_forward(together(spec_ref[at]), twists(twist_ref, at, rows), ahead_ref)
        k = together(jnp.concatenate([filt_ref[at]] * seqs, axis=1))
        cross = apart(times_conj(z, together(mixed_spec_ref[at])))
        cross = sum(cross[:, s * chans : (s + 1) * chans] for s in range(seqs))
        both = together(jnp.concatenate([apart(times_conj(z, k)), cross], axis=1))
        work_ref[at] = apart(fine_inverse(both, twists(twist_ref, at, rows + chans), back_ref))
        return carry

    lax.fori_loop(0, len(REPS) // BATCH, step, 0)
    rows_inverse(work_ref, ys_ref, rows + chans)
    per = d_ref.shape[2] // LANE
    bias = jnp.concatenate([bias_ref[...]] * seqs, axis=0)
    total = jnp.zeros((rows, LANE), f32)
    out_ref[out_ref.shape[0] - 1, rows:, :] = jnp.zeros((HEAD_ROWS, d_ref.shape[2]), bf16)
    for n in range(COARSE):
        at = (n // per, slice(0, rows), slice((n % per) * LANE, (n % per + 1) * LANE))
        d = xs_ref[n]
        y = ys_ref[n, :rows, :] + bias * d
        out_ref[at] = y.astype(bf16)
        if n % per == 0 and n > 0:
            heads_out(out_ref, n // per - 1, y)
        total = total + d * mixed_ref[at].astype(f32)
        dfilt_ref[:, n * LANE : (n + 1) * LANE] = ys_ref[n, rows:, :]
    total = sum(total[s * chans : (s + 1) * chans] for s in range(seqs))
    dbias_ref[...] = jnp.sum(total, axis=1, keepdims=True)


def takes(us):
    return pl.CostEstimate(flops=int(us * 1e9), bytes_accessed=int(us * 3e6), transcendentals=0)


def whole_call(us, body, out_shape, scratch, *args):
    return pl.pallas_call(
        body,
        cost_estimate=takes(us),
        out_shape=out_shape,
        in_specs=[pl.BlockSpec(memory_space=pltpu.VMEM)] * len(args),
        out_specs=jax.tree.map(lambda _: pl.BlockSpec(memory_space=pltpu.VMEM), out_shape),
        scratch_shapes=scratch,
        compiler_params=pltpu.CompilerParams(vmem_limit_bytes=vmem_limit),
    )(*args)


def filter_spectrum(filt):
    rows = filt.shape[0]
    return whole_call(
        8,
        filter_spectrum_body,
        jax.ShapeDtypeStruct((len(REPS), rows, 2 * LANE), f32),
        [pltpu.VMEM((COARSE, rows, LANE), f32)],
        filt,
        jnp.asarray(TWIST),
        jnp.asarray(AHEAD),
    )


def conv_forward(mixed, filt_spec, bias, seqs):
    blocks, rows, width = mixed.shape
    n = len(REPS)
    return whole_call(
        14,
        lambda *refs: conv_forward_body(seqs, *refs),
        (jax.ShapeDtypeStruct(mixed.shape, bf16), jax.ShapeDtypeStruct((n, rows, 2 * LANE), f32)),
        [pltpu.VMEM((COARSE, rows, LANE), f32), pltpu.VMEM((n, rows, 2 * LANE), f32)],
        mixed,
        filt_spec,
        bias,
        jnp.asarray(TWIST),
        jnp.asarray(AHEAD),
        jnp.asarray(BACK),
    )


def conv_backward(d_conv, mixed, mixed_spec, filt_spec, bias, seqs):
    blocks, rows, width = mixed.shape
    chans = rows // seqs
    n = len(REPS)
    return whole_call(
        16,
        lambda *refs: conv_backward_body(seqs, *refs),
        (
            jax.ShapeDtypeStruct((blocks, rows + HEAD_ROWS, width), bf16),
            jax.ShapeDtypeStruct((chans, LMAX), f32),
            jax.ShapeDtypeStruct((chans, 1), f32),
        ),
        [
            pltpu.VMEM((COARSE, rows, LANE), f32),
            pltpu.VMEM((n, rows, 2 * LANE), f32),
            pltpu.VMEM((n, rows + chans, 2 * LANE), f32),
            pltpu.VMEM((COARSE, rows + chans, LANE), f32),
        ],
        d_conv,
        mixed,
        mixed_spec,
        filt_spec,
        bias,
        jnp.asarray(TWIST),
        jnp.asarray(AHEAD),
        jnp.asarray(BACK),
    )


CHUNK = 48


def lanes_of(shape):
    return lax.broadcasted_iota(jnp.int32, shape, 1)


def side_by_side(block, seqs):
    chans = block.shape[0] // seqs
    return jnp.concatenate([block[s * chans : (s + 1) * chans] for s in range(seqs)], axis=1)


def stacked(values, seqs):
    width = values.shape[1] // seqs
    return jnp.concatenate([values[:, s * width : (s + 1) * width] for s in range(seqs)], axis=0)


def eights(values):
    return jnp.sum(values.reshape(values.shape[0] // 8, 8, values.shape[1]), axis=0)


def folded(values):
    return sum(values[:, i * LANE : (i + 1) * LANE] for i in range(values.shape[1] // LANE))


def row_totals(values):
    ones = jnp.ones((8, LANE), bf16)
    upper = values.astype(bf16)
    lower = (values - upper.astype(f32)).astype(bf16)
    return mm16(ones, upper, NT) + mm16(ones, lower, NT)


def padded_totals(values, width):
    extra = -values.shape[0] % width
    if extra:
        values = jnp.concatenate([values, jnp.zeros((extra, LANE), f32)], axis=0)
    totals = row_totals(values)
    return [totals[:, i * width : (i + 1) * width] for i in range(totals.shape[1] // width)]


def as_rows(totals, rows):
    halves = []
    for t in totals:
        upper = t.astype(bf16).astype(f32)
        halves += [upper, t - upper]
    place = lax.broadcasted_iota(jnp.int32, halves[0].shape, 0)
    tiles = []
    for first in range(0, rows, 8):
        tile = jnp.zeros_like(halves[0])
        for i, h in enumerate(halves[first : first + 8]):
            tile = jnp.where(place == i, h, tile)
        tiles.append(tile)
    return jnp.concatenate(tiles, axis=0).astype(bf16)


def chunk_rows(i):
    return pl.ds(pl.multiple_of(i * CHUNK, CHUNK), CHUNK)


def norm_stats(ref, dim):
    cols = ref.shape[1]
    zero = jnp.zeros((8, cols), f32)
    total = lax.fori_loop(0, dim // CHUNK, lambda i, t: t + eights(ref[chunk_rows(i), :]), zero)
    mean = jnp.sum(total, axis=0, keepdims=True) / dim

    def spread_sq(i, t):
        v = ref[chunk_rows(i), :] - mean
        return t + eights(v * v)

    var = jnp.sum(lax.fori_loop(0, dim // CHUNK, spread_sq, zero), axis=0, keepdims=True) / dim
    return mean, lax.rsqrt(var + epsilon)


def front_body(seqs, group, flag_ref, x_ref, xh_ref, w_ref, prm_ref, after_ref, xn_ref, stat_ref, gate_ref, pair_ref, projx0_ref, projx_ref, mixed_ref, heads_ref, xs, xb):
    devices, _, width = x_ref.shape
    dim, cols = xn_ref.shape
    chans = dim // devices
    step = pl.program_id(0)

    @pl.when(step == 0)
    def _():
        def gather(d, carry):
            at = pl.ds(pl.multiple_of(d * chans, 8), chans)
            row = side_by_side(x_ref[d].astype(f32), seqs)
            tail = xh_ref[d].astype(f32)
            tail = jnp.where(
                lanes_of((chans, LANE)) < LANE // 2, pltpu.roll(tail[chans : 2 * chans], LANE // 2, 1), tail[:chans]
            )
            xs[at, :] = jnp.concatenate([row, tail], axis=1)
            return carry

        lax.fori_loop(0, devices, gather, 0)
        mean, inverse = norm_stats(xs, dim)

        def scale(i, carry):
            at = chunk_rows(i)
            prm = prm_ref[at, :]
            v = (xs[at, :] - mean) * inverse * prm[:, 15:16] + prm[:, 16:17]
            xb[at, :] = v.astype(bf16)
            xn_ref[at, :] = v[:, :cols].astype(bf16)
            return carry

        lax.fori_loop(0, dim // CHUNK, scale, 0)
        stat_ref[0:8, :] = jnp.broadcast_to(mean[:, :cols], (8, cols))
        stat_ref[8:16, :] = jnp.broadcast_to(inverse[:, :cols], (8, cols))

    keep = (flag_ref[0] > 0).astype(f32)
    for g in range(group):
        prm = prm_ref[pl.ds(pl.multiple_of((step * group + g) * chans, 8), chans), :]
        proj = mm16(w_ref[g, PRM:, :], xb[...], NN)
        ys = []
        px = []
        for i in range(3):
            x = proj[i * chans : (i + 1) * chans] + prm[:, i : i + 1]
            tail = x[:, cols:] * keep
            px += [jnp.concatenate([x[:, :cols], tail], axis=1)]
            weights = [jnp.broadcast_to(prm[:, 6 + 3 * j + i : 7 + 3 * j + i], (chans, width)) for j in range(KS)]
            bias = jnp.broadcast_to(prm[:, 3 + i : 4 + i], (chans, width))
            parts = []
            for s in range(seqs):
                v = x[:, s * width : (s + 1) * width]
                wide = jnp.concatenate([tail if s == 0 else pltpu.roll(tail, LANE // 2, 1), v], axis=1)
                y = bias + weights[0] * v
                for j in range(1, KS):
                    y = y + weights[j] * pltpu.roll(wide, j, 1)[:, LANE:]
                parts.append(y)
            ys.append(jnp.concatenate(parts, axis=1))
        projx0_ref[g] = px[0].astype(bf16)
        projx_ref[g] = jnp.concatenate(px[1:], axis=0).astype(bf16)
        gate_ref[g] = ys[0]
        pair = jnp.concatenate(ys[1:], axis=0)
        pair_ref[g] = pair
        mixed_ref[g] = stacked(ys[1] * ys[2], seqs).astype(bf16)
        heads_ref[g] = first_tokens(pair, seqs).astype(bf16)


def first_tokens(values, seqs):
    width = values.shape[1] // seqs
    second = pltpu.roll(values[:, width : width + LANE], LANE // 2, 1)
    return jnp.where(lanes_of((values.shape[0], LANE)) < LANE // 2, values[:, :LANE], second)


def params(kind):
    return pltpu.CompilerParams(vmem_limit_bytes=vmem_limit, dimension_semantics=("arbitrary",))


def whole(a):
    return pl.BlockSpec(a.shape, lambda i: (0,) * len(a.shape), pipeline_mode=pl.Buffered(1))


def half(a, which):
    return pl.BlockSpec(
        (a.shape[0], a.shape[1] // 2, a.shape[2]), lambda i: (0, which, 0), pipeline_mode=pl.Buffered(1)
    )


def untouched():
    return pl.BlockSpec(memory_space=pl.ANY)


def by_group(a, group):
    return pl.BlockSpec((group,) + a.shape[1:], lambda i: (i,) + (0,) * (len(a.shape) - 1))


def smem():
    return pl.BlockSpec(memory_space=pltpu.SMEM)


def front(flag, x_cot, xh, weights, prm, after, seqs):
    devices, rows, width = x_cot.shape
    rows = rows // 2
    chans = rows // seqs
    dim = devices * chans
    cols = seqs * width
    group = 2
    sd = jax.ShapeDtypeStruct
    out = (
        sd((dim, cols), bf16),
        sd((16, cols), f32),
        sd((devices, chans, cols), f32),
        sd((devices, 2 * chans, cols), f32),
        sd((devices, chans, cols + LANE), bf16),
        sd((devices, 2 * chans, cols + LANE), bf16),
        sd((devices, rows, width), bf16),
        sd((devices, 2 * chans, LANE), bf16),
    )
    return pl.pallas_call(
        lambda *refs: front_body(seqs, group, *refs),
        cost_estimate=takes(16),
        grid=(devices // group,),
        out_shape=out,
        in_specs=[smem(), half(x_cot, 0), whole(xh), by_group(weights, group), whole(prm), untouched()],
        out_specs=(whole(out[0]), whole(out[1])) + tuple(by_group(o, group) for o in out[2:]),
        scratch_shapes=[pltpu.VMEM((dim, cols + LANE), f32), pltpu.VMEM((dim, cols + LANE), bf16)],
        compiler_params=params(0),
    )(flag, x_cot, xh, weights, prm, after)


def middle_body(
    seqs, group, lens_ref, conv_ref, x_ref, cot_ref, gate_ref, w_ref, out_w_ref, prm_ref,
    layer_ref, d_conv_ref, d_res_ref, p0_ref, p0h_ref, g_ref,
    cs, res, ds, xb, db, gb, acc_out, acc_in, folds, up_folds, stats,
):
    devices, _, width = x_ref.shape
    dim, cols = d_res_ref.shape
    chans = dim // devices
    hid = w_ref.shape[1] // 2
    step = pl.program_id(0)
    last = pl.num_programs(0) - 1
    lane = lanes_of((1, cols))
    live = jnp.zeros((1, cols), f32)
    for s in range(seqs):
        inside = (lane >= s * width) & (lane < (s + 1) * width) & (lens_ref[seqs] * width + lane - s * width < lens_ref[s])
        live = jnp.where(inside, 1.0, live)

    def device_rows(d):
        return pl.ds(pl.multiple_of(d * chans, 8), chans)

    @pl.when(step == 0)
    def _():
        def gather(d, carry):
            at = device_rows(d)
            cs[at, :] = side_by_side(conv_ref[d].astype(f32), seqs)
            res[at, :] = side_by_side(x_ref[d].astype(f32), seqs)
            ds[at, :] = live * side_by_side(cot_ref[d].astype(f32), seqs)
            return carry

        lax.fori_loop(0, devices, gather, 0)

        def gated(i, carry):
            at = chunk_rows(i)
            gb[at, :] = (cs[at, :] * gate_ref[at, :]).astype(bf16)
            d = ds[at, :]
            db[at, :] = d.astype(bf16)
            folds[3, at, :] = folded(d)
            acc_in[at, :] = jnp.zeros((CHUNK, cols), f32)
            return carry

        lax.fori_loop(0, dim // CHUNK, gated, 0)
        for n in range(dim // 256):
            at = slice(n * 256, (n + 1) * 256)
            acc_out[at, :] = mm16(out_w_ref[:, at], gb[...], TN)

        def add(i, carry):
            at = chunk_rows(i)
            res[at, :] = res[at, :] + acc_out[at, :] + prm_ref[at, 19:20]
            acc_out[at, :] = jnp.zeros((CHUNK, cols), f32)
            return carry

        lax.fori_loop(0, dim // CHUNK, add, 0)
        mean, inverse = norm_stats(res, dim)

        def scale(i, carry):
            at = chunk_rows(i)
            normed = (res[at, :] - mean) * inverse
            cs_norm = normed * prm_ref[at, 17:18] + prm_ref[at, 18:19]
            xb[at, :] = cs_norm.astype(bf16)
            return carry

        lax.fori_loop(0, dim // CHUNK, scale, 0)
        stats[0:8, :] = jnp.broadcast_to(mean, (8, cols))
        stats[8:16, :] = jnp.broadcast_to(inverse, (8, cols))

    up_b = []
    for g in range(group):
        prm = prm_ref[device_rows(step * group + g), :]
        up_b += [prm[:, 21 + m : 22 + m] for m in range(hid // chans)]
    up_b = jnp.concatenate(up_b, axis=0)
    up = w_ref[:, :hid, :].reshape(group * hid, dim)
    down = w_ref[:, hid:, :].reshape(group * hid, dim)
    u = mm16(up, xb[...], NN) + up_b
    d_act = mm16(down, db[...], NN)
    a, k = 0.044715, math.sqrt(2.0 / math.pi)
    sq = u * u
    t = jnp.tanh(u * (k + (k * a) * sq))
    half = 0.5 * (1.0 + t)
    act = (u * half).astype(bf16)
    d_u = d_act * (half + 0.5 * u * (1.0 - t * t) * (k + (3.0 * k * a) * sq))
    d_low = d_u.astype(bf16)
    up_folds[pl.ds(pl.multiple_of(step * group * hid, 8), group * hid), :] = folded(d_u)
    acc_out[...] += mm16(down, act, TN)
    acc_in[...] += mm16(up, d_low, TN)
    mine = pl.ds(step * group, group)
    g_ref[mine, :hid, :] = mm16(d_low, xb[...], NT).astype(bf16).reshape(group, hid, dim)
    g_ref[mine, hid : 2 * hid, :] = mm16(act, db[...], NT).astype(bf16).reshape(group, hid, dim)

    @pl.when(step == last)
    def _():
        mean, inverse = stats[0:1, :], stats[8:9, :]

        def result(i, t):
            at = chunk_rows(i)
            r = res[at, :]
            acc_out[at, :] = live * (r + acc_out[at, :] + prm_ref[at, 20:21])
            normed = (r - mean) * inverse
            d = acc_in[at, :]
            both = d * normed
            folds[0, at, :] = folded(both)
            folds[1, at, :] = folded(d)
            gain = prm_ref[at, 17:18]
            return t[0] + eights(d * gain), t[1] + eights(both * gain)

        zero = jnp.zeros((8, cols), f32)
        m1, m2 = lax.fori_loop(0, dim // CHUNK, result, (zero, zero))
        m1 = jnp.sum(m1, axis=0, keepdims=True) / dim
        m2 = jnp.sum(m2, axis=0, keepdims=True) / dim

        def residual(i, carry):
            at = chunk_rows(i)
            normed = (res[at, :] - mean) * inverse
            d = ds[at, :] + inverse * (acc_in[at, :] * prm_ref[at, 17:18] - m1 - normed * m2)
            d_res_ref[at, :] = d
            folds[2, at, :] = folded(d)
            db[at, :] = d.astype(bf16)
            return carry

        lax.fori_loop(0, dim // CHUNK, residual, 0)
        for n in range(dim // 256):
            at = slice(n * 256, (n + 1) * 256)
            acc_in[at, :] = mm16(out_w_ref[at, :], db[...], NN)
        some = 192 // chans
        for n in range(devices // some):
            g_out = mm16(gb[n * 192 : (n + 1) * 192, :], db[...], NT).reshape(some, chans, dim)
            g_ref[n * some : (n + 1) * some, 2 * hid :, :] = g_out.astype(bf16)

        def products(i, carry):
            at = chunk_rows(i)
            d = acc_in[at, :]
            p0 = d * cs[at, :]
            p0_ref[at, :] = p0
            p0h_ref[at, :] = first_tokens(p0, seqs)
            acc_in[at, :] = d * gate_ref[at, :]
            return carry

        lax.fori_loop(0, dim // CHUNK, products, 0)

        def scatter(d, carry):
            at = device_rows(d)
            layer_ref[d, : seqs * chans, :] = stacked(acc_out[at, :], seqs).astype(bf16)
            d_conv_ref[d] = stacked(acc_in[at, :], seqs).astype(bf16)
            totals = [padded_totals(folds[q, at, :], width)[0] for q in range(4)]
            totals += padded_totals(up_folds[pl.ds(pl.multiple_of(d * hid, 8), hid), :], width)
            layer_ref[d, seqs * chans :, :] = as_rows(totals, SUM_ROWS)
            return carry

        lax.fori_loop(0, devices, scatter, 0)


def middle(lens, conv, x_cot, gate, weights, out_w, prm, hid, seqs):
    devices, rows, width = conv.shape
    dim, cols = gate.shape
    chans = dim // devices
    group = 2
    sd = jax.ShapeDtypeStruct
    out = (
        sd((devices, rows + SUM_ROWS, width), bf16),
        sd((devices, rows, width), bf16),
        sd((dim, cols), f32),
        sd((dim, cols), f32),
        sd((dim, LANE), f32),
        sd((devices, 2 * hid + chans, dim), bf16),
    )
    big = pltpu.VMEM((dim, cols), f32)
    low = pltpu.VMEM((dim, cols), bf16)
    return pl.pallas_call(
        lambda *refs: middle_body(seqs, group, *refs),
        cost_estimate=takes(40),
        grid=(devices // group,),
        out_shape=out,
        in_specs=[
            smem(), whole(conv), half(x_cot, 0), half(x_cot, 1), whole(gate),
            pl.BlockSpec((group, 2 * hid, dim), lambda i: (i, 0, 0)), whole(out_w), whole(prm),
        ],
        out_specs=tuple(whole(o) for o in out),
        scratch_shapes=[
            big, big, big, low, low, low, big, big, pltpu.VMEM((4, dim, LANE), f32),
            pltpu.VMEM((devices * hid, LANE), f32), pltpu.VMEM((16, cols), f32),
        ],
        compiler_params=params(0),
    )(lens, conv, x_cot, x_cot, gate, weights, out_w, prm)


def short_back(seqs, prm, kinds, d_short, head, projx, width, cols):
    chans = prm.shape[0]
    d_proj = []
    totals = [[] for _ in range(2 + KS)]
    for n, i in enumerate(kinds):
        px = projx[n * chans : (n + 1) * chans]
        weights = [jnp.broadcast_to(prm[:, 6 + 3 * j + i : 7 + 3 * j + i], (chans, width)) for j in range(KS)]
        parts = []
        sums = [0.0] * (2 + KS)
        for s in range(seqs):
            at = slice(s * width, (s + 1) * width)
            d = d_short[n][:, at]
            x = px[:, at]
            tail = px[:, cols:]
            wide = jnp.concatenate([tail if s == 0 else pltpu.roll(tail, LANE // 2, 1), x], axis=1)
            after = jnp.concatenate([d, head[n] if s == 0 else pltpu.roll(head[n], LANE // 2, 1)], axis=1)
            y = weights[0] * d
            sums[1] = sums[1] + folded(d)
            sums[2] = sums[2] + folded(d * x)
            for j in range(1, KS):
                y = y + weights[j] * pltpu.roll(after, width + LANE - j, 1)[:, :width]
                sums[2 + j] = sums[2 + j] + folded(d * pltpu.roll(wide, j, 1)[:, LANE:])
            sums[0] = sums[0] + folded(y)
            parts.append(y)
        d_proj.append(jnp.concatenate(parts, axis=1))
        for k in range(2 + KS):
            totals[k].append(sums[k])
    d_low = jnp.concatenate(d_proj, axis=0).astype(bf16)
    return d_low, padded_totals(jnp.concatenate(sum(totals, []), axis=0), width)


def back_gate_body(seqs, group, p0_ref, p0h_ref, projx_ref, w_ref, prm_ref, xn_ref, g_ref, sums_ref, acc):
    dim, cols = xn_ref.shape
    chans = p0_ref.shape[1]
    step = pl.program_id(0)

    @pl.when(step == 0)
    def _():
        acc[...] = jnp.zeros_like(acc)

    for g in range(group):
        prm = prm_ref[pl.ds(pl.multiple_of((step * group + g) * chans, 8), chans), :]
        d_low, totals = short_back(
            seqs, prm, (0,), (p0_ref[g],), (p0h_ref[g],), projx_ref[g].astype(f32), cols // seqs, cols
        )
        sums_ref[g] = totals[0]
        acc[...] += mm16(w_ref[g, PRM : PRM + chans, :], d_low, TN)
        g_ref[g] = mm16(d_low, xn_ref[...], NT).astype(bf16)


def back_gate(p0, p0h, projx, weights, prm, xn, seqs):
    devices, chans, cols = p0.shape
    dim = xn.shape[0]
    group = 4
    sd = jax.ShapeDtypeStruct
    out = (
        sd((devices, chans, dim), bf16),
        sd((devices, 8, cols // seqs), f32),
        sd((dim, cols), f32),
    )
    return pl.pallas_call(
        lambda *refs: back_gate_body(seqs, group, *refs),
        cost_estimate=takes(12),
        grid=(devices // group,),
        out_shape=out,
        in_specs=[by_group(a, group) for a in (p0, p0h, projx, weights)] + [whole(prm), whole(xn)],
        out_specs=(by_group(out[0], group), by_group(out[1], group), whole(out[2])),
        compiler_params=params(0),
    )(p0, p0h, projx, weights, prm, xn)


def back_body(
    seqs, group, d_mixed_ref, pair_ref, heads_ref, projx_ref, w_ref, prm_ref, xn_ref, x_ref, stat_ref, d_res_ref, acc0_ref,
    sums0_ref, layer_ref, shared_ref, tail_ref, g_ref, acc, xs, folds, sums,
):
    devices, _, width = x_ref.shape
    dim, cols = xn_ref.shape
    chans = dim // devices
    step = pl.program_id(0)
    last = pl.num_programs(0) - 1

    @pl.when(step == 0)
    def _():
        acc[...] = acc0_ref[...]

    for g in range(group):
        prm = prm_ref[pl.ds(pl.multiple_of((step * group + g) * chans, 8), chans), :]
        block = d_mixed_ref[g].astype(f32)
        d_mixed = side_by_side(block[: seqs * chans], seqs)
        square = jnp.concatenate([block[seqs * chans :, :LANE], jnp.zeros((LANE - HEAD_ROWS, LANE), f32)], axis=0).T
        second = pltpu.roll(square[chans : 2 * chans], LANE // 2, 1)
        d_head = jnp.where(lanes_of((chans, LANE)) < LANE // 2, square[:chans], second)
        pair = pair_ref[g]
        pair_head = heads_ref[g].astype(f32)
        d_short = (d_mixed * pair[chans:], d_mixed * pair[:chans])
        head = (d_head * pair_head[chans:], d_head * pair_head[:chans])
        d_low, totals = short_back(seqs, prm, (1, 2), d_short, head, projx_ref[g].astype(f32), width, cols)
        for n, t in enumerate(totals):
            sums[n, step * group + g] = t
        acc[...] += mm16(w_ref[g, PRM + chans :, :], d_low, TN)
        g_ref[g] = mm16(d_low, xn_ref[...], NT).astype(bf16)

    @pl.when(step == last)
    def _():
        def gather(d, carry):
            xs[pl.ds(pl.multiple_of(d * chans, 8), chans), :] = side_by_side(x_ref[d].astype(f32), seqs)
            return carry

        lax.fori_loop(0, devices, gather, 0)
        mean, inverse = stat_ref[0:1, :], stat_ref[8:9, :]

        def first(i, t):
            at = chunk_rows(i)
            normed = (xs[at, :] - mean) * inverse
            d = acc[at, :]
            both = d * normed
            folds[0, at, :] = folded(both)
            folds[1, at, :] = folded(d)
            gain = prm_ref[at, 15:16]
            return t[0] + eights(d * gain), t[1] + eights(both * gain)

        zero = jnp.zeros((8, cols), f32)
        m1, m2 = lax.fori_loop(0, dim // CHUNK, first, (zero, zero))
        m1 = jnp.sum(m1, axis=0, keepdims=True) / dim
        m2 = jnp.sum(m2, axis=0, keepdims=True) / dim

        def second(i, carry):
            at = chunk_rows(i)
            normed = (xs[at, :] - mean) * inverse
            acc[at, :] = d_res_ref[at, :] + inverse * (acc[at, :] * prm_ref[at, 15:16] - m1 - normed * m2)
            return carry

        lax.fori_loop(0, dim // CHUNK, second, 0)

        rows = seqs * chans
        ends = [rows, 2 * rows + SUM_ROWS, 2 * rows + 2 * SUM_ROWS]

        def scatter(d, carry):
            at = pl.ds(pl.multiple_of(d * chans, 8), chans)
            tail_ref[d, : ends[0], :] = stacked(acc[at, :], seqs).astype(bf16)
            tail_ref[d, ends[0] : ends[1], :] = layer_ref[d]
            totals = [sums0_ref[d]] + [sums[n, d] for n in range(sums.shape[0])]
            totals += [padded_totals(folds[q, at, :], width)[0] for q in range(2)]
            tail_ref[d, ends[1] : ends[2], :] = as_rows(totals, SUM_ROWS)
            tail_ref[d, ends[2] :, :] = shared_ref[...]
            return carry

        lax.fori_loop(0, devices, scatter, 0)


def back(d_mixed, pair, heads, projx, weights, prm, xn, x_cot, stat, d_res, acc0, sums0, layer, shared, seqs):
    devices, rows, width = x_cot.shape
    rows = rows // 2
    dim, cols = xn.shape
    chans = dim // devices
    group = 2
    sd = jax.ShapeDtypeStruct
    pieces = -(-2 * (2 + KS) * chans // width)
    out = (
        sd((devices, 2 * rows + 2 * SUM_ROWS + shared.shape[0], width), bf16),
        sd((devices, 2 * chans, dim), bf16),
    )
    return pl.pallas_call(
        lambda *refs: back_body(seqs, group, *refs),
        cost_estimate=takes(20),
        grid=(devices // group,),
        out_shape=out,
        in_specs=[by_group(a, group) for a in (d_mixed, pair, heads, projx, weights)]
        + [whole(prm), whole(xn), half(x_cot, 0)]
        + [whole(a) for a in (stat, d_res, acc0, sums0, layer, shared)],
        out_specs=(whole(out[0]), by_group(out[1], group)),
        scratch_shapes=[
            pltpu.VMEM((dim, cols), f32), pltpu.VMEM((dim, cols), f32), pltpu.VMEM((2, dim, LANE), f32),
            pltpu.VMEM((pieces, devices, 8, width), f32),
        ],
        compiler_params=params(0),
    )(d_mixed, pair, heads, projx, weights, prm, xn, x_cot, stat, d_res, acc0, sums0, layer, shared)


def position_table():
    places = np.arange(LMAX)
    orders = np.arange(1, (EMB - 1) // 2 + 1)
    turns = 2.0 * math.pi * ((orders[:, None] * places[None, :]) % LMAX) / LMAX
    ramp = places[None, :] / (LMAX - 1)
    return np.concatenate([ramp, np.cos(turns), -np.sin(turns)], axis=0).astype(np.float32)


FEAT = position_table()


def mm(a, b, dims):
    return lax.dot_general(a, b, (dims, ((), ())), precision=highest, preferred_element_type=f32)


NN = ((1,), (0,))
TN = ((0,), (0,))
NT = ((1,), (1,))


def mm16(a, b, dims):
    return lax.dot_general(a, b, (dims, ((), ())), preferred_element_type=f32)


def exchange(values):
    return lax.all_to_all(values, "chan", split_axis=0, concat_axis=0, tiled=True)


def on_device(
    layer_in,
    seq_lengths,
    ln1_gain,
    first_norm_bias,
    in_weight,
    in_bias,
    short_weight,
    short_bias,
    filt_in,
    filt_in_bias,
    filt_mid,
    filt_mid_bias,
    sine_freq,
    filt_out,
    decay_rate,
    conv_bias,
    out_weight,
    out_bias,
    ln2_gain,
    second_norm_bias,
    up_weight,
    up_bias,
    down_weight,
    down_bias,
    cotangent,
):
    seqs, chans, _ = layer_in.shape
    devices = lax.axis_size("chan")
    groups = lax.axis_size("batch")
    width = LMAX // devices
    dim = chans * devices
    cols = seqs * width
    hid = up_weight.shape[0]
    ford = filt_mid.shape[0]
    place = lax.axis_index("chan")

    def to_blocks(values):
        return (
            values.reshape(seqs, chans, devices, width)
            .transpose(2, 0, 1, 3)
            .reshape(devices, seqs * chans, width)
        )

    def from_blocks(blocks):
        return (
            blocks.reshape(devices, seqs, chans, width)
            .transpose(1, 2, 0, 3)
            .reshape(seqs, chans, LMAX)
        )

    small = jnp.concatenate(
        [
            in_bias,
            short_bias,
            short_weight.reshape(3 * KS, chans),
            jnp.stack([ln1_gain, first_norm_bias, ln2_gain, second_norm_bias, out_bias, down_bias]),
            up_bias.reshape(hid // chans, chans),
        ],
        axis=0,
    )
    small = jnp.pad(small, ((0, PRM - small.shape[0]), (0, dim - chans)))
    in_rows = in_weight.transpose(1, 2, 0).reshape(3 * chans, dim)
    in_all = lax.all_gather(jnp.concatenate([small, in_rows], axis=0), "chan", axis=0)
    x = exchange(jnp.concatenate([to_blocks(layer_in), to_blocks(cotangent)], axis=1))
    rows = seqs * chans
    xh = lax.ppermute(x[:, :rows, width - LANE :], "chan", [(i, i + 1) for i in range(devices - 1)])
    rest = lax.all_gather(jnp.concatenate([up_weight, down_weight, out_weight], axis=0), "chan", axis=0)
    prm = in_all[:, :PRM, :chans].astype(f32).transpose(0, 2, 1).reshape(dim, PRM)
    out_w = rest[:, 2 * hid :].reshape(dim, dim)

    feat = jnp.asarray(FEAT)
    ramp = feat[0:1]
    rate = sine_freq[:, None]
    pre1 = mm(filt_in, feat, TN) + filt_in_bias[:, None]
    h1 = jnp.sin(rate * pre1)
    pre2 = mm(filt_mid, h1, TN) + filt_mid_bias[:, None]
    h2 = jnp.sin(rate * pre2)
    raw = mm(filt_out, h2, TN)
    falling = jnp.exp(-ramp * decay_rate[:, None])
    env = falling + decay_floor
    filt_spec = filter_spectrum(raw * env)
    bias_col = conv_bias[:, None]

    xn1, stat1, gate, pair, projx0, projx, mixed, heads = front(
        jnp.minimum(place, 1).reshape(1), x, xh, in_all, prm, filt_spec, seqs
    )
    mixed_chan = exchange(mixed)
    backward_hop = [(i + 1, i) for i in range(devices - 1)]
    heads = lax.ppermute(heads, "chan", backward_hop)
    conv_chan, mixed_spec = conv_forward(mixed_chan, filt_spec, bias_col, seqs)
    conv = exchange(conv_chan)

    lens = jnp.concatenate([seq_lengths, place.astype(jnp.int32).reshape(1)])
    layer, d_conv, d_res, p0, p0h, early = middle(
        lens, conv, x, gate.reshape(dim, cols), rest, out_w, prm, hid, seqs
    )
    d_conv_chan = exchange(d_conv)
    p0h = lax.ppermute(p0h, "chan", backward_hop)
    early = lax.psum_scatter(early, "chan", scatter_dimension=0, tiled=True)[0]

    swap = [(0, 1), (1, 0)]
    core = place % 2
    partner = [(i, i ^ 1) for i in range(devices)]
    same_core = [[b * devices + c for b in range(groups) for c in range(q, devices, 2)] for q in range(2)]

    def batch_total(values):
        return values + lax.ppermute(values, "batch", swap) if groups == 2 else lax.psum(values, "batch")

    def over_batch(table):
        if groups != 2:
            return lax.psum_scatter(table.astype(f32), "batch", scatter_dimension=1, tiled=True)
        half = dim // 2
        mine = lax.axis_index("batch") * half
        theirs = lax.dynamic_slice_in_dim(table, half - mine, half, 1)
        own = lax.dynamic_slice_in_dim(table, mine, half, 1)
        return own.astype(f32) + lax.ppermute(theirs, "batch", swap).astype(f32)

    def over_chip(table):
        table = table.reshape((devices // 2, 2) + table.shape[1:])
        own = lax.dynamic_index_in_dim(table, core, 1, False)
        theirs = lax.dynamic_index_in_dim(table, 1 - core, 1, False)
        return (own.astype(f32) + lax.ppermute(theirs, "chan", partner).astype(f32)).astype(bf16)

    def over_chips(both):
        rows = both.shape[1]
        both = both.reshape(devices // 2, rows, groups, dim // groups).transpose(2, 0, 1, 3)
        both = lax.all_to_all(
            both.reshape(groups * devices // 2, rows, dim // groups),
            ("batch", "chan"), split_axis=0, concat_axis=0, tiled=True, axis_index_groups=same_core,
        )
        return jnp.sum(both.astype(f32), axis=0)

    g_in0, sums0, acc0 = back_gate(
        p0.reshape(devices, chans, cols), p0h.reshape(devices, chans, LANE), projx0, in_all, prm, xn1, seqs
    )
    d_mixed_chan, d_filter, g_conv_bias = conv_backward(
        d_conv_chan, mixed_chan, mixed_spec, filt_spec, bias_col, seqs
    )
    g_in0 = over_chip(g_in0)
    d_mixed = exchange(d_mixed_chan)

    q = d_filter * env
    g_filt_out = mm(h2, q, NT)
    g_decay = -jnp.sum(d_filter * raw * falling * ramp, axis=1)
    u2 = mm(filt_out, q, NN) * jnp.cos(rate * pre2)
    fu2 = rate * u2
    u1 = mm(filt_mid, fu2, NN) * jnp.cos(rate * pre1)
    fu1 = rate * u1
    shared = [
        mm(feat, fu1, NT).reshape(-1),
        jnp.sum(fu1, axis=1),
        mm(h1, fu2, NT).reshape(-1),
        jnp.sum(fu2, axis=1),
        jnp.sum(u2 * pre2 + u1 * pre1, axis=1),
    ]
    apart_totals = [g_conv_bias[:, 0], g_decay, g_filt_out.reshape(-1)]
    total = batch_total(jnp.concatenate(shared + apart_totals))
    cut = [0]

    def take(*shape):
        n = math.prod(shape)
        part = total[cut[0] : cut[0] + n].reshape(shape)
        cut[0] += n
        return part

    shared = take(sum(v.shape[0] for v in shared)).astype(bf16)
    g_conv_b, g_decay_rate, g_filt_last = take(chans), take(chans), take(ford, chans)
    shared = jnp.pad(shared, (0, -shared.shape[0] % (32 * width))).reshape(-1, width)

    tail, g_in = back(
        d_mixed, pair, heads, projx, in_all, prm, xn1, x, stat1, d_res, acc0, sums0, layer, shared, seqs
    )
    tail = exchange(tail)
    in_grad = over_chips(jnp.concatenate([g_in0, over_chip(g_in)], axis=1))
    early = over_batch(early)
    up_grad, down_grad, out_grad = early[:hid], early[hid : 2 * hid], early[2 * hid :]

    grad_blocks, out_blocks = tail[:, :rows], tail[:, rows : 2 * rows]
    sums = jnp.sum(tail[:, 2 * rows : 2 * rows + SUM_ROWS].astype(f32), axis=0)
    sums2 = jnp.sum(tail[:, 2 * rows + SUM_ROWS : 2 * rows + 2 * SUM_ROWS].astype(f32), axis=0)
    sums = batch_total(jnp.concatenate([sums, sums2], axis=0))
    sums = sums[0::2] + sums[1::2]
    g_gain2, g_shift2, g_out_b, g_down_b = (sums[i, :chans] for i in range(4))
    g_up_b = sums[4, :hid]
    at = SUM_ROWS // 2
    count = (2 + KS) * chans
    pieces = -(-2 * count // width)
    short0 = sums[at, :count].reshape(2 + KS, 1, chans)
    short = sums[at + 1 : at + 1 + pieces].reshape(-1)[: 2 * count].reshape(2 + KS, 2, chans)
    short = jnp.concatenate([short0, short], axis=1)
    g_in_bias, g_short_bias, g_short_weight = short[0], short[1], short[2:]
    g_gain1, g_shift1 = (sums[at + 1 + pieces + i, :chans] for i in range(2))
    total = jnp.sum(tail[:, 2 * rows + 2 * SUM_ROWS :].astype(f32), axis=0).reshape(-1)
    cut[0] = 0
    g_filt_in, g_filt_in_bias = take(EMB, ford), take(ford)
    g_filt_mid, g_filt_mid_bias, g_sine = take(ford, ford), take(ford), take(ford)

    return (
        from_blocks(out_blocks),
        from_blocks(grad_blocks).astype(f32),
        g_gain1,
        g_shift1,
        in_grad.reshape(3, chans, dim // groups).transpose(2, 0, 1),
        g_in_bias,
        g_short_weight,
        g_short_bias,
        g_filt_in,
        g_filt_in_bias,
        g_filt_mid,
        g_filt_mid_bias,
        g_sine,
        g_filt_last,
        g_decay_rate,
        g_conv_b,
        out_grad,
        g_out_b,
        g_gain2,
        g_shift2,
        up_grad,
        g_up_b,
        down_grad,
        g_down_b,
    )


def solution(mesh):
    token = P("batch", "chan", None)
    chan = P("chan")
    rows = P("chan", None)
    two = P(None, "chan")
    three = P(None, None, "chan")
    in_specs = (
        token, P("batch"), chan, chan, three, two, three, two, P(), P(), P(), P(), P(), two, chan, chan,
        rows, chan, chan, chan, rows, chan, rows, chan, token,
    )
    table = P("chan", "batch")
    out_specs = (
        token, token, chan, chan, P("batch", None, "chan"), two, three, two, P(), P(), P(), P(), P(), two,
        chan, chan, table, chan, chan, chan, table, chan, table, chan,
    )
    return jax.shard_map(
        on_device, mesh=mesh, in_specs=in_specs, out_specs=out_specs, check_vma=False
    )
```

```python
import math

import jax
import jax.numpy as jnp
import numpy as np
from jax import lax
from jax.experimental import pallas as pl
from jax.experimental.pallas import tpu as pltpu
from jax.sharding import PartitionSpec as P

EMB = 33
KS = 3
LMAX = 4096
LANE = 128
COARSE = LMAX // LANE
REPS = tuple(ka + 8 * kb for ka, count in ((0, 5), (1, 8), (2, 8), (3, 8), (4, 4)) for kb in range(count))
PLACE = {k1: i for i, k1 in enumerate(REPS)}
epsilon = 1e-05
decay_floor = 0.05
highest = lax.Precision.HIGHEST
f32 = jnp.float32
bf16 = jnp.bfloat16
vmem_limit = 56 * 1024 * 1024
HEAD_ROWS = 16
SUM_ROWS = 16
BATCH = 3
PRM = 32


def unit(turns):
    angle = 2.0 * math.pi * turns
    return math.cos(angle), math.sin(angle)


def scaled(z, c, s):
    re, im = z
    if im is None:
        return re * c, re * s
    return re * c - im * s, re * s + im * c


def plus(a, b):
    return a[0] + b[0], a[1] + b[1]


def minus(a, b):
    return a[0] - b[0], a[1] - b[1]


def dft4(z, sign):
    s0, d0 = plus(z[0], z[2]), minus(z[0], z[2])
    s1, d1 = plus(z[1], z[3]), minus(z[1], z[3])
    turned = (-d1[1], d1[0]) if sign > 0 else (d1[1], -d1[0])
    return [plus(s0, s1), plus(d0, turned), minus(s0, s1), minus(d0, turned)]


def dft8(z, sign):
    even, odd = dft4(z[0::2], sign), dft4(z[1::2], sign)
    c = math.sqrt(0.5)
    o1 = odd[1]
    o3 = odd[3]
    if sign > 0:
        odd1 = ((o1[0] - o1[1]) * c, (o1[0] + o1[1]) * c)
        odd2 = (-odd[2][1], odd[2][0])
        odd3 = ((-o3[0] - o3[1]) * c, (o3[0] - o3[1]) * c)
    else:
        odd1 = ((o1[0] + o1[1]) * c, (o1[1] - o1[0]) * c)
        odd2 = (odd[2][1], -odd[2][0])
        odd3 = ((o3[1] - o3[0]) * c, (-o3[0] - o3[1]) * c)
    turned = [odd[0], odd1, odd2, odd3]
    return [plus(even[i], turned[i]) for i in range(4)] + [minus(even[i], turned[i]) for i in range(4)]


def coarse_forward(xs, put):
    c = math.sqrt(0.5)
    cols = {ka: [None] * 8 for ka in range(5)}
    for b in range(8):
        x0, x1, x2, x3 = xs[b], xs[8 + b], xs[16 + b], xs[24 + b]
        s02, d02, s13, d13 = x0 + x2, x0 - x2, x1 + x3, x1 - x3
        d13c, s13c = d13 * c, s13 * c
        cols[0][b] = s02 + s13
        cols[4][b] = scaled((s02 - s13, None), *unit(-4 * b / 64))
        cols[2][b] = scaled((d02, -d13), *unit(-2 * b / 64))
        cols[1][b] = scaled((x0 + d13c, -s13c - x2), *unit(-b / 64))
        cols[3][b] = scaled((x0 - d13c, x2 - s13c), *unit(-3 * b / 64))
    for ka in (1, 2, 3):
        for kb, z in enumerate(dft8(cols[ka], -1)):
            put(ka + 8 * kb, z)
    for kb, z in enumerate(dft8(cols[4], -1)[:4]):
        put(4 + 8 * kb, z)
    r = cols[0]
    s04, d04, s26, d26 = r[0] + r[4], r[0] - r[4], r[2] + r[6], r[2] - r[6]
    s15, d15, s37, d37 = r[1] + r[5], r[1] - r[5], r[3] + r[7], r[3] - r[7]
    p, q = (d15 - d37) * c, (d15 + d37) * c
    even, odd = s04 + s26, s15 + s37
    put(0, (even + odd, None))
    put(32, (even - odd, None))
    put(16, (s04 - s26, s37 - s15))
    put(8, (d04 + p, -d26 - q))
    put(24, (d04 - p, d26 - q))


def coarse_inverse(get):
    c = math.sqrt(0.5)
    u = {}
    for ka in (1, 2, 3):
        back = dft8([get(ka + 8 * kb) for kb in range(8)], 1)
        u[ka] = [scaled(back[b], *unit(b * ka / 64)) for b in range(8)]
    v0, v32 = get(0)[0], get(32)[0]
    v8, v16, v24 = get(8), get(16), get(24)
    flat = []
    for b in range(8):
        total = v0 + v32 if b % 2 == 0 else v0 - v32
        for kb, v in ((1, v8), (2, v16), (3, v24)):
            co, si = unit(b * kb / 8)
            if abs(co) > 1e-9:
                total = total + v[0] * (2.0 * co)
            if abs(si) > 1e-9:
                total = total - v[1] * (2.0 * si)
        flat.append(total)
    odd = [get(4 + 8 * kb) for kb in range(4)]
    odd = odd + [(z[0], -z[1]) for z in odd[::-1]]
    half = dft8(odd, 1)
    quarter = []
    for b in range(8):
        co, si = unit(4 * b / 64)
        quarter.append(half[b][0] * co - half[b][1] * si)
    out = [None] * COARSE
    for b in range(8):
        u1, u2, u3 = u[1][b], u[2][b], u[3][b]
        s, d = flat[b] + quarter[b], flat[b] - quarter[b]
        dr, sr = (u1[0] - u3[0]) * c, u1[0] + u3[0]
        si_, di = (u1[1] + u3[1]) * c, u1[1] - u3[1]
        out[b] = s + 2.0 * (sr + u2[0])
        out[16 + b] = s - 2.0 * (di + u2[0])
        out[8 + b] = d + 2.0 * (dr - si_ - u2[1])
        out[24 + b] = d + 2.0 * (u2[1] - dr - si_)
    return out


def transform_tables():
    fine = np.arange(LANE)
    angle = 2.0 * math.pi * ((fine[:, None] * fine[None, :]) % LANE) / LANE
    co, si = np.cos(angle), np.sin(angle)
    ahead = np.block([[co, -si], [si, co]])
    back = ahead.T / (2.0 * LMAX)
    reps = np.array(REPS)
    turn = 2.0 * math.pi * ((reps[:, None] * fine[None, :]) % (2 * LMAX)) / (2 * LMAX)
    twist = np.concatenate([np.cos(turn), -np.sin(turn)], axis=1)[:, None, :]

    def pieces(table):
        table = table.astype(np.float32)
        upper = table.astype(jnp.bfloat16)
        lower = (table - upper.astype(np.float32)).astype(jnp.bfloat16)
        return np.stack([upper, lower])

    return pieces(ahead), pieces(back), twist.astype(np.float32)


AHEAD, BACK, TWIST = transform_tables()


def three_pass(values, table_ref):
    upper = values.astype(bf16)
    lower = (values - upper.astype(f32)).astype(bf16)
    t0, t1 = table_ref[0], table_ref[1]
    return (
        jnp.dot(upper, t0, preferred_element_type=f32)
        + jnp.dot(lower, t0, preferred_element_type=f32)
        + jnp.dot(upper, t1, preferred_element_type=f32)
    )


def rows_forward(xs_ref, spec_ref, rows):
    def step(g, carry):
        at = pl.ds(pl.multiple_of(g * 8, 8), 8)
        xs = [xs_ref[n, at, :] for n in range(COARSE)]

        def put(k1, z):
            i = PLACE[k1]
            spec_ref[i, at, 0:LANE] = z[0]
            spec_ref[i, at, LANE : 2 * LANE] = jnp.zeros_like(z[0]) if z[1] is None else z[1]

        coarse_forward(xs, put)
        return carry

    lax.fori_loop(0, rows // 8, step, 0)


def rows_inverse(spec_ref, ys_ref, rows):
    def step(g, carry):
        at = pl.ds(pl.multiple_of(g * 8, 8), 8)

        def get(k1):
            i = PLACE[k1]
            return spec_ref[i, at, 0:LANE], spec_ref[i, at, LANE : 2 * LANE]

        for n, y in enumerate(coarse_inverse(get)):
            ys_ref[n, at, :] = y
        return carry

    lax.fori_loop(0, rows // 8, step, 0)


def fine_forward(spec, twist, ahead_ref):
    re, im = spec[:, :LANE], spec[:, LANE:]
    tr, ti = twist[:, :LANE], twist[:, LANE:]
    return three_pass(jnp.concatenate([re * tr - im * ti, re * ti + im * tr], axis=1), ahead_ref)


def fine_inverse(spec, twist, back_ref):
    v = three_pass(spec, back_ref)
    re, im = v[:, :LANE], v[:, LANE:]
    tr, ti = twist[:, :LANE], twist[:, LANE:]
    return jnp.concatenate([re * tr + im * ti, im * tr - re * ti], axis=1)


def times(a, b):
    ar, ai, br, bi = a[:, :LANE], a[:, LANE:], b[:, :LANE], b[:, LANE:]
    return jnp.concatenate([ar * br - ai * bi, ar * bi + ai * br], axis=1)


def times_conj(a, b):
    ar, ai, br, bi = a[:, :LANE], a[:, LANE:], b[:, :LANE], b[:, LANE:]
    return jnp.concatenate([ar * br + ai * bi, ai * br - ar * bi], axis=1)


def together(values):
    return values.reshape(values.shape[0] * values.shape[1], values.shape[2])


def apart(values):
    return values.reshape(BATCH, values.shape[0] // BATCH, values.shape[1])


def twists(twist_ref, at, rows):
    return together(jnp.broadcast_to(twist_ref[at], (BATCH, rows, 2 * LANE)))


def spread(blocks_ref, xs_ref):
    per = blocks_ref.shape[2] // LANE
    for n in range(COARSE):
        r = n % per
        xs_ref[n] = blocks_ref[n // per, :, r * LANE : (r + 1) * LANE].astype(f32)


def filter_spectrum_body(filter_ref, twist_ref, ahead_ref, out_ref, xs_ref):
    rows = filter_ref.shape[0]
    for n in range(COARSE):
        xs_ref[n] = filter_ref[:, n * LANE : (n + 1) * LANE]
    rows_forward(xs_ref, out_ref, rows)

    def step(i, carry):
        at = pl.ds(i * BATCH, BATCH)
        out_ref[at] = apart(fine_forward(together(out_ref[at]), twists(twist_ref, at, rows), ahead_ref))
        return carry

    lax.fori_loop(0, len(REPS) // BATCH, step, 0)


def conv_forward_body(seqs, mixed_ref, filt_ref, bias_ref, twist_ref, ahead_ref, back_ref, out_ref, spec_ref, xs_ref, work_ref):
    rows = mixed_ref.shape[1]
    spread(mixed_ref, xs_ref)
    rows_forward(xs_ref, spec_ref, rows)

    def step(i, carry):
        at = pl.ds(i * BATCH, BATCH)
        twist = twists(twist_ref, at, rows)
        z = fine_forward(together(spec_ref[at]), twist, ahead_ref)
        spec_ref[at] = apart(z)
        k = together(jnp.concatenate([filt_ref[at]] * seqs, axis=1))
        work_ref[at] = apart(fine_inverse(times(z, k), twist, back_ref))
        return carry

    lax.fori_loop(0, len(REPS) // BATCH, step, 0)
    ys_ref = xs_ref
    rows_inverse(work_ref, ys_ref, rows)
    per = mixed_ref.shape[2] // LANE
    bias = jnp.concatenate([bias_ref[...]] * seqs, axis=0)
    for n in range(COARSE):
        at = (n // per, slice(None), slice((n % per) * LANE, (n % per + 1) * LANE))
        out_ref[at] = (ys_ref[n] + bias * mixed_ref[at].astype(f32)).astype(bf16)


def heads_out(out_ref, block, y):
    rows, width = y.shape[0], out_ref.shape[2]
    square = jnp.concatenate([y, jnp.zeros((LANE - rows, LANE), f32)], axis=0) if rows < LANE else y
    head = square.T[:HEAD_ROWS]
    if width > LANE:
        head = jnp.concatenate([head, jnp.zeros((HEAD_ROWS, width - LANE), f32)], axis=1)
    out_ref[block, rows:, :] = head.astype(bf16)


def conv_backward_body(
    seqs, d_ref, mixed_ref, mixed_spec_ref, filt_ref, bias_ref, twist_ref, ahead_ref, back_ref, out_ref, dfilt_ref, dbias_ref, xs_ref, spec_ref, work_ref, ys_ref
):
    rows = d_ref.shape[1]
    chans = rows // seqs
    spread(d_ref, xs_ref)
    rows_forward(xs_ref, spec_ref, rows)

    def step(i, carry):
        at = pl.ds(i * BATCH, BATCH)
        z = fine_forward(together(spec_ref[at]), twists(twist_ref, at, rows), ahead_ref)
        k = together(jnp.concatenate([filt_ref[at]] * seqs, axis=1))
        cross = apart(times_conj(z, together(mixed_spec_ref[at])))
        cross = sum(cross[:, s * chans : (s + 1) * chans] for s in range(seqs))
        both = together(jnp.concatenate([apart(times_conj(z, k)), cross], axis=1))
        work_ref[at] = apart(fine_inverse(both, twists(twist_ref, at, rows + chans), back_ref))
        return carry

    lax.fori_loop(0, len(REPS) // BATCH, step, 0)
    rows_inverse(work_ref, ys_ref, rows + chans)
    per = d_ref.shape[2] // LANE
    bias = jnp.concatenate([bias_ref[...]] * seqs, axis=0)
    total = jnp.zeros((rows, LANE), f32)
    out_ref[out_ref.shape[0] - 1, rows:, :] = jnp.zeros((HEAD_ROWS, d_ref.shape[2]), bf16)
    for n in range(COARSE):
        at = (n // per, slice(0, rows), slice((n % per) * LANE, (n % per + 1) * LANE))
        d = xs_ref[n]
        y = ys_ref[n, :rows, :] + bias * d
        out_ref[at] = y.astype(bf16)
        if n % per == 0 and n > 0:
            heads_out(out_ref, n // per - 1, y)
        total = total + d * mixed_ref[at].astype(f32)
        dfilt_ref[:, n * LANE : (n + 1) * LANE] = ys_ref[n, rows:, :]
    total = sum(total[s * chans : (s + 1) * chans] for s in range(seqs))
    dbias_ref[...] = jnp.sum(total, axis=1, keepdims=True)


def takes(us):
    return pl.CostEstimate(flops=int(us * 1e9), bytes_accessed=int(us * 3e6), transcendentals=0)


def whole_call(us, body, out_shape, scratch, *args):
    return pl.pallas_call(
        body,
        cost_estimate=takes(us),
        out_shape=out_shape,
        in_specs=[pl.BlockSpec(memory_space=pltpu.VMEM)] * len(args),
        out_specs=jax.tree.map(lambda _: pl.BlockSpec(memory_space=pltpu.VMEM), out_shape),
        scratch_shapes=scratch,
        compiler_params=pltpu.CompilerParams(vmem_limit_bytes=vmem_limit),
    )(*args)


def filter_spectrum(filt):
    rows = filt.shape[0]
    return whole_call(
        8,
        filter_spectrum_body,
        jax.ShapeDtypeStruct((len(REPS), rows, 2 * LANE), f32),
        [pltpu.VMEM((COARSE, rows, LANE), f32)],
        filt,
        jnp.asarray(TWIST),
        jnp.asarray(AHEAD),
    )


def conv_forward(mixed, filt_spec, bias, seqs):
    blocks, rows, width = mixed.shape
    n = len(REPS)
    return whole_call(
        100,
        lambda *refs: conv_forward_body(seqs, *refs),
        (jax.ShapeDtypeStruct(mixed.shape, bf16), jax.ShapeDtypeStruct((n, rows, 2 * LANE), f32)),
        [pltpu.VMEM((COARSE, rows, LANE), f32), pltpu.VMEM((n, rows, 2 * LANE), f32)],
        mixed,
        filt_spec,
        bias,
        jnp.asarray(TWIST),
        jnp.asarray(AHEAD),
        jnp.asarray(BACK),
    )


def conv_backward(d_conv, mixed, mixed_spec, filt_spec, bias, seqs):
    blocks, rows, width = mixed.shape
    chans = rows // seqs
    n = len(REPS)
    return whole_call(
        100,
        lambda *refs: conv_backward_body(seqs, *refs),
        (
            jax.ShapeDtypeStruct((blocks, rows + HEAD_ROWS, width), bf16),
            jax.ShapeDtypeStruct((chans, LMAX), f32),
            jax.ShapeDtypeStruct((chans, 1), f32),
        ),
        [
            pltpu.VMEM((COARSE, rows, LANE), f32),
            pltpu.VMEM((n, rows, 2 * LANE), f32),
            pltpu.VMEM((n, rows + chans, 2 * LANE), f32),
            pltpu.VMEM((COARSE, rows + chans, LANE), f32),
        ],
        d_conv,
        mixed,
        mixed_spec,
        filt_spec,
        bias,
        jnp.asarray(TWIST),
        jnp.asarray(AHEAD),
        jnp.asarray(BACK),
    )


CHUNK = 48


def lanes_of(shape):
    return lax.broadcasted_iota(jnp.int32, shape, 1)


def side_by_side(block, seqs):
    chans = block.shape[0] // seqs
    return jnp.concatenate([block[s * chans : (s + 1) * chans] for s in range(seqs)], axis=1)


def stacked(values, seqs):
    width = values.shape[1] // seqs
    return jnp.concatenate([values[:, s * width : (s + 1) * width] for s in range(seqs)], axis=0)


def eights(values):
    return jnp.sum(values.reshape(values.shape[0] // 8, 8, values.shape[1]), axis=0)


def folded(values):
    return sum(values[:, i * LANE : (i + 1) * LANE] for i in range(values.shape[1] // LANE))


def row_totals(values):
    ones = jnp.ones((8, LANE), bf16)
    upper = values.astype(bf16)
    lower = (values - upper.astype(f32)).astype(bf16)
    return mm16(ones, upper, NT) + mm16(ones, lower, NT)


def padded_totals(values, width):
    extra = -values.shape[0] % width
    if extra:
        values = jnp.concatenate([values, jnp.zeros((extra, LANE), f32)], axis=0)
    totals = row_totals(values)
    return [totals[:, i * width : (i + 1) * width] for i in range(totals.shape[1] // width)]


def as_rows(totals, rows):
    halves = []
    for t in totals:
        upper = t.astype(bf16).astype(f32)
        halves += [upper, t - upper]
    place = lax.broadcasted_iota(jnp.int32, halves[0].shape, 0)
    tiles = []
    for first in range(0, rows, 8):
        tile = jnp.zeros_like(halves[0])
        for i, h in enumerate(halves[first : first + 8]):
            tile = jnp.where(place == i, h, tile)
        tiles.append(tile)
    return jnp.concatenate(tiles, axis=0).astype(bf16)


def chunk_rows(i):
    return pl.ds(pl.multiple_of(i * CHUNK, CHUNK), CHUNK)


def norm_stats(ref, dim):
    cols = ref.shape[1]
    zero = jnp.zeros((8, cols), f32)
    total = lax.fori_loop(0, dim // CHUNK, lambda i, t: t + eights(ref[chunk_rows(i), :]), zero)
    mean = jnp.sum(total, axis=0, keepdims=True) / dim

    def spread_sq(i, t):
        v = ref[chunk_rows(i), :] - mean
        return t + eights(v * v)

    var = jnp.sum(lax.fori_loop(0, dim // CHUNK, spread_sq, zero), axis=0, keepdims=True) / dim
    return mean, lax.rsqrt(var + epsilon)


def front_body(
    seqs, table_ref, x_ref, xh_ref, own_ref, other_ref, own_small, other_small, after_ref,
    prm_ref, xn_ref, stat_ref, gate_ref, pair_ref, projx0_ref, projx_ref, mixed_ref, heads_ref, xs, xb,
):
    devices, _, width = x_ref.shape
    dim, cols = xn_ref.shape
    chans = dim // devices
    turns = devices // 2
    step = pl.program_id(0)

    @pl.when(step == 0)
    def _():
        for turn in range(turns):
            for ref, (device, _) in zip((own_small, other_small), slots(table_ref, turns, turn)):
                small = jnp.concatenate([ref[turn].astype(f32), jnp.zeros((LANE - PRM, LANE), f32)], axis=0)
                prm_ref[pl.ds(pl.multiple_of(device * chans, 8), chans), :] = small.T[:chans, :PRM]

        def gather(d, carry):
            at = pl.ds(pl.multiple_of(d * chans, 8), chans)
            row = side_by_side(x_ref[d].astype(f32), seqs)
            tail = xh_ref[d].astype(f32)
            tail = jnp.where(
                lanes_of((chans, LANE)) < LANE // 2, pltpu.roll(tail[chans : 2 * chans], LANE // 2, 1), tail[:chans]
            )
            xs[at, :] = jnp.concatenate([row, tail], axis=1)
            return carry

        lax.fori_loop(0, devices, gather, 0)
        mean, inverse = norm_stats(xs, dim)

        def scale(i, carry):
            at = chunk_rows(i)
            prm = prm_ref[at, :]
            v = (xs[at, :] - mean) * inverse * prm[:, 15:16] + prm[:, 16:17]
            xb[at, :] = v.astype(bf16)
            xn_ref[at, :] = v[:, :cols].astype(bf16)
            return carry

        lax.fori_loop(0, dim // CHUNK, scale, 0)
        stat_ref[0:8, :] = jnp.broadcast_to(mean[:, :cols], (8, cols))
        stat_ref[8:16, :] = jnp.broadcast_to(inverse[:, :cols], (8, cols))

    keep = (table_ref[turns + 1] > 0).astype(f32)
    for w_ref, (device, g) in zip((own_ref, other_ref), slots(table_ref, turns, step)):
        prm = prm_ref[pl.ds(pl.multiple_of(device * chans, 8), chans), :]
        proj = mm16(w_ref[0, PRM:, :], xb[...], NN)
        ys = []
        px = []
        for i in range(3):
            x = proj[i * chans : (i + 1) * chans] + prm[:, i : i + 1]
            tail = x[:, cols:] * keep
            px += [jnp.concatenate([x[:, :cols], tail], axis=1)]
            weights = [jnp.broadcast_to(prm[:, 6 + 3 * j + i : 7 + 3 * j + i], (chans, width)) for j in range(KS)]
            bias = jnp.broadcast_to(prm[:, 3 + i : 4 + i], (chans, width))
            parts = []
            for s in range(seqs):
                v = x[:, s * width : (s + 1) * width]
                wide = jnp.concatenate([tail if s == 0 else pltpu.roll(tail, LANE // 2, 1), v], axis=1)
                y = bias + weights[0] * v
                for j in range(1, KS):
                    y = y + weights[j] * pltpu.roll(wide, j, 1)[:, LANE:]
                parts.append(y)
            ys.append(jnp.concatenate(parts, axis=1))
        projx0_ref[g] = px[0].astype(bf16)
        projx_ref[g] = jnp.concatenate(px[1:], axis=0).astype(bf16)
        gate_ref[g] = ys[0]
        pair = jnp.concatenate(ys[1:], axis=0)
        pair_ref[g] = pair
        mixed_ref[g] = stacked(ys[1] * ys[2], seqs).astype(bf16)
        heads_ref[g] = first_tokens(pair, seqs).astype(bf16)


def first_tokens(values, seqs):
    width = values.shape[1] // seqs
    second = pltpu.roll(values[:, width : width + LANE], LANE // 2, 1)
    return jnp.where(lanes_of((values.shape[0], LANE)) < LANE // 2, values[:, :LANE], second)


def whole(a):
    return pl.BlockSpec(a.shape, lambda i, t: (0,) * len(a.shape), pipeline_mode=pl.Buffered(1))


def untouched():
    return pl.BlockSpec(memory_space=pl.ANY)


def by_chip(a):
    return pl.BlockSpec((2,) + a.shape[1:], lambda i, t: (t[i],) + (0,) * (len(a.shape) - 1))


def by_turn(a, rows=None):
    return pl.BlockSpec((1, a.shape[1] if rows is None else rows, a.shape[2]), lambda i, t: (i, 0, 0))


def chip_call(us, body, table, turns, args, in_specs, out, out_specs, scratch):
    return pl.pallas_call(
        body,
        cost_estimate=takes(us),
        out_shape=out,
        grid_spec=pltpu.PrefetchScalarGridSpec(
            num_scalar_prefetch=1,
            grid=(turns,),
            in_specs=in_specs,
            out_specs=out_specs,
            scratch_shapes=scratch,
        ),
        compiler_params=pltpu.CompilerParams(vmem_limit_bytes=vmem_limit, dimension_semantics=("arbitrary",)),
    )(table, *args)


def slots(table_ref, turns, step):
    core = table_ref[turns]
    chip = table_ref[step]
    return ((2 * chip + core, core), (2 * chip + 1 - core, 1 - core))


def front(table, x, xh, own, other, before, seqs):
    devices, rows, width = x.shape
    chans = rows // seqs
    dim = devices * chans
    cols = seqs * width
    turns = devices // 2
    sd = jax.ShapeDtypeStruct
    out = (
        sd((dim, PRM), f32),
        sd((dim, cols), bf16),
        sd((16, cols), f32),
        sd((devices, chans, cols), f32),
        sd((devices, 2 * chans, cols), f32),
        sd((devices, chans, cols + LANE), bf16),
        sd((devices, 2 * chans, cols + LANE), bf16),
        sd((devices, rows, width), bf16),
        sd((devices, 2 * chans, LANE), bf16),
    )
    small = pl.BlockSpec((turns, PRM, LANE), lambda i, t: (0, 0, 0), pipeline_mode=pl.Buffered(1))
    return chip_call(
        100,
        lambda *refs: front_body(seqs, *refs),
        table,
        turns,
        (x, xh, own, other, own, other, before),
        [whole(x), whole(xh), by_turn(own), by_turn(other), small, small, untouched()],
        out,
        tuple(whole(o) for o in out[:3]) + tuple(by_chip(o) for o in out[3:]),
        [pltpu.VMEM((dim, cols + LANE), f32), pltpu.VMEM((dim, cols + LANE), bf16)],
    )


def middle_body(seqs, pieces, segments, table_ref, conv_ref, x_ref, cot_ref, gate_ref, prm_ref, *refs):
    weights = []
    for _ in range(pieces):
        weights.append([[refs[2 * (segments * core + n) : 2 * (segments * core + n) + 2] for n in range(segments)] for core in range(2)])
        refs = refs[4 * segments :]
    layer_ref, d_conv_ref, d_res_ref, p0_ref, p0h_ref = refs[:5]
    grads, refs = [refs[5 + 2 * p : 7 + 2 * p] for p in range(pieces)], refs[5 + 2 * pieces :]
    cs, res, ds, xb, db, gb, acc_out, acc_in, folds, up_folds, stats, out_w32 = refs[:12]
    out_w_refs = refs[12:]
    devices, _, width = x_ref.shape
    dim, cols = d_res_ref.shape
    chans = dim // devices
    hid = weights[0][0][0][0].shape[1] // 2
    turns = devices // 2
    part = dim // pieces
    group = table_ref[turns + 2 + seqs] if pieces == 2 else 0
    columns = [pl.ds(pl.multiple_of((group if p == 0 else 1 - group) * part, LANE), part) for p in range(pieces)]
    step = pl.program_id(0)
    last = pl.num_programs(0) - 1
    lane = lanes_of((1, cols))
    live = jnp.zeros((1, cols), f32)
    for s in range(seqs):
        position = table_ref[turns + 1] * width + lane - s * width
        inside = (lane >= s * width) & (lane < (s + 1) * width) & (position < table_ref[turns + 2 + s])
        live = jnp.where(inside, 1.0, live)

    def device_rows(d):
        return pl.ds(pl.multiple_of(d * chans, 8), chans)

    @pl.when(step == 0)
    def _():
        def gather(d, carry):
            at = device_rows(d)
            cs[at, :] = side_by_side(conv_ref[d].astype(f32), seqs)
            res[at, :] = side_by_side(x_ref[d].astype(f32), seqs)
            ds[at, :] = live * side_by_side(cot_ref[d].astype(f32), seqs)
            return carry

        lax.fori_loop(0, devices, gather, 0)
        for piece, out_w_ref in zip(weights, out_w_refs):
            for core, parts in enumerate(piece):
                turn = 0
                for _, out_rows in parts:
                    for n in range(out_rows.shape[0]):
                        device, _ = slots(table_ref, turns, turn)[core]
                        out_w32[device_rows(device), :] = out_rows[n].astype(f32)
                        turn += 1

            def narrow(i, carry):
                at = chunk_rows(i)
                out_w_ref[at, :] = out_w32[at, :].astype(bf16)
                return carry

            lax.fori_loop(0, dim // CHUNK, narrow, 0)

        def gated(i, carry):
            at = chunk_rows(i)
            gb[at, :] = (cs[at, :] * gate_ref[at, :]).astype(bf16)
            d = ds[at, :]
            db[at, :] = d.astype(bf16)
            folds[3, at, :] = folded(d)
            acc_in[at, :] = jnp.zeros((CHUNK, cols), f32)
            return carry

        lax.fori_loop(0, dim // CHUNK, gated, 0)
        for at, out_w_ref in zip(columns, out_w_refs):
            acc_out[at, :] = mm16(out_w_ref[...], gb[...], TN)

        def add(i, carry):
            at = chunk_rows(i)
            res[at, :] = res[at, :] + acc_out[at, :] + prm_ref[at, 19:20]
            acc_out[at, :] = jnp.zeros((CHUNK, cols), f32)
            return carry

        lax.fori_loop(0, dim // CHUNK, add, 0)
        mean, inverse = norm_stats(res, dim)

        def scale(i, carry):
            at = chunk_rows(i)
            normed = (res[at, :] - mean) * inverse
            cs_norm = normed * prm_ref[at, 17:18] + prm_ref[at, 18:19]
            xb[at, :] = cs_norm.astype(bf16)
            return carry

        lax.fori_loop(0, dim // CHUNK, scale, 0)
        stats[0:8, :] = jnp.broadcast_to(mean, (8, cols))
        stats[8:16, :] = jnp.broadcast_to(inverse, (8, cols))

    pair = slots(table_ref, turns, step)
    up_b = []
    for device, _ in pair:
        prm = prm_ref[device_rows(device), :]
        up_b += [prm[:, 21 + m : 22 + m] for m in range(hid // chans)]
    up_b = jnp.concatenate(up_b, axis=0)

    def now(parts, rows):
        blocks = [ref[0, rows, :] for ref, _ in parts]
        return blocks[0] if len(blocks) == 1 else jnp.where(step < turns // 2, blocks[0], blocks[1])

    ups = [jnp.concatenate([now(parts, slice(0, hid)) for parts in piece], axis=0) for piece in weights]
    downs = [jnp.concatenate([now(parts, slice(hid, 2 * hid)) for parts in piece], axis=0) for piece in weights]
    u = sum(mm16(up, xb[at, :], NN) for up, at in zip(ups, columns)) + up_b
    d_act = sum(mm16(down, db[at, :], NN) for down, at in zip(downs, columns))
    a, k = 0.044715, math.sqrt(2.0 / math.pi)
    sq = u * u
    t = jnp.tanh(u * (k + (k * a) * sq))
    half = 0.5 * (1.0 + t)
    act = (u * half).astype(bf16)
    d_u = d_act * (half + 0.5 * u * (1.0 - t * t) * (k + (3.0 * k * a) * sq))
    d_low = d_u.astype(bf16)
    fold = folded(d_u)
    for n, (device, _) in enumerate(pair):
        up_folds[pl.ds(pl.multiple_of(device * hid, 8), hid), :] = fold[n * hid : (n + 1) * hid]
    for up, down, at, g_refs in zip(ups, downs, columns, grads):
        g_up = mm16(d_low, xb[at, :], NT).astype(bf16)
        g_down = mm16(act, db[at, :], NT).astype(bf16)
        for n, g_ref in enumerate(g_refs):
            mine = slice(n * hid, (n + 1) * hid)
            g_ref[step, :hid, :] = g_up[mine]
            g_ref[step, hid : 2 * hid, :] = g_down[mine]
        acc_out[at, :] += mm16(down, act, TN)
        acc_in[at, :] += mm16(up, d_low, TN)

    @pl.when(step == last)
    def _():
        mean, inverse = stats[0:1, :], stats[8:9, :]

        def result(i, t):
            at = chunk_rows(i)
            r = res[at, :]
            acc_out[at, :] = live * (r + acc_out[at, :] + prm_ref[at, 20:21])
            normed = (r - mean) * inverse
            d = acc_in[at, :]
            both = d * normed
            folds[0, at, :] = folded(both)
            folds[1, at, :] = folded(d)
            gain = prm_ref[at, 17:18]
            return t[0] + eights(d * gain), t[1] + eights(both * gain)

        zero = jnp.zeros((8, cols), f32)
        m1, m2 = lax.fori_loop(0, dim // CHUNK, result, (zero, zero))
        m1 = jnp.sum(m1, axis=0, keepdims=True) / dim
        m2 = jnp.sum(m2, axis=0, keepdims=True) / dim

        def residual(i, carry):
            at = chunk_rows(i)
            normed = (res[at, :] - mean) * inverse
            d = ds[at, :] + inverse * (acc_in[at, :] * prm_ref[at, 17:18] - m1 - normed * m2)
            d_res_ref[at, :] = d
            folds[2, at, :] = folded(d)
            db[at, :] = d.astype(bf16)
            return carry

        lax.fori_loop(0, dim // CHUNK, residual, 0)
        for n in range(dim // 256):
            some = slice(n * 256, (n + 1) * 256)
            acc_in[some, :] = sum(mm16(w[some, :], db[at, :], NN) for w, at in zip(out_w_refs, columns))
        for at, g_refs in zip(columns, grads):
            for n in range(dim // 256):
                some = slice(n * 256, (n + 1) * 256)
                out_w32[some, :] = mm16(gb[some, :], db[at, :], NT)
            for turn in range(turns):
                for g_ref, (device, _) in zip(g_refs, slots(table_ref, turns, turn)):
                    g_ref[turn, 2 * hid :, :] = out_w32[device_rows(device), :].astype(bf16)

        def products(i, carry):
            at = chunk_rows(i)
            d = acc_in[at, :]
            p0 = d * cs[at, :]
            p0_ref[at, :] = p0
            p0h_ref[at, :] = first_tokens(p0, seqs)
            acc_in[at, :] = d * gate_ref[at, :]
            return carry

        lax.fori_loop(0, dim // CHUNK, products, 0)

        def scatter(d, carry):
            at = device_rows(d)
            layer_ref[d, : seqs * chans, :] = stacked(acc_out[at, :], seqs).astype(bf16)
            d_conv_ref[d] = stacked(acc_in[at, :], seqs).astype(bf16)
            totals = [padded_totals(folds[q, at, :], width)[0] for q in range(4)]
            totals += padded_totals(up_folds[pl.ds(pl.multiple_of(d * hid, 8), hid), :], width)
            layer_ref[d, seqs * chans :, :] = as_rows(totals, SUM_ROWS)
            return carry

        lax.fori_loop(0, devices, scatter, 0)


def middle(table, conv, x, cot, gate, matrices, prm, hid, seqs):
    devices, rows, width = conv.shape
    dim, cols = gate.shape
    chans = dim // devices
    turns = devices // 2
    pieces = len(matrices)
    part = dim // pieces
    sd = jax.ShapeDtypeStruct
    out = (
        sd((devices, rows + SUM_ROWS, width), bf16),
        sd((devices, rows, width), bf16),
        sd((dim, cols), f32),
        sd((dim, cols), f32),
        sd((dim, LANE), f32),
    ) + (sd((turns, 2 * hid + chans, part), bf16),) * (2 * pieces)
    big = pltpu.VMEM((dim, cols), f32)
    low = pltpu.VMEM((dim, cols), bf16)
    args, specs = [conv, x, cot, gate, prm], [whole(conv), whole(x), whole(cot), whole(gate), whole(prm)]
    segments = len(matrices[0][0])
    for piece in matrices:
        for parts in piece:
            first = 0
            for a in parts:
                count = a.shape[0]
                args += [a, a]
                specs += [
                    pl.BlockSpec((1, 2 * hid, part), lambda i, t, f=first, c=count: (jnp.clip(i - f, 0, c - 1), 0, 0)),
                    pl.BlockSpec(
                        (count, chans, part), lambda i, t: (0, 2 * hid // chans, 0), pipeline_mode=pl.Buffered(1)
                    ),
                ]
                first += count
    return chip_call(
        36,
        lambda *refs: middle_body(seqs, pieces, segments, *refs),
        table,
        turns,
        args,
        specs,
        out,
        tuple(whole(o) for o in out),
        [
            big, big, big, low, low, low, big, big, pltpu.VMEM((4, dim, LANE), f32),
            pltpu.VMEM((devices * hid, LANE), f32), pltpu.VMEM((16, cols), f32), pltpu.VMEM((dim, part), f32),
        ]
        + [pltpu.VMEM((dim, part), bf16)] * pieces,
    )


def short_back(seqs, prm, kinds, d_short, head, projx, width, cols):
    chans = prm.shape[0]
    d_proj = []
    totals = [[] for _ in range(2 + KS)]
    for n, i in enumerate(kinds):
        px = projx[n * chans : (n + 1) * chans]
        weights = [jnp.broadcast_to(prm[:, 6 + 3 * j + i : 7 + 3 * j + i], (chans, width)) for j in range(KS)]
        parts = []
        sums = [0.0] * (2 + KS)
        for s in range(seqs):
            at = slice(s * width, (s + 1) * width)
            d = d_short[n][:, at]
            x = px[:, at]
            tail = px[:, cols:]
            wide = jnp.concatenate([tail if s == 0 else pltpu.roll(tail, LANE // 2, 1), x], axis=1)
            after = jnp.concatenate([d, head[n] if s == 0 else pltpu.roll(head[n], LANE // 2, 1)], axis=1)
            y = weights[0] * d
            sums[1] = sums[1] + folded(d)
            sums[2] = sums[2] + folded(d * x)
            for j in range(1, KS):
                y = y + weights[j] * pltpu.roll(after, width + LANE - j, 1)[:, :width]
                sums[2 + j] = sums[2 + j] + folded(d * pltpu.roll(wide, j, 1)[:, LANE:])
            sums[0] = sums[0] + folded(y)
            parts.append(y)
        d_proj.append(jnp.concatenate(parts, axis=1))
        for k in range(2 + KS):
            totals[k].append(sums[k])
    d_low = jnp.concatenate(d_proj, axis=0).astype(bf16)
    return d_low, padded_totals(jnp.concatenate(sum(totals, []), axis=0), width)


def back_gate_body(seqs, table_ref, p0_ref, p0h_ref, projx_ref, own_ref, other_ref, prm_ref, xn_ref, g_ref, sums_ref, acc):
    dim, cols = xn_ref.shape
    chans = p0_ref.shape[1]
    step = pl.program_id(0)

    @pl.when(step == 0)
    def _():
        acc[...] = jnp.zeros_like(acc)

    turns = prm_ref.shape[0] // chans // 2
    for w_ref, (device, g) in zip((own_ref, other_ref), slots(table_ref, turns, step)):
        prm = prm_ref[pl.ds(pl.multiple_of(device * chans, 8), chans), :]
        d_low, totals = short_back(
            seqs, prm, (0,), (p0_ref[g],), (p0h_ref[g],), projx_ref[g].astype(f32), cols // seqs, cols
        )
        sums_ref[g] = totals[0]
        acc[...] += mm16(w_ref[0, PRM : PRM + chans, :], d_low, TN)
        g_ref[g] = mm16(d_low, xn_ref[...], NT).astype(bf16)


def back_gate(table, p0, p0h, projx, own, other, prm, xn, seqs):
    devices, chans, cols = p0.shape
    dim = xn.shape[0]
    sd = jax.ShapeDtypeStruct
    out = (
        sd((devices, chans, dim), bf16),
        sd((devices, 8, cols // seqs), f32),
        sd((dim, cols), f32),
    )
    return chip_call(
        2,
        lambda *refs: back_gate_body(seqs, *refs),
        table,
        devices // 2,
        (p0, p0h, projx, own, other, prm, xn),
        [by_chip(a) for a in (p0, p0h, projx)] + [by_turn(own), by_turn(other), whole(prm), whole(xn)],
        out,
        (by_chip(out[0]), by_chip(out[1]), whole(out[2])),
        [],
    )


def back_body(
    seqs, table_ref, d_mixed_ref, pair_ref, heads_ref, projx_ref, own_ref, other_ref, prm_ref, xn_ref, x_ref, stat_ref, d_res_ref,
    acc0_ref, sums0_ref, layer_ref, tail_ref, g_ref, acc, xs, folds, sums,
):
    devices, _, width = x_ref.shape
    dim, cols = xn_ref.shape
    chans = dim // devices
    step = pl.program_id(0)
    last = pl.num_programs(0) - 1

    @pl.when(step == 0)
    def _():
        acc[...] = acc0_ref[...]

    turns = devices // 2
    for w_ref, (device, g) in zip((own_ref, other_ref), slots(table_ref, turns, step)):
        prm = prm_ref[pl.ds(pl.multiple_of(device * chans, 8), chans), :]
        block = d_mixed_ref[g].astype(f32)
        d_mixed = side_by_side(block[: seqs * chans], seqs)
        square = jnp.concatenate([block[seqs * chans :, :LANE], jnp.zeros((LANE - HEAD_ROWS, LANE), f32)], axis=0).T
        second = pltpu.roll(square[chans : 2 * chans], LANE // 2, 1)
        d_head = jnp.where(lanes_of((chans, LANE)) < LANE // 2, square[:chans], second)
        pair = pair_ref[g]
        pair_head = heads_ref[g].astype(f32)
        d_short = (d_mixed * pair[chans:], d_mixed * pair[:chans])
        head = (d_head * pair_head[chans:], d_head * pair_head[:chans])
        d_low, totals = short_back(seqs, prm, (1, 2), d_short, head, projx_ref[g].astype(f32), width, cols)
        for n, t in enumerate(totals):
            sums[n, device] = t
        acc[...] += mm16(w_ref[0, PRM + chans :, :], d_low, TN)
        g_ref[g] = mm16(d_low, xn_ref[...], NT).astype(bf16)

    @pl.when(step == last)
    def _():
        def gather(d, carry):
            xs[pl.ds(pl.multiple_of(d * chans, 8), chans), :] = side_by_side(x_ref[d].astype(f32), seqs)
            return carry

        lax.fori_loop(0, devices, gather, 0)
        mean, inverse = stat_ref[0:1, :], stat_ref[8:9, :]

        def first(i, t):
            at = chunk_rows(i)
            normed = (xs[at, :] - mean) * inverse
            d = acc[at, :]
            both = d * normed
            folds[0, at, :] = folded(both)
            folds[1, at, :] = folded(d)
            gain = prm_ref[at, 15:16]
            return t[0] + eights(d * gain), t[1] + eights(both * gain)

        zero = jnp.zeros((8, cols), f32)
        m1, m2 = lax.fori_loop(0, dim // CHUNK, first, (zero, zero))
        m1 = jnp.sum(m1, axis=0, keepdims=True) / dim
        m2 = jnp.sum(m2, axis=0, keepdims=True) / dim

        def second(i, carry):
            at = chunk_rows(i)
            normed = (xs[at, :] - mean) * inverse
            acc[at, :] = d_res_ref[at, :] + inverse * (acc[at, :] * prm_ref[at, 15:16] - m1 - normed * m2)
            return carry

        lax.fori_loop(0, dim // CHUNK, second, 0)

        rows = seqs * chans

        def scatter(d, carry):
            at = pl.ds(pl.multiple_of(d * chans, 8), chans)
            tail_ref[d, :rows, :] = stacked(acc[at, :], seqs).astype(bf16)
            totals = [sums0_ref[d]] + [sums[n, d] for n in range(sums.shape[0])]
            totals += [padded_totals(folds[q, at, :], width)[0] for q in range(2)]
            tail_ref[d, rows : rows + SUM_ROWS, :] = as_rows(totals, SUM_ROWS)
            tail_ref[d, rows + SUM_ROWS :, :] = layer_ref[d]
            return carry

        lax.fori_loop(0, devices, scatter, 0)


def back(table, d_mixed, pair, heads, projx, own, other, prm, xn, x, stat, d_res, acc0, sums0, layer, seqs):
    devices, rows, width = x.shape
    dim, cols = xn.shape
    chans = dim // devices
    sd = jax.ShapeDtypeStruct
    pieces = -(-2 * (2 + KS) * chans // width)
    out = (
        sd((devices, 2 * rows + 2 * SUM_ROWS, width), bf16),
        sd((devices, 2 * chans, dim), bf16),
    )
    return chip_call(
        100,
        lambda *refs: back_body(seqs, *refs),
        table,
        devices // 2,
        (d_mixed, pair, heads, projx, own, other, prm, xn, x, stat, d_res, acc0, sums0, layer),
        [by_chip(a) for a in (d_mixed, pair, heads, projx)]
        + [by_turn(own), by_turn(other), whole(prm), whole(xn), whole(x)]
        + [whole(a) for a in (stat, d_res, acc0, sums0, layer)],
        out,
        (whole(out[0]), by_chip(out[1])),
        [
            pltpu.VMEM((dim, cols), f32), pltpu.VMEM((dim, cols), f32), pltpu.VMEM((2, dim, LANE), f32),
            pltpu.VMEM((pieces, devices, 8, width), f32),
        ],
    )


def position_table():
    places = np.arange(LMAX)
    orders = np.arange(1, (EMB - 1) // 2 + 1)
    turns = 2.0 * math.pi * ((orders[:, None] * places[None, :]) % LMAX) / LMAX
    ramp = places[None, :] / (LMAX - 1)
    return np.concatenate([ramp, np.cos(turns), -np.sin(turns)], axis=0).astype(np.float32)


FEAT = position_table()


def mm(a, b, dims):
    return lax.dot_general(a, b, (dims, ((), ())), precision=highest, preferred_element_type=f32)


NN = ((1,), (0,))
TN = ((0,), (0,))
NT = ((1,), (1,))


def filter_back_body(d_ref, raw_ref, fall_ref, h1_ref, h2_ref, c1_ref, c2_ref, pre1_ref, pre2_ref, feat_ref, mid_ref, last_ref, rate_ref,
                     g_in_ref, g_mid_ref, g_last_ref, g_rows_ref, g_decay_ref):
    chans = d_ref.shape[0]
    d = d_ref[...]
    q = d * (fall_ref[...] + decay_floor)
    g_last_ref[...] = mm(h2_ref[...], q, NT)
    decay = folded(d * raw_ref[...] * fall_ref[...] * feat_ref[0:1, :])
    g_decay_ref[...] = -jnp.sum(decay, axis=1, keepdims=True)
    u2 = mm(last_ref[...], q, NN) * c2_ref[...]
    rate = rate_ref[...]
    fu2 = rate * u2
    u1 = mm(mid_ref[...], fu2, NN) * c1_ref[...]
    fu1 = rate * u1
    g_in_ref[...] = mm(feat_ref[...], fu1, NT)
    g_mid_ref[...] = mm(h1_ref[...], fu2, NT)
    rows = jnp.concatenate([folded(fu1), folded(fu2), folded(u2 * pre2_ref[...] + u1 * pre1_ref[...])], axis=0)
    extra = jnp.zeros((-rows.shape[0] % LANE, LANE), f32)
    g_rows_ref[...] = row_totals(jnp.concatenate([rows, extra], axis=0))


def filter_back(*args):
    chans, ford, taps = args[0].shape[0], args[3].shape[0], args[9].shape[0]
    sd = jax.ShapeDtypeStruct
    out = (sd((taps, ford), f32), sd((ford, ford), f32), sd((ford, chans), f32), sd((8, -(-3 * ford // LANE) * LANE), f32), sd((chans, 1), f32))
    return whole_call(0.01, filter_back_body, out, [], *args)


def mm16(a, b, dims):
    return lax.dot_general(a, b, (dims, ((), ())), preferred_element_type=f32)


def ring_of(chips):
    zs = 4
    ys = chips // zs
    order = [(z, 0) for z in range(zs)]
    for y in range(1, ys):
        order += [(z, y) for z in (range(zs - 1, 0, -1) if y % 2 else range(1, zs))]
    order += [(0, y) for y in range(ys - 1, 0, -1)]
    return [z * ys + y for z, y in order]


def after(values, *others):
    return lax.optimization_barrier((values,) + others)[0]


def ring_hop(values, ring, by):
    chips = len(ring)
    moves = [(2 * ring[p] + q, 2 * ring[(p + by) % chips] + q) for p in range(chips) for q in range(2)]
    return lax.ppermute(values, "chan", moves)


class RingGather:
    def __init__(self, shard, ring):
        self.ring, self.hops = ring, len(ring) // 2
        self.cut = shard.shape[0] // 32 * 16
        self.behind, self.ahead = [shard], [shard]
        self.far = None

    def advance(self, upto, *others):
        while len(self.behind) <= min(upto, self.hops - 1):
            first, second = self.behind[-1], self.ahead[-1]
            if others:
                first, second = after(first, *others), after(second, *others)
            self.behind.append(ring_hop(first, self.ring, 1))
            self.ahead.append(ring_hop(second, self.ring, -1))
        if upto == self.hops:
            first, second = self.behind[-1][: self.cut], self.ahead[-1][self.cut :]
            if others:
                first, second = after(first, *others), after(second, *others)
            self.far = jnp.concatenate([ring_hop(first, self.ring, 1), ring_hop(second, self.ring, -1)], axis=0)

    def shards(self):
        return self.behind + self.ahead[1:] + [self.far]


def both_cores(shards):
    own = stack(shards)
    return own, lax.ppermute(own, "chan", [(i, i ^ 1) for i in range(2 * len(shards))])


def stack_body(*refs):
    for i, ref in enumerate(refs[:-1]):
        refs[-1][i] = ref[...]


def stack(shards):
    out = jax.ShapeDtypeStruct((len(shards),) + shards[0].shape, shards[0].dtype)
    return whole_call(0.01, stack_body, out, [], *shards)


def turn_table(ring):
    chips = len(ring)
    steps = [0] + [-k for k in range(1, chips // 2)] + [k for k in range(1, chips // 2)] + [chips // 2]
    table = np.zeros((chips, chips), np.int32)
    for p, chip in enumerate(ring):
        table[chip] = [ring[(p + k) % chips] for k in steps]
    return table


def exchange(values):
    return lax.all_to_all(values, "chan", split_axis=0, concat_axis=0, tiled=True)


def on_device(
    layer_in,
    seq_lengths,
    ln1_gain,
    first_norm_bias,
    in_weight,
    in_bias,
    short_weight,
    short_bias,
    filt_in,
    filt_in_bias,
    filt_mid,
    filt_mid_bias,
    sine_freq,
    filt_out,
    decay_rate,
    conv_bias,
    out_weight,
    out_bias,
    ln2_gain,
    second_norm_bias,
    up_weight,
    up_bias,
    down_weight,
    down_bias,
    cotangent,
):
    seqs, chans, _ = layer_in.shape
    devices = lax.axis_size("chan")
    groups = lax.axis_size("batch")
    width = LMAX // devices
    dim = chans * devices
    cols = seqs * width
    hid = up_weight.shape[0]
    ford = filt_mid.shape[0]
    place = lax.axis_index("chan")

    def to_blocks(values):
        return (
            values.reshape(seqs, chans, devices, width)
            .transpose(2, 0, 1, 3)
            .reshape(devices, seqs * chans, width)
        )

    def from_blocks(blocks):
        return (
            blocks.reshape(devices, seqs, chans, width)
            .transpose(1, 2, 0, 3)
            .reshape(seqs, chans, LMAX)
        )

    small = jnp.concatenate(
        [
            in_bias,
            short_bias,
            short_weight.reshape(3 * KS, chans),
            jnp.stack([ln1_gain, first_norm_bias, ln2_gain, second_norm_bias, out_bias, down_bias]),
            up_bias.reshape(hid // chans, chans),
        ],
        axis=0,
    )
    small = jnp.pad(small, ((0, PRM - small.shape[0]), (0, dim - chans)))
    in_rows = in_weight.transpose(1, 2, 0).reshape(3 * chans, dim)
    ring = ring_of(devices // 2)
    chips = devices // 2
    core = place % 2
    batch = lax.axis_index("batch")
    swap = [(0, 1), (1, 0)]
    partner = [(i, i ^ 1) for i in range(devices)]
    turns = lax.dynamic_index_in_dim(jnp.asarray(turn_table(ring)), place // 2, 0, False)
    table = jnp.concatenate(
        [turns, jnp.stack([core, place]).astype(jnp.int32), seq_lengths, batch.astype(jnp.int32).reshape(1)]
    )
    first = RingGather(jnp.concatenate([small, in_rows], axis=0), ring)
    first.advance(chips // 8)
    x = exchange(to_blocks(layer_in))
    rows = seqs * chans
    xh = lax.ppermute(x[:, :rows, width - LANE :], "chan", [(i, i + 1) for i in range(devices - 1)])

    feat = jnp.asarray(FEAT)
    ramp = feat[0:1]
    rate = sine_freq[:, None]
    pre1 = mm(filt_in, feat, TN) + filt_in_bias[:, None]
    h1, c1 = jnp.sin(rate * pre1), jnp.cos(rate * pre1)
    pre2 = mm(filt_mid, h1, TN) + filt_mid_bias[:, None]
    h2, c2 = jnp.sin(rate * pre2), jnp.cos(rate * pre2)
    raw = mm(filt_out, h2, TN)
    falling = jnp.exp(-ramp * decay_rate[:, None])
    first.advance(chips // 4, h1)
    filt = raw * (falling + decay_floor)
    first.advance(3 * chips // 8, filt, x)
    filt_spec = filter_spectrum(filt)
    first.advance(chips // 2, filt_spec)
    in_own, in_other = both_cores(first.shards())
    bias_col = conv_bias[:, None]

    late = jnp.concatenate([up_weight, down_weight, out_weight], axis=0)
    stepped = groups == 2 and chips == 8 and dim % (2 * LANE) == 0
    beside = [(i, i ^ 2) for i in range(devices)]
    along = [list(range(k, devices, 4)) for k in range(4)]

    def to_partner(values):
        return lax.ppermute(values, "chan", partner)

    if stepped:
        part = dim // 2
        late = lax.dynamic_slice_in_dim(late, batch * part, part, 1)
        near = lax.all_gather(late, "chan", axis=0, axis_index_groups=along)
    else:
        late = lax.all_gather(late, "chan", axis=0).reshape((chips, 2) + late.shape)
    prm, xn1, stat1, gate, pair, projx0, projx, mixed, heads = front(
        table, x, xh, in_own, in_other, filt_spec, seqs
    )
    mixed_chan = exchange(mixed)
    cot = exchange(after(to_blocks(cotangent), mixed_chan))
    if stepped:
        near = after(near, mixed)
        far = lax.ppermute(near, "chan", beside)
        near_across = lax.ppermute(near, "batch", swap)
        near_other = to_partner(near)
    backward_hop = [(i + 1, i) for i in range(devices - 1)]
    heads = lax.ppermute(heads, "chan", backward_hop)
    conv_chan, mixed_spec = conv_forward(mixed_chan, filt_spec, bias_col, seqs)
    conv = exchange(after(conv_chan, near_across, cot) if stepped else conv_chan)
    if stepped:
        far, near_across = after(far, conv_chan), after(near_across, conv_chan)
        far_across = lax.ppermute(far, "batch", swap)
        far_other, near_across_other = to_partner(far), to_partner(near_across)
        far_across_other = to_partner(far_across)
        matrices = [
            [[near, far], [near_other, far_other]],
            [[near_across, far_across], [near_across_other, far_across_other]],
        ]
        z = lax.iota(jnp.int32, 4) * 2
        y = (place // 2 % 2).astype(jnp.int32)
        order = jnp.concatenate([z + y, z + 1 - y])
    else:
        matrices = [[[lax.dynamic_index_in_dim(late, core, 1, False)], [lax.dynamic_index_in_dim(late, 1 - core, 1, False)]]]
        order = lax.iota(jnp.int32, chips)
    order = jnp.concatenate([order, table[chips:]])

    results = middle(order, conv, x, cot, gate.reshape(dim, cols), matrices, prm, hid, seqs)
    layer, d_conv, d_res, p0, p0h = results[:5]
    d_conv_chan = exchange(d_conv)
    p0h = lax.ppermute(p0h, "chan", backward_hop)

    def added(*values):
        return sum(v.astype(f32) for v in values).astype(bf16)

    if stepped:
        mine, mine_in = results[5], to_partner(results[6])
        theirs, theirs_in = results[7], to_partner(results[8])
        half = chips // 2
        far_theirs = added(theirs[half:], theirs_in[half:])
        near_theirs = added(theirs[:half], theirs_in[:half])
        d_conv_chan = after(d_conv_chan, far_theirs, near_theirs)
        far_theirs = lax.ppermute(far_theirs, "batch", swap)
        near_theirs = lax.ppermute(after(near_theirs, far_theirs), "batch", swap)
    else:
        early = added(results[5], to_partner(results[6]))

    if groups == 2:
        same_core = [list(range(q, devices, 2)) for q in range(2)]
    else:
        same_core = [[b * devices + c for b in range(groups) for c in range(q, devices, 2)] for q in range(2)]

    def batch_total(values):
        return values + lax.ppermute(values, "batch", swap) if groups == 2 else lax.psum(values, "batch")

    def over_batch(table):
        if groups != 2:
            return lax.psum_scatter(table.astype(f32), "batch", scatter_dimension=1, tiled=True)
        part = dim // 2
        axis = table.ndim - 1
        mine = lax.axis_index("batch") * part
        theirs = lax.dynamic_slice_in_dim(table, part - mine, part, axis)
        kept = lax.dynamic_slice_in_dim(table, mine, part, axis)
        return kept.astype(f32) + lax.ppermute(theirs, "batch", swap).astype(f32)

    def over_chip(table):
        table = table.reshape((devices // 2, 2) + table.shape[1:])
        own = lax.dynamic_index_in_dim(table, core, 1, False)
        theirs = lax.dynamic_index_in_dim(table, 1 - core, 1, False)
        return (own.astype(f32) + lax.ppermute(theirs, "chan", partner).astype(f32)).astype(bf16)

    def over_groups(both):
        return over_batch(both).astype(bf16) if groups == 2 else both

    def over_chips(both):
        rows = both.shape[1]
        if groups == 2:
            both = lax.all_to_all(
                both, "chan", split_axis=0, concat_axis=0, tiled=True, axis_index_groups=same_core
            )
        else:
            both = both.reshape(devices // 2, rows, groups, dim // groups).transpose(2, 0, 1, 3)
            both = lax.all_to_all(
                both.reshape(groups * devices // 2, rows, dim // groups),
                ("batch", "chan"), split_axis=0, concat_axis=0, tiled=True, axis_index_groups=same_core,
            )
        return jnp.sum(both.astype(f32), axis=0)

    d_mixed_chan, d_filter, g_conv_bias = conv_backward(
        d_conv_chan, mixed_chan, mixed_spec, filt_spec, bias_col, seqs
    )
    if stepped:
        d_mixed_chan = after(d_mixed_chan, far_theirs)
        far_mine = added(mine[half:], mine_in[half:], far_theirs)
        p0h = after(p0h, far_mine)
    g_in0, sums0, acc0 = back_gate(
        table, p0.reshape(devices, chans, cols), p0h.reshape(devices, chans, LANE), projx0, in_own, in_other, prm, xn1, seqs
    )
    g_in0 = over_chip(g_in0)
    d_mixed = exchange(d_mixed_chan)
    g_filt_in, g_filt_mid, g_filt_out, g_rows, g_decay = filter_back(
        d_filter, raw, falling, h1, h2, c1, c2, pre1, pre2, feat, filt_mid, filt_out, rate
    )
    shared = [g_filt_in.reshape(-1), g_filt_mid.reshape(-1), g_rows[0, : 3 * ford]]
    total = batch_total(
        jnp.concatenate(shared + [g_conv_bias[:, 0], g_decay[:, 0], g_filt_out.reshape(-1)])
    )
    if stepped:
        d_mixed = after(d_mixed, near_theirs)
        far_mine = lax.ppermute(far_mine, "chan", beside)
    else:
        chan_groups = [list(range(q, devices, 2)) for q in range(2)]
        early = lax.psum_scatter(early, "chan", scatter_dimension=0, tiled=True, axis_index_groups=chan_groups)[0]

    tail, g_in = back(
        table, d_mixed, pair, heads, projx, in_own, in_other, prm, xn1, x, stat1, d_res, acc0, sums0, layer, seqs
    )
    if stepped:
        tail = after(tail, far_mine)
        early = added(mine[:half], mine_in[:half], near_theirs, far_mine)
        g_in = after(g_in, early)
    tail = exchange(tail)
    g_in = over_groups(jnp.concatenate([g_in0, over_chip(g_in)], axis=1))
    if stepped:
        early = lax.psum_scatter(early, "chan", scatter_dimension=0, tiled=True, axis_index_groups=along)[0]

    cut = [0]

    def take(*shape):
        n = math.prod(shape)
        part = total[cut[0] : cut[0] + n].reshape(shape)
        cut[0] += n
        return part

    shared = take(sum(v.shape[0] for v in shared))
    shared = shared + lax.ppermute(shared, "chan", partner)
    g_conv_b, g_decay_rate, g_filt_last = take(chans), take(chans), take(ford, chans)
    n_shared = shared.shape[0]
    if groups != 2:
        shared = shared / groups
    line = g_in.shape[2]
    shared = jnp.pad(shared.astype(bf16), (0, -n_shared % (16 * line))).reshape(1, -1, line)
    shared = jnp.broadcast_to(shared, (devices // 2,) + shared.shape[1:])
    mine = 3 * chans
    in_grad = over_chips(jnp.concatenate([g_in, shared], axis=1))
    if groups == 2:
        total = in_grad[mine:].reshape(-1)
    else:
        total = lax.all_gather(in_grad[mine:], "batch", axis=1, tiled=True).reshape(-1)
    in_grad = in_grad[:mine]
    cut[0] = 0
    g_filt_in, g_filt_mid = take(EMB, ford), take(ford, ford)
    g_filt_in_bias, g_filt_mid_bias, g_sine = take(ford), take(ford), take(ford)

    early = after(early, in_grad)
    early = early.astype(f32) if stepped else over_batch(early)
    up_grad, down_grad, out_grad = early[:hid], early[hid : 2 * hid], early[2 * hid :]

    grad_blocks, out_blocks = tail[:, :rows], tail[:, rows + SUM_ROWS : 2 * rows + SUM_ROWS]
    sums = jnp.concatenate([tail[:, 2 * rows + SUM_ROWS :], tail[:, rows : rows + SUM_ROWS]], axis=1)
    sums = batch_total(jnp.sum(sums.astype(f32), axis=0))
    sums = sums[0::2] + sums[1::2]
    g_gain2, g_shift2, g_out_b, g_down_b = (sums[i, :chans] for i in range(4))
    g_up_b = sums[4, :hid]
    at = SUM_ROWS // 2
    count = (2 + KS) * chans
    pieces = -(-2 * count // width)
    short0 = sums[at, :count].reshape(2 + KS, 1, chans)
    short = sums[at + 1 : at + 1 + pieces].reshape(-1)[: 2 * count].reshape(2 + KS, 2, chans)
    short = jnp.concatenate([short0, short], axis=1)
    g_in_bias, g_short_bias, g_short_weight = short[0], short[1], short[2:]
    g_gain1, g_shift1 = (sums[at + 1 + pieces + i, :chans] for i in range(2))

    return (
        from_blocks(out_blocks),
        from_blocks(grad_blocks).astype(f32),
        g_gain1,
        g_shift1,
        in_grad.reshape(3, chans, dim // groups).transpose(2, 0, 1),
        g_in_bias,
        g_short_weight,
        g_short_bias,
        g_filt_in,
        g_filt_in_bias,
        g_filt_mid,
        g_filt_mid_bias,
        g_sine,
        g_filt_last,
        g_decay_rate,
        g_conv_b,
        out_grad,
        g_out_b,
        g_gain2,
        g_shift2,
        up_grad,
        g_up_b,
        down_grad,
        g_down_b,
    )


def solution(mesh):
    token = P("batch", "chan", None)
    chan = P("chan")
    rows = P("chan", None)
    two = P(None, "chan")
    three = P(None, None, "chan")
    in_specs = (
        token, P("batch"), chan, chan, three, two, three, two, P(), P(), P(), P(), P(), two, chan, chan,
        rows, chan, chan, chan, rows, chan, rows, chan, token,
    )
    table = P("chan", "batch")
    out_specs = (
        token, token, chan, chan, P("batch", None, "chan"), two, three, two, P(), P(), P(), P(), P(), two,
        chan, chan, table, chan, chan, chan, table, chan, table, chan,
    )
    return jax.shard_map(
        on_device, mesh=mesh, in_specs=in_specs, out_specs=out_specs, check_vma=False
    )
```

```python
import math

import jax
import jax.numpy as jnp
import numpy as np
from jax import lax
from jax.experimental import pallas as pl
from jax.experimental.pallas import tpu as pltpu
from jax.sharding import PartitionSpec as P

EMB = 33
KS = 3
LMAX = 4096
LANE = 128
COARSE = LMAX // LANE
REPS = tuple(ka + 8 * kb for ka, count in ((0, 5), (1, 8), (2, 8), (3, 8), (4, 4)) for kb in range(count))
PLACE = {k1: i for i, k1 in enumerate(REPS)}
epsilon = 1e-05
decay_floor = 0.05
highest = lax.Precision.HIGHEST
f32 = jnp.float32
bf16 = jnp.bfloat16
vmem_limit = 56 * 1024 * 1024
HEAD_ROWS = 16
SUM_ROWS = 16
BATCH = 3
PRM = 32


def unit(turns):
    angle = 2.0 * math.pi * turns
    return math.cos(angle), math.sin(angle)


def scaled(z, c, s):
    re, im = z
    if im is None:
        return re * c, re * s
    return re * c - im * s, re * s + im * c


def plus(a, b):
    return a[0] + b[0], a[1] + b[1]


def minus(a, b):
    return a[0] - b[0], a[1] - b[1]


def dft4(z, sign):
    s0, d0 = plus(z[0], z[2]), minus(z[0], z[2])
    s1, d1 = plus(z[1], z[3]), minus(z[1], z[3])
    turned = (-d1[1], d1[0]) if sign > 0 else (d1[1], -d1[0])
    return [plus(s0, s1), plus(d0, turned), minus(s0, s1), minus(d0, turned)]


def dft8(z, sign):
    even, odd = dft4(z[0::2], sign), dft4(z[1::2], sign)
    c = math.sqrt(0.5)
    o1 = odd[1]
    o3 = odd[3]
    if sign > 0:
        odd1 = ((o1[0] - o1[1]) * c, (o1[0] + o1[1]) * c)
        odd2 = (-odd[2][1], odd[2][0])
        odd3 = ((-o3[0] - o3[1]) * c, (o3[0] - o3[1]) * c)
    else:
        odd1 = ((o1[0] + o1[1]) * c, (o1[1] - o1[0]) * c)
        odd2 = (odd[2][1], -odd[2][0])
        odd3 = ((o3[1] - o3[0]) * c, (-o3[0] - o3[1]) * c)
    turned = [odd[0], odd1, odd2, odd3]
    return [plus(even[i], turned[i]) for i in range(4)] + [minus(even[i], turned[i]) for i in range(4)]


def coarse_forward(xs, put):
    c = math.sqrt(0.5)
    cols = {ka: [None] * 8 for ka in range(5)}
    for b in range(8):
        x0, x1, x2, x3 = xs[b], xs[8 + b], xs[16 + b], xs[24 + b]
        s02, d02, s13, d13 = x0 + x2, x0 - x2, x1 + x3, x1 - x3
        d13c, s13c = d13 * c, s13 * c
        cols[0][b] = s02 + s13
        cols[4][b] = scaled((s02 - s13, None), *unit(-4 * b / 64))
        cols[2][b] = scaled((d02, -d13), *unit(-2 * b / 64))
        cols[1][b] = scaled((x0 + d13c, -s13c - x2), *unit(-b / 64))
        cols[3][b] = scaled((x0 - d13c, x2 - s13c), *unit(-3 * b / 64))
    for ka in (1, 2, 3):
        for kb, z in enumerate(dft8(cols[ka], -1)):
            put(ka + 8 * kb, z)
    for kb, z in enumerate(dft8(cols[4], -1)[:4]):
        put(4 + 8 * kb, z)
    r = cols[0]
    s04, d04, s26, d26 = r[0] + r[4], r[0] - r[4], r[2] + r[6], r[2] - r[6]
    s15, d15, s37, d37 = r[1] + r[5], r[1] - r[5], r[3] + r[7], r[3] - r[7]
    p, q = (d15 - d37) * c, (d15 + d37) * c
    even, odd = s04 + s26, s15 + s37
    put(0, (even + odd, None))
    put(32, (even - odd, None))
    put(16, (s04 - s26, s37 - s15))
    put(8, (d04 + p, -d26 - q))
    put(24, (d04 - p, d26 - q))


def coarse_inverse(get):
    c = math.sqrt(0.5)
    u = {}
    for ka in (1, 2, 3):
        back = dft8([get(ka + 8 * kb) for kb in range(8)], 1)
        u[ka] = [scaled(back[b], *unit(b * ka / 64)) for b in range(8)]
    v0, v32 = get(0)[0], get(32)[0]
    v8, v16, v24 = get(8), get(16), get(24)
    flat = []
    for b in range(8):
        total = v0 + v32 if b % 2 == 0 else v0 - v32
        for kb, v in ((1, v8), (2, v16), (3, v24)):
            co, si = unit(b * kb / 8)
            if abs(co) > 1e-9:
                total = total + v[0] * (2.0 * co)
            if abs(si) > 1e-9:
                total = total - v[1] * (2.0 * si)
        flat.append(total)
    odd = [get(4 + 8 * kb) for kb in range(4)]
    odd = odd + [(z[0], -z[1]) for z in odd[::-1]]
    half = dft8(odd, 1)
    quarter = []
    for b in range(8):
        co, si = unit(4 * b / 64)
        quarter.append(half[b][0] * co - half[b][1] * si)
    out = [None] * COARSE
    for b in range(8):
        u1, u2, u3 = u[1][b], u[2][b], u[3][b]
        s, d = flat[b] + quarter[b], flat[b] - quarter[b]
        dr, sr = (u1[0] - u3[0]) * c, u1[0] + u3[0]
        si_, di = (u1[1] + u3[1]) * c, u1[1] - u3[1]
        out[b] = s + 2.0 * (sr + u2[0])
        out[16 + b] = s - 2.0 * (di + u2[0])
        out[8 + b] = d + 2.0 * (dr - si_ - u2[1])
        out[24 + b] = d + 2.0 * (u2[1] - dr - si_)
    return out


def transform_tables():
    fine = np.arange(LANE)
    angle = 2.0 * math.pi * ((fine[:, None] * fine[None, :]) % LANE) / LANE
    co, si = np.cos(angle), np.sin(angle)
    ahead = np.block([[co, -si], [si, co]])
    back = ahead.T / (2.0 * LMAX)
    reps = np.array(REPS)
    turn = 2.0 * math.pi * ((reps[:, None] * fine[None, :]) % (2 * LMAX)) / (2 * LMAX)
    twist = np.concatenate([np.cos(turn), -np.sin(turn)], axis=1)[:, None, :]

    def pieces(table):
        table = table.astype(np.float32)
        upper = table.astype(jnp.bfloat16)
        lower = (table - upper.astype(np.float32)).astype(jnp.bfloat16)
        return np.stack([upper, lower])

    return pieces(ahead), pieces(back), twist.astype(np.float32)


AHEAD, BACK, TWIST = transform_tables()


def three_pass(values, table_ref):
    upper = values.astype(bf16)
    lower = (values - upper.astype(f32)).astype(bf16)
    t0, t1 = table_ref[0], table_ref[1]
    return (
        jnp.dot(upper, t0, preferred_element_type=f32)
        + jnp.dot(lower, t0, preferred_element_type=f32)
        + jnp.dot(upper, t1, preferred_element_type=f32)
    )


def rows_forward(xs_ref, spec_ref, rows):
    def step(g, carry):
        at = pl.ds(pl.multiple_of(g * 8, 8), 8)
        xs = [xs_ref[n, at, :] for n in range(COARSE)]

        def put(k1, z):
            i = PLACE[k1]
            spec_ref[i, at, 0:LANE] = z[0]
            spec_ref[i, at, LANE : 2 * LANE] = jnp.zeros_like(z[0]) if z[1] is None else z[1]

        coarse_forward(xs, put)
        return carry

    lax.fori_loop(0, rows // 8, step, 0)


def rows_inverse(spec_ref, ys_ref, rows):
    def step(g, carry):
        at = pl.ds(pl.multiple_of(g * 8, 8), 8)

        def get(k1):
            i = PLACE[k1]
            return spec_ref[i, at, 0:LANE], spec_ref[i, at, LANE : 2 * LANE]

        for n, y in enumerate(coarse_inverse(get)):
            ys_ref[n, at, :] = y
        return carry

    lax.fori_loop(0, rows // 8, step, 0)


def fine_forward(spec, twist, ahead_ref):
    re, im = spec[:, :LANE], spec[:, LANE:]
    tr, ti = twist[:, :LANE], twist[:, LANE:]
    return three_pass(jnp.concatenate([re * tr - im * ti, re * ti + im * tr], axis=1), ahead_ref)


def fine_inverse(spec, twist, back_ref):
    v = three_pass(spec, back_ref)
    re, im = v[:, :LANE], v[:, LANE:]
    tr, ti = twist[:, :LANE], twist[:, LANE:]
    return jnp.concatenate([re * tr + im * ti, im * tr - re * ti], axis=1)


def times(a, b):
    ar, ai, br, bi = a[:, :LANE], a[:, LANE:], b[:, :LANE], b[:, LANE:]
    return jnp.concatenate([ar * br - ai * bi, ar * bi + ai * br], axis=1)


def times_conj(a, b):
    ar, ai, br, bi = a[:, :LANE], a[:, LANE:], b[:, :LANE], b[:, LANE:]
    return jnp.concatenate([ar * br + ai * bi, ai * br - ar * bi], axis=1)


def together(values):
    return values.reshape(values.shape[0] * values.shape[1], values.shape[2])


def apart(values):
    return values.reshape(BATCH, values.shape[0] // BATCH, values.shape[1])


def twists(twist_ref, at, rows):
    return together(jnp.broadcast_to(twist_ref[at], (BATCH, rows, 2 * LANE)))


def spread(blocks_ref, xs_ref):
    per = blocks_ref.shape[2] // LANE
    for n in range(COARSE):
        r = n % per
        xs_ref[n] = blocks_ref[n // per, :, r * LANE : (r + 1) * LANE].astype(f32)


def filter_spectrum_body(filter_ref, twist_ref, ahead_ref, out_ref, xs_ref):
    rows = filter_ref.shape[0]
    for n in range(COARSE):
        xs_ref[n] = filter_ref[:, n * LANE : (n + 1) * LANE]
    rows_forward(xs_ref, out_ref, rows)

    def step(i, carry):
        at = pl.ds(i * BATCH, BATCH)
        out_ref[at] = apart(fine_forward(together(out_ref[at]), twists(twist_ref, at, rows), ahead_ref))
        return carry

    lax.fori_loop(0, len(REPS) // BATCH, step, 0)


def conv_forward_body(seqs, mixed_ref, filt_ref, bias_ref, twist_ref, ahead_ref, back_ref, out_ref, spec_ref, xs_ref, work_ref):
    rows = mixed_ref.shape[1]
    spread(mixed_ref, xs_ref)
    rows_forward(xs_ref, spec_ref, rows)

    def step(i, carry):
        at = pl.ds(i * BATCH, BATCH)
        twist = twists(twist_ref, at, rows)
        z = fine_forward(together(spec_ref[at]), twist, ahead_ref)
        spec_ref[at] = apart(z)
        k = together(jnp.concatenate([filt_ref[at]] * seqs, axis=1))
        work_ref[at] = apart(fine_inverse(times(z, k), twist, back_ref))
        return carry

    lax.fori_loop(0, len(REPS) // BATCH, step, 0)
    ys_ref = xs_ref
    rows_inverse(work_ref, ys_ref, rows)
    per = mixed_ref.shape[2] // LANE
    bias = jnp.concatenate([bias_ref[...]] * seqs, axis=0)
    for n in range(COARSE):
        at = (n // per, slice(None), slice((n % per) * LANE, (n % per + 1) * LANE))
        out_ref[at] = (ys_ref[n] + bias * mixed_ref[at].astype(f32)).astype(bf16)


def heads_out(out_ref, block, y):
    rows, width = y.shape[0], out_ref.shape[2]
    square = jnp.concatenate([y, jnp.zeros((LANE - rows, LANE), f32)], axis=0) if rows < LANE else y
    head = square.T[:HEAD_ROWS]
    if width > LANE:
        head = jnp.concatenate([head, jnp.zeros((HEAD_ROWS, width - LANE), f32)], axis=1)
    out_ref[block, rows:, :] = head.astype(bf16)


def conv_backward_body(
    seqs, d_ref, mixed_ref, mixed_spec_ref, filt_ref, bias_ref, twist_ref, ahead_ref, back_ref, out_ref, dfilt_ref, dbias_ref, xs_ref, spec_ref, work_ref, ys_ref
):
    rows = d_ref.shape[1]
    chans = rows // seqs
    spread(d_ref, xs_ref)
    rows_forward(xs_ref, spec_ref, rows)

    def step(i, carry):
        at = pl.ds(i * BATCH, BATCH)
        z = fine_forward(together(spec_ref[at]), twists(twist_ref, at, rows), ahead_ref)
        k = together(jnp.concatenate([filt_ref[at]] * seqs, axis=1))
        cross = apart(times_conj(z, together(mixed_spec_ref[at])))
        cross = sum(cross[:, s * chans : (s + 1) * chans] for s in range(seqs))
        both = together(jnp.concatenate([apart(times_conj(z, k)), cross], axis=1))
        work_ref[at] = apart(fine_inverse(both, twists(twist_ref, at, rows + chans), back_ref))
        return carry

    lax.fori_loop(0, len(REPS) // BATCH, step, 0)
    rows_inverse(work_ref, ys_ref, rows + chans)
    per = d_ref.shape[2] // LANE
    bias = jnp.concatenate([bias_ref[...]] * seqs, axis=0)
    total = jnp.zeros((rows, LANE), f32)
    out_ref[out_ref.shape[0] - 1, rows:, :] = jnp.zeros((HEAD_ROWS, d_ref.shape[2]), bf16)
    for n in range(COARSE):
        at = (n // per, slice(0, rows), slice((n % per) * LANE, (n % per + 1) * LANE))
        d = xs_ref[n]
        y = ys_ref[n, :rows, :] + bias * d
        out_ref[at] = y.astype(bf16)
        if n % per == 0 and n > 0:
            heads_out(out_ref, n // per - 1, y)
        total = total + d * mixed_ref[at].astype(f32)
        dfilt_ref[:, n * LANE : (n + 1) * LANE] = ys_ref[n, rows:, :]
    total = sum(total[s * chans : (s + 1) * chans] for s in range(seqs))
    dbias_ref[...] = jnp.sum(total, axis=1, keepdims=True)


def takes(us):
    return pl.CostEstimate(flops=int(us * 1e9), bytes_accessed=int(us * 3e6), transcendentals=0)


def whole_call(us, body, out_shape, scratch, *args):
    return pl.pallas_call(
        body,
        cost_estimate=takes(us),
        out_shape=out_shape,
        in_specs=[pl.BlockSpec(memory_space=pltpu.VMEM)] * len(args),
        out_specs=jax.tree.map(lambda _: pl.BlockSpec(memory_space=pltpu.VMEM), out_shape),
        scratch_shapes=scratch,
        compiler_params=pltpu.CompilerParams(vmem_limit_bytes=vmem_limit),
    )(*args)


def filter_spectrum(filt):
    rows = filt.shape[0]
    return whole_call(
        8,
        filter_spectrum_body,
        jax.ShapeDtypeStruct((len(REPS), rows, 2 * LANE), f32),
        [pltpu.VMEM((COARSE, rows, LANE), f32)],
        filt,
        jnp.asarray(TWIST),
        jnp.asarray(AHEAD),
    )


def conv_forward(mixed, filt_spec, bias, seqs):
    blocks, rows, width = mixed.shape
    n = len(REPS)
    return whole_call(
        100,
        lambda *refs: conv_forward_body(seqs, *refs),
        (jax.ShapeDtypeStruct(mixed.shape, bf16), jax.ShapeDtypeStruct((n, rows, 2 * LANE), f32)),
        [pltpu.VMEM((COARSE, rows, LANE), f32), pltpu.VMEM((n, rows, 2 * LANE), f32)],
        mixed,
        filt_spec,
        bias,
        jnp.asarray(TWIST),
        jnp.asarray(AHEAD),
        jnp.asarray(BACK),
    )


def conv_backward(d_conv, mixed, mixed_spec, filt_spec, bias, seqs):
    blocks, rows, width = mixed.shape
    chans = rows // seqs
    n = len(REPS)
    return whole_call(
        100,
        lambda *refs: conv_backward_body(seqs, *refs),
        (
            jax.ShapeDtypeStruct((blocks, rows + HEAD_ROWS, width), bf16),
            jax.ShapeDtypeStruct((chans, LMAX), f32),
            jax.ShapeDtypeStruct((chans, 1), f32),
        ),
        [
            pltpu.VMEM((COARSE, rows, LANE), f32),
            pltpu.VMEM((n, rows, 2 * LANE), f32),
            pltpu.VMEM((n, rows + chans, 2 * LANE), f32),
            pltpu.VMEM((COARSE, rows + chans, LANE), f32),
        ],
        d_conv,
        mixed,
        mixed_spec,
        filt_spec,
        bias,
        jnp.asarray(TWIST),
        jnp.asarray(AHEAD),
        jnp.asarray(BACK),
    )


CHUNK = 48


def lanes_of(shape):
    return lax.broadcasted_iota(jnp.int32, shape, 1)


def side_by_side(block, seqs):
    chans = block.shape[0] // seqs
    return jnp.concatenate([block[s * chans : (s + 1) * chans] for s in range(seqs)], axis=1)


def stacked(values, seqs):
    width = values.shape[1] // seqs
    return jnp.concatenate([values[:, s * width : (s + 1) * width] for s in range(seqs)], axis=0)


def eights(values):
    return jnp.sum(values.reshape(values.shape[0] // 8, 8, values.shape[1]), axis=0)


def folded(values):
    return sum(values[:, i * LANE : (i + 1) * LANE] for i in range(values.shape[1] // LANE))


def row_totals(values):
    ones = jnp.ones((8, LANE), bf16)
    upper = values.astype(bf16)
    lower = (values - upper.astype(f32)).astype(bf16)
    return mm16(ones, upper, NT) + mm16(ones, lower, NT)


def padded_totals(values, width):
    extra = -values.shape[0] % width
    if extra:
        values = jnp.concatenate([values, jnp.zeros((extra, LANE), f32)], axis=0)
    totals = row_totals(values)
    return [totals[:, i * width : (i + 1) * width] for i in range(totals.shape[1] // width)]


def as_rows(totals, rows):
    halves = []
    for t in totals:
        upper = t.astype(bf16).astype(f32)
        halves += [upper, t - upper]
    place = lax.broadcasted_iota(jnp.int32, halves[0].shape, 0)
    tiles = []
    for first in range(0, rows, 8):
        tile = jnp.zeros_like(halves[0])
        for i, h in enumerate(halves[first : first + 8]):
            tile = jnp.where(place == i, h, tile)
        tiles.append(tile)
    return jnp.concatenate(tiles, axis=0).astype(bf16)


def chunk_rows(i):
    return pl.ds(pl.multiple_of(i * CHUNK, CHUNK), CHUNK)


def norm_stats(ref, dim):
    cols = ref.shape[1]
    zero = jnp.zeros((8, cols), f32)
    total = lax.fori_loop(0, dim // CHUNK, lambda i, t: t + eights(ref[chunk_rows(i), :]), zero)
    mean = jnp.sum(total, axis=0, keepdims=True) / dim

    def spread_sq(i, t):
        v = ref[chunk_rows(i), :] - mean
        return t + eights(v * v)

    var = jnp.sum(lax.fori_loop(0, dim // CHUNK, spread_sq, zero), axis=0, keepdims=True) / dim
    return mean, lax.rsqrt(var + epsilon)


def front_body(
    seqs, table_ref, x_ref, xh_ref, own_ref, other_ref, own_small, other_small, after_ref,
    prm_ref, xn_ref, stat_ref, gate_ref, pair_ref, projx0_ref, projx_ref, mixed_ref, heads_ref, xs, xb,
):
    devices, _, width = x_ref.shape
    dim, cols = xn_ref.shape
    chans = dim // devices
    turns = devices // 2
    step = pl.program_id(0)

    @pl.when(step == 0)
    def _():
        for turn in range(turns):
            for ref, (device, _) in zip((own_small, other_small), slots(table_ref, turns, turn)):
                small = jnp.concatenate([ref[turn].astype(f32), jnp.zeros((LANE - PRM, LANE), f32)], axis=0)
                prm_ref[pl.ds(pl.multiple_of(device * chans, 8), chans), :] = small.T[:chans, :PRM]

        def gather(d, carry):
            at = pl.ds(pl.multiple_of(d * chans, 8), chans)
            row = side_by_side(x_ref[d].astype(f32), seqs)
            tail = xh_ref[d].astype(f32)
            tail = jnp.where(
                lanes_of((chans, LANE)) < LANE // 2, pltpu.roll(tail[chans : 2 * chans], LANE // 2, 1), tail[:chans]
            )
            xs[at, :] = jnp.concatenate([row, tail], axis=1)
            return carry

        lax.fori_loop(0, devices, gather, 0)
        mean, inverse = norm_stats(xs, dim)

        def scale(i, carry):
            at = chunk_rows(i)
            prm = prm_ref[at, :]
            v = (xs[at, :] - mean) * inverse * prm[:, 15:16] + prm[:, 16:17]
            xb[at, :] = v.astype(bf16)
            xn_ref[at, :] = v[:, :cols].astype(bf16)
            return carry

        lax.fori_loop(0, dim // CHUNK, scale, 0)
        stat_ref[0:8, :] = jnp.broadcast_to(mean[:, :cols], (8, cols))
        stat_ref[8:16, :] = jnp.broadcast_to(inverse[:, :cols], (8, cols))

    keep = (table_ref[turns + 1] > 0).astype(f32)
    for w_ref, (device, g) in zip((own_ref, other_ref), slots(table_ref, turns, step)):
        prm = prm_ref[pl.ds(pl.multiple_of(device * chans, 8), chans), :]
        proj = mm16(w_ref[0, PRM:, :], xb[...], NN)
        ys = []
        px = []
        for i in range(3):
            x = proj[i * chans : (i + 1) * chans] + prm[:, i : i + 1]
            tail = x[:, cols:] * keep
            px += [jnp.concatenate([x[:, :cols], tail], axis=1)]
            weights = [jnp.broadcast_to(prm[:, 6 + 3 * j + i : 7 + 3 * j + i], (chans, width)) for j in range(KS)]
            bias = jnp.broadcast_to(prm[:, 3 + i : 4 + i], (chans, width))
            parts = []
            for s in range(seqs):
                v = x[:, s * width : (s + 1) * width]
                wide = jnp.concatenate([tail if s == 0 else pltpu.roll(tail, LANE // 2, 1), v], axis=1)
                y = bias + weights[0] * v
                for j in range(1, KS):
                    y = y + weights[j] * pltpu.roll(wide, j, 1)[:, LANE:]
                parts.append(y)
            ys.append(jnp.concatenate(parts, axis=1))
        projx0_ref[g] = px[0].astype(bf16)
        projx_ref[g] = jnp.concatenate(px[1:], axis=0).astype(bf16)
        gate_ref[g] = ys[0]
        pair = jnp.concatenate(ys[1:], axis=0)
        pair_ref[g] = pair
        mixed_ref[g] = stacked(ys[1] * ys[2], seqs).astype(bf16)
        heads_ref[g] = first_tokens(pair, seqs).astype(bf16)


def first_tokens(values, seqs):
    rows, width = values.shape[0], values.shape[1] // seqs
    pad = jnp.zeros((LANE - rows, LANE), f32)
    heads = []
    for s in range(seqs):
        tile = values[:, s * width : s * width + LANE]
        heads.append((jnp.concatenate([tile, pad], axis=0) if rows < LANE else tile).T[:8])
    return jnp.concatenate(heads, axis=0)


def token_columns(heads, rows):
    gap = jnp.zeros((LANE // 2 - 8, LANE), f32)
    return jnp.concatenate([heads[:8], gap, heads[8:], gap], axis=0).T[:rows]


def whole(a):
    return pl.BlockSpec(a.shape, lambda i, t: (0,) * len(a.shape), pipeline_mode=pl.Buffered(1))


def untouched():
    return pl.BlockSpec(memory_space=pl.ANY)


def by_chip(a):
    return pl.BlockSpec((2,) + a.shape[1:], lambda i, t: (t[i],) + (0,) * (len(a.shape) - 1))


def by_turn(a, rows=None):
    return pl.BlockSpec((1, a.shape[1] if rows is None else rows, a.shape[2]), lambda i, t: (i, 0, 0))


def chip_call(us, body, table, turns, args, in_specs, out, out_specs, scratch):
    return pl.pallas_call(
        body,
        cost_estimate=takes(us),
        out_shape=out,
        grid_spec=pltpu.PrefetchScalarGridSpec(
            num_scalar_prefetch=1,
            grid=(turns,),
            in_specs=in_specs,
            out_specs=out_specs,
            scratch_shapes=scratch,
        ),
        compiler_params=pltpu.CompilerParams(vmem_limit_bytes=vmem_limit, dimension_semantics=("arbitrary",)),
    )(table, *args)


def slots(table_ref, turns, step):
    core = table_ref[turns]
    chip = table_ref[step]
    return ((2 * chip + core, core), (2 * chip + 1 - core, 1 - core))


def front(table, x, xh, own, other, before, seqs):
    devices, rows, width = x.shape
    chans = rows // seqs
    dim = devices * chans
    cols = seqs * width
    turns = devices // 2
    sd = jax.ShapeDtypeStruct
    out = (
        sd((dim, PRM), f32),
        sd((dim, cols), bf16),
        sd((16, cols), f32),
        sd((devices, chans, cols), f32),
        sd((devices, 2 * chans, cols), f32),
        sd((devices, chans, cols + LANE), bf16),
        sd((devices, 2 * chans, cols + LANE), bf16),
        sd((devices, rows, width), bf16),
        sd((devices, 8 * seqs, LANE), bf16),
    )
    small = pl.BlockSpec((turns, PRM, LANE), lambda i, t: (0, 0, 0), pipeline_mode=pl.Buffered(1))
    return chip_call(
        100,
        lambda *refs: front_body(seqs, *refs),
        table,
        turns,
        (x, xh, own, other, own, other, before),
        [whole(x), whole(xh), by_turn(own), by_turn(other), small, small, untouched()],
        out,
        tuple(whole(o) for o in out[:3]) + tuple(by_chip(o) for o in out[3:]),
        [pltpu.VMEM((dim, cols + LANE), f32), pltpu.VMEM((dim, cols + LANE), bf16)],
    )


def middle_body(seqs, pieces, segments, table_ref, conv_ref, x_ref, cot_ref, gate_ref, prm_ref, *refs):
    weights = []
    for _ in range(pieces):
        weights.append([[refs[2 * (segments * core + n) : 2 * (segments * core + n) + 2] for n in range(segments)] for core in range(2)])
        refs = refs[4 * segments :]
    layer_ref, d_conv_ref, d_res_ref, p0_ref, p0h_ref = refs[:5]
    grads, refs = [refs[5 + 2 * p : 7 + 2 * p] for p in range(pieces)], refs[5 + 2 * pieces :]
    cs, res, ds, xb, db, gb, acc_out, acc_in, folds, up_folds, stats, out_w32, out_w_ref, gs = refs
    devices, _, width = x_ref.shape
    dim, cols = d_res_ref.shape
    chans = dim // devices
    hid = weights[0][0][0][0].shape[1] // 2 * pieces
    turns = devices // 2
    part, some_hid, some_out = dim // pieces, hid // pieces, chans // pieces
    group = table_ref[turns + 2 + seqs] if pieces == 2 else 0
    halves = [group, 1 - group][:pieces]
    columns = [pl.ds(pl.multiple_of(h * part, LANE), part) for h in halves]
    step = pl.program_id(0)
    last = pl.num_programs(0) - 1
    lane = lanes_of((1, cols))
    live = jnp.zeros((1, cols), f32)
    for s in range(seqs):
        position = table_ref[turns + 1] * width + lane - s * width
        inside = (lane >= s * width) & (lane < (s + 1) * width) & (position < table_ref[turns + 2 + s])
        live = jnp.where(inside, 1.0, live)

    def device_rows(d):
        return pl.ds(pl.multiple_of(d * chans, 8), chans)

    @pl.when(step == 0)
    def _():
        def gather(d, carry):
            at = device_rows(d)
            cs[at, :] = side_by_side(conv_ref[d].astype(f32), seqs)
            res[at, :] = side_by_side(x_ref[d].astype(f32), seqs)
            ds[at, :] = live * side_by_side(cot_ref[d].astype(f32), seqs)
            return carry

        lax.fori_loop(0, devices, gather, 0)
        for piece, h in zip(weights, halves):
            for core, parts in enumerate(piece):
                turn = 0
                for _, out_rows in parts:
                    for n in range(out_rows.shape[0]):
                        device, _ = slots(table_ref, turns, turn)[core]
                        at = pl.ds(pl.multiple_of(device * chans + h * some_out, 8), some_out)
                        out_w32[at, :] = out_rows[n].astype(f32)
                        turn += 1

        def gated(i, carry):
            at = chunk_rows(i)
            out_w_ref[at, :] = out_w32[at, :].astype(bf16)
            gb[at, :] = (cs[at, :] * gate_ref[at, :]).astype(bf16)
            d = ds[at, :]
            db[at, :] = d.astype(bf16)
            folds[3, at, :] = folded(d)
            acc_in[at, :] = jnp.zeros((CHUNK, cols), f32)
            return carry

        lax.fori_loop(0, dim // CHUNK, gated, 0)
        acc_out[...] = mm16(out_w_ref[...], gb[...], TN)

        def add(i, carry):
            at = chunk_rows(i)
            res[at, :] = res[at, :] + acc_out[at, :] + prm_ref[at, 19:20]
            acc_out[at, :] = jnp.zeros((CHUNK, cols), f32)
            return carry

        lax.fori_loop(0, dim // CHUNK, add, 0)
        mean, inverse = norm_stats(res, dim)

        def scale(i, carry):
            at = chunk_rows(i)
            normed = (res[at, :] - mean) * inverse
            cs_norm = normed * prm_ref[at, 17:18] + prm_ref[at, 18:19]
            xb[at, :] = cs_norm.astype(bf16)
            return carry

        lax.fori_loop(0, dim // CHUNK, scale, 0)
        stats[0:8, :] = jnp.broadcast_to(mean, (8, cols))
        stats[8:16, :] = jnp.broadcast_to(inverse, (8, cols))

    pair = slots(table_ref, turns, step)
    up_b = []
    for device, _ in pair:
        prm = prm_ref[device_rows(device), :]
        for h in halves:
            for m in range(some_hid // chans):
                first, second = 21 + m, 21 + m + (pieces - 1) * some_hid // chans
                up_b.append(jnp.where(h == 0, prm[:, first : first + 1], prm[:, second : second + 1]))
    up_b = jnp.concatenate(up_b, axis=0)

    def now(parts, rows):
        blocks = [ref[0, rows, :] for ref, _ in parts]
        return blocks[0] if len(blocks) == 1 else jnp.where(step < turns // 2, blocks[0], blocks[1])

    up = jnp.concatenate([now(piece[core], slice(0, some_hid)) for core in range(2) for piece in weights], axis=0)
    down = jnp.concatenate([now(piece[core], slice(some_hid, 2 * some_hid)) for core in range(2) for piece in weights], axis=0)
    u = mm16(up, xb[...], NN) + up_b
    d_act = mm16(down, db[...], NN)
    a, k = 0.044715, math.sqrt(2.0 / math.pi)
    sq = u * u
    t = jnp.tanh(u * (k + (k * a) * sq))
    half = 0.5 * (1.0 + t)
    act = (u * half).astype(bf16)
    d_u = d_act * (half + 0.5 * u * (1.0 - t * t) * (k + (3.0 * k * a) * sq))
    d_low = d_u.astype(bf16)
    fold = folded(d_u)
    acc_out[...] += mm16(down, act, TN)
    acc_in[...] += mm16(up, d_low, TN)
    spots = [(n, p, h) for n in range(2) for p, h in enumerate(halves)]
    for n, p, h in spots:
        rows = slice((n * pieces + p) * some_hid, (n * pieces + p + 1) * some_hid)
        up_folds[pl.ds(pl.multiple_of(pair[n][0] * hid + h * some_hid, 8), some_hid), :] = fold[rows]
    for left, right, first in ((d_low, xb, 0), (act, db, hid)):
        gs[...] = mm16(left, right[...], NT).astype(bf16)
        for n, p, h in spots:
            rows = slice((n * pieces + p) * some_hid, (n * pieces + p + 1) * some_hid)
            at = pl.ds(pl.multiple_of(first + h * some_hid, some_hid), some_hid)
            for g_refs, some in zip(grads, columns):
                g_refs[n][step, at, :] = gs[rows, some]

    @pl.when(step == last)
    def _():
        mean, inverse = stats[0:1, :], stats[8:9, :]

        def result(i, t):
            at = chunk_rows(i)
            r = res[at, :]
            acc_out[at, :] = live * (r + acc_out[at, :] + prm_ref[at, 20:21])
            normed = (r - mean) * inverse
            d = acc_in[at, :]
            both = d * normed
            folds[0, at, :] = folded(both)
            folds[1, at, :] = folded(d)
            gain = prm_ref[at, 17:18]
            return t[0] + eights(d * gain), t[1] + eights(both * gain)

        zero = jnp.zeros((8, cols), f32)
        m1, m2 = lax.fori_loop(0, dim // CHUNK, result, (zero, zero))
        m1 = jnp.sum(m1, axis=0, keepdims=True) / dim
        m2 = jnp.sum(m2, axis=0, keepdims=True) / dim

        def residual(i, carry):
            at = chunk_rows(i)
            normed = (res[at, :] - mean) * inverse
            d = ds[at, :] + inverse * (acc_in[at, :] * prm_ref[at, 17:18] - m1 - normed * m2)
            d_res_ref[at, :] = d
            folds[2, at, :] = folded(d)
            db[at, :] = d.astype(bf16)
            return carry

        lax.fori_loop(0, dim // CHUNK, residual, 0)
        for n in range(dim // 256):
            some = slice(n * 256, (n + 1) * 256)
            acc_in[some, :] = mm16(out_w_ref[some, :], db[...], NN)
            out_w32[some, :] = mm16(gb[some, :], db[...], NT)
        for g_refs, at in zip(grads, columns):
            for turn in range(turns):
                for g_ref, (device, _) in zip(g_refs, slots(table_ref, turns, turn)):
                    g_ref[turn, 2 * hid :, :] = out_w32[device_rows(device), at].astype(bf16)

        def products(i, carry):
            at = chunk_rows(i)
            d = acc_in[at, :]
            p0 = d * cs[at, :]
            p0_ref[at, :] = p0
            acc_in[at, :] = d * gate_ref[at, :]
            return carry

        lax.fori_loop(0, dim // CHUNK, products, 0)

        def scatter(d, carry):
            at = device_rows(d)
            p0h_ref[d] = first_tokens(p0_ref[at, :], seqs).astype(bf16)
            layer_ref[d, : seqs * chans, :] = stacked(acc_out[at, :], seqs).astype(bf16)
            d_conv_ref[d] = stacked(acc_in[at, :], seqs).astype(bf16)
            totals = [padded_totals(folds[q, at, :], width)[0] for q in range(4)]
            totals += padded_totals(up_folds[pl.ds(pl.multiple_of(d * hid, 8), hid), :], width)
            layer_ref[d, seqs * chans :, :] = as_rows(totals, SUM_ROWS)
            return carry

        lax.fori_loop(0, devices, scatter, 0)


def middle(table, conv, x, cot, gate, matrices, prm, hid, seqs):
    devices, rows, width = conv.shape
    dim, cols = gate.shape
    chans = dim // devices
    turns = devices // 2
    pieces = len(matrices)
    part, some_hid, some_out = dim // pieces, hid // pieces, chans // pieces
    sd = jax.ShapeDtypeStruct
    out = (
        sd((devices, rows + SUM_ROWS, width), bf16),
        sd((devices, rows, width), bf16),
        sd((dim, cols), f32),
        sd((dim, cols), f32),
        sd((devices, 8 * seqs, LANE), bf16),
    ) + (sd((turns, 2 * hid + chans, part), bf16),) * (2 * pieces)
    big = pltpu.VMEM((dim, cols), f32)
    low = pltpu.VMEM((dim, cols), bf16)
    args, specs = [conv, x, cot, gate, prm], [whole(conv), whole(x), whole(cot), whole(gate), whole(prm)]
    segments = len(matrices[0][0])
    for piece in matrices:
        for parts in piece:
            first = 0
            for a in parts:
                count = a.shape[0]
                args += [a, a]
                specs += [
                    pl.BlockSpec((1, 2 * some_hid, dim), lambda i, t, f=first, c=count: (jnp.clip(i - f, 0, c - 1), 0, 0)),
                    pl.BlockSpec(
                        (count, some_out, dim), lambda i, t: (0, 2 * some_hid // some_out, 0), pipeline_mode=pl.Buffered(1)
                    ),
                ]
                first += count
    return chip_call(
        36,
        lambda *refs: middle_body(seqs, pieces, segments, *refs),
        table,
        turns,
        args,
        specs,
        out,
        tuple(whole(o) for o in out),
        [
            big, big, big, low, low, low, big, big, pltpu.VMEM((4, dim, LANE), f32),
            pltpu.VMEM((devices * hid, LANE), f32), pltpu.VMEM((16, cols), f32), pltpu.VMEM((dim, dim), f32),
            pltpu.VMEM((dim, dim), bf16), pltpu.VMEM((2 * hid, dim), bf16),
        ],
    )


def short_back(seqs, prm, kinds, d_short, head, projx, width, cols):
    chans = prm.shape[0]
    d_proj = []
    totals = [[] for _ in range(2 + KS)]
    for n, i in enumerate(kinds):
        px = projx[n * chans : (n + 1) * chans]
        weights = [jnp.broadcast_to(prm[:, 6 + 3 * j + i : 7 + 3 * j + i], (chans, width)) for j in range(KS)]
        parts = []
        sums = [0.0] * (2 + KS)
        for s in range(seqs):
            at = slice(s * width, (s + 1) * width)
            d = d_short[n][:, at]
            x = px[:, at]
            tail = px[:, cols:]
            wide = jnp.concatenate([tail if s == 0 else pltpu.roll(tail, LANE // 2, 1), x], axis=1)
            after = jnp.concatenate([d, head[n] if s == 0 else pltpu.roll(head[n], LANE // 2, 1)], axis=1)
            y = weights[0] * d
            sums[1] = sums[1] + folded(d)
            sums[2] = sums[2] + folded(d * x)
            for j in range(1, KS):
                y = y + weights[j] * pltpu.roll(after, width + LANE - j, 1)[:, :width]
                sums[2 + j] = sums[2 + j] + folded(d * pltpu.roll(wide, j, 1)[:, LANE:])
            sums[0] = sums[0] + folded(y)
            parts.append(y)
        d_proj.append(jnp.concatenate(parts, axis=1))
        for k in range(2 + KS):
            totals[k].append(sums[k])
    d_low = jnp.concatenate(d_proj, axis=0).astype(bf16)
    return d_low, padded_totals(jnp.concatenate(sum(totals, []), axis=0), width)


def back_gate_body(seqs, table_ref, p0_ref, p0h_ref, projx_ref, own_ref, other_ref, prm_ref, xn_ref, g_ref, sums_ref, acc):
    dim, cols = xn_ref.shape
    chans = p0_ref.shape[1]
    step = pl.program_id(0)

    @pl.when(step == 0)
    def _():
        acc[...] = jnp.zeros_like(acc)

    turns = prm_ref.shape[0] // chans // 2
    for w_ref, (device, g) in zip((own_ref, other_ref), slots(table_ref, turns, step)):
        prm = prm_ref[pl.ds(pl.multiple_of(device * chans, 8), chans), :]
        d_low, totals = short_back(
            seqs, prm, (0,), (p0_ref[g],), (token_columns(p0h_ref[g].astype(f32), chans),), projx_ref[g].astype(f32), cols // seqs, cols
        )
        sums_ref[g] = totals[0]
        acc[...] += mm16(w_ref[0, PRM : PRM + chans, :], d_low, TN)
        g_ref[g] = mm16(d_low, xn_ref[...], NT).astype(bf16)


def back_gate(table, p0, p0h, projx, own, other, prm, xn, seqs):
    devices, chans, cols = p0.shape
    dim = xn.shape[0]
    sd = jax.ShapeDtypeStruct
    out = (
        sd((devices, chans, dim), bf16),
        sd((devices, 8, cols // seqs), f32),
        sd((dim, cols), f32),
    )
    return chip_call(
        2,
        lambda *refs: back_gate_body(seqs, *refs),
        table,
        devices // 2,
        (p0, p0h, projx, own, other, prm, xn),
        [by_chip(a) for a in (p0, p0h, projx)] + [by_turn(own), by_turn(other), whole(prm), whole(xn)],
        out,
        (by_chip(out[0]), by_chip(out[1]), whole(out[2])),
        [],
    )


def back_body(
    seqs, table_ref, d_mixed_ref, pair_ref, heads_ref, projx_ref, own_ref, other_ref, prm_ref, xn_ref, x_ref, stat_ref, d_res_ref,
    acc0_ref, sums0_ref, layer_ref, tail_ref, g_ref, acc, xs, folds, sums,
):
    devices, _, width = x_ref.shape
    dim, cols = xn_ref.shape
    chans = dim // devices
    step = pl.program_id(0)
    last = pl.num_programs(0) - 1

    @pl.when(step == 0)
    def _():
        acc[...] = acc0_ref[...]

    turns = devices // 2
    for w_ref, (device, g) in zip((own_ref, other_ref), slots(table_ref, turns, step)):
        prm = prm_ref[pl.ds(pl.multiple_of(device * chans, 8), chans), :]
        block = d_mixed_ref[g].astype(f32)
        d_mixed = side_by_side(block[: seqs * chans], seqs)
        square = jnp.concatenate([block[seqs * chans :, :LANE], jnp.zeros((LANE - HEAD_ROWS, LANE), f32)], axis=0).T
        second = pltpu.roll(square[chans : 2 * chans], LANE // 2, 1)
        d_head = jnp.where(lanes_of((chans, LANE)) < LANE // 2, square[:chans], second)
        pair = pair_ref[g]
        pair_head = token_columns(heads_ref[g].astype(f32), 2 * chans)
        d_short = (d_mixed * pair[chans:], d_mixed * pair[:chans])
        head = (d_head * pair_head[chans:], d_head * pair_head[:chans])
        d_low, totals = short_back(seqs, prm, (1, 2), d_short, head, projx_ref[g].astype(f32), width, cols)
        for n, t in enumerate(totals):
            sums[n, device] = t
        acc[...] += mm16(w_ref[0, PRM + chans :, :], d_low, TN)
        g_ref[g] = mm16(d_low, xn_ref[...], NT).astype(bf16)

    @pl.when(step == last)
    def _():
        def gather(d, carry):
            xs[pl.ds(pl.multiple_of(d * chans, 8), chans), :] = side_by_side(x_ref[d].astype(f32), seqs)
            return carry

        lax.fori_loop(0, devices, gather, 0)
        mean, inverse = stat_ref[0:1, :], stat_ref[8:9, :]

        def first(i, t):
            at = chunk_rows(i)
            normed = (xs[at, :] - mean) * inverse
            d = acc[at, :]
            both = d * normed
            folds[0, at, :] = folded(both)
            folds[1, at, :] = folded(d)
            gain = prm_ref[at, 15:16]
            return t[0] + eights(d * gain), t[1] + eights(both * gain)

        zero = jnp.zeros((8, cols), f32)
        m1, m2 = lax.fori_loop(0, dim // CHUNK, first, (zero, zero))
        m1 = jnp.sum(m1, axis=0, keepdims=True) / dim
        m2 = jnp.sum(m2, axis=0, keepdims=True) / dim

        def second(i, carry):
            at = chunk_rows(i)
            normed = (xs[at, :] - mean) * inverse
            acc[at, :] = d_res_ref[at, :] + inverse * (acc[at, :] * prm_ref[at, 15:16] - m1 - normed * m2)
            return carry

        lax.fori_loop(0, dim // CHUNK, second, 0)

        rows = seqs * chans

        def scatter(d, carry):
            at = pl.ds(pl.multiple_of(d * chans, 8), chans)
            tail_ref[d, :rows, :] = stacked(acc[at, :], seqs).astype(bf16)
            totals = [sums0_ref[d]] + [sums[n, d] for n in range(sums.shape[0])]
            totals += [padded_totals(folds[q, at, :], width)[0] for q in range(2)]
            tail_ref[d, rows : rows + SUM_ROWS, :] = as_rows(totals, SUM_ROWS)
            tail_ref[d, rows + SUM_ROWS :, :] = layer_ref[d]
            return carry

        lax.fori_loop(0, devices, scatter, 0)


def back(table, d_mixed, pair, heads, projx, own, other, prm, xn, x, stat, d_res, acc0, sums0, layer, seqs):
    devices, rows, width = x.shape
    dim, cols = xn.shape
    chans = dim // devices
    sd = jax.ShapeDtypeStruct
    pieces = -(-2 * (2 + KS) * chans // width)
    out = (
        sd((devices, 2 * rows + 2 * SUM_ROWS, width), bf16),
        sd((devices, 2 * chans, dim), bf16),
    )
    return chip_call(
        100,
        lambda *refs: back_body(seqs, *refs),
        table,
        devices // 2,
        (d_mixed, pair, heads, projx, own, other, prm, xn, x, stat, d_res, acc0, sums0, layer),
        [by_chip(a) for a in (d_mixed, pair, heads, projx)]
        + [by_turn(own), by_turn(other), whole(prm), whole(xn), whole(x)]
        + [whole(a) for a in (stat, d_res, acc0, sums0, layer)],
        out,
        (whole(out[0]), by_chip(out[1])),
        [
            pltpu.VMEM((dim, cols), f32), pltpu.VMEM((dim, cols), f32), pltpu.VMEM((2, dim, LANE), f32),
            pltpu.VMEM((pieces, devices, 8, width), f32),
        ],
    )


def position_table():
    places = np.arange(LMAX)
    orders = np.arange(1, (EMB - 1) // 2 + 1)
    turns = 2.0 * math.pi * ((orders[:, None] * places[None, :]) % LMAX) / LMAX
    ramp = places[None, :] / (LMAX - 1)
    return np.concatenate([ramp, np.cos(turns), -np.sin(turns)], axis=0).astype(np.float32)


FEAT = position_table()


def mm(a, b, dims):
    return lax.dot_general(a, b, (dims, ((), ())), precision=highest, preferred_element_type=f32)


NN = ((1,), (0,))
TN = ((0,), (0,))
NT = ((1,), (1,))


def filter_back_body(d_ref, raw_ref, fall_ref, h1_ref, h2_ref, c1_ref, c2_ref, pre1_ref, pre2_ref, feat_ref, mid_ref, last_ref, rate_ref,
                     g_in_ref, g_mid_ref, g_last_ref, g_rows_ref, g_decay_ref):
    chans = d_ref.shape[0]
    d = d_ref[...]
    q = d * (fall_ref[...] + decay_floor)
    g_last_ref[...] = mm(h2_ref[...], q, NT)
    decay = folded(d * raw_ref[...] * fall_ref[...] * feat_ref[0:1, :])
    g_decay_ref[...] = -jnp.sum(decay, axis=1, keepdims=True)
    u2 = mm(last_ref[...], q, NN) * c2_ref[...]
    rate = rate_ref[...]
    fu2 = rate * u2
    u1 = mm(mid_ref[...], fu2, NN) * c1_ref[...]
    fu1 = rate * u1
    g_in_ref[...] = mm(feat_ref[...], fu1, NT)
    g_mid_ref[...] = mm(h1_ref[...], fu2, NT)
    rows = jnp.concatenate([folded(fu1), folded(fu2), folded(u2 * pre2_ref[...] + u1 * pre1_ref[...])], axis=0)
    extra = jnp.zeros((-rows.shape[0] % LANE, LANE), f32)
    g_rows_ref[...] = row_totals(jnp.concatenate([rows, extra], axis=0))


def filter_back(*args):
    chans, ford, taps = args[0].shape[0], args[3].shape[0], args[9].shape[0]
    sd = jax.ShapeDtypeStruct
    out = (sd((taps, ford), f32), sd((ford, ford), f32), sd((ford, chans), f32), sd((8, -(-3 * ford // LANE) * LANE), f32), sd((chans, 1), f32))
    return whole_call(0.01, filter_back_body, out, [], *args)


def mm16(a, b, dims):
    return lax.dot_general(a, b, (dims, ((), ())), preferred_element_type=f32)


def ring_of(chips):
    zs = 4
    ys = chips // zs
    order = [(z, 0) for z in range(zs)]
    for y in range(1, ys):
        order += [(z, y) for z in (range(zs - 1, 0, -1) if y % 2 else range(1, zs))]
    order += [(0, y) for y in range(ys - 1, 0, -1)]
    return [z * ys + y for z, y in order]


def after(values, *others):
    return lax.optimization_barrier((values,) + others)[0]


def ring_hop(values, ring, by):
    chips = len(ring)
    moves = [(2 * ring[p] + q, 2 * ring[(p + by) % chips] + q) for p in range(chips) for q in range(2)]
    return lax.ppermute(values, "chan", moves)


class RingGather:
    def __init__(self, shard, ring):
        self.ring, self.hops = ring, len(ring) // 2
        self.cut = shard.shape[0] // 32 * 16
        self.behind, self.ahead = [shard], [shard]
        self.far = None

    def advance(self, upto, *others):
        while len(self.behind) <= min(upto, self.hops - 1):
            first, second = self.behind[-1], self.ahead[-1]
            if others:
                first, second = after(first, *others), after(second, *others)
            self.behind.append(ring_hop(first, self.ring, 1))
            self.ahead.append(ring_hop(second, self.ring, -1))
        if upto == self.hops:
            first, second = self.behind[-1][: self.cut], self.ahead[-1][self.cut :]
            if others:
                first, second = after(first, *others), after(second, *others)
            self.far = jnp.concatenate([ring_hop(first, self.ring, 1), ring_hop(second, self.ring, -1)], axis=0)

    def shards(self):
        return self.behind + self.ahead[1:] + [self.far]


def both_cores(shards):
    own = stack(shards)
    return own, lax.ppermute(own, "chan", [(i, i ^ 1) for i in range(2 * len(shards))])


def stack_body(*refs):
    for i, ref in enumerate(refs[:-1]):
        refs[-1][i] = ref[...]


def stack(shards):
    out = jax.ShapeDtypeStruct((len(shards),) + shards[0].shape, shards[0].dtype)
    return whole_call(0.01, stack_body, out, [], *shards)


def turn_table(ring):
    chips = len(ring)
    steps = [0] + [-k for k in range(1, chips // 2)] + [k for k in range(1, chips // 2)] + [chips // 2]
    table = np.zeros((chips, chips), np.int32)
    for p, chip in enumerate(ring):
        table[chip] = [ring[(p + k) % chips] for k in steps]
    return table


def exchange(values):
    return lax.all_to_all(values, "chan", split_axis=0, concat_axis=0, tiled=True)


def on_device(
    layer_in,
    seq_lengths,
    ln1_gain,
    first_norm_bias,
    in_weight,
    in_bias,
    short_weight,
    short_bias,
    filt_in,
    filt_in_bias,
    filt_mid,
    filt_mid_bias,
    sine_freq,
    filt_out,
    decay_rate,
    conv_bias,
    out_weight,
    out_bias,
    ln2_gain,
    second_norm_bias,
    up_weight,
    up_bias,
    down_weight,
    down_bias,
    cotangent,
):
    seqs, chans, _ = layer_in.shape
    devices = lax.axis_size("chan")
    groups = lax.axis_size("batch")
    width = LMAX // devices
    dim = chans * devices
    cols = seqs * width
    hid = up_weight.shape[0]
    ford = filt_mid.shape[0]
    place = lax.axis_index("chan")

    def to_blocks(values):
        return (
            values.reshape(seqs, chans, devices, width)
            .transpose(2, 0, 1, 3)
            .reshape(devices, seqs * chans, width)
        )

    def from_blocks(blocks):
        return (
            blocks.reshape(devices, seqs, chans, width)
            .transpose(1, 2, 0, 3)
            .reshape(seqs, chans, LMAX)
        )

    small = jnp.concatenate(
        [
            in_bias,
            short_bias,
            short_weight.reshape(3 * KS, chans),
            jnp.stack([ln1_gain, first_norm_bias, ln2_gain, second_norm_bias, out_bias, down_bias]),
            up_bias.reshape(hid // chans, chans),
        ],
        axis=0,
    )
    small = jnp.pad(small, ((0, PRM - small.shape[0]), (0, dim - chans)))
    in_rows = in_weight.transpose(1, 2, 0).reshape(3 * chans, dim)
    ring = ring_of(devices // 2)
    chips = devices // 2
    core = place % 2
    batch = lax.axis_index("batch")
    swap = [(0, 1), (1, 0)]
    partner = [(i, i ^ 1) for i in range(devices)]
    turns = lax.dynamic_index_in_dim(jnp.asarray(turn_table(ring)), place // 2, 0, False)
    table = jnp.concatenate(
        [turns, jnp.stack([core, place]).astype(jnp.int32), seq_lengths, batch.astype(jnp.int32).reshape(1)]
    )
    late = [up_weight, down_weight, out_weight]
    stepped = groups == 2 and chips == 8 and dim % (2 * LANE) == 0
    beside = [(i, i ^ 2) for i in range(devices)]
    along = [list(range(k, devices, 4)) for k in range(4)]

    def to_partner(values):
        return lax.ppermute(values, "chan", partner)

    if stepped:
        late = [lax.dynamic_slice_in_dim(a, batch * (a.shape[0] // 2), a.shape[0] // 2, 0) for a in late]
        late = jnp.concatenate(late, axis=0)
        near = lax.all_gather(late, "chan", axis=0, axis_index_groups=along)
    else:
        late = jnp.concatenate(late, axis=0)
        late = lax.all_gather(late, "chan", axis=0).reshape((chips, 2) + late.shape)
    first = RingGather(after(jnp.concatenate([small, in_rows], axis=0), late) if stepped else jnp.concatenate([small, in_rows], axis=0), ring)
    first.advance(chips // 8)
    x = exchange(to_blocks(layer_in))
    rows = seqs * chans
    xh = lax.ppermute(x[:, :rows, width - LANE :], "chan", [(i, i + 1) for i in range(devices - 1)])

    feat = jnp.asarray(FEAT)
    ramp = feat[0:1]
    rate = sine_freq[:, None]
    pre1 = mm(filt_in, feat, TN) + filt_in_bias[:, None]
    h1, c1 = jnp.sin(rate * pre1), jnp.cos(rate * pre1)
    pre2 = mm(filt_mid, h1, TN) + filt_mid_bias[:, None]
    h2, c2 = jnp.sin(rate * pre2), jnp.cos(rate * pre2)
    raw = mm(filt_out, h2, TN)
    falling = jnp.exp(-ramp * decay_rate[:, None])
    first.advance(chips // 4, h1)
    filt = raw * (falling + decay_floor)
    first.advance(3 * chips // 8, filt, x)
    filt_spec = filter_spectrum(filt)
    first.advance(chips // 2, filt_spec)
    in_own, in_other = both_cores(first.shards())
    bias_col = conv_bias[:, None]

    prm, xn1, stat1, gate, pair, projx0, projx, mixed, heads = front(
        table, x, xh, in_own, in_other, filt_spec, seqs
    )
    mixed_chan = exchange(mixed)
    cot = exchange(after(to_blocks(cotangent), mixed_chan))
    if stepped:
        near = after(near, mixed)
        far = lax.ppermute(near, "chan", beside)
        near_across = lax.ppermute(near, "batch", swap)
        near_other = to_partner(near)
    backward_hop = [(i + 1, i) for i in range(devices - 1)]
    heads = lax.ppermute(heads, "chan", backward_hop)
    conv_chan, mixed_spec = conv_forward(mixed_chan, filt_spec, bias_col, seqs)
    conv = exchange(after(conv_chan, near_across, cot, heads) if stepped else conv_chan)
    if stepped:
        far, near_across = after(far, conv_chan), after(near_across, conv_chan)
        far_across = lax.ppermute(far, "batch", swap)
        far_other, near_across_other = to_partner(far), to_partner(near_across)
        far_across_other = to_partner(far_across)
        matrices = [
            [[near, far], [near_other, far_other]],
            [[near_across, far_across], [near_across_other, far_across_other]],
        ]
        z = lax.iota(jnp.int32, 4) * 2
        y = (place // 2 % 2).astype(jnp.int32)
        order = jnp.concatenate([z + y, z + 1 - y])
    else:
        matrices = [[[lax.dynamic_index_in_dim(late, core, 1, False)], [lax.dynamic_index_in_dim(late, 1 - core, 1, False)]]]
        order = lax.iota(jnp.int32, chips)
    order = jnp.concatenate([order, table[chips:]])

    results = middle(order, conv, x, cot, gate.reshape(dim, cols), matrices, prm, hid, seqs)
    layer, d_conv, d_res, p0, p0h = results[:5]
    d_conv_chan = exchange(d_conv)
    p0h = lax.ppermute(p0h, "chan", backward_hop)

    def added(*values):
        return sum(v.astype(f32) for v in values).astype(bf16)

    if stepped:
        mine, mine_in = results[5], to_partner(results[6])
        theirs, theirs_in = results[7], to_partner(results[8])
        half = chips // 2
        far_theirs = added(theirs[half:], theirs_in[half:])
        near_theirs = added(theirs[:half], theirs_in[:half])
        d_conv_chan = after(d_conv_chan, far_theirs, near_theirs)
        far_theirs = lax.ppermute(far_theirs, "batch", swap)
        near_theirs = lax.ppermute(after(near_theirs, far_theirs), "batch", swap)
    else:
        early = added(results[5], to_partner(results[6]))

    if groups == 2:
        same_core = [list(range(q, devices, 2)) for q in range(2)]
    else:
        same_core = [[b * devices + c for b in range(groups) for c in range(q, devices, 2)] for q in range(2)]

    def batch_total(values):
        return values + lax.ppermute(values, "batch", swap) if groups == 2 else lax.psum(values, "batch")

    def over_batch(table):
        if groups != 2:
            return lax.psum_scatter(table.astype(f32), "batch", scatter_dimension=1, tiled=True)
        part = dim // 2
        axis = table.ndim - 1
        mine = lax.axis_index("batch") * part
        theirs = lax.dynamic_slice_in_dim(table, part - mine, part, axis)
        kept = lax.dynamic_slice_in_dim(table, mine, part, axis)
        return kept.astype(f32) + lax.ppermute(theirs, "batch", swap).astype(f32)

    def over_chip(table):
        table = table.reshape((devices // 2, 2) + table.shape[1:])
        own = lax.dynamic_index_in_dim(table, core, 1, False)
        theirs = lax.dynamic_index_in_dim(table, 1 - core, 1, False)
        return (own.astype(f32) + lax.ppermute(theirs, "chan", partner).astype(f32)).astype(bf16)

    def over_groups(both):
        return over_batch(both).astype(bf16) if groups == 2 else both

    def over_chips(both):
        rows = both.shape[1]
        if groups == 2:
            both = lax.all_to_all(
                both, "chan", split_axis=0, concat_axis=0, tiled=True, axis_index_groups=same_core
            )
        else:
            both = both.reshape(devices // 2, rows, groups, dim // groups).transpose(2, 0, 1, 3)
            both = lax.all_to_all(
                both.reshape(groups * devices // 2, rows, dim // groups),
                ("batch", "chan"), split_axis=0, concat_axis=0, tiled=True, axis_index_groups=same_core,
            )
        return jnp.sum(both.astype(f32), axis=0)

    d_mixed_chan, d_filter, g_conv_bias = conv_backward(
        d_conv_chan, mixed_chan, mixed_spec, filt_spec, bias_col, seqs
    )
    if stepped:
        d_mixed_chan = after(d_mixed_chan, far_theirs, p0h)
        far_mine = added(mine[half:], mine_in[half:], far_theirs)
        p0h = after(p0h, far_mine)
    g_in0, sums0, acc0 = back_gate(
        table, p0.reshape(devices, chans, cols), p0h, projx0, in_own, in_other, prm, xn1, seqs
    )
    g_in0 = over_chip(g_in0)
    d_mixed = exchange(d_mixed_chan)
    g_filt_in, g_filt_mid, g_filt_out, g_rows, g_decay = filter_back(
        d_filter, raw, falling, h1, h2, c1, c2, pre1, pre2, feat, filt_mid, filt_out, rate
    )
    shared = [g_filt_in.reshape(-1), g_filt_mid.reshape(-1), g_rows[0, : 3 * ford]]
    total = batch_total(
        jnp.concatenate(shared + [g_conv_bias[:, 0], g_decay[:, 0], g_filt_out.reshape(-1)])
    )
    if stepped:
        far_mine = lax.ppermute(far_mine, "chan", beside)
    else:
        chan_groups = [list(range(q, devices, 2)) for q in range(2)]
        early = lax.psum_scatter(early, "chan", scatter_dimension=0, tiled=True, axis_index_groups=chan_groups)[0]

    tail, g_in = back(
        table, d_mixed, pair, heads, projx, in_own, in_other, prm, xn1, x, stat1, d_res, acc0, sums0, layer, seqs
    )
    if stepped:
        tail = after(tail, far_mine, near_theirs)
        early = added(mine[:half], mine_in[:half], near_theirs, far_mine)
        g_in = after(g_in, early)
    tail = exchange(tail)
    g_in = over_groups(jnp.concatenate([g_in0, over_chip(g_in)], axis=1))
    if stepped:
        early = lax.psum_scatter(early, "chan", scatter_dimension=0, tiled=True, axis_index_groups=along)[0]

    cut = [0]

    def take(*shape):
        n = math.prod(shape)
        part = total[cut[0] : cut[0] + n].reshape(shape)
        cut[0] += n
        return part

    shared = take(sum(v.shape[0] for v in shared))
    shared = shared + lax.ppermute(shared, "chan", partner)
    g_conv_b, g_decay_rate, g_filt_last = take(chans), take(chans), take(ford, chans)
    n_shared = shared.shape[0]
    if groups != 2:
        shared = shared / groups
    line = g_in.shape[2]
    shared = jnp.pad(shared.astype(bf16), (0, -n_shared % (8 * line))).reshape(1, -1, line)
    shared = jnp.broadcast_to(shared, (devices // 2,) + shared.shape[1:])
    mine = 3 * chans
    in_grad = over_chips(jnp.concatenate([g_in, shared], axis=1))
    if groups == 2:
        total = in_grad[mine:].reshape(-1)
    else:
        total = lax.all_gather(in_grad[mine:], "batch", axis=1, tiled=True).reshape(-1)
    in_grad = in_grad[:mine]
    cut[0] = 0
    g_filt_in, g_filt_mid = take(EMB, ford), take(ford, ford)
    g_filt_in_bias, g_filt_mid_bias, g_sine = take(ford), take(ford), take(ford)

    early = after(early, in_grad)
    early = early.astype(f32) if stepped else over_batch(early)
    up_grad, down_grad, out_grad = early[:hid], early[hid : 2 * hid], early[2 * hid :]

    grad_blocks, out_blocks = tail[:, :rows], tail[:, rows + SUM_ROWS : 2 * rows + SUM_ROWS]
    sums = jnp.concatenate([tail[:, 2 * rows + SUM_ROWS :], tail[:, rows : rows + SUM_ROWS]], axis=1)
    sums = batch_total(jnp.sum(sums.astype(f32), axis=0))
    sums = sums[0::2] + sums[1::2]
    g_gain2, g_shift2, g_out_b, g_down_b = (sums[i, :chans] for i in range(4))
    g_up_b = sums[4, :hid]
    at = SUM_ROWS // 2
    count = (2 + KS) * chans
    pieces = -(-2 * count // width)
    short0 = sums[at, :count].reshape(2 + KS, 1, chans)
    short = sums[at + 1 : at + 1 + pieces].reshape(-1)[: 2 * count].reshape(2 + KS, 2, chans)
    short = jnp.concatenate([short0, short], axis=1)
    g_in_bias, g_short_bias, g_short_weight = short[0], short[1], short[2:]
    g_gain1, g_shift1 = (sums[at + 1 + pieces + i, :chans] for i in range(2))

    return (
        from_blocks(out_blocks),
        from_blocks(grad_blocks).astype(f32),
        g_gain1,
        g_shift1,
        in_grad.reshape(3, chans, dim // groups).transpose(2, 0, 1),
        g_in_bias,
        g_short_weight,
        g_short_bias,
        g_filt_in,
        g_filt_in_bias,
        g_filt_mid,
        g_filt_mid_bias,
        g_sine,
        g_filt_last,
        g_decay_rate,
        g_conv_b,
        out_grad,
        g_out_b,
        g_gain2,
        g_shift2,
        up_grad,
        g_up_b,
        down_grad,
        g_down_b,
    )


def solution(mesh):
    token = P("batch", "chan", None)
    chan = P("chan")
    rows = P("chan", None)
    two = P(None, "chan")
    three = P(None, None, "chan")
    in_specs = (
        token, P("batch"), chan, chan, three, two, three, two, P(), P(), P(), P(), P(), two, chan, chan,
        rows, chan, chan, chan, rows, chan, rows, chan, token,
    )
    table = P("chan", "batch")
    out_specs = (
        token, token, chan, chan, P("batch", None, "chan"), two, three, two, P(), P(), P(), P(), P(), two,
        chan, chan, table, chan, chan, chan, table, chan, table, chan,
    )
    return jax.shard_map(
        on_device, mesh=mesh, in_specs=in_specs, out_specs=out_specs, check_vma=False
    )
```

```python
import functools
import math

import jax
import jax.numpy as jnp
import numpy as np
from jax import lax
from jax.experimental import pallas as pl
from jax.experimental.pallas import tpu as pltpu
from jax.sharding import PartitionSpec as P

EMB = 33
KS = 3
LMAX = 4096
LANE = 128
COARSE = LMAX // LANE
REPS = tuple(ka + 8 * kb for ka, count in ((0, 5), (1, 8), (2, 8), (3, 8), (4, 4)) for kb in range(count))
PLACE = {k1: i for i, k1 in enumerate(REPS)}
epsilon = 1e-05
decay_floor = 0.05
highest = lax.Precision.HIGHEST
f32 = jnp.float32
bf16 = jnp.bfloat16
vmem_limit = 56 * 1024 * 1024
HEAD_ROWS = 16
SUM_ROWS = 16
BATCH = 11
PRM = 32


def unit(turns):
    angle = 2.0 * math.pi * turns
    return math.cos(angle), math.sin(angle)


def scaled(z, c, s):
    re, im = z
    if im is None:
        return re * c, re * s
    return re * c - im * s, re * s + im * c


def plus(a, b):
    return a[0] + b[0], a[1] + b[1]


def minus(a, b):
    return a[0] - b[0], a[1] - b[1]


def dft4(z, sign):
    s0, d0 = plus(z[0], z[2]), minus(z[0], z[2])
    s1, d1 = plus(z[1], z[3]), minus(z[1], z[3])
    turned = (-d1[1], d1[0]) if sign > 0 else (d1[1], -d1[0])
    return [plus(s0, s1), plus(d0, turned), minus(s0, s1), minus(d0, turned)]


def dft8(z, sign):
    even, odd = dft4(z[0::2], sign), dft4(z[1::2], sign)
    c = math.sqrt(0.5)
    o1 = odd[1]
    o3 = odd[3]
    if sign > 0:
        odd1 = ((o1[0] - o1[1]) * c, (o1[0] + o1[1]) * c)
        odd2 = (-odd[2][1], odd[2][0])
        odd3 = ((-o3[0] - o3[1]) * c, (o3[0] - o3[1]) * c)
    else:
        odd1 = ((o1[0] + o1[1]) * c, (o1[1] - o1[0]) * c)
        odd2 = (odd[2][1], -odd[2][0])
        odd3 = ((o3[1] - o3[0]) * c, (-o3[0] - o3[1]) * c)
    turned = [odd[0], odd1, odd2, odd3]
    return [plus(even[i], turned[i]) for i in range(4)] + [minus(even[i], turned[i]) for i in range(4)]


def coarse_forward(xs, put):
    c = math.sqrt(0.5)
    cols = {ka: [None] * 8 for ka in range(5)}
    for b in range(8):
        x0, x1, x2, x3 = xs[b], xs[8 + b], xs[16 + b], xs[24 + b]
        s02, d02, s13, d13 = x0 + x2, x0 - x2, x1 + x3, x1 - x3
        d13c, s13c = d13 * c, s13 * c
        cols[0][b] = s02 + s13
        cols[4][b] = scaled((s02 - s13, None), *unit(-4 * b / 64))
        cols[2][b] = scaled((d02, -d13), *unit(-2 * b / 64))
        cols[1][b] = scaled((x0 + d13c, -s13c - x2), *unit(-b / 64))
        cols[3][b] = scaled((x0 - d13c, x2 - s13c), *unit(-3 * b / 64))
    for ka in (1, 2, 3):
        for kb, z in enumerate(dft8(cols[ka], -1)):
            put(ka + 8 * kb, z)
    for kb, z in enumerate(dft8(cols[4], -1)[:4]):
        put(4 + 8 * kb, z)
    r = cols[0]
    s04, d04, s26, d26 = r[0] + r[4], r[0] - r[4], r[2] + r[6], r[2] - r[6]
    s15, d15, s37, d37 = r[1] + r[5], r[1] - r[5], r[3] + r[7], r[3] - r[7]
    p, q = (d15 - d37) * c, (d15 + d37) * c
    even, odd = s04 + s26, s15 + s37
    put(0, (even + odd, None))
    put(32, (even - odd, None))
    put(16, (s04 - s26, s37 - s15))
    put(8, (d04 + p, -d26 - q))
    put(24, (d04 - p, d26 - q))


def coarse_inverse(get):
    c = math.sqrt(0.5)
    u = {}
    for ka in (1, 2, 3):
        back = dft8([get(ka + 8 * kb) for kb in range(8)], 1)
        u[ka] = [scaled(back[b], *unit(b * ka / 64)) for b in range(8)]
    v0, v32 = get(0)[0], get(32)[0]
    v8, v16, v24 = get(8), get(16), get(24)
    flat = []
    for b in range(8):
        total = v0 + v32 if b % 2 == 0 else v0 - v32
        for kb, v in ((1, v8), (2, v16), (3, v24)):
            co, si = unit(b * kb / 8)
            if abs(co) > 1e-9:
                total = total + v[0] * (2.0 * co)
            if abs(si) > 1e-9:
                total = total - v[1] * (2.0 * si)
        flat.append(total)
    odd = [get(4 + 8 * kb) for kb in range(4)]
    odd = odd + [(z[0], -z[1]) for z in odd[::-1]]
    half = dft8(odd, 1)
    quarter = []
    for b in range(8):
        co, si = unit(4 * b / 64)
        quarter.append(half[b][0] * co - half[b][1] * si)
    out = [None] * COARSE
    for b in range(8):
        u1, u2, u3 = u[1][b], u[2][b], u[3][b]
        s, d = flat[b] + quarter[b], flat[b] - quarter[b]
        dr, sr = (u1[0] - u3[0]) * c, u1[0] + u3[0]
        si_, di = (u1[1] + u3[1]) * c, u1[1] - u3[1]
        out[b] = s + 2.0 * (sr + u2[0])
        out[16 + b] = s - 2.0 * (di + u2[0])
        out[8 + b] = d + 2.0 * (dr - si_ - u2[1])
        out[24 + b] = d + 2.0 * (u2[1] - dr - si_)
    return out


def transform_tables():
    fine = np.arange(LANE)
    angle = 2.0 * math.pi * ((fine[:, None] * fine[None, :]) % LANE) / LANE
    co, si = np.cos(angle), np.sin(angle)
    ahead = np.block([[co, -si], [si, co]])
    back = ahead.T / (2.0 * LMAX)
    reps = np.array(REPS)
    turn = 2.0 * math.pi * ((reps[:, None] * fine[None, :]) % (2 * LMAX)) / (2 * LMAX)
    twist = np.concatenate([np.cos(turn), -np.sin(turn)], axis=1)[:, None, :]

    def pieces(table):
        table = table.astype(np.float32)
        upper = table.astype(jnp.bfloat16)
        lower = (table - upper.astype(np.float32)).astype(jnp.bfloat16)
        return np.stack([upper, lower])

    return pieces(ahead), pieces(back), twist.astype(np.float32)


AHEAD, BACK, TWIST = transform_tables()


def three_pass(values, table_ref):
    upper = values.astype(bf16)
    lower = (values - upper.astype(f32)).astype(bf16)
    t0, t1 = table_ref[0], table_ref[1]
    return (
        jnp.dot(upper, t0, preferred_element_type=f32)
        + jnp.dot(lower, t0, preferred_element_type=f32)
        + jnp.dot(upper, t1, preferred_element_type=f32)
    )


def rows_forward(xs_ref, spec_ref, rows):
    def step(g, carry):
        at = pl.ds(pl.multiple_of(g * 8, 8), 8)
        xs = [xs_ref[n, at, :] for n in range(COARSE)]

        def put(k1, z):
            i = PLACE[k1]
            spec_ref[i, at, 0:LANE] = z[0]
            spec_ref[i, at, LANE : 2 * LANE] = jnp.zeros_like(z[0]) if z[1] is None else z[1]

        coarse_forward(xs, put)
        return carry

    lax.fori_loop(0, rows // 8, step, 0)


def rows_inverse(spec_ref, ys_ref, rows):
    def step(g, carry):
        at = pl.ds(pl.multiple_of(g * 8, 8), 8)

        def get(k1):
            i = PLACE[k1]
            return spec_ref[i, at, 0:LANE], spec_ref[i, at, LANE : 2 * LANE]

        for n, y in enumerate(coarse_inverse(get)):
            ys_ref[n, at, :] = y
        return carry

    lax.fori_loop(0, rows // 8, step, 0)


def fine_forward(spec, twist, ahead_ref):
    re, im = spec[:, :LANE], spec[:, LANE:]
    tr, ti = twist[:, :LANE], twist[:, LANE:]
    return three_pass(jnp.concatenate([re * tr - im * ti, re * ti + im * tr], axis=1), ahead_ref)


def fine_inverse(spec, twist, back_ref):
    v = three_pass(spec, back_ref)
    re, im = v[:, :LANE], v[:, LANE:]
    tr, ti = twist[:, :LANE], twist[:, LANE:]
    return jnp.concatenate([re * tr + im * ti, im * tr - re * ti], axis=1)


def times(a, b):
    ar, ai, br, bi = a[:, :LANE], a[:, LANE:], b[:, :LANE], b[:, LANE:]
    return jnp.concatenate([ar * br - ai * bi, ar * bi + ai * br], axis=1)


def times_conj(a, b):
    ar, ai, br, bi = a[:, :LANE], a[:, LANE:], b[:, :LANE], b[:, LANE:]
    return jnp.concatenate([ar * br + ai * bi, ai * br - ar * bi], axis=1)


def together(values):
    return values.reshape(values.shape[0] * values.shape[1], values.shape[2])


def apart(values):
    return values.reshape(BATCH, values.shape[0] // BATCH, values.shape[1])


def twists(twist_ref, at, rows):
    return together(jnp.broadcast_to(twist_ref[at], (BATCH, rows, 2 * LANE)))


def spread(blocks_ref, xs_ref):
    per = blocks_ref.shape[2] // LANE
    for n in range(COARSE):
        r = n % per
        xs_ref[n] = blocks_ref[n // per, :, r * LANE : (r + 1) * LANE].astype(f32)


def filter_spectrum_body(filter_ref, twist_ref, ahead_ref, out_ref, xs_ref):
    rows = filter_ref.shape[0]
    for n in range(COARSE):
        xs_ref[n] = filter_ref[:, n * LANE : (n + 1) * LANE]
    rows_forward(xs_ref, out_ref, rows)

    def step(i, carry):
        at = pl.ds(i * BATCH, BATCH)
        out_ref[at] = apart(fine_forward(together(out_ref[at]), twists(twist_ref, at, rows), ahead_ref))
        return carry

    lax.fori_loop(0, len(REPS) // BATCH, step, 0)


def conv_forward_body(seqs, mixed_ref, filt_ref, bias_ref, twist_ref, ahead_ref, back_ref, out_ref, spec_ref, xs_ref, work_ref):
    rows = mixed_ref.shape[1]
    spread(mixed_ref, xs_ref)
    rows_forward(xs_ref, spec_ref, rows)

    def step(i, carry):
        at = pl.ds(i * BATCH, BATCH)
        twist = twists(twist_ref, at, rows)
        z = fine_forward(together(spec_ref[at]), twist, ahead_ref)
        spec_ref[at] = apart(z)
        k = together(jnp.concatenate([filt_ref[at]] * seqs, axis=1))
        work_ref[at] = apart(fine_inverse(times(z, k), twist, back_ref))
        return carry

    lax.fori_loop(0, len(REPS) // BATCH, step, 0)
    ys_ref = xs_ref
    rows_inverse(work_ref, ys_ref, rows)
    per = mixed_ref.shape[2] // LANE
    bias = jnp.concatenate([bias_ref[...]] * seqs, axis=0)
    for n in range(COARSE):
        at = (n // per, slice(None), slice((n % per) * LANE, (n % per + 1) * LANE))
        out_ref[at] = (ys_ref[n] + bias * mixed_ref[at].astype(f32)).astype(bf16)


def heads_out(out_ref, block, y):
    rows, width = y.shape[0], out_ref.shape[2]
    square = jnp.concatenate([y, jnp.zeros((LANE - rows, LANE), f32)], axis=0) if rows < LANE else y
    head = square.T[:HEAD_ROWS]
    if width > LANE:
        head = jnp.concatenate([head, jnp.zeros((HEAD_ROWS, width - LANE), f32)], axis=1)
    out_ref[block, rows:, :] = head.astype(bf16)


def conv_backward_body(
    seqs, d_ref, mixed_ref, mixed_spec_ref, filt_ref, bias_ref, twist_ref, ahead_ref, back_ref, out_ref, dfilt_ref, dbias_ref, xs_ref, spec_ref, work_ref, ys_ref
):
    rows = d_ref.shape[1]
    chans = rows // seqs
    spread(d_ref, xs_ref)
    rows_forward(xs_ref, spec_ref, rows)

    def step(i, carry):
        at = pl.ds(i * BATCH, BATCH)
        z = fine_forward(together(spec_ref[at]), twists(twist_ref, at, rows), ahead_ref)
        k = together(jnp.concatenate([filt_ref[at]] * seqs, axis=1))
        cross = apart(times_conj(z, together(mixed_spec_ref[at])))
        cross = sum(cross[:, s * chans : (s + 1) * chans] for s in range(seqs))
        both = together(jnp.concatenate([apart(times_conj(z, k)), cross], axis=1))
        work_ref[at] = apart(fine_inverse(both, twists(twist_ref, at, rows + chans), back_ref))
        return carry

    lax.fori_loop(0, len(REPS) // BATCH, step, 0)
    rows_inverse(work_ref, ys_ref, rows + chans)
    per = d_ref.shape[2] // LANE
    bias = jnp.concatenate([bias_ref[...]] * seqs, axis=0)
    total = jnp.zeros((rows, LANE), f32)
    out_ref[out_ref.shape[0] - 1, rows:, :] = jnp.zeros((HEAD_ROWS, d_ref.shape[2]), bf16)
    for n in range(COARSE):
        at = (n // per, slice(0, rows), slice((n % per) * LANE, (n % per + 1) * LANE))
        d = xs_ref[n]
        y = ys_ref[n, :rows, :] + bias * d
        out_ref[at] = y.astype(bf16)
        if n % per == 0 and n > 0:
            heads_out(out_ref, n // per - 1, y)
        total = total + d * mixed_ref[at].astype(f32)
        dfilt_ref[:, n * LANE : (n + 1) * LANE] = ys_ref[n, rows:, :]
    total = sum(total[s * chans : (s + 1) * chans] for s in range(seqs))
    dbias_ref[...] = jnp.sum(total, axis=1, keepdims=True)


def takes(us):
    return pl.CostEstimate(flops=int(us * 1e9), bytes_accessed=int(us * 3e6), transcendentals=0)


def whole_call(us, body, out_shape, scratch, *args):
    return pl.pallas_call(
        body,
        cost_estimate=takes(us),
        out_shape=out_shape,
        in_specs=[pl.BlockSpec(memory_space=pltpu.VMEM)] * len(args),
        out_specs=jax.tree.map(lambda _: pl.BlockSpec(memory_space=pltpu.VMEM), out_shape),
        scratch_shapes=scratch,
        compiler_params=pltpu.CompilerParams(vmem_limit_bytes=vmem_limit),
    )(*args)


def filter_spectrum(filt):
    rows = filt.shape[0]
    return whole_call(
        8,
        filter_spectrum_body,
        jax.ShapeDtypeStruct((len(REPS), rows, 2 * LANE), f32),
        [pltpu.VMEM((COARSE, rows, LANE), f32)],
        filt,
        jnp.asarray(TWIST),
        jnp.asarray(AHEAD),
    )


def conv_forward(mixed, filt_spec, bias, seqs):
    blocks, rows, width = mixed.shape
    n = len(REPS)
    return whole_call(
        100,
        lambda *refs: conv_forward_body(seqs, *refs),
        (jax.ShapeDtypeStruct(mixed.shape, bf16), jax.ShapeDtypeStruct((n, rows, 2 * LANE), f32)),
        [pltpu.VMEM((COARSE, rows, LANE), f32), pltpu.VMEM((n, rows, 2 * LANE), f32)],
        mixed,
        filt_spec,
        bias,
        jnp.asarray(TWIST),
        jnp.asarray(AHEAD),
        jnp.asarray(BACK),
    )


def conv_backward(d_conv, mixed, mixed_spec, filt_spec, bias, seqs):
    blocks, rows, width = mixed.shape
    chans = rows // seqs
    n = len(REPS)
    return whole_call(
        100,
        lambda *refs: conv_backward_body(seqs, *refs),
        (
            jax.ShapeDtypeStruct((blocks, rows + HEAD_ROWS, width), bf16),
            jax.ShapeDtypeStruct((chans, LMAX), f32),
            jax.ShapeDtypeStruct((chans, 1), f32),
        ),
        [
            pltpu.VMEM((COARSE, rows, LANE), f32),
            pltpu.VMEM((n, rows, 2 * LANE), f32),
            pltpu.VMEM((n, rows + chans, 2 * LANE), f32),
            pltpu.VMEM((COARSE, rows + chans, LANE), f32),
        ],
        d_conv,
        mixed,
        mixed_spec,
        filt_spec,
        bias,
        jnp.asarray(TWIST),
        jnp.asarray(AHEAD),
        jnp.asarray(BACK),
    )


CHUNK = 48


def lanes_of(shape):
    return lax.broadcasted_iota(jnp.int32, shape, 1)


def side_by_side(block, seqs):
    chans = block.shape[0] // seqs
    return jnp.concatenate([block[s * chans : (s + 1) * chans] for s in range(seqs)], axis=1)


def stacked(values, seqs):
    width = values.shape[1] // seqs
    return jnp.concatenate([values[:, s * width : (s + 1) * width] for s in range(seqs)], axis=0)


def eights(values):
    return jnp.sum(values.reshape(values.shape[0] // 8, 8, values.shape[1]), axis=0)


def folded(values):
    return sum(values[:, i * LANE : (i + 1) * LANE] for i in range(values.shape[1] // LANE))


def row_totals(values):
    ones = jnp.ones((8, LANE), bf16)
    upper = values.astype(bf16)
    lower = (values - upper.astype(f32)).astype(bf16)
    return mm16(ones, upper, NT) + mm16(ones, lower, NT)


def padded_totals(values, width):
    extra = -values.shape[0] % width
    if extra:
        values = jnp.concatenate([values, jnp.zeros((extra, LANE), f32)], axis=0)
    totals = row_totals(values)
    return [totals[:, i * width : (i + 1) * width] for i in range(totals.shape[1] // width)]


def as_rows(totals, rows):
    halves = []
    for t in totals:
        upper = t.astype(bf16).astype(f32)
        halves += [upper, t - upper]
    place = lax.broadcasted_iota(jnp.int32, halves[0].shape, 0)
    tiles = []
    for first in range(0, rows, 8):
        tile = jnp.zeros_like(halves[0])
        for i, h in enumerate(halves[first : first + 8]):
            tile = jnp.where(place == i, h, tile)
        tiles.append(tile)
    return jnp.concatenate(tiles, axis=0).astype(bf16)


def chunk_rows(i):
    return pl.ds(pl.multiple_of(i * CHUNK, CHUNK), CHUNK)


def norm_stats(ref, dim):
    cols = ref.shape[1]
    zero = jnp.zeros((8, cols), f32)
    total = lax.fori_loop(0, dim // CHUNK, lambda i, t: t + eights(ref[chunk_rows(i), :]), zero)
    mean = jnp.sum(total, axis=0, keepdims=True) / dim

    def spread_sq(i, t):
        v = ref[chunk_rows(i), :] - mean
        return t + eights(v * v)

    var = jnp.sum(lax.fori_loop(0, dim // CHUNK, spread_sq, zero), axis=0, keepdims=True) / dim
    return mean, lax.rsqrt(var + epsilon)


def front_body(
    seqs, table_ref, x_ref, xh_ref, own_ref, other_ref, own_small, other_small, after_ref,
    prm_ref, xn_ref, stat_ref, gate_ref, pair_ref, projx0_ref, projx_ref, mixed_ref, heads_ref, xs, xb,
):
    devices, _, width = x_ref.shape
    dim, cols = xn_ref.shape
    chans = dim // devices
    turns = devices // 2
    step = pl.program_id(0)

    @pl.when(step == 0)
    def _():
        for turn in range(turns):
            for ref, (device, _) in zip((own_small, other_small), slots(table_ref, turns, turn)):
                small = jnp.concatenate([ref[turn].astype(f32), jnp.zeros((LANE - PRM, LANE), f32)], axis=0)
                prm_ref[pl.ds(pl.multiple_of(device * chans, 8), chans), :] = small.T[:chans, :PRM]

        def gather(d, carry):
            at = pl.ds(pl.multiple_of(d * chans, 8), chans)
            row = side_by_side(x_ref[d].astype(f32), seqs)
            tail = xh_ref[d].astype(f32)
            tail = jnp.where(
                lanes_of((chans, LANE)) < LANE // 2, pltpu.roll(tail[chans : 2 * chans], LANE // 2, 1), tail[:chans]
            )
            xs[at, :] = jnp.concatenate([row, tail], axis=1)
            return carry

        lax.fori_loop(0, devices, gather, 0)
        mean, inverse = norm_stats(xs, dim)

        def scale(i, carry):
            at = chunk_rows(i)
            prm = prm_ref[at, :]
            v = (xs[at, :] - mean) * inverse * prm[:, 15:16] + prm[:, 16:17]
            xb[at, :] = v.astype(bf16)
            xn_ref[at, :] = v[:, :cols].astype(bf16)
            return carry

        lax.fori_loop(0, dim // CHUNK, scale, 0)
        stat_ref[0:8, :] = jnp.broadcast_to(mean[:, :cols], (8, cols))
        stat_ref[8:16, :] = jnp.broadcast_to(inverse[:, :cols], (8, cols))

    keep = (table_ref[turns + 1] > 0).astype(f32)
    for w_ref, (device, g) in zip((own_ref, other_ref), slots(table_ref, turns, step)):
        prm = prm_ref[pl.ds(pl.multiple_of(device * chans, 8), chans), :]
        proj = mm16(w_ref[0, PRM:, :], xb[...], NN)
        ys = []
        px = []
        for i in range(3):
            x = proj[i * chans : (i + 1) * chans] + prm[:, i : i + 1]
            tail = x[:, cols:] * keep
            px += [jnp.concatenate([x[:, :cols], tail], axis=1)]
            weights = [jnp.broadcast_to(prm[:, 6 + 3 * j + i : 7 + 3 * j + i], (chans, width)) for j in range(KS)]
            bias = jnp.broadcast_to(prm[:, 3 + i : 4 + i], (chans, width))
            parts = []
            for s in range(seqs):
                v = x[:, s * width : (s + 1) * width]
                wide = jnp.concatenate([tail if s == 0 else pltpu.roll(tail, LANE // 2, 1), v], axis=1)
                y = bias + weights[0] * v
                for j in range(1, KS):
                    y = y + weights[j] * pltpu.roll(wide, j, 1)[:, LANE:]
                parts.append(y)
            ys.append(jnp.concatenate(parts, axis=1))
        projx0_ref[g] = px[0].astype(bf16)
        projx_ref[g] = jnp.concatenate(px[1:], axis=0).astype(bf16)
        gate_ref[g] = ys[0]
        pair = jnp.concatenate(ys[1:], axis=0)
        pair_ref[g] = pair
        mixed_ref[g] = stacked(ys[1] * ys[2], seqs).astype(bf16)
        heads_ref[g] = first_tokens(pair, seqs).astype(bf16)


def first_tokens(values, seqs):
    rows, width = values.shape[0], values.shape[1] // seqs
    pad = jnp.zeros((LANE - rows, LANE), f32)
    heads = []
    for s in range(seqs):
        tile = values[:, s * width : s * width + LANE]
        heads.append((jnp.concatenate([tile, pad], axis=0) if rows < LANE else tile).T[:8])
    return jnp.concatenate(heads, axis=0)


def token_columns(heads, rows):
    gap = jnp.zeros((LANE // 2 - 8, LANE), f32)
    return jnp.concatenate([heads[:8], gap, heads[8:], gap], axis=0).T[:rows]


def whole(a):
    return pl.BlockSpec(a.shape, lambda i, t: (0,) * len(a.shape), pipeline_mode=pl.Buffered(1))


def untouched():
    return pl.BlockSpec(memory_space=pl.ANY)


def by_chip(a):
    return pl.BlockSpec((2,) + a.shape[1:], lambda i, t: (t[i],) + (0,) * (len(a.shape) - 1))


def by_turn(a, rows=None):
    return pl.BlockSpec((1, a.shape[1] if rows is None else rows, a.shape[2]), lambda i, t: (i, 0, 0))


def chip_call(us, body, table, turns, args, in_specs, out, out_specs, scratch):
    return pl.pallas_call(
        body,
        cost_estimate=takes(us),
        out_shape=out,
        grid_spec=pltpu.PrefetchScalarGridSpec(
            num_scalar_prefetch=1,
            grid=(turns,),
            in_specs=in_specs,
            out_specs=out_specs,
            scratch_shapes=scratch,
        ),
        compiler_params=pltpu.CompilerParams(vmem_limit_bytes=vmem_limit, dimension_semantics=("arbitrary",)),
    )(table, *args)


def slots(table_ref, turns, step):
    core = table_ref[turns]
    chip = table_ref[step]
    return ((2 * chip + core, core), (2 * chip + 1 - core, 1 - core))


def front(table, x, xh, own, other, before, seqs):
    devices, rows, width = x.shape
    chans = rows // seqs
    dim = devices * chans
    cols = seqs * width
    turns = devices // 2
    sd = jax.ShapeDtypeStruct
    out = (
        sd((dim, PRM), f32),
        sd((dim, cols), bf16),
        sd((16, cols), f32),
        sd((devices, chans, cols), f32),
        sd((devices, 2 * chans, cols), f32),
        sd((devices, chans, cols + LANE), bf16),
        sd((devices, 2 * chans, cols + LANE), bf16),
        sd((devices, rows, width), bf16),
        sd((devices, 8 * seqs, LANE), bf16),
    )
    small = pl.BlockSpec((turns, PRM, LANE), lambda i, t: (0, 0, 0), pipeline_mode=pl.Buffered(1))
    return chip_call(
        2,
        lambda *refs: front_body(seqs, *refs),
        table,
        turns,
        (x, xh, own, other, own, other, before),
        [whole(x), whole(xh), by_turn(own), by_turn(other), small, small, untouched()],
        out,
        tuple(whole(o) for o in out[:3]) + tuple(by_chip(o) for o in out[3:]),
        [pltpu.VMEM((dim, cols + LANE), f32), pltpu.VMEM((dim, cols + LANE), bf16)],
    )


def middle_body(seqs, pieces, segments, per, table_ref, conv_ref, x_ref, cot_ref, gate_ref, prm_ref, *refs):
    weights = []
    for _ in range(pieces):
        weights.append([[refs[2 * (segments * core + n) : 2 * (segments * core + n) + 2] for n in range(segments)] for core in range(2)])
        refs = refs[4 * segments :]
    layer_ref, d_conv_ref, d_res_ref, p0_ref, p0h_ref = refs[:5]
    grads = [[refs[5 + segments * (2 * p + n) : 5 + segments * (2 * p + n + 1)] for n in range(2)] for p in range(pieces)]
    refs = refs[5 + 2 * pieces * segments :]
    cs, res, ds, xb, db, gb, acc_out, acc_in, folds, up_folds, stats, out_w32, out_w_ref, gs = refs
    devices, _, width = x_ref.shape
    dim, cols = d_res_ref.shape
    chans = dim // devices
    hid = weights[0][0][0][0].shape[1] // 2 * pieces
    turns = devices // 2
    part, some_hid, some_out = dim // pieces, hid // pieces, chans // pieces
    group = table_ref[turns + 2 + seqs] if pieces == 2 else 0
    halves = [group, 1 - group][:pieces]
    columns = [pl.ds(pl.multiple_of(h * part, LANE), part) for h in halves]
    step = pl.program_id(0)
    last = pl.num_programs(0) - 1
    lane = lanes_of((1, cols))
    live = jnp.zeros((1, cols), f32)
    for s in range(seqs):
        position = table_ref[turns + 1] * width + lane - s * width
        inside = (lane >= s * width) & (lane < (s + 1) * width) & (position < table_ref[turns + 2 + s])
        live = jnp.where(inside, 1.0, live)

    def device_rows(d):
        return pl.ds(pl.multiple_of(d * chans, 8), chans)

    @pl.when(step == 0)
    def _():
        def gather(d, carry):
            at = device_rows(d)
            cs[at, :] = side_by_side(conv_ref[d].astype(f32), seqs)
            res[at, :] = side_by_side(x_ref[d].astype(f32), seqs)
            ds[at, :] = live * side_by_side(cot_ref[d].astype(f32), seqs)
            return carry

        lax.fori_loop(0, devices, gather, 0)
        for piece, h in zip(weights, halves):
            for core, parts in enumerate(piece):
                turn = 0
                for _, out_rows in parts:
                    for n in range(out_rows.shape[0]):
                        device, _ = slots(table_ref, turns, turn)[core]
                        at = pl.ds(pl.multiple_of(device * chans + h * some_out, 8), some_out)
                        out_w32[at, :] = out_rows[n].astype(f32)
                        turn += 1

        def gated(i, carry):
            at = chunk_rows(i)
            out_w_ref[at, :] = out_w32[at, :].astype(bf16)
            gb[at, :] = (cs[at, :] * gate_ref[at, :]).astype(bf16)
            d = ds[at, :]
            db[at, :] = d.astype(bf16)
            folds[3, at, :] = folded(d)
            acc_in[at, :] = jnp.zeros((CHUNK, cols), f32)
            return carry

        lax.fori_loop(0, dim // CHUNK, gated, 0)
        acc_out[...] = mm16(out_w_ref[...], gb[...], TN)

        def add(i, carry):
            at = chunk_rows(i)
            res[at, :] = res[at, :] + acc_out[at, :] + prm_ref[at, 19:20]
            acc_out[at, :] = jnp.zeros((CHUNK, cols), f32)
            return carry

        lax.fori_loop(0, dim // CHUNK, add, 0)
        mean, inverse = norm_stats(res, dim)

        def scale(i, carry):
            at = chunk_rows(i)
            normed = (res[at, :] - mean) * inverse
            cs_norm = normed * prm_ref[at, 17:18] + prm_ref[at, 18:19]
            xb[at, :] = cs_norm.astype(bf16)
            return carry

        lax.fori_loop(0, dim // CHUNK, scale, 0)
        stats[0:8, :] = jnp.broadcast_to(mean, (8, cols))
        stats[8:16, :] = jnp.broadcast_to(inverse, (8, cols))

    pair = [device for j in range(per) for device, _ in slots(table_ref, turns, step * per + j)]
    up_b = []
    for device in pair:
        prm = prm_ref[device_rows(device), :]
        for h in halves:
            for m in range(some_hid // chans):
                first, second = 21 + m, 21 + m + (pieces - 1) * some_hid // chans
                up_b.append(jnp.where(h == 0, prm[:, first : first + 1], prm[:, second : second + 1]))
    up_b = jnp.concatenate(up_b, axis=0)

    def now(parts, rows, j):
        blocks = [ref[j, rows, :] for ref, _ in parts]
        return blocks[0] if len(blocks) == 1 else jnp.where(step * per < turns // 2, blocks[0], blocks[1])

    def rows_now(rows):
        return jnp.concatenate(
            [now(piece[core], rows, j) for j in range(per) for core in range(2) for piece in weights], axis=0
        )

    up, down = rows_now(slice(0, some_hid)), rows_now(slice(some_hid, 2 * some_hid))
    u = mm16(up, xb[...], NN) + up_b
    d_act = mm16(down, db[...], NN)
    a, k = 0.044715, math.sqrt(2.0 / math.pi)
    sq = u * u
    t = jnp.tanh(u * (k + (k * a) * sq))
    half = 0.5 * (1.0 + t)
    act = (u * half).astype(bf16)
    d_u = d_act * (half + 0.5 * u * (1.0 - t * t) * (k + (3.0 * k * a) * sq))
    d_low = d_u.astype(bf16)
    fold = folded(d_u)
    acc_out[...] += mm16(down, act, TN)
    acc_in[...] += mm16(up, d_low, TN)
    spots = [(n, p, h) for n in range(2 * per) for p, h in enumerate(halves)]
    for n, p, h in spots:
        rows = slice((n * pieces + p) * some_hid, (n * pieces + p + 1) * some_hid)
        up_folds[pl.ds(pl.multiple_of(pair[n] * hid + h * some_hid, 8), some_hid), :] = fold[rows]
    gs[0] = mm16(d_low, xb[...], NT).astype(bf16)
    gs[1] = mm16(act, db[...], NT).astype(bf16)

    def hand_out(k):
        for n, p, h in spots:
            rows = slice((n * pieces + p) * some_hid, (n * pieces + p + 1) * some_hid)
            for which in range(2):
                at = pl.ds(pl.multiple_of(which * hid + h * some_hid, some_hid), some_hid)
                for g_refs, some in zip(grads, columns):
                    g_refs[n % 2][k][step * per + n // 2 - k * (turns // segments), at, :] = gs[which, rows, some]

    for k in range(segments):
        count = turns // segments
        pl.when((step * per >= k * count) & (step * per < (k + 1) * count))(functools.partial(hand_out, k))

    @pl.when(step == last)
    def _():
        mean, inverse = stats[0:1, :], stats[8:9, :]

        def result(i, t):
            at = chunk_rows(i)
            r = res[at, :]
            acc_out[at, :] = live * (r + acc_out[at, :] + prm_ref[at, 20:21])
            normed = (r - mean) * inverse
            d = acc_in[at, :]
            both = d * normed
            folds[0, at, :] = folded(both)
            folds[1, at, :] = folded(d)
            gain = prm_ref[at, 17:18]
            return t[0] + eights(d * gain), t[1] + eights(both * gain)

        zero = jnp.zeros((8, cols), f32)
        m1, m2 = lax.fori_loop(0, dim // CHUNK, result, (zero, zero))
        m1 = jnp.sum(m1, axis=0, keepdims=True) / dim
        m2 = jnp.sum(m2, axis=0, keepdims=True) / dim

        def residual(i, carry):
            at = chunk_rows(i)
            normed = (res[at, :] - mean) * inverse
            d = ds[at, :] + inverse * (acc_in[at, :] * prm_ref[at, 17:18] - m1 - normed * m2)
            d_res_ref[at, :] = d
            folds[2, at, :] = folded(d)
            db[at, :] = d.astype(bf16)
            return carry

        lax.fori_loop(0, dim // CHUNK, residual, 0)
        for n in range(dim // 256):
            some = slice(n * 256, (n + 1) * 256)
            acc_in[some, :] = mm16(out_w_ref[some, :], db[...], NN)
            out_w32[some, :] = mm16(gb[some, :], db[...], NT)
        for g_refs, at in zip(grads, columns):
            for turn in range(turns):
                for g_ref, (device, _) in zip(g_refs, slots(table_ref, turns, turn)):
                    count = turns // segments
                    g_ref[turn // count][turn % count, 2 * hid :, :] = out_w32[device_rows(device), at].astype(bf16)

        def products(i, carry):
            at = chunk_rows(i)
            d = acc_in[at, :]
            p0 = d * cs[at, :]
            p0_ref[at, :] = p0
            acc_in[at, :] = d * gate_ref[at, :]
            return carry

        lax.fori_loop(0, dim // CHUNK, products, 0)

        def scatter(d, carry):
            at = device_rows(d)
            p0h_ref[d] = first_tokens(p0_ref[at, :], seqs).astype(bf16)
            layer_ref[d, : seqs * chans, :] = stacked(acc_out[at, :], seqs).astype(bf16)
            d_conv_ref[d] = stacked(acc_in[at, :], seqs).astype(bf16)
            totals = [padded_totals(folds[q, at, :], width)[0] for q in range(4)]
            totals += padded_totals(up_folds[pl.ds(pl.multiple_of(d * hid, 8), hid), :], width)
            layer_ref[d, seqs * chans :, :] = as_rows(totals, SUM_ROWS)
            return carry

        lax.fori_loop(0, devices, scatter, 0)


def middle(table, conv, x, cot, gate, matrices, prm, hid, seqs):
    devices, rows, width = conv.shape
    dim, cols = gate.shape
    chans = dim // devices
    turns = devices // 2
    pieces, segments = len(matrices), len(matrices[0][0])
    part, some_hid, some_out = dim // pieces, hid // pieces, chans // pieces
    sd = jax.ShapeDtypeStruct
    out = (
        sd((devices, rows + SUM_ROWS, width), bf16),
        sd((devices, rows, width), bf16),
        sd((dim, cols), f32),
        sd((dim, cols), f32),
        sd((devices, 8 * seqs, LANE), bf16),
    ) + (sd((turns // segments, 2 * hid + chans, part), bf16),) * (2 * pieces * segments)
    big = pltpu.VMEM((dim, cols), f32)
    low = pltpu.VMEM((dim, cols), bf16)
    args, specs = [conv, x, cot, gate, prm], [whole(conv), whole(x), whole(cot), whole(gate), whole(prm)]
    per = 2
    for piece in matrices:
        for parts in piece:
            first = 0
            for a in parts:
                count = a.shape[0]
                args += [a, a]
                specs += [
                    pl.BlockSpec(
                        (per, 2 * some_hid, dim),
                        lambda i, t, f=first // per, c=count // per: (jnp.clip(i - f, 0, c - 1), 0, 0),
                    ),
                    pl.BlockSpec(
                        (count, some_out, dim), lambda i, t: (0, 2 * some_hid // some_out, 0), pipeline_mode=pl.Buffered(1)
                    ),
                ]
                first += count
    return chip_call(
        36,
        lambda *refs: middle_body(seqs, pieces, segments, per, *refs),
        table,
        turns // per,
        args,
        specs,
        out,
        tuple(whole(o) for o in out),
        [
            big, big, big, low, low, low, big, big, pltpu.VMEM((4, dim, LANE), f32),
            pltpu.VMEM((devices * hid, LANE), f32), pltpu.VMEM((16, cols), f32), pltpu.VMEM((dim, dim), f32),
            pltpu.VMEM((dim, dim), bf16), pltpu.VMEM((2, 2 * per * hid, dim), bf16),
        ],
    )


def short_back(seqs, prm, kinds, d_short, head, projx, width, cols):
    chans = prm.shape[0]
    d_proj = []
    totals = [[] for _ in range(2 + KS)]
    for n, i in enumerate(kinds):
        px = projx[n * chans : (n + 1) * chans]
        weights = [jnp.broadcast_to(prm[:, 6 + 3 * j + i : 7 + 3 * j + i], (chans, width)) for j in range(KS)]
        parts = []
        sums = [0.0] * (2 + KS)
        for s in range(seqs):
            at = slice(s * width, (s + 1) * width)
            d = d_short[n][:, at]
            x = px[:, at]
            tail = px[:, cols:]
            wide = jnp.concatenate([tail if s == 0 else pltpu.roll(tail, LANE // 2, 1), x], axis=1)
            after = jnp.concatenate([d, head[n] if s == 0 else pltpu.roll(head[n], LANE // 2, 1)], axis=1)
            y = weights[0] * d
            sums[1] = sums[1] + folded(d)
            sums[2] = sums[2] + folded(d * x)
            for j in range(1, KS):
                y = y + weights[j] * pltpu.roll(after, width + LANE - j, 1)[:, :width]
                sums[2 + j] = sums[2 + j] + folded(d * pltpu.roll(wide, j, 1)[:, LANE:])
            sums[0] = sums[0] + folded(y)
            parts.append(y)
        d_proj.append(jnp.concatenate(parts, axis=1))
        for k in range(2 + KS):
            totals[k].append(sums[k])
    d_low = jnp.concatenate(d_proj, axis=0).astype(bf16)
    return d_low, padded_totals(jnp.concatenate(sum(totals, []), axis=0), width)


def back_gate_body(seqs, table_ref, p0_ref, p0h_ref, projx_ref, own_ref, other_ref, prm_ref, xn_ref, g_ref, sums_ref, acc):
    dim, cols = xn_ref.shape
    chans = p0_ref.shape[1]
    step = pl.program_id(0)

    @pl.when(step == 0)
    def _():
        acc[...] = jnp.zeros_like(acc)

    turns = prm_ref.shape[0] // chans // 2
    for w_ref, (device, g) in zip((own_ref, other_ref), slots(table_ref, turns, step)):
        prm = prm_ref[pl.ds(pl.multiple_of(device * chans, 8), chans), :]
        d_low, totals = short_back(
            seqs, prm, (0,), (p0_ref[g],), (token_columns(p0h_ref[g].astype(f32), chans),), projx_ref[g].astype(f32), cols // seqs, cols
        )
        sums_ref[g] = totals[0]
        acc[...] += mm16(w_ref[0, PRM : PRM + chans, :], d_low, TN)
        g_ref[g] = mm16(d_low, xn_ref[...], NT).astype(bf16)


def back_gate(table, p0, p0h, projx, own, other, prm, xn, seqs):
    devices, chans, cols = p0.shape
    dim = xn.shape[0]
    sd = jax.ShapeDtypeStruct
    out = (
        sd((devices, chans, dim), bf16),
        sd((devices, 8, cols // seqs), f32),
        sd((dim, cols), f32),
    )
    return chip_call(
        2,
        lambda *refs: back_gate_body(seqs, *refs),
        table,
        devices // 2,
        (p0, p0h, projx, own, other, prm, xn),
        [by_chip(a) for a in (p0, p0h, projx)] + [by_turn(own), by_turn(other), whole(prm), whole(xn)],
        out,
        (by_chip(out[0]), by_chip(out[1]), whole(out[2])),
        [],
    )


def back_body(
    seqs, table_ref, d_mixed_ref, pair_ref, heads_ref, projx_ref, own_ref, other_ref, prm_ref, xn_ref, x_ref, stat_ref, d_res_ref,
    acc0_ref, sums0_ref, tail_ref, g_ref, acc, xs, folds, sums,
):
    devices, _, width = x_ref.shape
    dim, cols = xn_ref.shape
    chans = dim // devices
    step = pl.program_id(0)
    last = pl.num_programs(0) - 1

    @pl.when(step == 0)
    def _():
        acc[...] = acc0_ref[...]

    turns = devices // 2
    for w_ref, (device, g) in zip((own_ref, other_ref), slots(table_ref, turns, step)):
        prm = prm_ref[pl.ds(pl.multiple_of(device * chans, 8), chans), :]
        block = d_mixed_ref[g].astype(f32)
        d_mixed = side_by_side(block[: seqs * chans], seqs)
        square = jnp.concatenate([block[seqs * chans :, :LANE], jnp.zeros((LANE - HEAD_ROWS, LANE), f32)], axis=0).T
        second = pltpu.roll(square[chans : 2 * chans], LANE // 2, 1)
        d_head = jnp.where(lanes_of((chans, LANE)) < LANE // 2, square[:chans], second)
        pair = pair_ref[g]
        pair_head = token_columns(heads_ref[g].astype(f32), 2 * chans)
        d_short = (d_mixed * pair[chans:], d_mixed * pair[:chans])
        head = (d_head * pair_head[chans:], d_head * pair_head[:chans])
        d_low, totals = short_back(seqs, prm, (1, 2), d_short, head, projx_ref[g].astype(f32), width, cols)
        for n, t in enumerate(totals):
            sums[n, device] = t
        acc[...] += mm16(w_ref[0, PRM + chans :, :], d_low, TN)
        g_ref[g] = mm16(d_low, xn_ref[...], NT).astype(bf16)

    @pl.when(step == last)
    def _():
        def gather(d, carry):
            xs[pl.ds(pl.multiple_of(d * chans, 8), chans), :] = side_by_side(x_ref[d].astype(f32), seqs)
            return carry

        lax.fori_loop(0, devices, gather, 0)
        mean, inverse = stat_ref[0:1, :], stat_ref[8:9, :]

        def first(i, t):
            at = chunk_rows(i)
            normed = (xs[at, :] - mean) * inverse
            d = acc[at, :]
            both = d * normed
            folds[0, at, :] = folded(both)
            folds[1, at, :] = folded(d)
            gain = prm_ref[at, 15:16]
            return t[0] + eights(d * gain), t[1] + eights(both * gain)

        zero = jnp.zeros((8, cols), f32)
        m1, m2 = lax.fori_loop(0, dim // CHUNK, first, (zero, zero))
        m1 = jnp.sum(m1, axis=0, keepdims=True) / dim
        m2 = jnp.sum(m2, axis=0, keepdims=True) / dim

        def second(i, carry):
            at = chunk_rows(i)
            normed = (xs[at, :] - mean) * inverse
            acc[at, :] = d_res_ref[at, :] + inverse * (acc[at, :] * prm_ref[at, 15:16] - m1 - normed * m2)
            return carry

        lax.fori_loop(0, dim // CHUNK, second, 0)

        rows = seqs * chans

        def scatter(d, carry):
            at = pl.ds(pl.multiple_of(d * chans, 8), chans)
            tail_ref[d, :rows, :] = stacked(acc[at, :], seqs).astype(bf16)
            totals = [sums0_ref[d]] + [sums[n, d] for n in range(sums.shape[0])]
            totals += [padded_totals(folds[q, at, :], width)[0] for q in range(2)]
            tail_ref[d, rows : rows + SUM_ROWS, :] = as_rows(totals, SUM_ROWS)
            return carry

        lax.fori_loop(0, devices, scatter, 0)


def back(table, d_mixed, pair, heads, projx, own, other, prm, xn, x, stat, d_res, acc0, sums0, seqs):
    devices, rows, width = x.shape
    dim, cols = xn.shape
    chans = dim // devices
    sd = jax.ShapeDtypeStruct
    pieces = -(-2 * (2 + KS) * chans // width)
    out = (
        sd((devices, rows + SUM_ROWS, width), bf16),
        sd((devices, 2 * chans, dim), bf16),
    )
    return chip_call(
        100,
        lambda *refs: back_body(seqs, *refs),
        table,
        devices // 2,
        (d_mixed, pair, heads, projx, own, other, prm, xn, x, stat, d_res, acc0, sums0),
        [by_chip(a) for a in (d_mixed, pair, heads, projx)]
        + [by_turn(own), by_turn(other), whole(prm), whole(xn), whole(x)]
        + [whole(a) for a in (stat, d_res, acc0, sums0)],
        out,
        (whole(out[0]), by_chip(out[1])),
        [
            pltpu.VMEM((dim, cols), f32), pltpu.VMEM((dim, cols), f32), pltpu.VMEM((2, dim, LANE), f32),
            pltpu.VMEM((pieces, devices, 8, width), f32),
        ],
    )


def position_table():
    places = np.arange(LMAX)
    orders = np.arange(1, (EMB - 1) // 2 + 1)
    turns = 2.0 * math.pi * ((orders[:, None] * places[None, :]) % LMAX) / LMAX
    ramp = places[None, :] / (LMAX - 1)
    return np.concatenate([ramp, np.cos(turns), -np.sin(turns)], axis=0).astype(np.float32)


FEAT = position_table()


def mm(a, b, dims):
    return lax.dot_general(a, b, (dims, ((), ())), precision=highest, preferred_element_type=f32)


NN = ((1,), (0,))
TN = ((0,), (0,))
NT = ((1,), (1,))


def mm_split(a, b, dims):
    a_upper, b_upper = a.astype(bf16), b.astype(bf16)
    a_lower, b_lower = (a - a_upper.astype(f32)).astype(bf16), (b - b_upper.astype(f32)).astype(bf16)
    return mm16(a_upper, b_upper, dims) + mm16(a_lower, b_upper, dims) + mm16(a_upper, b_lower, dims)


def filter_back_body(d_ref, raw_ref, fall_ref, h1_ref, h2_ref, c1_ref, c2_ref, pre1_ref, pre2_ref, feat_ref, mid_ref, last_ref, rate_ref,
                     g_in_ref, g_mid_ref, g_last_ref, g_rows_ref, g_decay_ref):
    chans = d_ref.shape[0]
    d = d_ref[...]
    q = d * (fall_ref[...] + decay_floor)
    g_last_ref[...] = mm_split(h2_ref[...], q, NT)
    decay = folded(d * raw_ref[...] * fall_ref[...] * feat_ref[0:1, :])
    g_decay_ref[...] = -jnp.sum(decay, axis=1, keepdims=True)
    u2 = mm_split(last_ref[...], q, NN) * c2_ref[...]
    rate = rate_ref[...]
    fu2 = rate * u2
    u1 = mm_split(mid_ref[...], fu2, NN) * c1_ref[...]
    fu1 = rate * u1
    g_in_ref[...] = mm_split(feat_ref[...], fu1, NT)
    g_mid_ref[...] = mm_split(h1_ref[...], fu2, NT)
    rows = jnp.concatenate([folded(fu1), folded(fu2), folded(u2 * pre2_ref[...] + u1 * pre1_ref[...])], axis=0)
    extra = jnp.zeros((-rows.shape[0] % LANE, LANE), f32)
    g_rows_ref[...] = row_totals(jnp.concatenate([rows, extra], axis=0))


def filter_back(*args):
    chans, ford, taps = args[0].shape[0], args[3].shape[0], args[9].shape[0]
    sd = jax.ShapeDtypeStruct
    out = (sd((taps, ford), f32), sd((ford, ford), f32), sd((ford, chans), f32), sd((8, -(-3 * ford // LANE) * LANE), f32), sd((chans, 1), f32))
    return whole_call(0.01, filter_back_body, out, [], *args)


def mm16(a, b, dims):
    return lax.dot_general(a, b, (dims, ((), ())), preferred_element_type=f32)


def ring_of(chips):
    zs = 4
    ys = chips // zs
    order = [(z, 0) for z in range(zs)]
    for y in range(1, ys):
        order += [(z, y) for z in (range(zs - 1, 0, -1) if y % 2 else range(1, zs))]
    order += [(0, y) for y in range(ys - 1, 0, -1)]
    return [z * ys + y for z, y in order]


def after(values, *others):
    return lax.optimization_barrier((values,) + others)[0]


def ring_hop(values, ring, by):
    chips = len(ring)
    moves = [(2 * ring[p] + q, 2 * ring[(p + by) % chips] + q) for p in range(chips) for q in range(2)]
    return lax.ppermute(values, "chan", moves)


class RingGather:
    def __init__(self, shard, ring):
        self.ring, self.hops = ring, len(ring) // 2
        self.cut = shard.shape[0] // 32 * 16
        self.behind, self.ahead = [shard], [shard]
        self.far = None

    def advance(self, upto, *others):
        while len(self.behind) <= min(upto, self.hops - 1):
            first, second = self.behind[-1], self.ahead[-1]
            if others:
                first, second = after(first, *others), after(second, *others)
            self.behind.append(ring_hop(first, self.ring, 1))
            self.ahead.append(ring_hop(second, self.ring, -1))
        if upto == self.hops:
            first, second = self.behind[-1][: self.cut], self.ahead[-1][self.cut :]
            if others:
                first, second = after(first, *others), after(second, *others)
            self.far = jnp.concatenate([ring_hop(first, self.ring, 1), ring_hop(second, self.ring, -1)], axis=0)

    def shards(self):
        return self.behind + self.ahead[1:] + [self.far]


def both_cores(shards):
    own = stack(shards)
    return own, lax.ppermute(own, "chan", [(i, i ^ 1) for i in range(2 * len(shards))])


def stack_body(*refs):
    for i, ref in enumerate(refs[:-1]):
        refs[-1][i] = ref[...]


def stack(shards):
    out = jax.ShapeDtypeStruct((len(shards),) + shards[0].shape, shards[0].dtype)
    return whole_call(0.01, stack_body, out, [], *shards)


def turn_table(ring):
    chips = len(ring)
    steps = [0] + [-k for k in range(1, chips // 2)] + [k for k in range(1, chips // 2)] + [chips // 2]
    table = np.zeros((chips, chips), np.int32)
    for p, chip in enumerate(ring):
        table[chip] = [ring[(p + k) % chips] for k in steps]
    return table


def exchange(values):
    return lax.all_to_all(values, "chan", split_axis=0, concat_axis=0, tiled=True)


def on_device(
    layer_in,
    seq_lengths,
    ln1_gain,
    first_norm_bias,
    in_weight,
    in_bias,
    short_weight,
    short_bias,
    filt_in,
    filt_in_bias,
    filt_mid,
    filt_mid_bias,
    sine_freq,
    filt_out,
    decay_rate,
    conv_bias,
    out_weight,
    out_bias,
    ln2_gain,
    second_norm_bias,
    up_weight,
    up_bias,
    down_weight,
    down_bias,
    cotangent,
):
    seqs, chans, _ = layer_in.shape
    devices = lax.axis_size("chan")
    groups = lax.axis_size("batch")
    width = LMAX // devices
    dim = chans * devices
    cols = seqs * width
    hid = up_weight.shape[0]
    ford = filt_mid.shape[0]
    place = lax.axis_index("chan")

    def to_blocks(values):
        return (
            values.reshape(seqs, chans, devices, width)
            .transpose(2, 0, 1, 3)
            .reshape(devices, seqs * chans, width)
        )

    def from_blocks(blocks):
        return (
            blocks.reshape(devices, seqs, chans, width)
            .transpose(1, 2, 0, 3)
            .reshape(seqs, chans, LMAX)
        )

    small = jnp.concatenate(
        [
            in_bias,
            short_bias,
            short_weight.reshape(3 * KS, chans),
            jnp.stack([ln1_gain, first_norm_bias, ln2_gain, second_norm_bias, out_bias, down_bias]),
            up_bias.reshape(hid // chans, chans),
        ],
        axis=0,
    )
    small = jnp.pad(small, ((0, PRM - small.shape[0]), (0, dim - chans)))
    in_rows = in_weight.transpose(1, 2, 0).reshape(3 * chans, dim)
    ring = ring_of(devices // 2)
    chips = devices // 2
    core = place % 2
    batch = lax.axis_index("batch")
    swap = [(0, 1), (1, 0)]
    partner = [(i, i ^ 1) for i in range(devices)]
    turns = lax.dynamic_index_in_dim(jnp.asarray(turn_table(ring)), place // 2, 0, False)
    table = jnp.concatenate(
        [turns, jnp.stack([core, place]).astype(jnp.int32), seq_lengths, batch.astype(jnp.int32).reshape(1)]
    )
    late = [up_weight, down_weight, out_weight]
    stepped = groups == 2 and chips == 8 and dim % (2 * LANE) == 0
    beside = [(i, i ^ 2) for i in range(devices)]
    along = [list(range(k, devices, 4)) for k in range(4)]

    def to_partner(values):
        return lax.ppermute(values, "chan", partner)

    if stepped:
        late = [lax.dynamic_slice_in_dim(a, batch * (a.shape[0] // 2), a.shape[0] // 2, 0) for a in late]
        late = jnp.concatenate(late, axis=0)
        near = lax.all_gather(late, "chan", axis=0, axis_index_groups=along)
    else:
        late = jnp.concatenate(late, axis=0)
        late = lax.all_gather(late, "chan", axis=0).reshape((chips, 2) + late.shape)
    first = RingGather(after(jnp.concatenate([small, in_rows], axis=0), late) if stepped else jnp.concatenate([small, in_rows], axis=0), ring)
    first.advance(chips // 8)
    x = exchange(to_blocks(layer_in))
    rows = seqs * chans
    xh = lax.ppermute(x[:, :rows, width - LANE :], "chan", [(i, i + 1) for i in range(devices - 1)])

    feat = jnp.asarray(FEAT)
    ramp = feat[0:1]
    rate = sine_freq[:, None]
    pre1 = mm(filt_in, feat, TN) + filt_in_bias[:, None]
    h1, c1 = jnp.sin(rate * pre1), jnp.cos(rate * pre1)
    pre2 = mm(filt_mid, h1, TN) + filt_mid_bias[:, None]
    h2, c2 = jnp.sin(rate * pre2), jnp.cos(rate * pre2)
    raw = mm(filt_out, h2, TN)
    falling = jnp.exp(-ramp * decay_rate[:, None])
    first.advance(chips // 4, h1)
    filt = raw * (falling + decay_floor)
    first.advance(3 * chips // 8, filt, x)
    filt_spec = filter_spectrum(filt)
    first.advance(chips // 2, filt_spec)
    in_own, in_other = both_cores(first.shards())
    bias_col = conv_bias[:, None]

    prm, xn1, stat1, gate, pair, projx0, projx, mixed, heads = front(
        table, x, xh, in_own, in_other, filt_spec, seqs
    )
    mixed_chan = exchange(mixed)
    cot = exchange(after(to_blocks(cotangent), mixed_chan))
    if stepped:
        near = after(near, mixed)
        far = lax.ppermute(near, "chan", beside)
        near_across = lax.ppermute(near, "batch", swap)
        near_other = to_partner(near)
    backward_hop = [(i + 1, i) for i in range(devices - 1)]
    heads = lax.ppermute(heads, "chan", backward_hop)
    conv_chan, mixed_spec = conv_forward(mixed_chan, filt_spec, bias_col, seqs)
    conv = exchange(after(conv_chan, near_across, cot, heads) if stepped else conv_chan)
    if stepped:
        far, near_across = after(far, conv_chan), after(near_across, conv_chan)
        far_across = lax.ppermute(far, "batch", swap)
        far_other, near_across_other = to_partner(far), to_partner(near_across)
        far_across_other = to_partner(far_across)
        matrices = [
            [[near, far], [near_other, far_other]],
            [[near_across, far_across], [near_across_other, far_across_other]],
        ]
        z = lax.iota(jnp.int32, 4) * 2
        y = (place // 2 % 2).astype(jnp.int32)
        order = jnp.concatenate([z + y, z + 1 - y])
    else:
        matrices = [[[lax.dynamic_index_in_dim(late, core, 1, False)], [lax.dynamic_index_in_dim(late, 1 - core, 1, False)]]]
        order = lax.iota(jnp.int32, chips)
    order = jnp.concatenate([order, table[chips:]])

    results = middle(order, conv, x, cot, gate.reshape(dim, cols), matrices, prm, hid, seqs)
    layer, d_conv, d_res, p0, p0h = results[:5]
    d_conv_chan = exchange(d_conv)
    p0h = lax.ppermute(p0h, "chan", backward_hop)

    def added(*values):
        return sum(v.astype(f32) for v in values).astype(bf16)

    if stepped:
        near_mine, far_mine = (results[5], results[7]), (results[6], results[8])
        near_theirs, far_theirs = (results[9], results[11]), (results[10], results[12])
        far_theirs = added(far_theirs[0], to_partner(far_theirs[1]))
        d_conv_chan = after(d_conv_chan, far_theirs)
        far_theirs = lax.ppermute(far_theirs, "batch", swap)
        near_theirs = added(near_theirs[0], to_partner(after(near_theirs[1], d_conv_chan)))
        near_theirs = lax.ppermute(after(near_theirs, far_theirs), "batch", swap)
        far_mine = far_mine[0], to_partner(after(far_mine[1], d_conv_chan))
        near_mine = near_mine[0], to_partner(after(near_mine[1], d_conv_chan))
    else:
        early = added(results[5], to_partner(results[6]))

    if groups == 2:
        same_core = [list(range(q, devices, 2)) for q in range(2)]
    else:
        same_core = [[b * devices + c for b in range(groups) for c in range(q, devices, 2)] for q in range(2)]

    def batch_total(values):
        return values + lax.ppermute(values, "batch", swap) if groups == 2 else lax.psum(values, "batch")

    def over_batch(table):
        if groups != 2:
            return lax.psum_scatter(table.astype(f32), "batch", scatter_dimension=1, tiled=True)
        part = dim // 2
        axis = table.ndim - 1
        mine = lax.axis_index("batch") * part
        theirs = lax.dynamic_slice_in_dim(table, part - mine, part, axis)
        kept = lax.dynamic_slice_in_dim(table, mine, part, axis)
        return kept.astype(f32) + lax.ppermute(theirs, "batch", swap).astype(f32)

    def over_chip(table):
        table = table.reshape((devices // 2, 2) + table.shape[1:])
        own = lax.dynamic_index_in_dim(table, core, 1, False)
        theirs = lax.dynamic_index_in_dim(table, 1 - core, 1, False)
        return (own.astype(f32) + lax.ppermute(theirs, "chan", partner).astype(f32)).astype(bf16)

    def over_groups(both):
        return over_batch(both).astype(bf16) if groups == 2 else both

    def over_chips(both):
        rows = both.shape[1]
        if groups == 2:
            both = lax.all_to_all(
                both, "chan", split_axis=0, concat_axis=0, tiled=True, axis_index_groups=same_core
            )
        else:
            both = both.reshape(devices // 2, rows, groups, dim // groups).transpose(2, 0, 1, 3)
            both = lax.all_to_all(
                both.reshape(groups * devices // 2, rows, dim // groups),
                ("batch", "chan"), split_axis=0, concat_axis=0, tiled=True, axis_index_groups=same_core,
            )
        return jnp.sum(both.astype(f32), axis=0)

    d_mixed_chan, d_filter, g_conv_bias = conv_backward(
        d_conv_chan, mixed_chan, mixed_spec, filt_spec, bias_col, seqs
    )
    if stepped:
        d_mixed_chan = after(d_mixed_chan, far_theirs, p0h)
        far_mine = added(*far_mine, far_theirs)
        p0h = after(p0h, far_mine)
    g_in0, sums0, acc0 = back_gate(
        table, p0.reshape(devices, chans, cols), p0h, projx0, in_own, in_other, prm, xn1, seqs
    )
    g_in0 = over_chip(g_in0)
    d_mixed = exchange(d_mixed_chan)
    layer = exchange(after(layer, d_mixed))
    if stepped:
        far_mine = lax.ppermute(far_mine, "chan", beside)
    else:
        chan_groups = [list(range(q, devices, 2)) for q in range(2)]
        early = lax.psum_scatter(early, "chan", scatter_dimension=0, tiled=True, axis_index_groups=chan_groups)[0]

    tail, g_in = back(
        table, d_mixed, pair, heads, projx, in_own, in_other, prm, xn1, x, stat1, d_res, acc0, sums0, seqs
    )
    if stepped:
        tail = after(tail, far_mine, near_theirs, layer)
        early = added(*near_mine, near_theirs, far_mine)
        early = after(early, g_in)
        d_filter = after(d_filter, early)
    tail = exchange(tail)
    g_filt_in, g_filt_mid, g_filt_out, g_rows, g_decay = filter_back(
        d_filter, raw, falling, h1, h2, c1, c2, pre1, pre2, feat, filt_mid, filt_out, rate
    )
    shared = [g_filt_in.reshape(-1), g_filt_mid.reshape(-1), g_rows[0, : 3 * ford]]
    total = batch_total(
        jnp.concatenate(shared + [g_conv_bias[:, 0], g_decay[:, 0], g_filt_out.reshape(-1)])
    )
    g_in = over_groups(jnp.concatenate([g_in0, over_chip(g_in)], axis=1))
    if stepped:
        early = lax.psum_scatter(early, "chan", scatter_dimension=0, tiled=True, axis_index_groups=along)[0]

    cut = [0]

    def take(*shape):
        n = math.prod(shape)
        part = total[cut[0] : cut[0] + n].reshape(shape)
        cut[0] += n
        return part

    shared = take(sum(v.shape[0] for v in shared))
    shared = shared + lax.ppermute(shared, "chan", partner)
    g_conv_b, g_decay_rate, g_filt_last = take(chans), take(chans), take(ford, chans)
    n_shared = shared.shape[0]
    if groups != 2:
        shared = shared / groups
    line = g_in.shape[2]
    shared = jnp.pad(shared.astype(bf16), (0, -n_shared % (8 * line))).reshape(1, -1, line)
    shared = jnp.broadcast_to(shared, (devices // 2,) + shared.shape[1:])
    mine = 3 * chans
    in_grad = over_chips(jnp.concatenate([g_in, shared], axis=1))
    if groups == 2:
        total = in_grad[mine:].reshape(-1)
    else:
        total = lax.all_gather(in_grad[mine:], "batch", axis=1, tiled=True).reshape(-1)
    in_grad = in_grad[:mine]
    cut[0] = 0
    g_filt_in, g_filt_mid = take(EMB, ford), take(ford, ford)
    g_filt_in_bias, g_filt_mid_bias, g_sine = take(ford), take(ford), take(ford)

    early = after(early, in_grad)
    early = early.astype(f32) if stepped else over_batch(early)
    up_grad, down_grad, out_grad = early[:hid], early[hid : 2 * hid], early[2 * hid :]

    grad_blocks, out_blocks = tail[:, :rows], layer[:, :rows]
    sums = jnp.concatenate([layer[:, rows:], tail[:, rows:]], axis=1)
    sums = batch_total(jnp.sum(sums.astype(f32), axis=0))
    sums = sums[0::2] + sums[1::2]
    g_gain2, g_shift2, g_out_b, g_down_b = (sums[i, :chans] for i in range(4))
    g_up_b = sums[4, :hid]
    at = SUM_ROWS // 2
    count = (2 + KS) * chans
    pieces = -(-2 * count // width)
    short0 = sums[at, :count].reshape(2 + KS, 1, chans)
    short = sums[at + 1 : at + 1 + pieces].reshape(-1)[: 2 * count].reshape(2 + KS, 2, chans)
    short = jnp.concatenate([short0, short], axis=1)
    g_in_bias, g_short_bias, g_short_weight = short[0], short[1], short[2:]
    g_gain1, g_shift1 = (sums[at + 1 + pieces + i, :chans] for i in range(2))

    return (
        from_blocks(out_blocks),
        from_blocks(grad_blocks).astype(f32),
        g_gain1,
        g_shift1,
        in_grad.reshape(3, chans, dim // groups).transpose(2, 0, 1),
        g_in_bias,
        g_short_weight,
        g_short_bias,
        g_filt_in,
        g_filt_in_bias,
        g_filt_mid,
        g_filt_mid_bias,
        g_sine,
        g_filt_last,
        g_decay_rate,
        g_conv_b,
        out_grad,
        g_out_b,
        g_gain2,
        g_shift2,
        up_grad,
        g_up_b,
        down_grad,
        g_down_b,
    )


def solution(mesh):
    token = P("batch", "chan", None)
    chan = P("chan")
    rows = P("chan", None)
    two = P(None, "chan")
    three = P(None, None, "chan")
    in_specs = (
        token, P("batch"), chan, chan, three, two, three, two, P(), P(), P(), P(), P(), two, chan, chan,
        rows, chan, chan, chan, rows, chan, rows, chan, token,
    )
    table = P("chan", "batch")
    out_specs = (
        token, token, chan, chan, P("batch", None, "chan"), two, three, two, P(), P(), P(), P(), P(), two,
        chan, chan, table, chan, chan, chan, table, chan, table, chan,
    )
    return jax.shard_map(
        on_device, mesh=mesh, in_specs=in_specs, out_specs=out_specs, check_vma=False
    )
```

```python
import functools
import math

import jax
import jax.numpy as jnp
import numpy as np
from jax import lax
from jax.experimental import pallas as pl
from jax.experimental.pallas import tpu as pltpu
from jax.sharding import PartitionSpec as P

EMB = 33
KS = 3
LMAX = 4096
LANE = 128
COARSE = LMAX // LANE
REPS = tuple(ka + 8 * kb for ka, count in ((0, 5), (1, 8), (2, 8), (3, 8), (4, 4)) for kb in range(count))
PLACE = {k1: i for i, k1 in enumerate(REPS)}
epsilon = 1e-05
decay_floor = 0.05
highest = lax.Precision.HIGHEST
f32 = jnp.float32
bf16 = jnp.bfloat16
vmem_limit = 56 * 1024 * 1024
HEAD_ROWS = 16
SUM_ROWS = 16
BATCH = 11
PRM = 32
SMALL = PRM // 2


def unit(turns):
    angle = 2.0 * math.pi * turns
    return math.cos(angle), math.sin(angle)


def scaled(z, c, s):
    re, im = z
    if im is None:
        return re * c, re * s
    return re * c - im * s, re * s + im * c


def plus(a, b):
    return a[0] + b[0], a[1] + b[1]


def minus(a, b):
    return a[0] - b[0], a[1] - b[1]


def dft4(z, sign):
    s0, d0 = plus(z[0], z[2]), minus(z[0], z[2])
    s1, d1 = plus(z[1], z[3]), minus(z[1], z[3])
    turned = (-d1[1], d1[0]) if sign > 0 else (d1[1], -d1[0])
    return [plus(s0, s1), plus(d0, turned), minus(s0, s1), minus(d0, turned)]


def dft8(z, sign):
    even, odd = dft4(z[0::2], sign), dft4(z[1::2], sign)
    c = math.sqrt(0.5)
    o1 = odd[1]
    o3 = odd[3]
    if sign > 0:
        odd1 = ((o1[0] - o1[1]) * c, (o1[0] + o1[1]) * c)
        odd2 = (-odd[2][1], odd[2][0])
        odd3 = ((-o3[0] - o3[1]) * c, (o3[0] - o3[1]) * c)
    else:
        odd1 = ((o1[0] + o1[1]) * c, (o1[1] - o1[0]) * c)
        odd2 = (odd[2][1], -odd[2][0])
        odd3 = ((o3[1] - o3[0]) * c, (-o3[0] - o3[1]) * c)
    turned = [odd[0], odd1, odd2, odd3]
    return [plus(even[i], turned[i]) for i in range(4)] + [minus(even[i], turned[i]) for i in range(4)]


def coarse_forward(xs, put):
    c = math.sqrt(0.5)
    cols = {ka: [None] * 8 for ka in range(5)}
    for b in range(8):
        x0, x1, x2, x3 = xs[b], xs[8 + b], xs[16 + b], xs[24 + b]
        s02, d02, s13, d13 = x0 + x2, x0 - x2, x1 + x3, x1 - x3
        d13c, s13c = d13 * c, s13 * c
        cols[0][b] = s02 + s13
        cols[4][b] = scaled((s02 - s13, None), *unit(-4 * b / 64))
        cols[2][b] = scaled((d02, -d13), *unit(-2 * b / 64))
        cols[1][b] = scaled((x0 + d13c, -s13c - x2), *unit(-b / 64))
        cols[3][b] = scaled((x0 - d13c, x2 - s13c), *unit(-3 * b / 64))
    for ka in (1, 2, 3):
        for kb, z in enumerate(dft8(cols[ka], -1)):
            put(ka + 8 * kb, z)
    for kb, z in enumerate(dft8(cols[4], -1)[:4]):
        put(4 + 8 * kb, z)
    r = cols[0]
    s04, d04, s26, d26 = r[0] + r[4], r[0] - r[4], r[2] + r[6], r[2] - r[6]
    s15, d15, s37, d37 = r[1] + r[5], r[1] - r[5], r[3] + r[7], r[3] - r[7]
    p, q = (d15 - d37) * c, (d15 + d37) * c
    even, odd = s04 + s26, s15 + s37
    put(0, (even + odd, None))
    put(32, (even - odd, None))
    put(16, (s04 - s26, s37 - s15))
    put(8, (d04 + p, -d26 - q))
    put(24, (d04 - p, d26 - q))


def coarse_inverse(get):
    c = math.sqrt(0.5)
    u = {}
    for ka in (1, 2, 3):
        back = dft8([get(ka + 8 * kb) for kb in range(8)], 1)
        u[ka] = [scaled(back[b], *unit(b * ka / 64)) for b in range(8)]
    v0, v32 = get(0)[0], get(32)[0]
    v8, v16, v24 = get(8), get(16), get(24)
    flat = []
    for b in range(8):
        total = v0 + v32 if b % 2 == 0 else v0 - v32
        for kb, v in ((1, v8), (2, v16), (3, v24)):
            co, si = unit(b * kb / 8)
            if abs(co) > 1e-9:
                total = total + v[0] * (2.0 * co)
            if abs(si) > 1e-9:
                total = total - v[1] * (2.0 * si)
        flat.append(total)
    odd = [get(4 + 8 * kb) for kb in range(4)]
    odd = odd + [(z[0], -z[1]) for z in odd[::-1]]
    half = dft8(odd, 1)
    quarter = []
    for b in range(8):
        co, si = unit(4 * b / 64)
        quarter.append(half[b][0] * co - half[b][1] * si)
    out = [None] * COARSE
    for b in range(8):
        u1, u2, u3 = u[1][b], u[2][b], u[3][b]
        s, d = flat[b] + quarter[b], flat[b] - quarter[b]
        dr, sr = (u1[0] - u3[0]) * c, u1[0] + u3[0]
        si_, di = (u1[1] + u3[1]) * c, u1[1] - u3[1]
        out[b] = s + 2.0 * (sr + u2[0])
        out[16 + b] = s - 2.0 * (di + u2[0])
        out[8 + b] = d + 2.0 * (dr - si_ - u2[1])
        out[24 + b] = d + 2.0 * (u2[1] - dr - si_)
    return out


def transform_tables():
    fine = np.arange(LANE)
    angle = 2.0 * math.pi * ((fine[:, None] * fine[None, :]) % LANE) / LANE
    co, si = np.cos(angle), np.sin(angle)
    ahead = np.block([[co, -si], [si, co]])
    back = ahead.T / (2.0 * LMAX)
    reps = np.array(REPS)
    turn = 2.0 * math.pi * ((reps[:, None] * fine[None, :]) % (2 * LMAX)) / (2 * LMAX)
    twist = np.concatenate([np.cos(turn), -np.sin(turn)], axis=1)[:, None, :]

    def pieces(table):
        table = table.astype(np.float32)
        upper = table.astype(jnp.bfloat16)
        lower = (table - upper.astype(np.float32)).astype(jnp.bfloat16)
        return np.stack([upper, lower])

    return pieces(ahead), pieces(back), twist.astype(np.float32)


AHEAD, BACK, TWIST = transform_tables()


def three_pass(values, table_ref):
    upper = values.astype(bf16)
    lower = (values - upper.astype(f32)).astype(bf16)
    t0, t1 = table_ref[0], table_ref[1]
    return (
        jnp.dot(upper, t0, preferred_element_type=f32)
        + jnp.dot(lower, t0, preferred_element_type=f32)
        + jnp.dot(upper, t1, preferred_element_type=f32)
    )


def rows_forward(xs_ref, spec_ref, rows):
    def step(g, carry):
        at = pl.ds(pl.multiple_of(g * 8, 8), 8)
        xs = [xs_ref[n, at, :] for n in range(COARSE)]

        def put(k1, z):
            i = PLACE[k1]
            spec_ref[i, at, 0:LANE] = z[0]
            spec_ref[i, at, LANE : 2 * LANE] = jnp.zeros_like(z[0]) if z[1] is None else z[1]

        coarse_forward(xs, put)
        return carry

    lax.fori_loop(0, rows // 8, step, 0)


def rows_inverse(spec_ref, ys_ref, rows):
    def step(g, carry):
        at = pl.ds(pl.multiple_of(g * 8, 8), 8)

        def get(k1):
            i = PLACE[k1]
            return spec_ref[i, at, 0:LANE], spec_ref[i, at, LANE : 2 * LANE]

        for n, y in enumerate(coarse_inverse(get)):
            ys_ref[n, at, :] = y
        return carry

    lax.fori_loop(0, rows // 8, step, 0)


def fine_forward(spec, twist, ahead_ref):
    re, im = spec[:, :LANE], spec[:, LANE:]
    tr, ti = twist[:, :LANE], twist[:, LANE:]
    return three_pass(jnp.concatenate([re * tr - im * ti, re * ti + im * tr], axis=1), ahead_ref)


def fine_inverse(spec, twist, back_ref):
    v = three_pass(spec, back_ref)
    re, im = v[:, :LANE], v[:, LANE:]
    tr, ti = twist[:, :LANE], twist[:, LANE:]
    return jnp.concatenate([re * tr + im * ti, im * tr - re * ti], axis=1)


def times(a, b):
    ar, ai, br, bi = a[:, :LANE], a[:, LANE:], b[:, :LANE], b[:, LANE:]
    return jnp.concatenate([ar * br - ai * bi, ar * bi + ai * br], axis=1)


def times_conj(a, b):
    ar, ai, br, bi = a[:, :LANE], a[:, LANE:], b[:, :LANE], b[:, LANE:]
    return jnp.concatenate([ar * br + ai * bi, ai * br - ar * bi], axis=1)


def together(values):
    return values.reshape(values.shape[0] * values.shape[1], values.shape[2])


def apart(values):
    return values.reshape(BATCH, values.shape[0] // BATCH, values.shape[1])


def twists(twist_ref, at, rows):
    return together(jnp.broadcast_to(twist_ref[at], (BATCH, rows, 2 * LANE)))


def spread(blocks_ref, xs_ref):
    per = blocks_ref.shape[2] // LANE
    for n in range(COARSE):
        r = n % per
        xs_ref[n] = blocks_ref[n // per, :, r * LANE : (r + 1) * LANE].astype(f32)


def filter_spectrum_body(filter_ref, twist_ref, ahead_ref, out_ref, xs_ref):
    rows = filter_ref.shape[0]
    for n in range(COARSE):
        xs_ref[n] = filter_ref[:, n * LANE : (n + 1) * LANE]
    rows_forward(xs_ref, out_ref, rows)

    def step(i, carry):
        at = pl.ds(i * BATCH, BATCH)
        out_ref[at] = apart(fine_forward(together(out_ref[at]), twists(twist_ref, at, rows), ahead_ref))
        return carry

    lax.fori_loop(0, len(REPS) // BATCH, step, 0)


def conv_forward_body(seqs, mixed_ref, filt_ref, bias_ref, twist_ref, ahead_ref, back_ref, out_ref, spec_ref, xs_ref, work_ref):
    rows = mixed_ref.shape[1]
    spread(mixed_ref, xs_ref)
    rows_forward(xs_ref, spec_ref, rows)

    def step(i, carry):
        at = pl.ds(i * BATCH, BATCH)
        twist = twists(twist_ref, at, rows)
        z = fine_forward(together(spec_ref[at]), twist, ahead_ref)
        spec_ref[at] = apart(z)
        k = together(jnp.concatenate([filt_ref[at]] * seqs, axis=1))
        work_ref[at] = apart(fine_inverse(times(z, k), twist, back_ref))
        return carry

    lax.fori_loop(0, len(REPS) // BATCH, step, 0)
    ys_ref = xs_ref
    rows_inverse(work_ref, ys_ref, rows)
    per = mixed_ref.shape[2] // LANE
    bias = jnp.concatenate([bias_ref[...]] * seqs, axis=0)
    for n in range(COARSE):
        at = (n // per, slice(None), slice((n % per) * LANE, (n % per + 1) * LANE))
        out_ref[at] = (ys_ref[n] + bias * mixed_ref[at].astype(f32)).astype(bf16)


def heads_out(out_ref, block, y):
    rows, width = y.shape[0], out_ref.shape[2]
    square = jnp.concatenate([y, jnp.zeros((LANE - rows, LANE), f32)], axis=0) if rows < LANE else y
    head = square.T[:HEAD_ROWS]
    if width > LANE:
        head = jnp.concatenate([head, jnp.zeros((HEAD_ROWS, width - LANE), f32)], axis=1)
    out_ref[block, rows:, :] = head.astype(bf16)


def conv_backward_body(
    seqs, d_ref, mixed_ref, mixed_spec_ref, filt_ref, bias_ref, twist_ref, ahead_ref, back_ref, out_ref, dfilt_ref, dbias_ref, xs_ref, spec_ref, work_ref, ys_ref
):
    rows = d_ref.shape[1]
    chans = rows // seqs
    spread(d_ref, xs_ref)
    rows_forward(xs_ref, spec_ref, rows)

    def step(i, carry):
        at = pl.ds(i * BATCH, BATCH)
        z = fine_forward(together(spec_ref[at]), twists(twist_ref, at, rows), ahead_ref)
        k = together(jnp.concatenate([filt_ref[at]] * seqs, axis=1))
        cross = apart(times_conj(z, together(mixed_spec_ref[at])))
        cross = sum(cross[:, s * chans : (s + 1) * chans] for s in range(seqs))
        both = together(jnp.concatenate([apart(times_conj(z, k)), cross], axis=1))
        work_ref[at] = apart(fine_inverse(both, twists(twist_ref, at, rows + chans), back_ref))
        return carry

    lax.fori_loop(0, len(REPS) // BATCH, step, 0)
    rows_inverse(work_ref, ys_ref, rows + chans)
    per = d_ref.shape[2] // LANE
    bias = jnp.concatenate([bias_ref[...]] * seqs, axis=0)
    total = jnp.zeros((rows, LANE), f32)
    out_ref[out_ref.shape[0] - 1, rows:, :] = jnp.zeros((HEAD_ROWS, d_ref.shape[2]), bf16)
    for n in range(COARSE):
        at = (n // per, slice(0, rows), slice((n % per) * LANE, (n % per + 1) * LANE))
        d = xs_ref[n]
        y = ys_ref[n, :rows, :] + bias * d
        out_ref[at] = y.astype(bf16)
        if n % per == 0 and n > 0:
            heads_out(out_ref, n // per - 1, y)
        total = total + d * mixed_ref[at].astype(f32)
        dfilt_ref[:, n * LANE : (n + 1) * LANE] = ys_ref[n, rows:, :]
    total = sum(total[s * chans : (s + 1) * chans] for s in range(seqs))
    dbias_ref[...] = jnp.sum(total, axis=1, keepdims=True)


def takes(us):
    return pl.CostEstimate(flops=int(us * 1e9), bytes_accessed=int(us * 3e6), transcendentals=0)


def whole_call(us, body, out_shape, scratch, *args):
    return pl.pallas_call(
        body,
        cost_estimate=takes(us),
        out_shape=out_shape,
        in_specs=[pl.BlockSpec(memory_space=pltpu.VMEM)] * len(args),
        out_specs=jax.tree.map(lambda _: pl.BlockSpec(memory_space=pltpu.VMEM), out_shape),
        scratch_shapes=scratch,
        compiler_params=pltpu.CompilerParams(vmem_limit_bytes=vmem_limit),
    )(*args)


def filter_spectrum(filt):
    rows = filt.shape[0]
    return whole_call(
        8,
        filter_spectrum_body,
        jax.ShapeDtypeStruct((len(REPS), rows, 2 * LANE), f32),
        [pltpu.VMEM((COARSE, rows, LANE), f32)],
        filt,
        jnp.asarray(TWIST),
        jnp.asarray(AHEAD),
    )


def conv_forward(mixed, filt_spec, bias, seqs):
    blocks, rows, width = mixed.shape
    n = len(REPS)
    return whole_call(
        100,
        lambda *refs: conv_forward_body(seqs, *refs),
        (jax.ShapeDtypeStruct(mixed.shape, bf16), jax.ShapeDtypeStruct((n, rows, 2 * LANE), f32)),
        [pltpu.VMEM((COARSE, rows, LANE), f32), pltpu.VMEM((n, rows, 2 * LANE), f32)],
        mixed,
        filt_spec,
        bias,
        jnp.asarray(TWIST),
        jnp.asarray(AHEAD),
        jnp.asarray(BACK),
    )


def conv_backward(d_conv, mixed, mixed_spec, filt_spec, bias, seqs):
    blocks, rows, width = mixed.shape
    chans = rows // seqs
    n = len(REPS)
    return whole_call(
        100,
        lambda *refs: conv_backward_body(seqs, *refs),
        (
            jax.ShapeDtypeStruct((blocks, rows + HEAD_ROWS, width), bf16),
            jax.ShapeDtypeStruct((chans, LMAX), f32),
            jax.ShapeDtypeStruct((chans, 1), f32),
        ),
        [
            pltpu.VMEM((COARSE, rows, LANE), f32),
            pltpu.VMEM((n, rows, 2 * LANE), f32),
            pltpu.VMEM((n, rows + chans, 2 * LANE), f32),
            pltpu.VMEM((COARSE, rows + chans, LANE), f32),
        ],
        d_conv,
        mixed,
        mixed_spec,
        filt_spec,
        bias,
        jnp.asarray(TWIST),
        jnp.asarray(AHEAD),
        jnp.asarray(BACK),
    )


CHUNK = 48


def lanes_of(shape):
    return lax.broadcasted_iota(jnp.int32, shape, 1)


def side_by_side(block, seqs):
    chans = block.shape[0] // seqs
    return jnp.concatenate([block[s * chans : (s + 1) * chans] for s in range(seqs)], axis=1)


def stacked(values, seqs):
    width = values.shape[1] // seqs
    return jnp.concatenate([values[:, s * width : (s + 1) * width] for s in range(seqs)], axis=0)


def eights(values):
    return jnp.sum(values.reshape(values.shape[0] // 8, 8, values.shape[1]), axis=0)


def folded(values):
    return sum(values[:, i * LANE : (i + 1) * LANE] for i in range(values.shape[1] // LANE))


def row_totals(values):
    ones = jnp.ones((8, LANE), bf16)
    upper = values.astype(bf16)
    lower = (values - upper.astype(f32)).astype(bf16)
    return mm16(ones, upper, NT) + mm16(ones, lower, NT)


def padded_totals(values, width):
    extra = -values.shape[0] % width
    if extra:
        values = jnp.concatenate([values, jnp.zeros((extra, LANE), f32)], axis=0)
    totals = row_totals(values)
    return [totals[:, i * width : (i + 1) * width] for i in range(totals.shape[1] // width)]


def as_rows(totals, rows):
    halves = []
    for t in totals:
        upper = t.astype(bf16).astype(f32)
        halves += [upper, t - upper]
    place = lax.broadcasted_iota(jnp.int32, halves[0].shape, 0)
    tiles = []
    for first in range(0, rows, 8):
        tile = jnp.zeros_like(halves[0])
        for i, h in enumerate(halves[first : first + 8]):
            tile = jnp.where(place == i, h, tile)
        tiles.append(tile)
    return jnp.concatenate(tiles, axis=0).astype(bf16)


def chunk_rows(i):
    return pl.ds(pl.multiple_of(i * CHUNK, CHUNK), CHUNK)


def norm_stats(ref, dim):
    cols = ref.shape[1]
    zero = jnp.zeros((8, cols), f32)
    total = lax.fori_loop(0, dim // CHUNK, lambda i, t: t + eights(ref[chunk_rows(i), :]), zero)
    mean = jnp.sum(total, axis=0, keepdims=True) / dim

    def spread_sq(i, t):
        v = ref[chunk_rows(i), :] - mean
        return t + eights(v * v)

    var = jnp.sum(lax.fori_loop(0, dim // CHUNK, spread_sq, zero), axis=0, keepdims=True) / dim
    return mean, lax.rsqrt(var + epsilon)


def front_body(
    seqs, table_ref, x_ref, xh_ref, own_ref, other_ref, own_small, other_small, after_ref,
    prm_ref, xn_ref, stat_ref, gate_ref, pair_ref, projx0_ref, projx_ref, mixed_ref, heads_ref, xs, xb,
):
    devices, _, width = x_ref.shape
    dim, cols = xn_ref.shape
    chans = dim // devices
    turns = devices // 2
    step = pl.program_id(0)

    @pl.when(step == 0)
    def _():
        for turn in range(turns):
            for ref, (device, _) in zip((own_small, other_small), slots(table_ref, turns, turn)):
                small = ref[turn].astype(f32)
                small = jnp.concatenate([small[:, :LANE], small[:, LANE:], jnp.zeros((LANE - PRM, LANE), f32)], axis=0)
                prm_ref[pl.ds(pl.multiple_of(device * chans, 8), chans), :] = small.T[:chans, :PRM]

        def gather(d, carry):
            at = pl.ds(pl.multiple_of(d * chans, 8), chans)
            row = side_by_side(x_ref[d].astype(f32), seqs)
            tail = xh_ref[d].astype(f32)
            tail = jnp.where(
                lanes_of((chans, LANE)) < LANE // 2, pltpu.roll(tail[chans : 2 * chans], LANE // 2, 1), tail[:chans]
            )
            xs[at, :] = jnp.concatenate([row, tail], axis=1)
            return carry

        lax.fori_loop(0, devices, gather, 0)
        mean, inverse = norm_stats(xs, dim)

        def scale(i, carry):
            at = chunk_rows(i)
            prm = prm_ref[at, :]
            v = (xs[at, :] - mean) * inverse * prm[:, 15:16] + prm[:, 16:17]
            xb[at, :] = v.astype(bf16)
            xn_ref[at, :] = v[:, :cols].astype(bf16)
            return carry

        lax.fori_loop(0, dim // CHUNK, scale, 0)
        stat_ref[0:8, :] = jnp.broadcast_to(mean[:, :cols], (8, cols))
        stat_ref[8:16, :] = jnp.broadcast_to(inverse[:, :cols], (8, cols))

    keep = (table_ref[turns + 1] > 0).astype(f32)
    for w_ref, (device, g) in zip((own_ref, other_ref), slots(table_ref, turns, step)):
        prm = prm_ref[pl.ds(pl.multiple_of(device * chans, 8), chans), :]
        proj = mm16(w_ref[0, SMALL:, :], xb[...], NN)
        ys = []
        px = []
        for i in range(3):
            x = proj[i * chans : (i + 1) * chans] + prm[:, i : i + 1]
            tail = x[:, cols:] * keep
            px += [jnp.concatenate([x[:, :cols], tail], axis=1)]
            weights = [jnp.broadcast_to(prm[:, 6 + 3 * j + i : 7 + 3 * j + i], (chans, width)) for j in range(KS)]
            bias = jnp.broadcast_to(prm[:, 3 + i : 4 + i], (chans, width))
            parts = []
            for s in range(seqs):
                v = x[:, s * width : (s + 1) * width]
                wide = jnp.concatenate([tail if s == 0 else pltpu.roll(tail, LANE // 2, 1), v], axis=1)
                y = bias + weights[0] * v
                for j in range(1, KS):
                    y = y + weights[j] * pltpu.roll(wide, j, 1)[:, LANE:]
                parts.append(y)
            ys.append(jnp.concatenate(parts, axis=1))
        projx0_ref[g] = px[0].astype(bf16)
        projx_ref[g] = jnp.concatenate(px[1:], axis=0).astype(bf16)
        gate_ref[g] = ys[0]
        pair = jnp.concatenate(ys[1:], axis=0)
        pair_ref[g] = pair
        mixed_ref[g] = stacked(ys[1] * ys[2], seqs).astype(bf16)
        heads_ref[g] = first_tokens(pair, seqs).astype(bf16)


def first_tokens(values, seqs):
    rows, width = values.shape[0], values.shape[1] // seqs
    pad = jnp.zeros((LANE - rows, LANE), f32)
    heads = []
    for s in range(seqs):
        tile = values[:, s * width : s * width + LANE]
        heads.append((jnp.concatenate([tile, pad], axis=0) if rows < LANE else tile).T[:8])
    return jnp.concatenate(heads, axis=0)


def token_columns(heads, rows):
    gap = jnp.zeros((LANE // 2 - 8, LANE), f32)
    return jnp.concatenate([heads[:8], gap, heads[8:], gap], axis=0).T[:rows]


def whole(a):
    return pl.BlockSpec(a.shape, lambda i, t: (0,) * len(a.shape), pipeline_mode=pl.Buffered(1))


def untouched():
    return pl.BlockSpec(memory_space=pl.ANY)


def by_chip(a):
    return pl.BlockSpec((2,) + a.shape[1:], lambda i, t: (t[i],) + (0,) * (len(a.shape) - 1))


def by_turn(a, rows=None):
    return pl.BlockSpec((1, a.shape[1] if rows is None else rows, a.shape[2]), lambda i, t: (i, 0, 0))


def chip_call(us, body, table, turns, args, in_specs, out, out_specs, scratch):
    return pl.pallas_call(
        body,
        cost_estimate=takes(us),
        out_shape=out,
        grid_spec=pltpu.PrefetchScalarGridSpec(
            num_scalar_prefetch=1,
            grid=(turns,),
            in_specs=in_specs,
            out_specs=out_specs,
            scratch_shapes=scratch,
        ),
        compiler_params=pltpu.CompilerParams(vmem_limit_bytes=vmem_limit, dimension_semantics=("arbitrary",)),
    )(table, *args)


def slots(table_ref, turns, step):
    core = table_ref[turns]
    chip = table_ref[step]
    return ((2 * chip + core, core), (2 * chip + 1 - core, 1 - core))


def front(table, x, xh, own, other, before, seqs):
    devices, rows, width = x.shape
    chans = rows // seqs
    dim = devices * chans
    cols = seqs * width
    turns = devices // 2
    sd = jax.ShapeDtypeStruct
    out = (
        sd((dim, PRM), f32),
        sd((dim, cols), bf16),
        sd((16, cols), f32),
        sd((devices, chans, cols), f32),
        sd((devices, 2 * chans, cols), f32),
        sd((devices, chans, cols + LANE), bf16),
        sd((devices, 2 * chans, cols + LANE), bf16),
        sd((devices, rows, width), bf16),
        sd((devices, 8 * seqs, LANE), bf16),
    )
    small = pl.BlockSpec((turns, SMALL, 2 * LANE), lambda i, t: (0, 0, 0), pipeline_mode=pl.Buffered(1))
    return chip_call(
        2,
        lambda *refs: front_body(seqs, *refs),
        table,
        turns,
        (x, xh, own, other, own, other, before),
        [whole(x), whole(xh), by_turn(own), by_turn(other), small, small, untouched()],
        out,
        tuple(whole(o) for o in out[:3]) + tuple(by_chip(o) for o in out[3:]),
        [pltpu.VMEM((dim, cols + LANE), f32), pltpu.VMEM((dim, cols + LANE), bf16)],
    )


def middle_body(seqs, pieces, segments, per, table_ref, conv_ref, x_ref, cot_ref, gate_ref, prm_ref, *refs):
    weights = []
    for _ in range(pieces):
        weights.append([[refs[2 * (segments * core + n) : 2 * (segments * core + n) + 2] for n in range(segments)] for core in range(2)])
        refs = refs[4 * segments :]
    layer_ref, d_conv_ref, d_res_ref, p0_ref, p0h_ref = refs[:5]
    grads = [[refs[5 + segments * (2 * p + n) : 5 + segments * (2 * p + n + 1)] for n in range(2)] for p in range(pieces)]
    refs = refs[5 + 2 * pieces * segments :]
    cs, res, ds, xb, db, gb, acc_out, acc_in, folds, up_folds, stats, out_w32, out_w_ref, gs = refs
    devices, _, width = x_ref.shape
    dim, cols = d_res_ref.shape
    chans = dim // devices
    hid = weights[0][0][0][0].shape[1] // 2 * pieces
    turns = devices // 2
    part, some_hid, some_out = dim // pieces, hid // pieces, chans // pieces
    group = table_ref[turns + 2 + seqs] if pieces == 2 else 0
    halves = [group, 1 - group][:pieces]
    columns = [pl.ds(pl.multiple_of(h * part, LANE), part) for h in halves]
    step = pl.program_id(0)
    last = pl.num_programs(0) - 1
    lane = lanes_of((1, cols))
    live = jnp.zeros((1, cols), f32)
    for s in range(seqs):
        position = table_ref[turns + 1] * width + lane - s * width
        inside = (lane >= s * width) & (lane < (s + 1) * width) & (position < table_ref[turns + 2 + s])
        live = jnp.where(inside, 1.0, live)

    def device_rows(d):
        return pl.ds(pl.multiple_of(d * chans, 8), chans)

    @pl.when(step == 0)
    def _():
        def gather(d, carry):
            at = device_rows(d)
            cs[at, :] = side_by_side(conv_ref[d].astype(f32), seqs)
            res[at, :] = side_by_side(x_ref[d].astype(f32), seqs)
            ds[at, :] = live * side_by_side(cot_ref[d].astype(f32), seqs)
            return carry

        lax.fori_loop(0, devices, gather, 0)
        for piece, h in zip(weights, halves):
            for core, parts in enumerate(piece):
                turn = 0
                for _, out_rows in parts:
                    for n in range(out_rows.shape[0]):
                        device, _ = slots(table_ref, turns, turn)[core]
                        at = pl.ds(pl.multiple_of(device * chans + h * some_out, 8), some_out)
                        out_w32[at, :] = out_rows[n].astype(f32)
                        turn += 1

        def gated(i, carry):
            at = chunk_rows(i)
            out_w_ref[at, :] = out_w32[at, :].astype(bf16)
            gb[at, :] = (cs[at, :] * gate_ref[at, :]).astype(bf16)
            d = ds[at, :]
            db[at, :] = d.astype(bf16)
            folds[3, at, :] = folded(d)
            acc_in[at, :] = jnp.zeros((CHUNK, cols), f32)
            return carry

        lax.fori_loop(0, dim // CHUNK, gated, 0)
        acc_out[...] = mm16(out_w_ref[...], gb[...], TN)

        def add(i, carry):
            at = chunk_rows(i)
            res[at, :] = res[at, :] + acc_out[at, :] + prm_ref[at, 19:20]
            acc_out[at, :] = jnp.zeros((CHUNK, cols), f32)
            return carry

        lax.fori_loop(0, dim // CHUNK, add, 0)
        mean, inverse = norm_stats(res, dim)

        def scale(i, carry):
            at = chunk_rows(i)
            normed = (res[at, :] - mean) * inverse
            cs_norm = normed * prm_ref[at, 17:18] + prm_ref[at, 18:19]
            xb[at, :] = cs_norm.astype(bf16)
            return carry

        lax.fori_loop(0, dim // CHUNK, scale, 0)
        stats[0:8, :] = jnp.broadcast_to(mean, (8, cols))
        stats[8:16, :] = jnp.broadcast_to(inverse, (8, cols))

    pair = [device for j in range(per) for device, _ in slots(table_ref, turns, step * per + j)]
    up_b = []
    for device in pair:
        prm = prm_ref[device_rows(device), :]
        for h in halves:
            for m in range(some_hid // chans):
                first, second = 21 + m, 21 + m + (pieces - 1) * some_hid // chans
                up_b.append(jnp.where(h == 0, prm[:, first : first + 1], prm[:, second : second + 1]))
    up_b = jnp.concatenate(up_b, axis=0)

    def now(parts, rows, j):
        blocks = [ref[j, rows, :] for ref, _ in parts]
        return blocks[0] if len(blocks) == 1 else jnp.where(step * per < turns // 2, blocks[0], blocks[1])

    def rows_now(rows):
        return jnp.concatenate(
            [now(piece[core], rows, j) for j in range(per) for core in range(2) for piece in weights], axis=0
        )

    up, down = rows_now(slice(0, some_hid)), rows_now(slice(some_hid, 2 * some_hid))
    u = mm16(up, xb[...], NN) + up_b
    d_act = mm16(down, db[...], NN)
    a, k = 0.044715, math.sqrt(2.0 / math.pi)
    sq = u * u
    t = jnp.tanh(u * (k + (k * a) * sq))
    half = 0.5 * (1.0 + t)
    act = (u * half).astype(bf16)
    d_u = d_act * (half + 0.5 * u * (1.0 - t * t) * (k + (3.0 * k * a) * sq))
    d_low = d_u.astype(bf16)
    fold = folded(d_u)
    acc_out[...] += mm16(down, act, TN)
    acc_in[...] += mm16(up, d_low, TN)
    spots = [(n, p, h) for n in range(2 * per) for p, h in enumerate(halves)]
    for n, p, h in spots:
        rows = slice((n * pieces + p) * some_hid, (n * pieces + p + 1) * some_hid)
        up_folds[pl.ds(pl.multiple_of(pair[n] * hid + h * some_hid, 8), some_hid), :] = fold[rows]
    gs[0] = mm16(d_low, xb[...], NT).astype(bf16)
    gs[1] = mm16(act, db[...], NT).astype(bf16)

    def hand_out(k):
        for n, p, h in spots:
            rows = slice((n * pieces + p) * some_hid, (n * pieces + p + 1) * some_hid)
            for which in range(2):
                at = pl.ds(pl.multiple_of(which * hid + h * some_hid, some_hid), some_hid)
                for g_refs, some in zip(grads, columns):
                    g_refs[n % 2][k][step * per + n // 2 - k * (turns // segments), at, :] = gs[which, rows, some]

    for k in range(segments):
        count = turns // segments
        pl.when((step * per >= k * count) & (step * per < (k + 1) * count))(functools.partial(hand_out, k))

    @pl.when(step == last)
    def _():
        mean, inverse = stats[0:1, :], stats[8:9, :]

        def result(i, t):
            at = chunk_rows(i)
            r = res[at, :]
            acc_out[at, :] = live * (r + acc_out[at, :] + prm_ref[at, 20:21])
            normed = (r - mean) * inverse
            d = acc_in[at, :]
            both = d * normed
            folds[0, at, :] = folded(both)
            folds[1, at, :] = folded(d)
            gain = prm_ref[at, 17:18]
            return t[0] + eights(d * gain), t[1] + eights(both * gain)

        zero = jnp.zeros((8, cols), f32)
        m1, m2 = lax.fori_loop(0, dim // CHUNK, result, (zero, zero))
        m1 = jnp.sum(m1, axis=0, keepdims=True) / dim
        m2 = jnp.sum(m2, axis=0, keepdims=True) / dim

        def residual(i, carry):
            at = chunk_rows(i)
            normed = (res[at, :] - mean) * inverse
            d = ds[at, :] + inverse * (acc_in[at, :] * prm_ref[at, 17:18] - m1 - normed * m2)
            d_res_ref[at, :] = d
            folds[2, at, :] = folded(d)
            db[at, :] = d.astype(bf16)
            return carry

        lax.fori_loop(0, dim // CHUNK, residual, 0)
        for n in range(dim // 256):
            some = slice(n * 256, (n + 1) * 256)
            acc_in[some, :] = mm16(out_w_ref[some, :], db[...], NN)
            out_w32[some, :] = mm16(gb[some, :], db[...], NT)
        for g_refs, at in zip(grads, columns):
            for turn in range(turns):
                for g_ref, (device, _) in zip(g_refs, slots(table_ref, turns, turn)):
                    count = turns // segments
                    g_ref[turn // count][turn % count, 2 * hid :, :] = out_w32[device_rows(device), at].astype(bf16)

        def products(i, carry):
            at = chunk_rows(i)
            d = acc_in[at, :]
            p0 = d * cs[at, :]
            p0_ref[at, :] = p0
            acc_in[at, :] = d * gate_ref[at, :]
            return carry

        lax.fori_loop(0, dim // CHUNK, products, 0)

        def scatter(d, carry):
            at = device_rows(d)
            p0h_ref[d] = first_tokens(p0_ref[at, :], seqs).astype(bf16)
            layer_ref[d, : seqs * chans, :] = stacked(acc_out[at, :], seqs).astype(bf16)
            d_conv_ref[d] = stacked(acc_in[at, :], seqs).astype(bf16)
            totals = [padded_totals(folds[q, at, :], width)[0] for q in range(4)]
            totals += padded_totals(up_folds[pl.ds(pl.multiple_of(d * hid, 8), hid), :], width)
            layer_ref[d, seqs * chans :, :] = as_rows(totals, SUM_ROWS)
            return carry

        lax.fori_loop(0, devices, scatter, 0)


def middle(table, conv, x, cot, gate, matrices, prm, hid, seqs):
    devices, rows, width = conv.shape
    dim, cols = gate.shape
    chans = dim // devices
    turns = devices // 2
    pieces, segments = len(matrices), len(matrices[0][0])
    part, some_hid, some_out = dim // pieces, hid // pieces, chans // pieces
    sd = jax.ShapeDtypeStruct
    out = (
        sd((devices, rows + SUM_ROWS, width), bf16),
        sd((devices, rows, width), bf16),
        sd((dim, cols), f32),
        sd((dim, cols), f32),
        sd((devices, 8 * seqs, LANE), bf16),
    ) + (sd((turns // segments, 2 * hid + chans, part), bf16),) * (2 * pieces * segments)
    big = pltpu.VMEM((dim, cols), f32)
    low = pltpu.VMEM((dim, cols), bf16)
    args, specs = [conv, x, cot, gate, prm], [whole(conv), whole(x), whole(cot), whole(gate), whole(prm)]
    per = 2
    for piece in matrices:
        for parts in piece:
            first = 0
            for a in parts:
                count = a.shape[0]
                args += [a, a]
                specs += [
                    pl.BlockSpec(
                        (per, 2 * some_hid, dim),
                        lambda i, t, f=first // per, c=count // per: (jnp.clip(i - f, 0, c - 1), 0, 0),
                    ),
                    pl.BlockSpec(
                        (count, some_out, dim), lambda i, t: (0, 2 * some_hid // some_out, 0), pipeline_mode=pl.Buffered(1)
                    ),
                ]
                first += count
    return chip_call(
        36,
        lambda *refs: middle_body(seqs, pieces, segments, per, *refs),
        table,
        turns // per,
        args,
        specs,
        out,
        tuple(whole(o) for o in out),
        [
            big, big, big, low, low, low, big, big, pltpu.VMEM((4, dim, LANE), f32),
            pltpu.VMEM((devices * hid, LANE), f32), pltpu.VMEM((16, cols), f32), pltpu.VMEM((dim, dim), f32),
            pltpu.VMEM((dim, dim), bf16), pltpu.VMEM((2, 2 * per * hid, dim), bf16),
        ],
    )


def short_back(seqs, prm, kinds, d_short, head, projx, width, cols):
    chans = prm.shape[0]
    d_proj = []
    totals = [[] for _ in range(2 + KS)]
    for n, i in enumerate(kinds):
        px = projx[n * chans : (n + 1) * chans]
        weights = [jnp.broadcast_to(prm[:, 6 + 3 * j + i : 7 + 3 * j + i], (chans, width)) for j in range(KS)]
        parts = []
        sums = [0.0] * (2 + KS)
        for s in range(seqs):
            at = slice(s * width, (s + 1) * width)
            d = d_short[n][:, at]
            x = px[:, at]
            tail = px[:, cols:]
            wide = jnp.concatenate([tail if s == 0 else pltpu.roll(tail, LANE // 2, 1), x], axis=1)
            after = jnp.concatenate([d, head[n] if s == 0 else pltpu.roll(head[n], LANE // 2, 1)], axis=1)
            y = weights[0] * d
            sums[1] = sums[1] + folded(d)
            sums[2] = sums[2] + folded(d * x)
            for j in range(1, KS):
                y = y + weights[j] * pltpu.roll(after, width + LANE - j, 1)[:, :width]
                sums[2 + j] = sums[2 + j] + folded(d * pltpu.roll(wide, j, 1)[:, LANE:])
            sums[0] = sums[0] + folded(y)
            parts.append(y)
        d_proj.append(jnp.concatenate(parts, axis=1))
        for k in range(2 + KS):
            totals[k].append(sums[k])
    d_low = jnp.concatenate(d_proj, axis=0).astype(bf16)
    return d_low, padded_totals(jnp.concatenate(sum(totals, []), axis=0), width)


def back_gate_body(seqs, table_ref, p0_ref, p0h_ref, projx_ref, own_ref, other_ref, prm_ref, xn_ref, g_ref, sums_ref, acc):
    dim, cols = xn_ref.shape
    chans = p0_ref.shape[1]
    step = pl.program_id(0)

    @pl.when(step == 0)
    def _():
        acc[...] = jnp.zeros_like(acc)

    turns = prm_ref.shape[0] // chans // 2
    for w_ref, (device, g) in zip((own_ref, other_ref), slots(table_ref, turns, step)):
        prm = prm_ref[pl.ds(pl.multiple_of(device * chans, 8), chans), :]
        d_low, totals = short_back(
            seqs, prm, (0,), (p0_ref[g],), (token_columns(p0h_ref[g].astype(f32), chans),), projx_ref[g].astype(f32), cols // seqs, cols
        )
        sums_ref[g] = totals[0]
        acc[...] += mm16(w_ref[0, SMALL : SMALL + chans, :], d_low, TN)
        g_ref[g] = mm16(d_low, xn_ref[...], NT).astype(bf16)


def back_gate(table, p0, p0h, projx, own, other, prm, xn, seqs):
    devices, chans, cols = p0.shape
    dim = xn.shape[0]
    sd = jax.ShapeDtypeStruct
    out = (
        sd((devices, chans, dim), bf16),
        sd((devices, 8, cols // seqs), f32),
        sd((dim, cols), f32),
    )
    return chip_call(
        2,
        lambda *refs: back_gate_body(seqs, *refs),
        table,
        devices // 2,
        (p0, p0h, projx, own, other, prm, xn),
        [by_chip(a) for a in (p0, p0h, projx)] + [by_turn(own), by_turn(other), whole(prm), whole(xn)],
        out,
        (by_chip(out[0]), by_chip(out[1]), whole(out[2])),
        [],
    )


def back_body(
    seqs, table_ref, d_mixed_ref, pair_ref, heads_ref, projx_ref, own_ref, other_ref, prm_ref, xn_ref, x_ref, stat_ref, d_res_ref,
    acc0_ref, sums0_ref, tail_ref, g_ref, acc, xs, folds, sums,
):
    devices, _, width = x_ref.shape
    dim, cols = xn_ref.shape
    chans = dim // devices
    step = pl.program_id(0)
    last = pl.num_programs(0) - 1

    @pl.when(step == 0)
    def _():
        acc[...] = acc0_ref[...]

    turns = devices // 2
    for w_ref, (device, g) in zip((own_ref, other_ref), slots(table_ref, turns, step)):
        prm = prm_ref[pl.ds(pl.multiple_of(device * chans, 8), chans), :]
        block = d_mixed_ref[g].astype(f32)
        d_mixed = side_by_side(block[: seqs * chans], seqs)
        square = jnp.concatenate([block[seqs * chans :, :LANE], jnp.zeros((LANE - HEAD_ROWS, LANE), f32)], axis=0).T
        second = pltpu.roll(square[chans : 2 * chans], LANE // 2, 1)
        d_head = jnp.where(lanes_of((chans, LANE)) < LANE // 2, square[:chans], second)
        pair = pair_ref[g]
        pair_head = token_columns(heads_ref[g].astype(f32), 2 * chans)
        d_short = (d_mixed * pair[chans:], d_mixed * pair[:chans])
        head = (d_head * pair_head[chans:], d_head * pair_head[:chans])
        d_low, totals = short_back(seqs, prm, (1, 2), d_short, head, projx_ref[g].astype(f32), width, cols)
        for n, t in enumerate(totals):
            sums[n, device] = t
        acc[...] += mm16(w_ref[0, SMALL + chans :, :], d_low, TN)
        g_ref[g] = mm16(d_low, xn_ref[...], NT).astype(bf16)

    @pl.when(step == last)
    def _():
        def gather(d, carry):
            xs[pl.ds(pl.multiple_of(d * chans, 8), chans), :] = side_by_side(x_ref[d].astype(f32), seqs)
            return carry

        lax.fori_loop(0, devices, gather, 0)
        mean, inverse = stat_ref[0:1, :], stat_ref[8:9, :]

        def first(i, t):
            at = chunk_rows(i)
            normed = (xs[at, :] - mean) * inverse
            d = acc[at, :]
            both = d * normed
            folds[0, at, :] = folded(both)
            folds[1, at, :] = folded(d)
            gain = prm_ref[at, 15:16]
            return t[0] + eights(d * gain), t[1] + eights(both * gain)

        zero = jnp.zeros((8, cols), f32)
        m1, m2 = lax.fori_loop(0, dim // CHUNK, first, (zero, zero))
        m1 = jnp.sum(m1, axis=0, keepdims=True) / dim
        m2 = jnp.sum(m2, axis=0, keepdims=True) / dim

        def second(i, carry):
            at = chunk_rows(i)
            normed = (xs[at, :] - mean) * inverse
            acc[at, :] = d_res_ref[at, :] + inverse * (acc[at, :] * prm_ref[at, 15:16] - m1 - normed * m2)
            return carry

        lax.fori_loop(0, dim // CHUNK, second, 0)

        rows = seqs * chans

        def scatter(d, carry):
            at = pl.ds(pl.multiple_of(d * chans, 8), chans)
            tail_ref[d, :rows, :] = stacked(acc[at, :], seqs).astype(bf16)
            totals = [sums0_ref[d]] + [sums[n, d] for n in range(sums.shape[0])]
            totals += [padded_totals(folds[q, at, :], width)[0] for q in range(2)]
            tail_ref[d, rows : rows + SUM_ROWS, :] = as_rows(totals, SUM_ROWS)
            return carry

        lax.fori_loop(0, devices, scatter, 0)


def back(table, d_mixed, pair, heads, projx, own, other, prm, xn, x, stat, d_res, acc0, sums0, seqs):
    devices, rows, width = x.shape
    dim, cols = xn.shape
    chans = dim // devices
    sd = jax.ShapeDtypeStruct
    pieces = -(-2 * (2 + KS) * chans // width)
    out = (
        sd((devices, rows + SUM_ROWS, width), bf16),
        sd((devices, 2 * chans, dim), bf16),
    )
    return chip_call(
        100,
        lambda *refs: back_body(seqs, *refs),
        table,
        devices // 2,
        (d_mixed, pair, heads, projx, own, other, prm, xn, x, stat, d_res, acc0, sums0),
        [by_chip(a) for a in (d_mixed, pair, heads, projx)]
        + [by_turn(own), by_turn(other), whole(prm), whole(xn), whole(x)]
        + [whole(a) for a in (stat, d_res, acc0, sums0)],
        out,
        (whole(out[0]), by_chip(out[1])),
        [
            pltpu.VMEM((dim, cols), f32), pltpu.VMEM((dim, cols), f32), pltpu.VMEM((2, dim, LANE), f32),
            pltpu.VMEM((pieces, devices, 8, width), f32),
        ],
    )


def position_table():
    places = np.arange(LMAX)
    orders = np.arange(1, (EMB - 1) // 2 + 1)
    turns = 2.0 * math.pi * ((orders[:, None] * places[None, :]) % LMAX) / LMAX
    ramp = places[None, :] / (LMAX - 1)
    return np.concatenate([ramp, np.cos(turns), -np.sin(turns)], axis=0).astype(np.float32)


FEAT = position_table()


def mm(a, b, dims):
    return lax.dot_general(a, b, (dims, ((), ())), precision=highest, preferred_element_type=f32)


NN = ((1,), (0,))
TN = ((0,), (0,))
NT = ((1,), (1,))


def mm_split(a, b, dims):
    a_upper, b_upper = a.astype(bf16), b.astype(bf16)
    a_lower, b_lower = (a - a_upper.astype(f32)).astype(bf16), (b - b_upper.astype(f32)).astype(bf16)
    return mm16(a_upper, b_upper, dims) + mm16(a_lower, b_upper, dims) + mm16(a_upper, b_lower, dims)


def filter_back_body(d_ref, raw_ref, fall_ref, h1_ref, h2_ref, c1_ref, c2_ref, pre1_ref, pre2_ref, feat_ref, mid_ref, last_ref, rate_ref,
                     g_in_ref, g_mid_ref, g_last_ref, g_rows_ref, g_decay_ref):
    chans = d_ref.shape[0]
    d = d_ref[...]
    q = d * (fall_ref[...] + decay_floor)
    g_last_ref[...] = mm_split(h2_ref[...], q, NT)
    decay = folded(d * raw_ref[...] * fall_ref[...] * feat_ref[0:1, :])
    g_decay_ref[...] = -jnp.sum(decay, axis=1, keepdims=True)
    u2 = mm_split(last_ref[...], q, NN) * c2_ref[...]
    rate = rate_ref[...]
    fu2 = rate * u2
    u1 = mm_split(mid_ref[...], fu2, NN) * c1_ref[...]
    fu1 = rate * u1
    g_in_ref[...] = mm_split(feat_ref[...], fu1, NT)
    g_mid_ref[...] = mm_split(h1_ref[...], fu2, NT)
    rows = jnp.concatenate([folded(fu1), folded(fu2), folded(u2 * pre2_ref[...] + u1 * pre1_ref[...])], axis=0)
    extra = jnp.zeros((-rows.shape[0] % LANE, LANE), f32)
    g_rows_ref[...] = row_totals(jnp.concatenate([rows, extra], axis=0))


def filter_back(*args):
    chans, ford, taps = args[0].shape[0], args[3].shape[0], args[9].shape[0]
    sd = jax.ShapeDtypeStruct
    out = (sd((taps, ford), f32), sd((ford, ford), f32), sd((ford, chans), f32), sd((8, -(-3 * ford // LANE) * LANE), f32), sd((chans, 1), f32))
    return whole_call(0.01, filter_back_body, out, [], *args)


def mm16(a, b, dims):
    return lax.dot_general(a, b, (dims, ((), ())), preferred_element_type=f32)


def ring_of(chips):
    zs = 4
    ys = chips // zs
    order = [(z, 0) for z in range(zs)]
    for y in range(1, ys):
        order += [(z, y) for z in (range(zs - 1, 0, -1) if y % 2 else range(1, zs))]
    order += [(0, y) for y in range(ys - 1, 0, -1)]
    return [z * ys + y for z, y in order]


def after(values, *others):
    return lax.optimization_barrier((values,) + others)[0]


def ring_hop(values, ring, by):
    chips = len(ring)
    moves = [(2 * ring[p] + q, 2 * ring[(p + by) % chips] + q) for p in range(chips) for q in range(2)]
    return lax.ppermute(values, "chan", moves)


class RingGather:
    def __init__(self, shard, ring):
        self.ring, self.hops = ring, len(ring) // 2
        self.cut = shard.shape[0] // 32 * 16
        self.behind, self.ahead = [shard], [shard]
        self.far = None

    def advance(self, upto, *others):
        while len(self.behind) <= min(upto, self.hops - 1):
            first, second = self.behind[-1], self.ahead[-1]
            if others:
                first, second = after(first, *others), after(second, *others)
            self.behind.append(ring_hop(first, self.ring, 1))
            self.ahead.append(ring_hop(second, self.ring, -1))
        if upto == self.hops:
            first, second = self.behind[-1][: self.cut], self.ahead[-1][self.cut :]
            if others:
                first, second = after(first, *others), after(second, *others)
            self.far = jnp.concatenate([ring_hop(first, self.ring, 1), ring_hop(second, self.ring, -1)], axis=0)

    def shards(self):
        return self.behind + self.ahead[1:] + [self.far]


def both_cores(shards):
    own = stack(shards)
    return own, lax.ppermute(own, "chan", [(i, i ^ 1) for i in range(2 * len(shards))])


def stack_body(*refs):
    for i, ref in enumerate(refs[:-1]):
        refs[-1][i] = ref[...]


def stack(shards):
    out = jax.ShapeDtypeStruct((len(shards),) + shards[0].shape, shards[0].dtype)
    return whole_call(0.01, stack_body, out, [], *shards)


def turn_table(ring):
    chips = len(ring)
    steps = [0] + [-k for k in range(1, chips // 2)] + [k for k in range(1, chips // 2)] + [chips // 2]
    table = np.zeros((chips, chips), np.int32)
    for p, chip in enumerate(ring):
        table[chip] = [ring[(p + k) % chips] for k in steps]
    return table


def exchange(values):
    return lax.all_to_all(values, "chan", split_axis=0, concat_axis=0, tiled=True)


def on_device(
    layer_in,
    seq_lengths,
    ln1_gain,
    first_norm_bias,
    in_weight,
    in_bias,
    short_weight,
    short_bias,
    filt_in,
    filt_in_bias,
    filt_mid,
    filt_mid_bias,
    sine_freq,
    filt_out,
    decay_rate,
    conv_bias,
    out_weight,
    out_bias,
    ln2_gain,
    second_norm_bias,
    up_weight,
    up_bias,
    down_weight,
    down_bias,
    cotangent,
):
    seqs, chans, _ = layer_in.shape
    devices = lax.axis_size("chan")
    groups = lax.axis_size("batch")
    width = LMAX // devices
    dim = chans * devices
    cols = seqs * width
    hid = up_weight.shape[0]
    ford = filt_mid.shape[0]
    place = lax.axis_index("chan")

    def to_blocks(values):
        return (
            values.reshape(seqs, chans, devices, width)
            .transpose(2, 0, 1, 3)
            .reshape(devices, seqs * chans, width)
        )

    def from_blocks(blocks):
        return (
            blocks.reshape(devices, seqs, chans, width)
            .transpose(1, 2, 0, 3)
            .reshape(seqs, chans, LMAX)
        )

    small = jnp.concatenate(
        [
            in_bias,
            short_bias,
            short_weight.reshape(3 * KS, chans),
            jnp.stack([ln1_gain, first_norm_bias, ln2_gain, second_norm_bias, out_bias, down_bias]),
            up_bias.reshape(hid // chans, chans),
        ],
        axis=0,
    )
    small = jnp.pad(small, ((0, PRM - small.shape[0]), (0, LANE - chans)))
    small = jnp.concatenate([small[:SMALL], small[SMALL:], jnp.zeros((SMALL, dim - 2 * LANE), bf16)], axis=1)
    in_rows = in_weight.transpose(1, 2, 0).reshape(3 * chans, dim)
    ring = ring_of(devices // 2)
    chips = devices // 2
    core = place % 2
    batch = lax.axis_index("batch")
    swap = [(0, 1), (1, 0)]
    partner = [(i, i ^ 1) for i in range(devices)]
    turns = lax.dynamic_index_in_dim(jnp.asarray(turn_table(ring)), place // 2, 0, False)
    table = jnp.concatenate(
        [turns, jnp.stack([core, place]).astype(jnp.int32), seq_lengths, batch.astype(jnp.int32).reshape(1)]
    )
    late = [up_weight, down_weight, out_weight]
    stepped = groups == 2 and chips == 8 and dim % (2 * LANE) == 0
    beside = [(i, i ^ 2) for i in range(devices)]
    along = [list(range(k, devices, 4)) for k in range(4)]

    def to_partner(values):
        return lax.ppermute(values, "chan", partner)

    if stepped:
        late = [lax.dynamic_slice_in_dim(a, batch * (a.shape[0] // 2), a.shape[0] // 2, 0) for a in late]
        late = jnp.concatenate(late, axis=0)
        near = lax.all_gather(late, "chan", axis=0, axis_index_groups=along)
    else:
        late = jnp.concatenate(late, axis=0)
        late = lax.all_gather(late, "chan", axis=0).reshape((chips, 2) + late.shape)
    first = RingGather(after(jnp.concatenate([small, in_rows], axis=0), late) if stepped else jnp.concatenate([small, in_rows], axis=0), ring)
    first.advance(chips // 8)
    x = exchange(to_blocks(layer_in))
    rows = seqs * chans
    xh = lax.ppermute(x[:, :rows, width - LANE :], "chan", [(i, i + 1) for i in range(devices - 1)])

    feat = jnp.asarray(FEAT)
    ramp = feat[0:1]
    rate = sine_freq[:, None]
    pre1 = mm(filt_in, feat, TN) + filt_in_bias[:, None]
    h1, c1 = jnp.sin(rate * pre1), jnp.cos(rate * pre1)
    pre2 = mm(filt_mid, h1, TN) + filt_mid_bias[:, None]
    h2, c2 = jnp.sin(rate * pre2), jnp.cos(rate * pre2)
    raw = mm(filt_out, h2, TN)
    falling = jnp.exp(-ramp * decay_rate[:, None])
    first.advance(chips // 4, h1)
    filt = raw * (falling + decay_floor)
    first.advance(3 * chips // 8, filt, x)
    filt_spec = filter_spectrum(filt)
    first.advance(chips // 2, filt_spec)
    in_own, in_other = both_cores(first.shards())
    bias_col = conv_bias[:, None]

    prm, xn1, stat1, gate, pair, projx0, projx, mixed, heads = front(
        table, x, xh, in_own, in_other, filt_spec, seqs
    )
    mixed_chan = exchange(mixed)
    cot = exchange(after(to_blocks(cotangent), mixed_chan))
    if stepped:
        near = after(near, mixed)
        far = lax.ppermute(near, "chan", beside)
        near_across = lax.ppermute(near, "batch", swap)
        near_other = to_partner(near)
    backward_hop = [(i + 1, i) for i in range(devices - 1)]
    heads = lax.ppermute(heads, "chan", backward_hop)
    conv_chan, mixed_spec = conv_forward(mixed_chan, filt_spec, bias_col, seqs)
    conv = exchange(after(conv_chan, near_across, cot, heads) if stepped else conv_chan)
    if stepped:
        far, near_across = after(far, conv_chan), after(near_across, conv_chan)
        far_across = lax.ppermute(far, "batch", swap)
        far_other, near_across_other = to_partner(far), to_partner(near_across)
        far_across_other = to_partner(far_across)
        matrices = [
            [[near, far], [near_other, far_other]],
            [[near_across, far_across], [near_across_other, far_across_other]],
        ]
        z = lax.iota(jnp.int32, 4) * 2
        y = (place // 2 % 2).astype(jnp.int32)
        order = jnp.concatenate([z + y, z + 1 - y])
    else:
        matrices = [[[lax.dynamic_index_in_dim(late, core, 1, False)], [lax.dynamic_index_in_dim(late, 1 - core, 1, False)]]]
        order = lax.iota(jnp.int32, chips)
    order = jnp.concatenate([order, table[chips:]])

    results = middle(order, conv, x, cot, gate.reshape(dim, cols), matrices, prm, hid, seqs)
    layer, d_conv, d_res, p0, p0h = results[:5]
    d_conv_chan = exchange(d_conv)
    p0h = lax.ppermute(p0h, "chan", backward_hop)

    def added(*values):
        return sum(v.astype(f32) for v in values).astype(bf16)

    if stepped:
        near_mine, far_mine = (results[5], results[7]), (results[6], results[8])
        near_theirs, far_theirs = (results[9], results[11]), (results[10], results[12])
        far_theirs = added(far_theirs[0], to_partner(far_theirs[1]))
        d_conv_chan = after(d_conv_chan, far_theirs)
        far_theirs = lax.ppermute(far_theirs, "batch", swap)
        near_theirs = added(near_theirs[0], to_partner(after(near_theirs[1], d_conv_chan)))
        near_theirs = lax.ppermute(after(near_theirs, far_theirs), "batch", swap)
        far_mine = far_mine[0], to_partner(after(far_mine[1], d_conv_chan))
        near_mine = near_mine[0], to_partner(after(near_mine[1], d_conv_chan))
    else:
        early = added(results[5], to_partner(results[6]))

    if groups == 2:
        same_core = [list(range(q, devices, 2)) for q in range(2)]
    else:
        same_core = [[b * devices + c for b in range(groups) for c in range(q, devices, 2)] for q in range(2)]

    def batch_total(values):
        return values + lax.ppermute(values, "batch", swap) if groups == 2 else lax.psum(values, "batch")

    def over_batch(table):
        if groups != 2:
            return lax.psum_scatter(table.astype(f32), "batch", scatter_dimension=1, tiled=True)
        part = dim // 2
        axis = table.ndim - 1
        mine = lax.axis_index("batch") * part
        theirs = lax.dynamic_slice_in_dim(table, part - mine, part, axis)
        kept = lax.dynamic_slice_in_dim(table, mine, part, axis)
        return kept.astype(f32) + lax.ppermute(theirs, "batch", swap).astype(f32)

    def over_chip(table):
        table = table.reshape((devices // 2, 2) + table.shape[1:])
        own = lax.dynamic_index_in_dim(table, core, 1, False)
        theirs = lax.dynamic_index_in_dim(table, 1 - core, 1, False)
        return (own.astype(f32) + lax.ppermute(theirs, "chan", partner).astype(f32)).astype(bf16)

    def over_groups(both):
        return over_batch(both).astype(bf16) if groups == 2 else both

    def over_chips(both):
        rows = both.shape[1]
        if groups == 2:
            both = lax.all_to_all(
                both, "chan", split_axis=0, concat_axis=0, tiled=True, axis_index_groups=same_core
            )
        else:
            both = both.reshape(devices // 2, rows, groups, dim // groups).transpose(2, 0, 1, 3)
            both = lax.all_to_all(
                both.reshape(groups * devices // 2, rows, dim // groups),
                ("batch", "chan"), split_axis=0, concat_axis=0, tiled=True, axis_index_groups=same_core,
            )
        return jnp.sum(both.astype(f32), axis=0)

    d_mixed_chan, d_filter, g_conv_bias = conv_backward(
        d_conv_chan, mixed_chan, mixed_spec, filt_spec, bias_col, seqs
    )
    if stepped:
        d_mixed_chan = after(d_mixed_chan, far_theirs, p0h)
        far_mine = added(*far_mine, far_theirs)
        p0h = after(p0h, far_mine)
    g_in0, sums0, acc0 = back_gate(
        table, p0.reshape(devices, chans, cols), p0h, projx0, in_own, in_other, prm, xn1, seqs
    )
    g_in0 = over_chip(g_in0)
    d_mixed = exchange(d_mixed_chan)
    layer = exchange(after(layer, d_mixed))
    if stepped:
        far_mine = lax.ppermute(far_mine, "chan", beside)
    else:
        chan_groups = [list(range(q, devices, 2)) for q in range(2)]
        early = lax.psum_scatter(early, "chan", scatter_dimension=0, tiled=True, axis_index_groups=chan_groups)[0]

    tail, g_in = back(
        table, d_mixed, pair, heads, projx, in_own, in_other, prm, xn1, x, stat1, d_res, acc0, sums0, seqs
    )
    if stepped:
        tail = after(tail, far_mine, near_theirs, layer)
        early = added(*near_mine, near_theirs, far_mine)
        early = after(early, g_in)
        d_filter = after(d_filter, early)
    tail = exchange(tail)
    g_filt_in, g_filt_mid, g_filt_out, g_rows, g_decay = filter_back(
        d_filter, raw, falling, h1, h2, c1, c2, pre1, pre2, feat, filt_mid, filt_out, rate
    )
    shared = [g_filt_in.reshape(-1), g_filt_mid.reshape(-1), g_rows[0, : 3 * ford]]
    total = batch_total(
        jnp.concatenate(shared + [g_conv_bias[:, 0], g_decay[:, 0], g_filt_out.reshape(-1)])
    )
    g_in = over_groups(jnp.concatenate([g_in0, over_chip(g_in)], axis=1))
    if stepped:
        early = lax.psum_scatter(early, "chan", scatter_dimension=0, tiled=True, axis_index_groups=along)[0]

    cut = [0]

    def take(*shape):
        n = math.prod(shape)
        part = total[cut[0] : cut[0] + n].reshape(shape)
        cut[0] += n
        return part

    shared = take(sum(v.shape[0] for v in shared))
    shared = shared + lax.ppermute(shared, "chan", partner)
    g_conv_b, g_decay_rate, g_filt_last = take(chans), take(chans), take(ford, chans)
    n_shared = shared.shape[0]
    if groups != 2:
        shared = shared / groups
    line = g_in.shape[2]
    shared = jnp.pad(shared.astype(bf16), (0, -n_shared % (8 * line))).reshape(1, -1, line)
    shared = jnp.broadcast_to(shared, (devices // 2,) + shared.shape[1:])
    mine = 3 * chans
    in_grad = over_chips(jnp.concatenate([g_in, shared], axis=1))
    if groups == 2:
        total = in_grad[mine:].reshape(-1)
    else:
        total = lax.all_gather(in_grad[mine:], "batch", axis=1, tiled=True).reshape(-1)
    in_grad = in_grad[:mine]
    cut[0] = 0
    g_filt_in, g_filt_mid = take(EMB, ford), take(ford, ford)
    g_filt_in_bias, g_filt_mid_bias, g_sine = take(ford), take(ford), take(ford)

    early = after(early, in_grad)
    early = early.astype(f32) if stepped else over_batch(early)
    up_grad, down_grad, out_grad = early[:hid], early[hid : 2 * hid], early[2 * hid :]

    grad_blocks, out_blocks = tail[:, :rows], layer[:, :rows]
    sums = jnp.concatenate([layer[:, rows:], tail[:, rows:]], axis=1)
    sums = batch_total(jnp.sum(sums.astype(f32), axis=0))
    sums = sums[0::2] + sums[1::2]
    g_gain2, g_shift2, g_out_b, g_down_b = (sums[i, :chans] for i in range(4))
    g_up_b = sums[4, :hid]
    at = SUM_ROWS // 2
    count = (2 + KS) * chans
    pieces = -(-2 * count // width)
    short0 = sums[at, :count].reshape(2 + KS, 1, chans)
    short = sums[at + 1 : at + 1 + pieces].reshape(-1)[: 2 * count].reshape(2 + KS, 2, chans)
    short = jnp.concatenate([short0, short], axis=1)
    g_in_bias, g_short_bias, g_short_weight = short[0], short[1], short[2:]
    g_gain1, g_shift1 = (sums[at + 1 + pieces + i, :chans] for i in range(2))

    return (
        from_blocks(out_blocks),
        from_blocks(grad_blocks).astype(f32),
        g_gain1,
        g_shift1,
        in_grad.reshape(3, chans, dim // groups).transpose(2, 0, 1),
        g_in_bias,
        g_short_weight,
        g_short_bias,
        g_filt_in,
        g_filt_in_bias,
        g_filt_mid,
        g_filt_mid_bias,
        g_sine,
        g_filt_last,
        g_decay_rate,
        g_conv_b,
        out_grad,
        g_out_b,
        g_gain2,
        g_shift2,
        up_grad,
        g_up_b,
        down_grad,
        g_down_b,
    )


def solution(mesh):
    token = P("batch", "chan", None)
    chan = P("chan")
    rows = P("chan", None)
    two = P(None, "chan")
    three = P(None, None, "chan")
    in_specs = (
        token, P("batch"), chan, chan, three, two, three, two, P(), P(), P(), P(), P(), two, chan, chan,
        rows, chan, chan, chan, rows, chan, rows, chan, token,
    )
    table = P("chan", "batch")
    out_specs = (
        token, token, chan, chan, P("batch", None, "chan"), two, three, two, P(), P(), P(), P(), P(), two,
        chan, chan, table, chan, chan, chan, table, chan, table, chan,
    )
    return jax.shard_map(
        on_device, mesh=mesh, in_specs=in_specs, out_specs=out_specs, check_vma=False
    )
```

```python
import functools
import math

import jax
import jax.numpy as jnp
import numpy as np
from jax import lax
from jax.experimental import pallas as pl
from jax.experimental.pallas import tpu as pltpu
from jax.sharding import PartitionSpec as P

EMB = 33
KS = 3
LMAX = 4096
LANE = 128
COARSE = LMAX // LANE
REPS = tuple(ka + 8 * kb for ka, count in ((0, 5), (1, 8), (2, 8), (3, 8), (4, 4)) for kb in range(count))
PLACE = {k1: i for i, k1 in enumerate(REPS)}
epsilon = 1e-05
decay_floor = 0.05
highest = lax.Precision.HIGHEST
f32 = jnp.float32
bf16 = jnp.bfloat16
vmem_limit = 56 * 1024 * 1024
HEAD_ROWS = 16
SUM_ROWS = 16
BATCH = 11
PRM = 32
SMALL = PRM // 2


def unit(turns):
    angle = 2.0 * math.pi * turns
    return math.cos(angle), math.sin(angle)


def scaled(z, c, s):
    re, im = z
    if im is None:
        return re * c, re * s
    return re * c - im * s, re * s + im * c


def plus(a, b):
    return a[0] + b[0], a[1] + b[1]


def minus(a, b):
    return a[0] - b[0], a[1] - b[1]


def dft4(z, sign):
    s0, d0 = plus(z[0], z[2]), minus(z[0], z[2])
    s1, d1 = plus(z[1], z[3]), minus(z[1], z[3])
    turned = (-d1[1], d1[0]) if sign > 0 else (d1[1], -d1[0])
    return [plus(s0, s1), plus(d0, turned), minus(s0, s1), minus(d0, turned)]


def dft8(z, sign):
    even, odd = dft4(z[0::2], sign), dft4(z[1::2], sign)
    c = math.sqrt(0.5)
    o1 = odd[1]
    o3 = odd[3]
    if sign > 0:
        odd1 = ((o1[0] - o1[1]) * c, (o1[0] + o1[1]) * c)
        odd2 = (-odd[2][1], odd[2][0])
        odd3 = ((-o3[0] - o3[1]) * c, (o3[0] - o3[1]) * c)
    else:
        odd1 = ((o1[0] + o1[1]) * c, (o1[1] - o1[0]) * c)
        odd2 = (odd[2][1], -odd[2][0])
        odd3 = ((o3[1] - o3[0]) * c, (-o3[0] - o3[1]) * c)
    turned = [odd[0], odd1, odd2, odd3]
    return [plus(even[i], turned[i]) for i in range(4)] + [minus(even[i], turned[i]) for i in range(4)]


def coarse_forward(xs, put):
    c = math.sqrt(0.5)
    cols = {ka: [None] * 8 for ka in range(5)}
    for b in range(8):
        x0, x1, x2, x3 = xs[b], xs[8 + b], xs[16 + b], xs[24 + b]
        s02, d02, s13, d13 = x0 + x2, x0 - x2, x1 + x3, x1 - x3
        d13c, s13c = d13 * c, s13 * c
        cols[0][b] = s02 + s13
        cols[4][b] = scaled((s02 - s13, None), *unit(-4 * b / 64))
        cols[2][b] = scaled((d02, -d13), *unit(-2 * b / 64))
        cols[1][b] = scaled((x0 + d13c, -s13c - x2), *unit(-b / 64))
        cols[3][b] = scaled((x0 - d13c, x2 - s13c), *unit(-3 * b / 64))
    for ka in (1, 2, 3):
        for kb, z in enumerate(dft8(cols[ka], -1)):
            put(ka + 8 * kb, z)
    for kb, z in enumerate(dft8(cols[4], -1)[:4]):
        put(4 + 8 * kb, z)
    r = cols[0]
    s04, d04, s26, d26 = r[0] + r[4], r[0] - r[4], r[2] + r[6], r[2] - r[6]
    s15, d15, s37, d37 = r[1] + r[5], r[1] - r[5], r[3] + r[7], r[3] - r[7]
    p, q = (d15 - d37) * c, (d15 + d37) * c
    even, odd = s04 + s26, s15 + s37
    put(0, (even + odd, None))
    put(32, (even - odd, None))
    put(16, (s04 - s26, s37 - s15))
    put(8, (d04 + p, -d26 - q))
    put(24, (d04 - p, d26 - q))


def coarse_inverse(get):
    c = math.sqrt(0.5)
    u = {}
    for ka in (1, 2, 3):
        back = dft8([get(ka + 8 * kb) for kb in range(8)], 1)
        u[ka] = [scaled(back[b], *unit(b * ka / 64)) for b in range(8)]
    v0, v32 = get(0)[0], get(32)[0]
    v8, v16, v24 = get(8), get(16), get(24)
    flat = []
    for b in range(8):
        total = v0 + v32 if b % 2 == 0 else v0 - v32
        for kb, v in ((1, v8), (2, v16), (3, v24)):
            co, si = unit(b * kb / 8)
            if abs(co) > 1e-9:
                total = total + v[0] * (2.0 * co)
            if abs(si) > 1e-9:
                total = total - v[1] * (2.0 * si)
        flat.append(total)
    odd = [get(4 + 8 * kb) for kb in range(4)]
    odd = odd + [(z[0], -z[1]) for z in odd[::-1]]
    half = dft8(odd, 1)
    quarter = []
    for b in range(8):
        co, si = unit(4 * b / 64)
        quarter.append(half[b][0] * co - half[b][1] * si)
    out = [None] * COARSE
    for b in range(8):
        u1, u2, u3 = u[1][b], u[2][b], u[3][b]
        s, d = flat[b] + quarter[b], flat[b] - quarter[b]
        dr, sr = (u1[0] - u3[0]) * c, u1[0] + u3[0]
        si_, di = (u1[1] + u3[1]) * c, u1[1] - u3[1]
        out[b] = s + 2.0 * (sr + u2[0])
        out[16 + b] = s - 2.0 * (di + u2[0])
        out[8 + b] = d + 2.0 * (dr - si_ - u2[1])
        out[24 + b] = d + 2.0 * (u2[1] - dr - si_)
    return out


def transform_tables():
    fine = np.arange(LANE)
    angle = 2.0 * math.pi * ((fine[:, None] * fine[None, :]) % LANE) / LANE
    co, si = np.cos(angle), np.sin(angle)
    ahead = np.block([[co, -si], [si, co]])
    back = ahead.T / (2.0 * LMAX)
    reps = np.array(REPS)
    turn = 2.0 * math.pi * ((reps[:, None] * fine[None, :]) % (2 * LMAX)) / (2 * LMAX)
    twist = np.concatenate([np.cos(turn), -np.sin(turn)], axis=1)[:, None, :]

    def pieces(table):
        table = table.astype(np.float32)
        upper = table.astype(jnp.bfloat16)
        lower = (table - upper.astype(np.float32)).astype(jnp.bfloat16)
        return np.stack([upper, lower])

    return pieces(ahead), pieces(back), twist.astype(np.float32)


AHEAD, BACK, TWIST = transform_tables()


def three_pass(values, table_ref):
    upper = values.astype(bf16)
    lower = (values - upper.astype(f32)).astype(bf16)
    t0, t1 = table_ref[0], table_ref[1]
    return (
        jnp.dot(upper, t0, preferred_element_type=f32)
        + jnp.dot(lower, t0, preferred_element_type=f32)
        + jnp.dot(upper, t1, preferred_element_type=f32)
    )


def rows_forward(xs_ref, spec_ref, rows):
    def step(g, carry):
        at = pl.ds(pl.multiple_of(g * 8, 8), 8)
        xs = [xs_ref[n, at, :] for n in range(COARSE)]

        def put(k1, z):
            i = PLACE[k1]
            spec_ref[i, at, 0:LANE] = z[0]
            spec_ref[i, at, LANE : 2 * LANE] = jnp.zeros_like(z[0]) if z[1] is None else z[1]

        coarse_forward(xs, put)
        return carry

    lax.fori_loop(0, rows // 8, step, 0)


def rows_inverse(spec_ref, ys_ref, rows):
    def step(g, carry):
        at = pl.ds(pl.multiple_of(g * 8, 8), 8)

        def get(k1):
            i = PLACE[k1]
            return spec_ref[i, at, 0:LANE], spec_ref[i, at, LANE : 2 * LANE]

        for n, y in enumerate(coarse_inverse(get)):
            ys_ref[n, at, :] = y
        return carry

    lax.fori_loop(0, rows // 8, step, 0)


def fine_forward(spec, twist, ahead_ref):
    re, im = spec[:, :LANE], spec[:, LANE:]
    tr, ti = twist[:, :LANE], twist[:, LANE:]
    return three_pass(jnp.concatenate([re * tr - im * ti, re * ti + im * tr], axis=1), ahead_ref)


def fine_inverse(spec, twist, back_ref):
    v = three_pass(spec, back_ref)
    re, im = v[:, :LANE], v[:, LANE:]
    tr, ti = twist[:, :LANE], twist[:, LANE:]
    return jnp.concatenate([re * tr + im * ti, im * tr - re * ti], axis=1)


def times(a, b):
    ar, ai, br, bi = a[:, :LANE], a[:, LANE:], b[:, :LANE], b[:, LANE:]
    return jnp.concatenate([ar * br - ai * bi, ar * bi + ai * br], axis=1)


def times_conj(a, b):
    ar, ai, br, bi = a[:, :LANE], a[:, LANE:], b[:, :LANE], b[:, LANE:]
    return jnp.concatenate([ar * br + ai * bi, ai * br - ar * bi], axis=1)


def together(values):
    return values.reshape(values.shape[0] * values.shape[1], values.shape[2])


def apart(values):
    return values.reshape(BATCH, values.shape[0] // BATCH, values.shape[1])


def twists(twist_ref, at, rows):
    return together(jnp.broadcast_to(twist_ref[at], (BATCH, rows, 2 * LANE)))


def spread(blocks_ref, xs_ref):
    per = blocks_ref.shape[2] // LANE
    for n in range(COARSE):
        r = n % per
        xs_ref[n] = blocks_ref[n // per, :, r * LANE : (r + 1) * LANE].astype(f32)


def filter_spectrum_body(filter_ref, twist_ref, ahead_ref, out_ref, xs_ref):
    rows = filter_ref.shape[0]
    for n in range(COARSE):
        xs_ref[n] = filter_ref[:, n * LANE : (n + 1) * LANE]
    rows_forward(xs_ref, out_ref, rows)

    def step(i, carry):
        at = pl.ds(i * BATCH, BATCH)
        out_ref[at] = apart(fine_forward(together(out_ref[at]), twists(twist_ref, at, rows), ahead_ref))
        return carry

    lax.fori_loop(0, len(REPS) // BATCH, step, 0)


def conv_forward_body(seqs, mixed_ref, filt_ref, bias_ref, twist_ref, ahead_ref, back_ref, out_ref, spec_ref, xs_ref, work_ref):
    rows = mixed_ref.shape[1]
    spread(mixed_ref, xs_ref)
    rows_forward(xs_ref, work_ref, rows)

    def step(i, carry):
        at = pl.ds(i * BATCH, BATCH)
        twist = twists(twist_ref, at, rows)
        z = fine_forward(together(work_ref[at]), twist, ahead_ref)
        spec_ref[at] = apart(z).astype(bf16)
        k = together(jnp.concatenate([filt_ref[at]] * seqs, axis=1))
        work_ref[at] = apart(fine_inverse(times(z, k), twist, back_ref))
        return carry

    lax.fori_loop(0, len(REPS) // BATCH, step, 0)
    ys_ref = xs_ref
    rows_inverse(work_ref, ys_ref, rows)
    per = mixed_ref.shape[2] // LANE
    bias = jnp.concatenate([bias_ref[...]] * seqs, axis=0)
    for n in range(COARSE):
        at = (n // per, slice(None), slice((n % per) * LANE, (n % per + 1) * LANE))
        out_ref[at] = (ys_ref[n] + bias * mixed_ref[at].astype(f32)).astype(bf16)


def heads_out(out_ref, block, y):
    rows, width = y.shape[0], out_ref.shape[2]
    square = jnp.concatenate([y, jnp.zeros((LANE - rows, LANE), f32)], axis=0) if rows < LANE else y
    head = square.T[:HEAD_ROWS]
    if width > LANE:
        head = jnp.concatenate([head, jnp.zeros((HEAD_ROWS, width - LANE), f32)], axis=1)
    out_ref[block, rows:, :] = head.astype(bf16)


def conv_backward_body(
    seqs, d_ref, mixed_ref, mixed_spec_ref, filt_ref, bias_ref, twist_ref, ahead_ref, back_ref, out_ref, dfilt_ref, dbias_ref, xs_ref, spec_ref, work_ref, ys_ref
):
    rows = d_ref.shape[1]
    chans = rows // seqs
    spread(d_ref, xs_ref)
    rows_forward(xs_ref, spec_ref, rows)

    def step(i, carry):
        at = pl.ds(i * BATCH, BATCH)
        z = fine_forward(together(spec_ref[at]), twists(twist_ref, at, rows), ahead_ref)
        k = together(jnp.concatenate([filt_ref[at]] * seqs, axis=1))
        cross = apart(times_conj(z, together(mixed_spec_ref[at].astype(f32))))
        cross = sum(cross[:, s * chans : (s + 1) * chans] for s in range(seqs))
        both = together(jnp.concatenate([apart(times_conj(z, k)), cross], axis=1))
        work_ref[at] = apart(fine_inverse(both, twists(twist_ref, at, rows + chans), back_ref))
        return carry

    lax.fori_loop(0, len(REPS) // BATCH, step, 0)
    rows_inverse(work_ref, ys_ref, rows + chans)
    per = d_ref.shape[2] // LANE
    bias = jnp.concatenate([bias_ref[...]] * seqs, axis=0)
    total = jnp.zeros((rows, LANE), f32)
    out_ref[out_ref.shape[0] - 1, rows:, :] = jnp.zeros((HEAD_ROWS, d_ref.shape[2]), bf16)
    for n in range(COARSE):
        at = (n // per, slice(0, rows), slice((n % per) * LANE, (n % per + 1) * LANE))
        d = xs_ref[n]
        y = ys_ref[n, :rows, :] + bias * d
        out_ref[at] = y.astype(bf16)
        if n % per == 0 and n > 0:
            heads_out(out_ref, n // per - 1, y)
        total = total + d * mixed_ref[at].astype(f32)
        dfilt_ref[:, n * LANE : (n + 1) * LANE] = ys_ref[n, rows:, :]
    total = sum(total[s * chans : (s + 1) * chans] for s in range(seqs))
    dbias_ref[...] = jnp.sum(total, axis=1, keepdims=True)


def takes(us):
    return pl.CostEstimate(flops=int(us * 1e9), bytes_accessed=int(us * 3e6), transcendentals=0)


def whole_call(us, body, out_shape, scratch, *args):
    return pl.pallas_call(
        body,
        cost_estimate=takes(us),
        out_shape=out_shape,
        in_specs=[pl.BlockSpec(memory_space=pltpu.VMEM)] * len(args),
        out_specs=jax.tree.map(lambda _: pl.BlockSpec(memory_space=pltpu.VMEM), out_shape),
        scratch_shapes=scratch,
        compiler_params=pltpu.CompilerParams(vmem_limit_bytes=vmem_limit),
    )(*args)


def filter_spectrum(filt):
    rows = filt.shape[0]
    return whole_call(
        8,
        filter_spectrum_body,
        jax.ShapeDtypeStruct((len(REPS), rows, 2 * LANE), f32),
        [pltpu.VMEM((COARSE, rows, LANE), f32)],
        filt,
        jnp.asarray(TWIST),
        jnp.asarray(AHEAD),
    )


def conv_forward(mixed, filt_spec, bias, seqs):
    blocks, rows, width = mixed.shape
    n = len(REPS)
    return whole_call(
        100,
        lambda *refs: conv_forward_body(seqs, *refs),
        (jax.ShapeDtypeStruct(mixed.shape, bf16), jax.ShapeDtypeStruct((n, rows, 2 * LANE), bf16)),
        [pltpu.VMEM((COARSE, rows, LANE), f32), pltpu.VMEM((n, rows, 2 * LANE), f32)],
        mixed,
        filt_spec,
        bias,
        jnp.asarray(TWIST),
        jnp.asarray(AHEAD),
        jnp.asarray(BACK),
    )


def conv_backward(d_conv, mixed, mixed_spec, filt_spec, bias, seqs):
    blocks, rows, width = mixed.shape
    chans = rows // seqs
    n = len(REPS)
    return whole_call(
        100,
        lambda *refs: conv_backward_body(seqs, *refs),
        (
            jax.ShapeDtypeStruct((blocks, rows + HEAD_ROWS, width), bf16),
            jax.ShapeDtypeStruct((chans, LMAX), f32),
            jax.ShapeDtypeStruct((chans, 1), f32),
        ),
        [
            pltpu.VMEM((COARSE, rows, LANE), f32),
            pltpu.VMEM((n, rows, 2 * LANE), f32),
            pltpu.VMEM((n, rows + chans, 2 * LANE), f32),
            pltpu.VMEM((COARSE, rows + chans, LANE), f32),
        ],
        d_conv,
        mixed,
        mixed_spec,
        filt_spec,
        bias,
        jnp.asarray(TWIST),
        jnp.asarray(AHEAD),
        jnp.asarray(BACK),
    )


CHUNK = 48


def lanes_of(shape):
    return lax.broadcasted_iota(jnp.int32, shape, 1)


def side_by_side(block, seqs):
    chans = block.shape[0] // seqs
    return jnp.concatenate([block[s * chans : (s + 1) * chans] for s in range(seqs)], axis=1)


def stacked(values, seqs):
    width = values.shape[1] // seqs
    return jnp.concatenate([values[:, s * width : (s + 1) * width] for s in range(seqs)], axis=0)


def eights(values):
    return jnp.sum(values.reshape(values.shape[0] // 8, 8, values.shape[1]), axis=0)


def folded(values):
    return sum(values[:, i * LANE : (i + 1) * LANE] for i in range(values.shape[1] // LANE))


def row_totals(values):
    ones = jnp.ones((8, LANE), bf16)
    upper = values.astype(bf16)
    lower = (values - upper.astype(f32)).astype(bf16)
    return mm16(ones, upper, NT) + mm16(ones, lower, NT)


def padded_totals(values, width):
    extra = -values.shape[0] % width
    if extra:
        values = jnp.concatenate([values, jnp.zeros((extra, LANE), f32)], axis=0)
    totals = row_totals(values)
    return [totals[:, i * width : (i + 1) * width] for i in range(totals.shape[1] // width)]


def as_rows(totals, rows):
    halves = []
    for t in totals:
        upper = t.astype(bf16).astype(f32)
        halves += [upper, t - upper]
    place = lax.broadcasted_iota(jnp.int32, halves[0].shape, 0)
    tiles = []
    for first in range(0, rows, 8):
        tile = jnp.zeros_like(halves[0])
        for i, h in enumerate(halves[first : first + 8]):
            tile = jnp.where(place == i, h, tile)
        tiles.append(tile)
    return jnp.concatenate(tiles, axis=0).astype(bf16)


def chunk_rows(i):
    return pl.ds(pl.multiple_of(i * CHUNK, CHUNK), CHUNK)


def norm_stats(ref, dim):
    cols = ref.shape[1]
    zero = jnp.zeros((8, cols), f32)
    total = lax.fori_loop(0, dim // CHUNK, lambda i, t: t + eights(ref[chunk_rows(i), :]), zero)
    mean = jnp.sum(total, axis=0, keepdims=True) / dim

    def spread_sq(i, t):
        v = ref[chunk_rows(i), :] - mean
        return t + eights(v * v)

    var = jnp.sum(lax.fori_loop(0, dim // CHUNK, spread_sq, zero), axis=0, keepdims=True) / dim
    return mean, lax.rsqrt(var + epsilon)


def front_body(
    seqs, table_ref, x_ref, xh_ref, own_ref, other_ref, own_small, other_small, after_ref,
    prm_ref, xn_ref, stat_ref, gate_ref, pair_ref, projx0_ref, projx_ref, mixed_ref, heads_ref, xs, xb,
):
    devices, _, width = x_ref.shape
    dim, cols = xn_ref.shape
    chans = dim // devices
    turns = devices // 2
    step = pl.program_id(0)

    @pl.when(step == 0)
    def _():
        for turn in range(turns):
            for ref, (device, _) in zip((own_small, other_small), slots(table_ref, turns, turn)):
                small = ref[turn].astype(f32)
                small = jnp.concatenate([small[:, :LANE], small[:, LANE:], jnp.zeros((LANE - PRM, LANE), f32)], axis=0)
                prm_ref[pl.ds(pl.multiple_of(device * chans, 8), chans), :] = small.T[:chans, :PRM]

        def gather(d, carry):
            at = pl.ds(pl.multiple_of(d * chans, 8), chans)
            row = side_by_side(x_ref[d].astype(f32), seqs)
            tail = xh_ref[d].astype(f32)
            tail = jnp.where(
                lanes_of((chans, LANE)) < LANE // 2, pltpu.roll(tail[chans : 2 * chans], LANE // 2, 1), tail[:chans]
            )
            xs[at, :] = jnp.concatenate([row, tail], axis=1)
            return carry

        lax.fori_loop(0, devices, gather, 0)
        mean, inverse = norm_stats(xs, dim)

        def scale(i, carry):
            at = chunk_rows(i)
            prm = prm_ref[at, :]
            v = (xs[at, :] - mean) * inverse * prm[:, 15:16] + prm[:, 16:17]
            xb[at, :] = v.astype(bf16)
            xn_ref[at, :] = v[:, :cols].astype(bf16)
            return carry

        lax.fori_loop(0, dim // CHUNK, scale, 0)
        stat_ref[0:8, :] = jnp.broadcast_to(mean[:, :cols], (8, cols))
        stat_ref[8:16, :] = jnp.broadcast_to(inverse[:, :cols], (8, cols))

    keep = (table_ref[turns + 1] > 0).astype(f32)
    for w_ref, (device, g) in zip((own_ref, other_ref), slots(table_ref, turns, step)):
        prm = prm_ref[pl.ds(pl.multiple_of(device * chans, 8), chans), :]
        proj = mm16(w_ref[0, SMALL:, :], xb[...], NN)
        ys = []
        px = []
        for i in range(3):
            x = proj[i * chans : (i + 1) * chans] + prm[:, i : i + 1]
            tail = x[:, cols:] * keep
            px += [jnp.concatenate([x[:, :cols], tail], axis=1)]
            weights = [jnp.broadcast_to(prm[:, 6 + 3 * j + i : 7 + 3 * j + i], (chans, width)) for j in range(KS)]
            bias = jnp.broadcast_to(prm[:, 3 + i : 4 + i], (chans, width))
            parts = []
            for s in range(seqs):
                v = x[:, s * width : (s + 1) * width]
                wide = jnp.concatenate([tail if s == 0 else pltpu.roll(tail, LANE // 2, 1), v], axis=1)
                y = bias + weights[0] * v
                for j in range(1, KS):
                    y = y + weights[j] * pltpu.roll(wide, j, 1)[:, LANE:]
                parts.append(y)
            ys.append(jnp.concatenate(parts, axis=1))
        projx0_ref[g] = px[0].astype(bf16)
        projx_ref[g] = jnp.concatenate(px[1:], axis=0).astype(bf16)
        gate_ref[g] = ys[0]
        pair = jnp.concatenate(ys[1:], axis=0)
        pair_ref[g] = pair.astype(bf16)
        mixed_ref[g] = stacked(ys[1] * ys[2], seqs).astype(bf16)
        heads_ref[g] = first_tokens(pair, seqs).astype(bf16)


def first_tokens(values, seqs):
    rows, width = values.shape[0], values.shape[1] // seqs
    pad = jnp.zeros((LANE - rows, LANE), f32)
    heads = []
    for s in range(seqs):
        tile = values[:, s * width : s * width + LANE]
        heads.append((jnp.concatenate([tile, pad], axis=0) if rows < LANE else tile).T[:8])
    return jnp.concatenate(heads, axis=0)


def token_columns(heads, rows):
    gap = jnp.zeros((LANE // 2 - 8, LANE), f32)
    return jnp.concatenate([heads[:8], gap, heads[8:], gap], axis=0).T[:rows]


def whole(a):
    return pl.BlockSpec(a.shape, lambda i, t: (0,) * len(a.shape), pipeline_mode=pl.Buffered(1))


def untouched():
    return pl.BlockSpec(memory_space=pl.ANY)


def by_chip(a):
    return pl.BlockSpec((2,) + a.shape[1:], lambda i, t: (t[i],) + (0,) * (len(a.shape) - 1))


def by_turn(a, rows=None):
    return pl.BlockSpec((1, a.shape[1] if rows is None else rows, a.shape[2]), lambda i, t: (i, 0, 0))


def chip_call(us, body, table, turns, args, in_specs, out, out_specs, scratch):
    return pl.pallas_call(
        body,
        cost_estimate=takes(us),
        out_shape=out,
        grid_spec=pltpu.PrefetchScalarGridSpec(
            num_scalar_prefetch=1,
            grid=(turns,),
            in_specs=in_specs,
            out_specs=out_specs,
            scratch_shapes=scratch,
        ),
        compiler_params=pltpu.CompilerParams(vmem_limit_bytes=vmem_limit, dimension_semantics=("arbitrary",)),
    )(table, *args)


def slots(table_ref, turns, step):
    core = table_ref[turns]
    chip = table_ref[step]
    return ((2 * chip + core, core), (2 * chip + 1 - core, 1 - core))


def front(table, x, xh, own, other, before, seqs):
    devices, rows, width = x.shape
    chans = rows // seqs
    dim = devices * chans
    cols = seqs * width
    turns = devices // 2
    sd = jax.ShapeDtypeStruct
    out = (
        sd((dim, PRM), f32),
        sd((dim, cols), bf16),
        sd((16, cols), f32),
        sd((devices, chans, cols), f32),
        sd((devices, 2 * chans, cols), bf16),
        sd((devices, chans, cols + LANE), bf16),
        sd((devices, 2 * chans, cols + LANE), bf16),
        sd((devices, rows, width), bf16),
        sd((devices, 8 * seqs, LANE), bf16),
    )
    small = pl.BlockSpec((turns, SMALL, 2 * LANE), lambda i, t: (0, 0, 0), pipeline_mode=pl.Buffered(1))
    return chip_call(
        2,
        lambda *refs: front_body(seqs, *refs),
        table,
        turns,
        (x, xh, own, other, own, other, before),
        [whole(x), whole(xh), by_turn(own), by_turn(other), small, small, untouched()],
        out,
        tuple(whole(o) for o in out[:3]) + tuple(by_chip(o) for o in out[3:]),
        [pltpu.VMEM((dim, cols + LANE), f32), pltpu.VMEM((dim, cols + LANE), bf16)],
    )


def middle_body(seqs, pieces, segments, per, table_ref, conv_ref, x_ref, cot_ref, gate_ref, prm_ref, *refs):
    weights = []
    for _ in range(pieces):
        weights.append([[refs[2 * (segments * core + n) : 2 * (segments * core + n) + 2] for n in range(segments)] for core in range(2)])
        refs = refs[4 * segments :]
    layer_ref, d_conv_ref, d_res_ref, p0_ref, p0h_ref = refs[:5]
    grads = [[refs[5 + segments * (2 * p + n) : 5 + segments * (2 * p + n + 1)] for n in range(2)] for p in range(pieces)]
    refs = refs[5 + 2 * pieces * segments :]
    cs, res, ds, xb, db, gb, acc_out, acc_in, folds, up_folds, stats, out_w32, out_w_ref, gs = refs
    devices, _, width = x_ref.shape
    dim, cols = d_res_ref.shape
    chans = dim // devices
    hid = weights[0][0][0][0].shape[1] // 2 * pieces
    turns = devices // 2
    part, some_hid, some_out = dim // pieces, hid // pieces, chans // pieces
    group = table_ref[turns + 2 + seqs] if pieces == 2 else 0
    halves = [group, 1 - group][:pieces]
    columns = [pl.ds(pl.multiple_of(h * part, LANE), part) for h in halves]
    step = pl.program_id(0)
    last = pl.num_programs(0) - 1
    lane = lanes_of((1, cols))
    live = jnp.zeros((1, cols), f32)
    for s in range(seqs):
        position = table_ref[turns + 1] * width + lane - s * width
        inside = (lane >= s * width) & (lane < (s + 1) * width) & (position < table_ref[turns + 2 + s])
        live = jnp.where(inside, 1.0, live)

    def device_rows(d):
        return pl.ds(pl.multiple_of(d * chans, 8), chans)

    @pl.when(step == 0)
    def _():
        def gather(d, carry):
            at = device_rows(d)
            cs[at, :] = side_by_side(conv_ref[d].astype(f32), seqs)
            res[at, :] = side_by_side(x_ref[d].astype(f32), seqs)
            ds[at, :] = live * side_by_side(cot_ref[d].astype(f32), seqs)
            return carry

        lax.fori_loop(0, devices, gather, 0)
        for piece, h in zip(weights, halves):
            for core, parts in enumerate(piece):
                turn = 0
                for _, out_rows in parts:
                    for n in range(out_rows.shape[0]):
                        device, _ = slots(table_ref, turns, turn)[core]
                        at = pl.ds(pl.multiple_of(device * chans + h * some_out, 8), some_out)
                        out_w32[at, :] = out_rows[n].astype(f32)
                        turn += 1

        def gated(i, carry):
            at = chunk_rows(i)
            out_w_ref[at, :] = out_w32[at, :].astype(bf16)
            gb[at, :] = (cs[at, :] * gate_ref[at, :]).astype(bf16)
            d = ds[at, :]
            db[at, :] = d.astype(bf16)
            folds[3, at, :] = folded(d)
            acc_in[at, :] = jnp.zeros((CHUNK, cols), f32)
            return carry

        lax.fori_loop(0, dim // CHUNK, gated, 0)
        acc_out[...] = mm16(out_w_ref[...], gb[...], TN)

        def add(i, carry):
            at = chunk_rows(i)
            res[at, :] = res[at, :] + acc_out[at, :] + prm_ref[at, 19:20]
            acc_out[at, :] = jnp.zeros((CHUNK, cols), f32)
            return carry

        lax.fori_loop(0, dim // CHUNK, add, 0)
        mean, inverse = norm_stats(res, dim)

        def scale(i, carry):
            at = chunk_rows(i)
            normed = (res[at, :] - mean) * inverse
            cs_norm = normed * prm_ref[at, 17:18] + prm_ref[at, 18:19]
            xb[at, :] = cs_norm.astype(bf16)
            return carry

        lax.fori_loop(0, dim // CHUNK, scale, 0)
        stats[0:8, :] = jnp.broadcast_to(mean, (8, cols))
        stats[8:16, :] = jnp.broadcast_to(inverse, (8, cols))

    pair = [device for j in range(per) for device, _ in slots(table_ref, turns, step * per + j)]
    up_b = []
    for device in pair:
        prm = prm_ref[device_rows(device), :]
        for h in halves:
            for m in range(some_hid // chans):
                first, second = 21 + m, 21 + m + (pieces - 1) * some_hid // chans
                up_b.append(jnp.where(h == 0, prm[:, first : first + 1], prm[:, second : second + 1]))
    up_b = jnp.concatenate(up_b, axis=0)

    def now(parts, rows, j):
        blocks = [ref[j, rows, :] for ref, _ in parts]
        return blocks[0] if len(blocks) == 1 else jnp.where(step * per < turns // 2, blocks[0], blocks[1])

    def rows_now(rows):
        return jnp.concatenate(
            [now(piece[core], rows, j) for j in range(per) for core in range(2) for piece in weights], axis=0
        )

    up, down = rows_now(slice(0, some_hid)), rows_now(slice(some_hid, 2 * some_hid))
    u = mm16(up, xb[...], NN) + up_b
    d_act = mm16(down, db[...], NN)
    a, k = 0.044715, math.sqrt(2.0 / math.pi)
    sq = u * u
    t = jnp.tanh(u * (k + (k * a) * sq))
    half = 0.5 * (1.0 + t)
    act = (u * half).astype(bf16)
    d_u = d_act * (half + 0.5 * u * (1.0 - t * t) * (k + (3.0 * k * a) * sq))
    d_low = d_u.astype(bf16)
    fold = folded(d_u)
    acc_out[...] += mm16(down, act, TN)
    acc_in[...] += mm16(up, d_low, TN)
    spots = [(n, p, h) for n in range(2 * per) for p, h in enumerate(halves)]
    for n, p, h in spots:
        rows = slice((n * pieces + p) * some_hid, (n * pieces + p + 1) * some_hid)
        up_folds[pl.ds(pl.multiple_of(pair[n] * hid + h * some_hid, 8), some_hid), :] = fold[rows]
    gs[0] = mm16(d_low, xb[...], NT).astype(bf16)
    gs[1] = mm16(act, db[...], NT).astype(bf16)

    def hand_out(k):
        for n, p, h in spots:
            rows = slice((n * pieces + p) * some_hid, (n * pieces + p + 1) * some_hid)
            for which in range(2):
                at = pl.ds(pl.multiple_of(which * hid + h * some_hid, some_hid), some_hid)
                for g_refs, some in zip(grads, columns):
                    g_refs[n % 2][k][step * per + n // 2 - k * (turns // segments), at, :] = gs[which, rows, some]

    for k in range(segments):
        count = turns // segments
        pl.when((step * per >= k * count) & (step * per < (k + 1) * count))(functools.partial(hand_out, k))

    @pl.when(step == last)
    def _():
        mean, inverse = stats[0:1, :], stats[8:9, :]

        def result(i, t):
            at = chunk_rows(i)
            r = res[at, :]
            acc_out[at, :] = live * (r + acc_out[at, :] + prm_ref[at, 20:21])
            normed = (r - mean) * inverse
            d = acc_in[at, :]
            both = d * normed
            folds[0, at, :] = folded(both)
            folds[1, at, :] = folded(d)
            gain = prm_ref[at, 17:18]
            return t[0] + eights(d * gain), t[1] + eights(both * gain)

        zero = jnp.zeros((8, cols), f32)
        m1, m2 = lax.fori_loop(0, dim // CHUNK, result, (zero, zero))
        m1 = jnp.sum(m1, axis=0, keepdims=True) / dim
        m2 = jnp.sum(m2, axis=0, keepdims=True) / dim

        def residual(i, carry):
            at = chunk_rows(i)
            normed = (res[at, :] - mean) * inverse
            d = ds[at, :] + inverse * (acc_in[at, :] * prm_ref[at, 17:18] - m1 - normed * m2)
            d_res_ref[at, :] = d
            folds[2, at, :] = folded(d)
            db[at, :] = d.astype(bf16)
            return carry

        lax.fori_loop(0, dim // CHUNK, residual, 0)
        for n in range(dim // 256):
            some = slice(n * 256, (n + 1) * 256)
            acc_in[some, :] = mm16(out_w_ref[some, :], db[...], NN)
            out_w32[some, :] = mm16(gb[some, :], db[...], NT)
        for g_refs, at in zip(grads, columns):
            for turn in range(turns):
                for g_ref, (device, _) in zip(g_refs, slots(table_ref, turns, turn)):
                    count = turns // segments
                    g_ref[turn // count][turn % count, 2 * hid :, :] = out_w32[device_rows(device), at].astype(bf16)

        def products(i, carry):
            at = chunk_rows(i)
            d = acc_in[at, :]
            p0 = d * cs[at, :]
            p0_ref[at, :] = p0
            acc_in[at, :] = d * gate_ref[at, :]
            return carry

        lax.fori_loop(0, dim // CHUNK, products, 0)

        def scatter(d, carry):
            at = device_rows(d)
            p0h_ref[d] = first_tokens(p0_ref[at, :], seqs).astype(bf16)
            layer_ref[d, : seqs * chans, :] = stacked(acc_out[at, :], seqs).astype(bf16)
            d_conv_ref[d] = stacked(acc_in[at, :], seqs).astype(bf16)
            totals = [padded_totals(folds[q, at, :], width)[0] for q in range(4)]
            totals += padded_totals(up_folds[pl.ds(pl.multiple_of(d * hid, 8), hid), :], width)
            layer_ref[d, seqs * chans :, :] = as_rows(totals, SUM_ROWS)
            return carry

        lax.fori_loop(0, devices, scatter, 0)


def middle(table, conv, x, cot, gate, matrices, prm, hid, seqs):
    devices, rows, width = conv.shape
    dim, cols = gate.shape
    chans = dim // devices
    turns = devices // 2
    pieces, segments = len(matrices), len(matrices[0][0])
    part, some_hid, some_out = dim // pieces, hid // pieces, chans // pieces
    sd = jax.ShapeDtypeStruct
    out = (
        sd((devices, rows + SUM_ROWS, width), bf16),
        sd((devices, rows, width), bf16),
        sd((dim, cols), f32),
        sd((dim, cols), f32),
        sd((devices, 8 * seqs, LANE), bf16),
    ) + (sd((turns // segments, 2 * hid + chans, part), bf16),) * (2 * pieces * segments)
    big = pltpu.VMEM((dim, cols), f32)
    low = pltpu.VMEM((dim, cols), bf16)
    args, specs = [conv, x, cot, gate, prm], [whole(conv), whole(x), whole(cot), whole(gate), whole(prm)]
    per = 2
    for piece in matrices:
        for parts in piece:
            first = 0
            for a in parts:
                count = a.shape[0]
                args += [a, a]
                specs += [
                    pl.BlockSpec(
                        (per, 2 * some_hid, dim),
                        lambda i, t, f=first // per, c=count // per: (jnp.clip(i - f, 0, c - 1), 0, 0),
                    ),
                    pl.BlockSpec(
                        (count, some_out, dim), lambda i, t: (0, 2 * some_hid // some_out, 0), pipeline_mode=pl.Buffered(1)
                    ),
                ]
                first += count
    return chip_call(
        36,
        lambda *refs: middle_body(seqs, pieces, segments, per, *refs),
        table,
        turns // per,
        args,
        specs,
        out,
        tuple(whole(o) for o in out),
        [
            big, big, big, low, low, low, big, big, pltpu.VMEM((4, dim, LANE), f32),
            pltpu.VMEM((devices * hid, LANE), f32), pltpu.VMEM((16, cols), f32), pltpu.VMEM((dim, dim), f32),
            pltpu.VMEM((dim, dim), bf16), pltpu.VMEM((2, 2 * per * hid, dim), bf16),
        ],
    )


def short_back(seqs, prm, kinds, d_short, head, projx, width, cols):
    chans = prm.shape[0]
    d_proj = []
    totals = [[] for _ in range(2 + KS)]
    for n, i in enumerate(kinds):
        px = projx[n * chans : (n + 1) * chans]
        weights = [jnp.broadcast_to(prm[:, 6 + 3 * j + i : 7 + 3 * j + i], (chans, width)) for j in range(KS)]
        parts = []
        sums = [0.0] * (2 + KS)
        for s in range(seqs):
            at = slice(s * width, (s + 1) * width)
            d = d_short[n][:, at]
            x = px[:, at]
            tail = px[:, cols:]
            wide = jnp.concatenate([tail if s == 0 else pltpu.roll(tail, LANE // 2, 1), x], axis=1)
            after = jnp.concatenate([d, head[n] if s == 0 else pltpu.roll(head[n], LANE // 2, 1)], axis=1)
            y = weights[0] * d
            sums[1] = sums[1] + folded(d)
            sums[2] = sums[2] + folded(d * x)
            for j in range(1, KS):
                y = y + weights[j] * pltpu.roll(after, width + LANE - j, 1)[:, :width]
                sums[2 + j] = sums[2 + j] + folded(d * pltpu.roll(wide, j, 1)[:, LANE:])
            sums[0] = sums[0] + folded(y)
            parts.append(y)
        d_proj.append(jnp.concatenate(parts, axis=1))
        for k in range(2 + KS):
            totals[k].append(sums[k])
    d_low = jnp.concatenate(d_proj, axis=0).astype(bf16)
    return d_low, padded_totals(jnp.concatenate(sum(totals, []), axis=0), width)


def back_gate_body(seqs, table_ref, p0_ref, p0h_ref, projx_ref, own_ref, other_ref, prm_ref, xn_ref, g_ref, sums_ref, acc):
    dim, cols = xn_ref.shape
    chans = p0_ref.shape[1]
    step = pl.program_id(0)

    @pl.when(step == 0)
    def _():
        acc[...] = jnp.zeros_like(acc)

    turns = prm_ref.shape[0] // chans // 2
    for w_ref, (device, g) in zip((own_ref, other_ref), slots(table_ref, turns, step)):
        prm = prm_ref[pl.ds(pl.multiple_of(device * chans, 8), chans), :]
        d_low, totals = short_back(
            seqs, prm, (0,), (p0_ref[g],), (token_columns(p0h_ref[g].astype(f32), chans),), projx_ref[g].astype(f32), cols // seqs, cols
        )
        sums_ref[g] = totals[0]
        acc[...] += mm16(w_ref[0, SMALL : SMALL + chans, :], d_low, TN)
        g_ref[g] = mm16(d_low, xn_ref[...], NT).astype(bf16)


def back_gate(table, p0, p0h, projx, own, other, prm, xn, seqs):
    devices, chans, cols = p0.shape
    dim = xn.shape[0]
    sd = jax.ShapeDtypeStruct
    out = (
        sd((devices, chans, dim), bf16),
        sd((devices, 8, cols // seqs), f32),
        sd((dim, cols), f32),
    )
    return chip_call(
        2,
        lambda *refs: back_gate_body(seqs, *refs),
        table,
        devices // 2,
        (p0, p0h, projx, own, other, prm, xn),
        [by_chip(a) for a in (p0, p0h, projx)] + [by_turn(own), by_turn(other), whole(prm), whole(xn)],
        out,
        (by_chip(out[0]), by_chip(out[1]), whole(out[2])),
        [],
    )


def back_body(
    seqs, table_ref, d_mixed_ref, pair_ref, heads_ref, projx_ref, own_ref, other_ref, prm_ref, xn_ref, x_ref, stat_ref, d_res_ref,
    acc0_ref, sums0_ref, tail_ref, g_ref, acc, xs, folds, sums,
):
    devices, _, width = x_ref.shape
    dim, cols = xn_ref.shape
    chans = dim // devices
    step = pl.program_id(0)
    last = pl.num_programs(0) - 1

    @pl.when(step == 0)
    def _():
        acc[...] = acc0_ref[...]

    turns = devices // 2
    for w_ref, (device, g) in zip((own_ref, other_ref), slots(table_ref, turns, step)):
        prm = prm_ref[pl.ds(pl.multiple_of(device * chans, 8), chans), :]
        block = d_mixed_ref[g].astype(f32)
        d_mixed = side_by_side(block[: seqs * chans], seqs)
        square = jnp.concatenate([block[seqs * chans :, :LANE], jnp.zeros((LANE - HEAD_ROWS, LANE), f32)], axis=0).T
        second = pltpu.roll(square[chans : 2 * chans], LANE // 2, 1)
        d_head = jnp.where(lanes_of((chans, LANE)) < LANE // 2, square[:chans], second)
        pair = pair_ref[g].astype(f32)
        pair_head = token_columns(heads_ref[g].astype(f32), 2 * chans)
        d_short = (d_mixed * pair[chans:], d_mixed * pair[:chans])
        head = (d_head * pair_head[chans:], d_head * pair_head[:chans])
        d_low, totals = short_back(seqs, prm, (1, 2), d_short, head, projx_ref[g].astype(f32), width, cols)
        for n, t in enumerate(totals):
            sums[n, device] = t
        acc[...] += mm16(w_ref[0, SMALL + chans :, :], d_low, TN)
        g_ref[g] = mm16(d_low, xn_ref[...], NT).astype(bf16)

    @pl.when(step == last)
    def _():
        def gather(d, carry):
            xs[pl.ds(pl.multiple_of(d * chans, 8), chans), :] = side_by_side(x_ref[d].astype(f32), seqs)
            return carry

        lax.fori_loop(0, devices, gather, 0)
        mean, inverse = stat_ref[0:1, :], stat_ref[8:9, :]

        def first(i, t):
            at = chunk_rows(i)
            normed = (xs[at, :] - mean) * inverse
            d = acc[at, :]
            both = d * normed
            folds[0, at, :] = folded(both)
            folds[1, at, :] = folded(d)
            gain = prm_ref[at, 15:16]
            return t[0] + eights(d * gain), t[1] + eights(both * gain)

        zero = jnp.zeros((8, cols), f32)
        m1, m2 = lax.fori_loop(0, dim // CHUNK, first, (zero, zero))
        m1 = jnp.sum(m1, axis=0, keepdims=True) / dim
        m2 = jnp.sum(m2, axis=0, keepdims=True) / dim

        def second(i, carry):
            at = chunk_rows(i)
            normed = (xs[at, :] - mean) * inverse
            acc[at, :] = d_res_ref[at, :] + inverse * (acc[at, :] * prm_ref[at, 15:16] - m1 - normed * m2)
            return carry

        lax.fori_loop(0, dim // CHUNK, second, 0)

        rows = seqs * chans

        def scatter(d, carry):
            at = pl.ds(pl.multiple_of(d * chans, 8), chans)
            tail_ref[d, :rows, :] = stacked(acc[at, :], seqs).astype(bf16)
            totals = [sums0_ref[d]] + [sums[n, d] for n in range(sums.shape[0])]
            totals += [padded_totals(folds[q, at, :], width)[0] for q in range(2)]
            tail_ref[d, rows : rows + SUM_ROWS, :] = as_rows(totals, SUM_ROWS)
            return carry

        lax.fori_loop(0, devices, scatter, 0)


def back(table, d_mixed, pair, heads, projx, own, other, prm, xn, x, stat, d_res, acc0, sums0, seqs):
    devices, rows, width = x.shape
    dim, cols = xn.shape
    chans = dim // devices
    sd = jax.ShapeDtypeStruct
    pieces = -(-2 * (2 + KS) * chans // width)
    out = (
        sd((devices, rows + SUM_ROWS, width), bf16),
        sd((devices, 2 * chans, dim), bf16),
    )
    return chip_call(
        100,
        lambda *refs: back_body(seqs, *refs),
        table,
        devices // 2,
        (d_mixed, pair, heads, projx, own, other, prm, xn, x, stat, d_res, acc0, sums0),
        [by_chip(a) for a in (d_mixed, pair, heads, projx)]
        + [by_turn(own), by_turn(other), whole(prm), whole(xn), whole(x)]
        + [whole(a) for a in (stat, d_res, acc0, sums0)],
        out,
        (whole(out[0]), by_chip(out[1])),
        [
            pltpu.VMEM((dim, cols), f32), pltpu.VMEM((dim, cols), f32), pltpu.VMEM((2, dim, LANE), f32),
            pltpu.VMEM((pieces, devices, 8, width), f32),
        ],
    )


def position_table():
    places = np.arange(LMAX)
    orders = np.arange(1, (EMB - 1) // 2 + 1)
    turns = 2.0 * math.pi * ((orders[:, None] * places[None, :]) % LMAX) / LMAX
    ramp = places[None, :] / (LMAX - 1)
    return np.concatenate([ramp, np.cos(turns), -np.sin(turns)], axis=0).astype(np.float32)


FEAT = position_table()


def mm(a, b, dims):
    return lax.dot_general(a, b, (dims, ((), ())), precision=highest, preferred_element_type=f32)


NN = ((1,), (0,))
TN = ((0,), (0,))
NT = ((1,), (1,))


def mm_split(a, b, dims):
    a_upper, b_upper = a.astype(bf16), b.astype(bf16)
    a_lower, b_lower = (a - a_upper.astype(f32)).astype(bf16), (b - b_upper.astype(f32)).astype(bf16)
    return mm16(a_upper, b_upper, dims) + mm16(a_lower, b_upper, dims) + mm16(a_upper, b_lower, dims)


def filter_back_body(d_ref, raw_ref, fall_ref, h1_ref, h2_ref, c1_ref, c2_ref, pre1_ref, pre2_ref, feat_ref, mid_ref, last_ref, rate_ref,
                     g_in_ref, g_mid_ref, g_last_ref, g_rows_ref, g_decay_ref):
    chans = d_ref.shape[0]
    d = d_ref[...]
    q = d * (fall_ref[...] + decay_floor)
    g_last_ref[...] = mm_split(h2_ref[...], q, NT)
    decay = folded(d * raw_ref[...] * fall_ref[...] * feat_ref[0:1, :])
    g_decay_ref[...] = -jnp.sum(decay, axis=1, keepdims=True)
    u2 = mm_split(last_ref[...], q, NN) * c2_ref[...]
    rate = rate_ref[...]
    fu2 = rate * u2
    u1 = mm_split(mid_ref[...], fu2, NN) * c1_ref[...]
    fu1 = rate * u1
    g_in_ref[...] = mm_split(feat_ref[...], fu1, NT)
    g_mid_ref[...] = mm_split(h1_ref[...], fu2, NT)
    rows = jnp.concatenate([folded(fu1), folded(fu2), folded(u2 * pre2_ref[...] + u1 * pre1_ref[...])], axis=0)
    extra = jnp.zeros((-rows.shape[0] % LANE, LANE), f32)
    g_rows_ref[...] = row_totals(jnp.concatenate([rows, extra], axis=0))


def filter_back(*args):
    chans, ford, taps = args[0].shape[0], args[3].shape[0], args[9].shape[0]
    sd = jax.ShapeDtypeStruct
    out = (sd((taps, ford), f32), sd((ford, ford), f32), sd((ford, chans), f32), sd((8, -(-3 * ford // LANE) * LANE), f32), sd((chans, 1), f32))
    return whole_call(0.01, filter_back_body, out, [], *args)


def mm16(a, b, dims):
    return lax.dot_general(a, b, (dims, ((), ())), preferred_element_type=f32)


def ring_of(chips):
    zs = 4
    ys = chips // zs
    order = [(z, 0) for z in range(zs)]
    for y in range(1, ys):
        order += [(z, y) for z in (range(zs - 1, 0, -1) if y % 2 else range(1, zs))]
    order += [(0, y) for y in range(ys - 1, 0, -1)]
    return [z * ys + y for z, y in order]


def after(values, *others):
    return lax.optimization_barrier((values,) + others)[0]


def ring_hop(values, ring, by):
    chips = len(ring)
    moves = [(2 * ring[p] + q, 2 * ring[(p + by) % chips] + q) for p in range(chips) for q in range(2)]
    return lax.ppermute(values, "chan", moves)


class RingGather:
    def __init__(self, shard, ring):
        self.ring, self.hops = ring, len(ring) // 2
        self.cut = shard.shape[0] // 32 * 16
        self.behind, self.ahead = [shard], [shard]
        self.far = None

    def advance(self, upto, *others):
        while len(self.behind) <= min(upto, self.hops - 1):
            first, second = self.behind[-1], self.ahead[-1]
            if others:
                first, second = after(first, *others), after(second, *others)
            self.behind.append(ring_hop(first, self.ring, 1))
            self.ahead.append(ring_hop(second, self.ring, -1))
        if upto == self.hops:
            first, second = self.behind[-1][: self.cut], self.ahead[-1][self.cut :]
            if others:
                first, second = after(first, *others), after(second, *others)
            self.far = jnp.concatenate([ring_hop(first, self.ring, 1), ring_hop(second, self.ring, -1)], axis=0)

    def shards(self):
        return self.behind + self.ahead[1:] + [self.far]


def both_cores(shards):
    own = stack(shards)
    return own, lax.ppermute(own, "chan", [(i, i ^ 1) for i in range(2 * len(shards))])


def stack_body(*refs):
    for i, ref in enumerate(refs[:-1]):
        refs[-1][i] = ref[...]


def stack(shards):
    out = jax.ShapeDtypeStruct((len(shards),) + shards[0].shape, shards[0].dtype)
    return whole_call(0.01, stack_body, out, [], *shards)


def turn_table(ring):
    chips = len(ring)
    steps = [0] + [-k for k in range(1, chips // 2)] + [k for k in range(1, chips // 2)] + [chips // 2]
    table = np.zeros((chips, chips), np.int32)
    for p, chip in enumerate(ring):
        table[chip] = [ring[(p + k) % chips] for k in steps]
    return table


def exchange(values):
    return lax.all_to_all(values, "chan", split_axis=0, concat_axis=0, tiled=True)


def on_device(
    layer_in,
    seq_lengths,
    ln1_gain,
    first_norm_bias,
    in_weight,
    in_bias,
    short_weight,
    short_bias,
    filt_in,
    filt_in_bias,
    filt_mid,
    filt_mid_bias,
    sine_freq,
    filt_out,
    decay_rate,
    conv_bias,
    out_weight,
    out_bias,
    ln2_gain,
    second_norm_bias,
    up_weight,
    up_bias,
    down_weight,
    down_bias,
    cotangent,
):
    seqs, chans, _ = layer_in.shape
    devices = lax.axis_size("chan")
    groups = lax.axis_size("batch")
    width = LMAX // devices
    dim = chans * devices
    cols = seqs * width
    hid = up_weight.shape[0]
    ford = filt_mid.shape[0]
    place = lax.axis_index("chan")

    def to_blocks(values):
        return (
            values.reshape(seqs, chans, devices, width)
            .transpose(2, 0, 1, 3)
            .reshape(devices, seqs * chans, width)
        )

    def from_blocks(blocks):
        return (
            blocks.reshape(devices, seqs, chans, width)
            .transpose(1, 2, 0, 3)
            .reshape(seqs, chans, LMAX)
        )

    small = jnp.concatenate(
        [
            in_bias,
            short_bias,
            short_weight.reshape(3 * KS, chans),
            jnp.stack([ln1_gain, first_norm_bias, ln2_gain, second_norm_bias, out_bias, down_bias]),
            up_bias.reshape(hid // chans, chans),
        ],
        axis=0,
    )
    small = jnp.pad(small, ((0, PRM - small.shape[0]), (0, LANE - chans)))
    small = jnp.concatenate([small[:SMALL], small[SMALL:], jnp.zeros((SMALL, dim - 2 * LANE), bf16)], axis=1)
    in_rows = in_weight.transpose(1, 2, 0).reshape(3 * chans, dim)
    ring = ring_of(devices // 2)
    chips = devices // 2
    core = place % 2
    batch = lax.axis_index("batch")
    swap = [(0, 1), (1, 0)]
    partner = [(i, i ^ 1) for i in range(devices)]
    turns = lax.dynamic_index_in_dim(jnp.asarray(turn_table(ring)), place // 2, 0, False)
    table = jnp.concatenate(
        [turns, jnp.stack([core, place]).astype(jnp.int32), seq_lengths, batch.astype(jnp.int32).reshape(1)]
    )
    late = [up_weight, down_weight, out_weight]
    stepped = groups == 2 and chips == 8 and dim % (2 * LANE) == 0
    beside = [(i, i ^ 2) for i in range(devices)]
    along = [list(range(k, devices, 4)) for k in range(4)]

    def to_partner(values):
        return lax.ppermute(values, "chan", partner)

    if stepped:
        late = [lax.dynamic_slice_in_dim(a, batch * (a.shape[0] // 2), a.shape[0] // 2, 0) for a in late]
        late = jnp.concatenate(late, axis=0)
        near = lax.all_gather(late, "chan", axis=0, axis_index_groups=along)
    else:
        late = jnp.concatenate(late, axis=0)
        late = lax.all_gather(late, "chan", axis=0).reshape((chips, 2) + late.shape)
    first = RingGather(after(jnp.concatenate([small, in_rows], axis=0), late) if stepped else jnp.concatenate([small, in_rows], axis=0), ring)
    first.advance(chips // 8)
    x = exchange(to_blocks(layer_in))
    rows = seqs * chans
    xh = lax.ppermute(x[:, :rows, width - LANE :], "chan", [(i, i + 1) for i in range(devices - 1)])

    feat = jnp.asarray(FEAT)
    ramp = feat[0:1]
    rate = sine_freq[:, None]
    pre1 = mm(filt_in, feat, TN) + filt_in_bias[:, None]
    h1, c1 = jnp.sin(rate * pre1), jnp.cos(rate * pre1)
    pre2 = mm(filt_mid, h1, TN) + filt_mid_bias[:, None]
    h2, c2 = jnp.sin(rate * pre2), jnp.cos(rate * pre2)
    raw = mm(filt_out, h2, TN)
    falling = jnp.exp(-ramp * decay_rate[:, None])
    first.advance(chips // 4, h1)
    filt = raw * (falling + decay_floor)
    first.advance(3 * chips // 8, filt, x)
    filt_spec = filter_spectrum(filt)
    first.advance(chips // 2, filt_spec)
    in_own, in_other = both_cores(first.shards())
    bias_col = conv_bias[:, None]

    prm, xn1, stat1, gate, pair, projx0, projx, mixed, heads = front(
        table, x, xh, in_own, in_other, filt_spec, seqs
    )
    mixed_chan = exchange(mixed)
    cot = exchange(after(to_blocks(cotangent), mixed_chan))
    if stepped:
        near = after(near, mixed)
        far = lax.ppermute(near, "chan", beside)
        near_across = lax.ppermute(near, "batch", swap)
        near_other = to_partner(near)
    backward_hop = [(i + 1, i) for i in range(devices - 1)]
    heads = lax.ppermute(heads, "chan", backward_hop)
    conv_chan, mixed_spec = conv_forward(mixed_chan, filt_spec, bias_col, seqs)
    conv = exchange(after(conv_chan, near_across, cot, heads) if stepped else conv_chan)
    if stepped:
        far, near_across = after(far, conv_chan), after(near_across, conv_chan)
        far_across = lax.ppermute(far, "batch", swap)
        far_other, near_across_other = to_partner(far), to_partner(near_across)
        far_across_other = to_partner(far_across)
        matrices = [
            [[near, far], [near_other, far_other]],
            [[near_across, far_across], [near_across_other, far_across_other]],
        ]
        z = lax.iota(jnp.int32, 4) * 2
        y = (place // 2 % 2).astype(jnp.int32)
        order = jnp.concatenate([z + y, z + 1 - y])
    else:
        matrices = [[[lax.dynamic_index_in_dim(late, core, 1, False)], [lax.dynamic_index_in_dim(late, 1 - core, 1, False)]]]
        order = lax.iota(jnp.int32, chips)
    order = jnp.concatenate([order, table[chips:]])

    results = middle(order, conv, x, cot, gate.reshape(dim, cols), matrices, prm, hid, seqs)
    layer, d_conv, d_res, p0, p0h = results[:5]
    d_conv_chan = exchange(d_conv)
    p0h = lax.ppermute(p0h, "chan", backward_hop)

    def added(*values):
        return sum(v.astype(f32) for v in values).astype(bf16)

    if stepped:
        near_mine, far_mine = (results[5], results[7]), (results[6], results[8])
        near_theirs, far_theirs = (results[9], results[11]), (results[10], results[12])
        far_theirs = added(far_theirs[0], to_partner(far_theirs[1]))
        d_conv_chan = after(d_conv_chan, far_theirs)
        far_theirs = lax.ppermute(far_theirs, "batch", swap)
        near_theirs = added(near_theirs[0], to_partner(after(near_theirs[1], d_conv_chan)))
        near_theirs = lax.ppermute(after(near_theirs, far_theirs), "batch", swap)
        far_mine = far_mine[0], to_partner(after(far_mine[1], d_conv_chan))
        near_mine = near_mine[0], to_partner(after(near_mine[1], d_conv_chan))
    else:
        early = added(results[5], to_partner(results[6]))

    if groups == 2:
        same_core = [list(range(q, devices, 2)) for q in range(2)]
    else:
        same_core = [[b * devices + c for b in range(groups) for c in range(q, devices, 2)] for q in range(2)]

    def batch_total(values):
        return values + lax.ppermute(values, "batch", swap) if groups == 2 else lax.psum(values, "batch")

    def over_batch(table):
        if groups != 2:
            return lax.psum_scatter(table.astype(f32), "batch", scatter_dimension=1, tiled=True)
        part = dim // 2
        axis = table.ndim - 1
        mine = lax.axis_index("batch") * part
        theirs = lax.dynamic_slice_in_dim(table, part - mine, part, axis)
        kept = lax.dynamic_slice_in_dim(table, mine, part, axis)
        return kept.astype(f32) + lax.ppermute(theirs, "batch", swap).astype(f32)

    def over_chip(table):
        table = table.reshape((devices // 2, 2) + table.shape[1:])
        own = lax.dynamic_index_in_dim(table, core, 1, False)
        theirs = lax.dynamic_index_in_dim(table, 1 - core, 1, False)
        return (own.astype(f32) + lax.ppermute(theirs, "chan", partner).astype(f32)).astype(bf16)

    def over_groups(both):
        return over_batch(both).astype(bf16) if groups == 2 else both

    def over_chips(both):
        rows = both.shape[1]
        if groups == 2:
            both = lax.all_to_all(
                both, "chan", split_axis=0, concat_axis=0, tiled=True, axis_index_groups=same_core
            )
        else:
            both = both.reshape(devices // 2, rows, groups, dim // groups).transpose(2, 0, 1, 3)
            both = lax.all_to_all(
                both.reshape(groups * devices // 2, rows, dim // groups),
                ("batch", "chan"), split_axis=0, concat_axis=0, tiled=True, axis_index_groups=same_core,
            )
        return jnp.sum(both.astype(f32), axis=0)

    d_mixed_chan, d_filter, g_conv_bias = conv_backward(
        d_conv_chan, mixed_chan, mixed_spec, filt_spec, bias_col, seqs
    )
    if stepped:
        d_mixed_chan = after(d_mixed_chan, far_theirs, p0h)
        far_mine = added(*far_mine, far_theirs)
        p0h = after(p0h, far_mine)
    g_in0, sums0, acc0 = back_gate(
        table, p0.reshape(devices, chans, cols), p0h, projx0, in_own, in_other, prm, xn1, seqs
    )
    g_in0 = over_chip(g_in0)
    d_mixed = exchange(d_mixed_chan)
    layer = exchange(after(layer, d_mixed))
    if stepped:
        far_mine = lax.ppermute(far_mine, "chan", beside)
    else:
        chan_groups = [list(range(q, devices, 2)) for q in range(2)]
        early = lax.psum_scatter(early, "chan", scatter_dimension=0, tiled=True, axis_index_groups=chan_groups)[0]

    tail, g_in = back(
        table, d_mixed, pair, heads, projx, in_own, in_other, prm, xn1, x, stat1, d_res, acc0, sums0, seqs
    )
    if stepped:
        tail = after(tail, far_mine, near_theirs, layer)
        early = added(*near_mine, near_theirs, far_mine)
        early = after(early, g_in)
        d_filter = after(d_filter, early)
    tail = exchange(tail)
    g_filt_in, g_filt_mid, g_filt_out, g_rows, g_decay = filter_back(
        d_filter, raw, falling, h1, h2, c1, c2, pre1, pre2, feat, filt_mid, filt_out, rate
    )
    shared = [g_filt_in.reshape(-1), g_filt_mid.reshape(-1), g_rows[0, : 3 * ford]]
    total = batch_total(
        jnp.concatenate(shared + [g_conv_bias[:, 0], g_decay[:, 0], g_filt_out.reshape(-1)])
    )
    g_in = over_groups(jnp.concatenate([g_in0, over_chip(g_in)], axis=1))
    if stepped:
        early = lax.psum_scatter(early, "chan", scatter_dimension=0, tiled=True, axis_index_groups=along)[0]

    cut = [0]

    def take(*shape):
        n = math.prod(shape)
        part = total[cut[0] : cut[0] + n].reshape(shape)
        cut[0] += n
        return part

    shared = take(sum(v.shape[0] for v in shared))
    shared = shared + lax.ppermute(shared, "chan", partner)
    g_conv_b, g_decay_rate, g_filt_last = take(chans), take(chans), take(ford, chans)
    n_shared = shared.shape[0]
    if groups != 2:
        shared = shared / groups
    line = g_in.shape[2]
    shared = jnp.pad(shared.astype(bf16), (0, -n_shared % (8 * line))).reshape(1, -1, line)
    shared = jnp.broadcast_to(shared, (devices // 2,) + shared.shape[1:])
    mine = 3 * chans
    in_grad = over_chips(jnp.concatenate([g_in, shared], axis=1))
    if groups == 2:
        total = in_grad[mine:].reshape(-1)
    else:
        total = lax.all_gather(in_grad[mine:], "batch", axis=1, tiled=True).reshape(-1)
    in_grad = in_grad[:mine]
    cut[0] = 0
    g_filt_in, g_filt_mid = take(EMB, ford), take(ford, ford)
    g_filt_in_bias, g_filt_mid_bias, g_sine = take(ford), take(ford), take(ford)

    early = after(early, in_grad)
    early = early.astype(f32) if stepped else over_batch(early)
    up_grad, down_grad, out_grad = early[:hid], early[hid : 2 * hid], early[2 * hid :]

    grad_blocks, out_blocks = tail[:, :rows], layer[:, :rows]
    sums = jnp.concatenate([layer[:, rows:], tail[:, rows:]], axis=1)
    sums = batch_total(jnp.sum(sums.astype(f32), axis=0))
    sums = sums[0::2] + sums[1::2]
    g_gain2, g_shift2, g_out_b, g_down_b = (sums[i, :chans] for i in range(4))
    g_up_b = sums[4, :hid]
    at = SUM_ROWS // 2
    count = (2 + KS) * chans
    pieces = -(-2 * count // width)
    short0 = sums[at, :count].reshape(2 + KS, 1, chans)
    short = sums[at + 1 : at + 1 + pieces].reshape(-1)[: 2 * count].reshape(2 + KS, 2, chans)
    short = jnp.concatenate([short0, short], axis=1)
    g_in_bias, g_short_bias, g_short_weight = short[0], short[1], short[2:]
    g_gain1, g_shift1 = (sums[at + 1 + pieces + i, :chans] for i in range(2))

    return (
        from_blocks(out_blocks),
        from_blocks(grad_blocks).astype(f32),
        g_gain1,
        g_shift1,
        in_grad.reshape(3, chans, dim // groups).transpose(2, 0, 1),
        g_in_bias,
        g_short_weight,
        g_short_bias,
        g_filt_in,
        g_filt_in_bias,
        g_filt_mid,
        g_filt_mid_bias,
        g_sine,
        g_filt_last,
        g_decay_rate,
        g_conv_b,
        out_grad,
        g_out_b,
        g_gain2,
        g_shift2,
        up_grad,
        g_up_b,
        down_grad,
        g_down_b,
    )


def solution(mesh):
    token = P("batch", "chan", None)
    chan = P("chan")
    rows = P("chan", None)
    two = P(None, "chan")
    three = P(None, None, "chan")
    in_specs = (
        token, P("batch"), chan, chan, three, two, three, two, P(), P(), P(), P(), P(), two, chan, chan,
        rows, chan, chan, chan, rows, chan, rows, chan, token,
    )
    table = P("chan", "batch")
    out_specs = (
        token, token, chan, chan, P("batch", None, "chan"), two, three, two, P(), P(), P(), P(), P(), two,
        chan, chan, table, chan, chan, chan, table, chan, table, chan,
    )
    return jax.shard_map(
        on_device, mesh=mesh, in_specs=in_specs, out_specs=out_specs, check_vma=False
    )
```
